32 devices in a mesh: wq: 16 (over z, x, core), np: 2 (over y).
Axes of the slice: x: 2, y: 2, z: 4, core: 2. Of those that a mesh axis runs over, the one named last changes fastest.
Arguments:
- q_embed: bfloat16 [16384, 768], P(('wq', 'np')), may hold values from -6 to 6
- p_embed: bfloat16 [49152, 768], P(('wq', 'np')), may hold values from -6 to 6
- q_len: int32 [256], P(('wq', 'np')), may hold values from 16 to 64, as said below
- p_len: int32 [192], P(('wq', 'np')), may hold values from 64 to 256, as said below
- q_set: int32 [256], P(('wq', 'np')), may hold values from 0 to 3, as said below
- p_set: int32 [192], P(('wq', 'np')), may hold values from 0 to 3
- gold: int32 [256], P(('wq', 'np')), may hold values from 0 to 191, as said below
- query_key_value_weight: bfloat16 [2, 768, 2304], P(None, 'wq', 'np'), may hold values from -0.21875 to 0.21875
- attention_output_weight: bfloat16 [2, 768, 768], P(None, 'wq', 'np'), may hold values from -0.625 to 0.625
- up_weight: bfloat16 [2, 768, 3072], P(None, 'wq', 'np'), may hold values from -0.21875 to 0.21875
- down_weight: bfloat16 [2, 3072, 768], P(None, 'wq', 'np'), may hold values from -0.109375 to 0.109375
- vectors: bfloat16 [2, 8, 768], P(None, 'np', 'wq')
- hidden_bias: bfloat16 [2, 3072], P(None, ('wq', 'np')), may hold values from -1.5 to 1.5
Outputs:
- loss: float32 [], replicated
- q_out: bfloat16 [16384, 768], P(('wq', 'np'))
- p_out: bfloat16 [49152, 768], P(('wq', 'np'))
- grad_q_embed: float32 [16384, 768], P(('wq', 'np'))
- grad_p_embed: float32 [49152, 768], P(('wq', 'np'))
- grad_w_qkv: float32 [2, 768, 2304], P(None, 'wq', 'np')
- grad_w_out: float32 [2, 768, 768], P(None, 'wq', 'np')
- grad_w_in: float32 [2, 768, 3072], P(None, 'wq', 'np')
- grad_w_back: float32 [2, 3072, 768], P(None, 'wq', 'np')
- grad_vectors: float32 [2, 8, 768], P(None, 'np', 'wq')
- grad_b_in: float32 [2, 3072], P(None, ('wq', 'np'))
The draws below stay inside these ranges and needn't reach their ends.
Inputs may be any that keep to these rules, and one draw needn't show every extreme that they name: `q_len`: some question has all 64 tokens. `p_len`: some passage has all 256 tokens. `q_set`: equal to the dataset of the question's gold passage. `gold`: an index among all 192 passages.
All inputs are finite; a program needn't handle non-finite values.
Results may differ from the reference program's by a relative error of at most 0.024.
Values may be sent and summed in bfloat16 or wider, within the bound.
A program may use at most 320 MiB of HBM per device.

```python
import math
import jax
import jax.numpy as jnp
from jax import lax

D = 768
HEADS = 12
FF = 3072
LQ = 64
LP = 256
NSETS = 4
NQ = 256
NP = 192


def sets_and_gold(key):
    passage_sets = jax.random.randint(jax.random.fold_in(key, 101), (NP,), 0, NSETS)
    gold_index = jax.random.randint(jax.random.fold_in(key, 102), (NQ,), 0, NP)
    return (passage_sets.astype(jnp.int32), gold_index.astype(jnp.int32))


def draw_p_set(key, part):
    return sets_and_gold(key)[0]


def draw_gold(key, part):
    return sets_and_gold(key)[1]


def draw_q_set(key, part):
    passage_sets, gold_index = sets_and_gold(key)
    return passage_sets[gold_index].astype(jnp.int32)


def ragged_lengths(key, seq_total, longest):
    drawn = jax.random.randint(jax.random.fold_in(key, 1), (seq_total,), longest // 4, longest + 1)
    chosen = jax.random.randint(jax.random.fold_in(key, 2), (), 0, seq_total)
    return jnp.where(jnp.arange(seq_total) == chosen, longest, drawn).astype(jnp.int32)


def draw_q_len(key, part):
    key = jax.random.fold_in(key, 3)
    return ragged_lengths(key, NQ, LQ)


def draw_p_len(key, part):
    key = jax.random.fold_in(key, 4)
    return ragged_lengths(key, NP, LP)


def draw_vectors(key, part):
    key = jax.random.fold_in(key, 5)
    values = 0.2 * jax.random.normal(key, (2, 8, D), jnp.float32)
    row_index = jnp.arange(8)[None, :, None]
    gain_rows = (row_index == 3) | (row_index == 6)
    return jnp.where(gain_rows, 1.0 + 0.5 * values, values).astype(jnp.bfloat16)


def levels(stream_key, shape, split, low, high):
    factor_of, own = 1.0, jax.random.fold_in(stream_key, 6)
    for dim, shards_of in split:
        heights = jnp.exp(jax.random.uniform(jax.random.fold_in(own, dim), (shards_of,), jnp.float32, low / len(split), high / len(split)))
        factor_of = factor_of * jnp.repeat(heights, shape[dim] // shards_of).reshape([-1 if axis == dim else 1 for axis in range(len(shape))])
    return factor_of


def scatter_about(rng, dims, deviation, limit, cuts=(), held_as=jnp.bfloat16):
    array = jax.random.normal(rng, dims, jnp.float32) * deviation
    if len(cuts) > 0:
        array = levels(rng, dims, cuts, -0.22, 0.18) * array
    return jnp.clip(array, min=-limit, max=limit).astype(held_as)


def setup_inputs(seed: int = 0) -> dict:
    seeds = jax.random.split(jax.random.key(seed), 14)
    q_embed = scatter_about(seeds[0], (NQ * LQ, D), 1.0, 6.0, ((0, 32),))
    p_embed = scatter_about(seeds[1], (NP * LP, D), 1.0, 6.0, ((0, 32),))
    q_len = draw_q_len(jax.random.fold_in(seeds[13], 71), 0)
    p_len = draw_p_len(jax.random.fold_in(seeds[13], 71), 0)
    q_set = draw_q_set(jax.random.fold_in(seeds[13], 71), 0)
    p_set = draw_p_set(jax.random.fold_in(seeds[13], 71), 0)
    gold = draw_gold(jax.random.fold_in(seeds[13], 71), 0)
    query_key_value_weight = scatter_about(seeds[7], (2, D, 3 * D), D ** -0.5, 0.21875, ((1, 16), (2, 2)))
    attention_output_weight = scatter_about(seeds[8], (2, D, D), (D // 8) ** -0.5, 0.625, ((1, 16), (2, 2)))
    up_weight = scatter_about(seeds[9], (2, D, FF), D ** -0.5, 0.21875, ((1, 16), (2, 2)))
    down_weight = scatter_about(seeds[10], (2, FF, D), FF ** -0.5, 0.109375, ((1, 16), (2, 2)))
    vectors = draw_vectors(jax.random.fold_in(seeds[13], 71), 0)
    hidden_bias = scatter_about(seeds[12], (2, FF), 0.3, 1.5, ((1, 32),))
    return {"q_embed": q_embed, "p_embed": p_embed, "q_len": q_len, "p_len": p_len, "q_set": q_set, "p_set": p_set, "gold": gold, "query_key_value_weight": query_key_value_weight, "attention_output_weight": attention_output_weight, "up_weight": up_weight, "down_weight": down_weight, "vectors": vectors, "hidden_bias": hidden_bias}


@jax.custom_vjp
def reduced_copy(v):
    return lax.optimization_barrier(v.astype(jnp.bfloat16)).astype(jnp.float32)

@jax.custom_vjp
def reduced_backward(v):
    return v

def low_keep(v):
    return (reduced_copy(v), None)

def low_pass(kept, grad):
    return (grad,)

def back_keep(v):
    return (v, None)

def back_low(kept, grad):
    return (reduced_copy(grad),)
reduced_copy.defvjp(low_keep, low_pass)
reduced_backward.defvjp(back_keep, back_low)
FULL_PRECISION = lax.Precision.HIGHEST
NEGATIVE = -1e+30
EPSILON = 1e-12

def layer_norm(inputs, gain_row, offset):
    centred = inputs - lax.optimization_barrier(jnp.mean(inputs, axis=-1, keepdims=True))
    spread = lax.optimization_barrier(jnp.mean(centred * centred, axis=-1, keepdims=True))
    return centred * lax.rsqrt(spread + EPSILON) * gain_row + offset

def smooth_gate(values):
    return jax.nn.gelu(values, approximate=True)

def encode(token_rows, lengths, query_key_value_weight, attention_output_weight, up_weight, down_weight, vectors, hidden_bias):
    seq_count, seq_length, model_width = token_rows.shape
    head_size = model_width // HEADS
    head_shape = (seq_count, seq_length, HEADS, head_size)
    projected_rows = jnp.einsum('ryh,hz->ryz', token_rows, query_key_value_weight, precision=FULL_PRECISION)
    queries = reduced_backward(reduced_copy(projected_rows[..., :model_width] + vectors[0]))
    keys_low = reduced_backward(reduced_copy(projected_rows[..., model_width:2 * model_width]))
    values = reduced_backward(reduced_copy(projected_rows[..., 2 * model_width:] + vectors[1]))
    scores = jnp.einsum('sqhc,skhc->shqk', queries.reshape(head_shape), keys_low.reshape(head_shape), precision=FULL_PRECISION)
    scores = reduced_backward(scores * head_size ** (-0.5))
    live_mask = jnp.arange(seq_length)[None, :] < lengths[:, None]
    scores = jnp.where(live_mask[:, None, None, :], scores, NEGATIVE)
    totals = jax.nn.logsumexp(scores, axis=-1, keepdims=True)
    soft_low = reduced_copy(jnp.exp(scores - totals))
    attended_tokens = jnp.einsum('shqk,skhc->sqhc', soft_low, values.reshape(head_shape), precision=FULL_PRECISION)
    attended_tokens = reduced_backward(reduced_copy(attended_tokens.reshape(seq_count, seq_length, model_width)))
    residual_branch = reduced_backward(jnp.einsum('ryh,hz->ryz', attended_tokens, attention_output_weight, precision=FULL_PRECISION) + vectors[2])
    first_normed = layer_norm(token_rows + residual_branch, vectors[3], vectors[4])
    hidden_rows = reduced_backward(jnp.einsum('wmy,yh->wmh', reduced_copy(first_normed), up_weight, precision=FULL_PRECISION) + hidden_bias)
    activated_hidden = reduced_copy(smooth_gate(hidden_rows))
    feedforward_output = reduced_backward(jnp.einsum('ruh,hj->ruj', activated_hidden, down_weight, precision=FULL_PRECISION) + vectors[5])
    return layer_norm(first_normed + feedforward_output, vectors[6], vectors[7])

def encode_all(token_rows, lengths, params):
    seq_count, seq_length, model_width = token_rows.shape
    group_size = math.gcd(seq_count, max(1, 4096 // seq_length))
    blocks = token_rows.reshape(seq_count // group_size, group_size, seq_length, model_width)
    spans = lengths.reshape(seq_count // group_size, group_size)
    encode_saved = jax.checkpoint(encode)

    def advance(carried, pieces):
        return (carried, encode_saved(pieces[0], pieces[1], *params))
    unused_carry, encoded = lax.scan(advance, jnp.zeros((), jnp.float32), (blocks, spans))
    return encoded.reshape(seq_count, seq_length, model_width)

def reference(q_embed, p_embed, q_len, p_len, q_set, p_set, gold, query_key_value_weight, attention_output_weight, up_weight, down_weight, vectors, hidden_bias):
    floats = tuple((member.astype(jnp.float32) for member in (q_embed, p_embed, query_key_value_weight, attention_output_weight, up_weight, down_weight, vectors, hidden_bias)))

    def forward(q_tokens, p_tokens, qkv_all, out_all, in_all, back_all, vector_all, bias_all):
        q_params = (qkv_all[0], out_all[0], in_all[0], back_all[0], vector_all[0], bias_all[0])
        p_params = (qkv_all[1], out_all[1], in_all[1], back_all[1], vector_all[1], bias_all[1])
        q_encoded = encode_all(q_tokens.reshape(NQ, LQ, D), q_len, q_params)
        p_encoded = encode_all(p_tokens.reshape(NP, LP, D), p_len, p_params)
        q_heads = reduced_copy(q_encoded[:, 0, :])
        p_heads = reduced_copy(p_encoded[:, 0, :])
        similar = reduced_backward(jnp.dot(q_heads, p_heads.T, precision=FULL_PRECISION, preferred_element_type=jnp.float32) * D ** (-0.5))
        column = jnp.arange(NP)
        is_gold = column[None, :] == gold[:, None]
        usable = (q_set[:, None] == p_set[None, :]) | is_gold
        masked = jnp.where(usable, similar, NEGATIVE)
        log_total = jax.nn.logsumexp(masked, axis=1)
        gold_score = lax.optimization_barrier(jnp.sum(jnp.where(is_gold, similar, 0.0), axis=1))
        loss_sum = jnp.sum(log_total - gold_score)
        return (loss_sum, q_encoded.reshape(NQ * LQ, D), p_encoded.reshape(NP * LP, D))
    outputs, back_fn = jax.vjp(forward, *floats)
    loss_sum, q_out, p_out = outputs
    grads = back_fn((jnp.ones_like(loss_sum), jnp.zeros_like(q_out), jnp.zeros_like(p_out)))
    return (loss_sum / NQ, q_out.astype(jnp.bfloat16), p_out.astype(jnp.bfloat16), grads[0], grads[1], grads[2], grads[3], grads[4], grads[5], grads[6], grads[7])
```

```python
import math

import jax
import jax.numpy as jnp
from jax import lax
from jax.sharding import PartitionSpec as P

HEADS = 12


EPSILON = 1e-12
NEGATIVE = -1e30


def layer_norm(inputs, gain_row, offset):
    centred = inputs - jnp.mean(inputs, axis=-1, keepdims=True)
    spread = jnp.mean(centred * centred, axis=-1, keepdims=True)
    return centred * lax.rsqrt(spread + EPSILON) * gain_row + offset


def smooth_gate(values):
    return jax.nn.gelu(values, approximate=True)


def gather_weights(
    query_key_value_weight, attention_output_weight, up_weight, down_weight, vectors, hidden_bias
):
    np_parts = (
        lax.all_gather(query_key_value_weight, "np", axis=2, tiled=True),
        lax.all_gather(attention_output_weight, "np", axis=2, tiled=True),
        lax.all_gather(up_weight, "np", axis=2, tiled=True),
        lax.all_gather(down_weight, "np", axis=2, tiled=True),
        lax.all_gather(vectors, "np", axis=1, tiled=True),
        lax.all_gather(hidden_bias, "np", axis=1, tiled=True),
    )
    return (
        lax.all_gather(np_parts[0], "wq", axis=1, tiled=True),
        lax.all_gather(np_parts[1], "wq", axis=1, tiled=True),
        lax.all_gather(np_parts[2], "wq", axis=1, tiled=True),
        lax.all_gather(np_parts[3], "wq", axis=1, tiled=True),
        lax.all_gather(np_parts[4], "wq", axis=2, tiled=True),
        lax.all_gather(np_parts[5], "wq", axis=1, tiled=True),
    )


def head_split(matrix, seq_count):
    row_count, model_width = matrix.shape
    return matrix.reshape(seq_count, row_count // seq_count, HEADS, model_width // HEADS)


def attention_scores(queries, keys_low, lengths):
    seq_count = lengths.shape[0]
    split_q = head_split(queries, seq_count)
    scores = jnp.einsum(
        "sqhc,skhc->shqk",
        split_q,
        head_split(keys_low, seq_count),
        preferred_element_type=jnp.float32,
    )
    scores = scores * split_q.shape[3] ** (-0.5)
    live_mask = jnp.arange(split_q.shape[1])[None, :] < lengths[:, None]
    return jnp.where(live_mask[:, None, None, :], scores, NEGATIVE)


def first_rows(matrix, seq_count):
    row_count, width = matrix.shape
    return matrix.reshape(seq_count, row_count // seq_count, width)[:, 0, :]


def encode_forward(token_rows, lengths, weights):
    (
        query_key_value_weight,
        attention_output_weight,
        up_weight,
        down_weight,
        vectors,
        hidden_bias,
    ) = weights
    row_count, model_width = token_rows.shape
    seq_count = lengths.shape[0]
    vec_f32 = vectors.astype(jnp.float32)
    projected_rows = jnp.dot(token_rows, query_key_value_weight, preferred_element_type=jnp.float32)
    queries = (projected_rows[:, :model_width] + vec_f32[0]).astype(jnp.bfloat16)
    keys_low = projected_rows[:, model_width : 2 * model_width].astype(jnp.bfloat16)
    values = (projected_rows[:, 2 * model_width :] + vec_f32[1]).astype(jnp.bfloat16)
    scores = attention_scores(queries, keys_low, lengths)
    totals = jax.nn.logsumexp(scores, axis=-1, keepdims=True)
    soft_low = jnp.exp(scores - totals).astype(jnp.bfloat16)
    attended_tokens = jnp.einsum(
        "shqk,skhc->sqhc",
        soft_low,
        head_split(values, seq_count),
        preferred_element_type=jnp.float32,
    )
    attended_tokens = attended_tokens.reshape(row_count, model_width).astype(jnp.bfloat16)
    residual_branch = (
        jnp.dot(attended_tokens, attention_output_weight, preferred_element_type=jnp.float32)
        + vec_f32[2]
    )
    pre_one = token_rows.astype(jnp.float32) + residual_branch
    first_normed = layer_norm(pre_one, vec_f32[3], vec_f32[4])
    normed_low = first_normed.astype(jnp.bfloat16)
    hidden_rows = jnp.dot(
        normed_low, up_weight, preferred_element_type=jnp.float32
    ) + hidden_bias.astype(jnp.float32)
    activated_hidden = smooth_gate(hidden_rows).astype(jnp.bfloat16)
    feedforward_output = (
        jnp.dot(activated_hidden, down_weight, preferred_element_type=jnp.float32) + vec_f32[5]
    )
    pre_two = first_normed + feedforward_output
    encoded_low = layer_norm(pre_two, vec_f32[6], vec_f32[7]).astype(jnp.bfloat16)
    soft_first = jnp.exp(scores[:, :, 0, :] - totals[:, :, 0, :])
    stored = (
        first_rows(queries, seq_count),
        keys_low,
        values,
        soft_first,
        first_rows(attended_tokens, seq_count),
        first_rows(pre_one, seq_count),
        first_rows(normed_low, seq_count),
        first_rows(hidden_rows, seq_count),
        first_rows(activated_hidden, seq_count),
        first_rows(pre_two, seq_count),
    )
    return (encoded_low, stored)


def norm_back(pre, gain_row, grad_out):
    centred = pre - jnp.mean(pre, axis=-1, keepdims=True)
    inverse = lax.rsqrt(jnp.mean(centred * centred, axis=-1, keepdims=True) + EPSILON)
    scaled = grad_out * gain_row
    inner = jnp.mean(scaled * centred, axis=-1, keepdims=True)
    grad_in = inverse * (
        scaled - jnp.mean(scaled, axis=-1, keepdims=True) - centred * (inverse * inverse * inner)
    )
    return (grad_in, jnp.sum(grad_out * centred * inverse, axis=0), jnp.sum(grad_out, axis=0))


def encode_backward(token_rows, weights, stored, grad_first):
    (
        query_key_value_weight,
        attention_output_weight,
        up_weight,
        down_weight,
        vectors,
        hidden_bias,
    ) = weights
    (
        queries,
        keys_low,
        values,
        soft_first,
        attended,
        pre_one,
        normed_low,
        hidden_rows,
        activated_hidden,
        pre_two,
    ) = stored
    seq_count, model_width = queries.shape
    seq_length = token_rows.shape[0] // seq_count
    head_width = model_width // HEADS
    scaling = head_width ** (-0.5)
    vec_f32 = vectors.astype(jnp.float32)
    grad_two, gain_two, shift_two = norm_back(pre_two, vec_f32[6], grad_first)
    grad_ffn = grad_two.astype(jnp.bfloat16)
    grad_activated = jnp.einsum(
        "rd,fd->rf", grad_ffn, down_weight, preferred_element_type=jnp.float32
    )
    grad_hidden = jax.vjp(smooth_gate, hidden_rows)[1](grad_activated)[0].astype(jnp.bfloat16)
    grad_normed = grad_two + jnp.einsum(
        "rf,df->rd", grad_hidden, up_weight, preferred_element_type=jnp.float32
    )
    grad_one, gain_one, shift_one = norm_back(pre_one, vec_f32[3], grad_normed)
    grad_branch = grad_one.astype(jnp.bfloat16)
    grad_attended = jnp.einsum(
        "re,de->rd", grad_branch, attention_output_weight, preferred_element_type=jnp.float32
    ).astype(jnp.bfloat16)
    grad_heads = grad_attended.reshape(seq_count, HEADS, head_width)
    grad_soft = jnp.einsum(
        "shc,skhc->shk",
        grad_heads,
        head_split(values, seq_count),
        preferred_element_type=jnp.float32,
    )
    row_inner = jnp.sum(soft_first * grad_soft, axis=-1, keepdims=True)
    grad_scores = (soft_first * (grad_soft - row_inner)).astype(jnp.bfloat16)
    soft_low = soft_first.astype(jnp.bfloat16)
    grad_queries = (
        jnp.einsum(
            "shk,skhc->shc",
            grad_scores,
            head_split(keys_low, seq_count),
            preferred_element_type=jnp.float32,
        )
        * scaling
    )
    grad_q_low = grad_queries.reshape(seq_count, model_width).astype(jnp.bfloat16)
    tokens = token_rows.reshape(seq_count, seq_length, model_width)
    both = jnp.concatenate([grad_scores, soft_low], axis=1)
    mixed = jnp.einsum("sgk,skd->sgd", both, tokens, preferred_element_type=jnp.float32).astype(
        jnp.bfloat16
    )
    scaled_queries = (queries.astype(jnp.float32) * scaling).astype(jnp.bfloat16)
    split_weight = query_key_value_weight.reshape(model_width, 3, HEADS, head_width)
    back_rows = jnp.concatenate(
        [
            jnp.einsum(
                "shc,dhc->shd",
                scaled_queries.reshape(seq_count, HEADS, head_width),
                split_weight[:, 1],
                preferred_element_type=jnp.float32,
            ),
            jnp.einsum(
                "shc,dhc->shd",
                grad_heads,
                split_weight[:, 2],
                preferred_element_type=jnp.float32,
            ),
        ],
        axis=1,
    ).astype(jnp.bfloat16)
    grad_tokens = jnp.einsum("sgk,sgd->skd", both, back_rows, preferred_element_type=jnp.float32)
    first_extra = grad_one + jnp.einsum(
        "se,de->sd",
        grad_q_low,
        query_key_value_weight[:, :model_width],
        preferred_element_type=jnp.float32,
    )
    is_first = (jnp.arange(seq_length) == 0)[None, :, None]
    grad_tokens = grad_tokens + jnp.where(is_first, first_extra[:, None, :], 0.0)
    soft_total = jnp.sum(soft_low.astype(jnp.float32), axis=-1, keepdims=True)
    vector_parts = jnp.stack(
        [
            jnp.sum(grad_q_low.astype(jnp.float32), axis=0),
            jnp.sum(grad_heads.astype(jnp.float32) * soft_total, axis=0).reshape(model_width),
            jnp.sum(grad_branch.astype(jnp.float32), axis=0),
            gain_one,
            shift_one,
            jnp.sum(grad_ffn.astype(jnp.float32), axis=0),
            gain_two,
            shift_two,
        ]
    )
    bias_part = jnp.sum(grad_hidden.astype(jnp.float32), axis=0)
    left = (
        activated_hidden,
        normed_low,
        attended,
        jnp.concatenate(
            [jnp.broadcast_to(tokens[:, :1, :], (seq_count, HEADS, model_width)), mixed], axis=1
        ),
    )
    right = (
        grad_ffn,
        grad_hidden,
        grad_branch,
        jnp.concatenate([grad_q_low, scaled_queries, grad_attended], axis=1),
    )
    return (
        grad_tokens.reshape(token_rows.shape),
        left,
        right,
        vector_parts,
        bias_part,
    )


def left_message(left, wq_size, np_size):
    activated, normed, attended, mixed = left
    rows, groups, model_width = mixed.shape
    part = model_width // wq_size
    columns = 3 * model_width // np_size
    head_width = model_width // HEADS
    group = math.gcd(head_width, columns)
    mixed = jnp.repeat(mixed, head_width // group, axis=1)
    mixed = mixed.reshape(rows, np_size, columns // group, wq_size, part)
    mixed = mixed.transpose(3, 1, 0, 2, 4).reshape(wq_size, np_size, rows, columns // group * part)

    def same(matrix):
        pieces = matrix.reshape(rows, wq_size, -1).transpose(1, 0, 2)
        return jnp.broadcast_to(pieces[:, None], (wq_size, np_size) + pieces.shape[1:])

    return jnp.concatenate([same(activated), same(normed), same(attended), mixed], axis=3)


def right_message(right, np_size):
    rows = right[0].shape[0]
    return jnp.concatenate(
        [member.reshape(rows, np_size, -1).transpose(1, 0, 2) for member in right], axis=2
    )


def weight_grads(left, right, model_width, ff_width, wq_size, np_size):
    rows = left.shape[0]
    part, ff_part = model_width // wq_size, ff_width // wq_size
    columns = 3 * model_width // np_size
    group = math.gcd(model_width // HEADS, columns)
    right_sizes = (model_width // np_size, ff_width // np_size, model_width // np_size)
    cut = [ff_part, ff_part + part, ff_part + 2 * part]
    activated, normed, attended, mixed = jnp.split(left, cut, axis=1)
    cut = [right_sizes[0], right_sizes[0] + right_sizes[1], sum(right_sizes)]
    grad_ffn, grad_hidden, grad_branch, grad_projected = jnp.split(right, cut, axis=1)

    def outer(one, two):
        return jnp.einsum("sd,se->de", one, two, preferred_element_type=jnp.float32)

    w_qkv = jnp.einsum(
        "sgd,sgc->dgc",
        mixed.reshape(rows, columns // group, part),
        grad_projected.reshape(rows, columns // group, group),
        preferred_element_type=jnp.float32,
    ).reshape(part, columns)
    return (
        w_qkv,
        outer(attended, grad_branch),
        outer(normed, grad_hidden),
        outer(activated, grad_ffn),
    )


def shards(
    q_embed,
    p_embed,
    q_len,
    p_len,
    q_set,
    p_set,
    gold,
    query_key_value_weight,
    attention_output_weight,
    up_weight,
    down_weight,
    vectors,
    hidden_bias,
):
    gathered = gather_weights(
        query_key_value_weight,
        attention_output_weight,
        up_weight,
        down_weight,
        vectors,
        hidden_bias,
    )
    wq_size, np_size = lax.axis_size("wq"), lax.axis_size("np")
    both_axes = ("wq", "np")
    q_weights = tuple((member[0] for member in gathered))
    p_weights = tuple((member[1] for member in gathered))
    p_encoded, p_stored = encode_forward(p_embed, p_len, p_weights)
    q_encoded, q_stored = encode_forward(q_embed, q_len, q_weights)
    model_width = q_embed.shape[1]
    ff_width = gathered[2].shape[2]
    q_count = q_len.shape[0]
    p_count = p_len.shape[0]
    own_heads = jnp.concatenate([first_rows(q_encoded, q_count), first_rows(p_encoded, p_count)])
    heads = lax.all_gather(own_heads, both_axes, axis=0)
    marks = lax.all_gather(jnp.concatenate([q_set, gold, p_set]), both_axes, axis=0)
    q_heads = heads[:, :q_count].reshape(-1, model_width)
    p_heads = heads[:, q_count:].reshape(-1, model_width)
    q_sets = marks[:, :q_count].reshape(-1)
    golds = marks[:, q_count : 2 * q_count].reshape(-1)
    p_sets = marks[:, 2 * q_count :].reshape(-1)
    scaling = model_width ** (-0.5)
    similar = (
        jnp.einsum("qd,pd->qp", q_heads, p_heads, preferred_element_type=jnp.float32) * scaling
    )
    is_gold = jnp.arange(p_heads.shape[0], dtype=jnp.int32)[None, :] == golds[:, None]
    usable = (q_sets[:, None] == p_sets[None, :]) | is_gold
    masked = jnp.where(usable, similar, NEGATIVE)
    highest = jnp.max(masked, axis=1)
    total = jnp.sum(jnp.where(usable, jnp.exp(masked - highest[:, None]), 0.0), axis=1)
    log_total = highest + jnp.log(total)
    gold_score = jnp.sum(jnp.where(is_gold, similar, 0.0), axis=1)
    loss = jnp.mean(log_total - gold_score)
    soft_rows = jnp.where(usable, jnp.exp(masked - log_total[:, None]), 0.0)
    grad_similar = (soft_rows - is_gold.astype(jnp.float32)).astype(jnp.bfloat16)
    me = lax.axis_index("wq") * np_size + lax.axis_index("np")
    grad_q_first = (
        jnp.einsum(
            "qp,pd->qd",
            lax.dynamic_slice_in_dim(grad_similar, me * q_count, q_count, 0),
            p_heads,
            preferred_element_type=jnp.float32,
        )
        * scaling
    )
    grad_p_first = (
        jnp.einsum(
            "qp,qd->pd",
            lax.dynamic_slice_in_dim(grad_similar, me * p_count, p_count, 1),
            q_heads,
            preferred_element_type=jnp.float32,
        )
        * scaling
    )
    q_back = encode_backward(q_embed, q_weights, q_stored, grad_q_first)
    p_back = encode_backward(p_embed, p_weights, p_stored, grad_p_first)
    left = jnp.concatenate(
        [left_message(member[1], wq_size, np_size) for member in (q_back, p_back)], axis=2
    )
    left = left.reshape((wq_size * np_size,) + left.shape[2:])
    left = lax.all_to_all(left, both_axes, 0, 0)
    right = jnp.concatenate([right_message(member[2], np_size) for member in (q_back, p_back)], axis=1)
    right = lax.all_gather(lax.all_to_all(right, "np", 0, 0), "wq", axis=0)
    right = right.reshape((wq_size * np_size,) + right.shape[2:])
    sums = jnp.concatenate(
        [
            jnp.stack([q_back[3], p_back[3]])
            .reshape(2, np_size, -1, wq_size, model_width // wq_size)
            .transpose(3, 1, 0, 2, 4)
            .reshape(wq_size * np_size, -1),
            jnp.stack([q_back[4], p_back[4]])
            .reshape(2, wq_size * np_size, -1)
            .transpose(1, 0, 2)
            .reshape(wq_size * np_size, -1),
        ],
        axis=1,
    )
    sums = jnp.sum(lax.all_to_all(sums, both_axes, 0, 0), axis=0)
    grad_vectors = sums[: sums.shape[0] - 2 * ff_width // (wq_size * np_size)].reshape(
        2, -1, model_width // wq_size
    )
    grad_b_in = sums[sums.shape[0] - 2 * ff_width // (wq_size * np_size) :].reshape(2, -1)
    q_weight_grads = weight_grads(
        left[:, :q_count].reshape(-1, left.shape[2]),
        right[:, :q_count].reshape(-1, right.shape[2]),
        model_width,
        ff_width,
        wq_size,
        np_size,
    )
    p_weight_grads = weight_grads(
        left[:, q_count:].reshape(-1, left.shape[2]),
        right[:, q_count:].reshape(-1, right.shape[2]),
        model_width,
        ff_width,
        wq_size,
        np_size,
    )
    shared = tuple(jnp.stack(pair) for pair in zip(q_weight_grads, p_weight_grads))
    return (
        loss,
        q_encoded,
        p_encoded,
        q_back[0],
        p_back[0],
        shared[0],
        shared[1],
        shared[2],
        shared[3],
        grad_vectors,
        grad_b_in,
    )


def solution(mesh):
    return jax.shard_map(
        shards,
        mesh=mesh,
        in_specs=(
            P(("wq", "np"), None),
            P(("wq", "np"), None),
            P(("wq", "np")),
            P(("wq", "np")),
            P(("wq", "np")),
            P(("wq", "np")),
            P(("wq", "np")),
            P(None, "wq", "np"),
            P(None, "wq", "np"),
            P(None, "wq", "np"),
            P(None, "wq", "np"),
            P(None, "np", "wq"),
            P(None, ("wq", "np")),
        ),
        out_specs=(
            P(),
            P(("wq", "np"), None),
            P(("wq", "np"), None),
            P(("wq", "np"), None),
            P(("wq", "np"), None),
            P(None, "wq", "np"),
            P(None, "wq", "np"),
            P(None, "wq", "np"),
            P(None, "wq", "np"),
            P(None, "np", "wq"),
            P(None, ("wq", "np")),
        ),
        check_vma=False,
    )
```

```python
import functools
import math

import jax
import jax.numpy as jnp
from jax import lax
from jax.experimental import pallas as pl
from jax.experimental.pallas import tpu as pltpu
from jax.sharding import PartitionSpec as P

HEADS = 12


EPSILON = 1e-12
NEGATIVE = -1e30


def layer_norm(inputs, gain_row, offset):
    centred = inputs - jnp.mean(inputs, axis=-1, keepdims=True)
    spread = jnp.mean(centred * centred, axis=-1, keepdims=True)
    return centred * lax.rsqrt(spread + EPSILON) * gain_row + offset


def smooth_gate(values):
    return jax.nn.gelu(values, approximate=True)


def gather_weights(
    query_key_value_weight, attention_output_weight, up_weight, down_weight, vectors, hidden_bias
):
    np_parts = (
        lax.all_gather(query_key_value_weight, "np", axis=2, tiled=True),
        lax.all_gather(attention_output_weight, "np", axis=2, tiled=True),
        lax.all_gather(up_weight, "np", axis=2, tiled=True),
        lax.all_gather(down_weight, "np", axis=2, tiled=True),
        lax.all_gather(vectors, "np", axis=1, tiled=True),
        lax.all_gather(hidden_bias, "np", axis=1, tiled=True),
    )
    return (
        lax.all_gather(np_parts[0], "wq", axis=1, tiled=True),
        lax.all_gather(np_parts[1], "wq", axis=1, tiled=True),
        lax.all_gather(np_parts[2], "wq", axis=1, tiled=True),
        lax.all_gather(np_parts[3], "wq", axis=1, tiled=True),
        lax.all_gather(np_parts[4], "wq", axis=2, tiled=True),
        lax.all_gather(np_parts[5], "wq", axis=1, tiled=True),
    )


def head_split(matrix, seq_count):
    row_count, model_width = matrix.shape
    return matrix.reshape(seq_count, row_count // seq_count, HEADS, model_width // HEADS)


def attention_scores(queries, keys_low, lengths):
    seq_count = lengths.shape[0]
    split_q = head_split(queries, seq_count)
    scores = jnp.einsum(
        "sqhc,skhc->shqk",
        split_q,
        head_split(keys_low, seq_count),
        preferred_element_type=jnp.float32,
    )
    scores = scores * split_q.shape[3] ** (-0.5)
    live_mask = jnp.arange(split_q.shape[1])[None, :] < lengths[:, None]
    return jnp.where(live_mask[:, None, None, :], scores, NEGATIVE)


def first_rows(matrix, seq_count):
    row_count, width = matrix.shape
    return matrix.reshape(seq_count, row_count // seq_count, width)[:, 0, :]


def encode_forward(token_rows, lengths, weights):
    (
        query_key_value_weight,
        attention_output_weight,
        up_weight,
        down_weight,
        vectors,
        hidden_bias,
    ) = weights
    row_count, model_width = token_rows.shape
    seq_count = lengths.shape[0]
    vec_f32 = vectors.astype(jnp.float32)
    projected_rows = jnp.dot(token_rows, query_key_value_weight, preferred_element_type=jnp.float32)
    queries = (projected_rows[:, :model_width] + vec_f32[0]).astype(jnp.bfloat16)
    keys_low = projected_rows[:, model_width : 2 * model_width].astype(jnp.bfloat16)
    values = (projected_rows[:, 2 * model_width :] + vec_f32[1]).astype(jnp.bfloat16)
    scores = attention_scores(queries, keys_low, lengths)
    totals = jax.nn.logsumexp(scores, axis=-1, keepdims=True)
    soft_low = jnp.exp(scores - totals).astype(jnp.bfloat16)
    attended_tokens = jnp.einsum(
        "shqk,skhc->sqhc",
        soft_low,
        head_split(values, seq_count),
        preferred_element_type=jnp.float32,
    )
    attended_tokens = attended_tokens.reshape(row_count, model_width).astype(jnp.bfloat16)
    residual_branch = (
        jnp.dot(attended_tokens, attention_output_weight, preferred_element_type=jnp.float32)
        + vec_f32[2]
    )
    pre_one = token_rows.astype(jnp.float32) + residual_branch
    first_normed = layer_norm(pre_one, vec_f32[3], vec_f32[4])
    normed_low = first_normed.astype(jnp.bfloat16)
    hidden_rows = jnp.dot(
        normed_low, up_weight, preferred_element_type=jnp.float32
    ) + hidden_bias.astype(jnp.float32)
    activated_hidden = smooth_gate(hidden_rows).astype(jnp.bfloat16)
    feedforward_output = (
        jnp.dot(activated_hidden, down_weight, preferred_element_type=jnp.float32) + vec_f32[5]
    )
    pre_two = first_normed + feedforward_output
    encoded_low = layer_norm(pre_two, vec_f32[6], vec_f32[7]).astype(jnp.bfloat16)
    soft_first = jnp.exp(scores[:, :, 0, :] - totals[:, :, 0, :])
    stored = (
        first_rows(queries, seq_count),
        keys_low,
        values,
        soft_first,
        first_rows(attended_tokens, seq_count),
        first_rows(pre_one, seq_count),
        first_rows(normed_low, seq_count),
        first_rows(hidden_rows, seq_count),
        first_rows(activated_hidden, seq_count),
        first_rows(pre_two, seq_count),
    )
    return (encoded_low, stored)


def norm_back(pre, gain_row, grad_out):
    centred = pre - jnp.mean(pre, axis=-1, keepdims=True)
    inverse = lax.rsqrt(jnp.mean(centred * centred, axis=-1, keepdims=True) + EPSILON)
    scaled = grad_out * gain_row
    inner = jnp.mean(scaled * centred, axis=-1, keepdims=True)
    grad_in = inverse * (
        scaled - jnp.mean(scaled, axis=-1, keepdims=True) - centred * (inverse * inverse * inner)
    )
    return (grad_in, jnp.sum(grad_out * centred * inverse, axis=0), jnp.sum(grad_out, axis=0))


def encode_backward(token_rows, weights, stored, grad_first):
    (
        query_key_value_weight,
        attention_output_weight,
        up_weight,
        down_weight,
        vectors,
        hidden_bias,
    ) = weights
    (
        queries,
        keys_low,
        values,
        soft_first,
        attended,
        pre_one,
        normed_low,
        hidden_rows,
        activated_hidden,
        pre_two,
    ) = stored
    seq_count, model_width = queries.shape
    seq_length = token_rows.shape[0] // seq_count
    head_width = model_width // HEADS
    scaling = head_width ** (-0.5)
    vec_f32 = vectors.astype(jnp.float32)
    grad_two, gain_two, shift_two = norm_back(pre_two, vec_f32[6], grad_first)
    grad_ffn = grad_two.astype(jnp.bfloat16)
    grad_activated = jnp.einsum(
        "rd,fd->rf", grad_ffn, down_weight, preferred_element_type=jnp.float32
    )
    grad_hidden = jax.vjp(smooth_gate, hidden_rows)[1](grad_activated)[0].astype(jnp.bfloat16)
    grad_normed = grad_two + jnp.einsum(
        "rf,df->rd", grad_hidden, up_weight, preferred_element_type=jnp.float32
    )
    grad_one, gain_one, shift_one = norm_back(pre_one, vec_f32[3], grad_normed)
    grad_branch = grad_one.astype(jnp.bfloat16)
    grad_attended = jnp.einsum(
        "re,de->rd", grad_branch, attention_output_weight, preferred_element_type=jnp.float32
    ).astype(jnp.bfloat16)
    grad_heads = grad_attended.reshape(seq_count, HEADS, head_width)
    grad_soft = jnp.einsum(
        "shc,skhc->shk",
        grad_heads,
        head_split(values, seq_count),
        preferred_element_type=jnp.float32,
    )
    row_inner = jnp.sum(soft_first * grad_soft, axis=-1, keepdims=True)
    grad_scores = (soft_first * (grad_soft - row_inner)).astype(jnp.bfloat16)
    soft_low = soft_first.astype(jnp.bfloat16)
    grad_queries = (
        jnp.einsum(
            "shk,skhc->shc",
            grad_scores,
            head_split(keys_low, seq_count),
            preferred_element_type=jnp.float32,
        )
        * scaling
    )
    grad_q_low = grad_queries.reshape(seq_count, model_width).astype(jnp.bfloat16)
    tokens = token_rows.reshape(seq_count, seq_length, model_width)
    both = jnp.concatenate([grad_scores, soft_low], axis=1)
    mixed = jnp.einsum("sgk,skd->sgd", both, tokens, preferred_element_type=jnp.float32).astype(
        jnp.bfloat16
    )
    scaled_queries = (queries.astype(jnp.float32) * scaling).astype(jnp.bfloat16)
    split_weight = query_key_value_weight.reshape(model_width, 3, HEADS, head_width)
    back_rows = jnp.concatenate(
        [
            jnp.einsum(
                "shc,dhc->shd",
                scaled_queries.reshape(seq_count, HEADS, head_width),
                split_weight[:, 1],
                preferred_element_type=jnp.float32,
            ),
            jnp.einsum(
                "shc,dhc->shd",
                grad_heads,
                split_weight[:, 2],
                preferred_element_type=jnp.float32,
            ),
        ],
        axis=1,
    ).astype(jnp.bfloat16)
    grad_tokens = jnp.einsum("sgk,sgd->skd", both, back_rows, preferred_element_type=jnp.float32)
    first_extra = grad_one + jnp.einsum(
        "se,de->sd",
        grad_q_low,
        query_key_value_weight[:, :model_width],
        preferred_element_type=jnp.float32,
    )
    is_first = (jnp.arange(seq_length) == 0)[None, :, None]
    grad_tokens = grad_tokens + jnp.where(is_first, first_extra[:, None, :], 0.0)
    soft_total = jnp.sum(soft_low.astype(jnp.float32), axis=-1, keepdims=True)
    vector_parts = jnp.stack(
        [
            jnp.sum(grad_q_low.astype(jnp.float32), axis=0),
            jnp.sum(grad_heads.astype(jnp.float32) * soft_total, axis=0).reshape(model_width),
            jnp.sum(grad_branch.astype(jnp.float32), axis=0),
            gain_one,
            shift_one,
            jnp.sum(grad_ffn.astype(jnp.float32), axis=0),
            gain_two,
            shift_two,
        ]
    )
    bias_part = jnp.sum(grad_hidden.astype(jnp.float32), axis=0)
    left = (
        activated_hidden,
        normed_low,
        attended,
        jnp.concatenate(
            [jnp.broadcast_to(tokens[:, :1, :], (seq_count, HEADS, model_width)), mixed], axis=1
        ),
    )
    right = (
        grad_ffn,
        grad_hidden,
        grad_branch,
        jnp.concatenate([grad_q_low, scaled_queries, grad_attended], axis=1),
    )
    return (
        grad_tokens.reshape(token_rows.shape),
        left,
        right,
        vector_parts,
        bias_part,
    )


def left_message(left, wq_size, np_size):
    activated, normed, attended, mixed = left
    rows, groups, model_width = mixed.shape
    part = model_width // wq_size
    columns = 3 * model_width // np_size
    head_width = model_width // HEADS
    group = math.gcd(head_width, columns)
    mixed = jnp.repeat(mixed, head_width // group, axis=1)
    mixed = mixed.reshape(rows, np_size, columns // group, wq_size, part)
    mixed = mixed.transpose(3, 1, 0, 2, 4).reshape(wq_size, np_size, rows, columns // group * part)

    def same(matrix):
        pieces = matrix.reshape(rows, wq_size, -1).transpose(1, 0, 2)
        return jnp.broadcast_to(pieces[:, None], (wq_size, np_size) + pieces.shape[1:])

    return jnp.concatenate([same(activated), same(normed), same(attended), mixed], axis=3)


def right_message(right, np_size):
    rows = right[0].shape[0]
    return jnp.concatenate(
        [member.reshape(rows, np_size, -1).transpose(1, 0, 2) for member in right], axis=2
    )


def weight_grads(left, right, model_width, ff_width, wq_size, np_size):
    rows = left.shape[0]
    part, ff_part = model_width // wq_size, ff_width // wq_size
    columns = 3 * model_width // np_size
    group = math.gcd(model_width // HEADS, columns)
    right_sizes = (model_width // np_size, ff_width // np_size, model_width // np_size)
    cut = [ff_part, ff_part + part, ff_part + 2 * part]
    activated, normed, attended, mixed = jnp.split(left, cut, axis=1)
    cut = [right_sizes[0], right_sizes[0] + right_sizes[1], sum(right_sizes)]
    grad_ffn, grad_hidden, grad_branch, grad_projected = jnp.split(right, cut, axis=1)

    def outer(one, two):
        return jnp.einsum("sd,se->de", one, two, preferred_element_type=jnp.float32)

    w_qkv = jnp.einsum(
        "sgd,sgc->dgc",
        mixed.reshape(rows, columns // group, part),
        grad_projected.reshape(rows, columns // group, group),
        preferred_element_type=jnp.float32,
    ).reshape(part, columns)
    return (
        w_qkv,
        outer(attended, grad_branch),
        outer(normed, grad_hidden),
        outer(activated, grad_ffn),
    )


MESH = pl.DeviceIdType.MESH

def ag_schedule(n_units, starts):
    out = []
    for t in range(max(starts) + 7):
        for u in sorted(range(n_units), key=lambda u: (starts[u], u)):
            s = t - starts[u]
            if 0 <= s <= 6: out.append((u, s))
    return out

class Gather:
    def __init__(self, units, ins, outs, send, recv):
        self.units, self.ins, self.outs, self.send, self.recv = units, ins, outs, send, recv
        w, self.y = lax.axis_index("wq"), lax.axis_index("np")
        self.w = w
        self.z, self.x, self.c = w // 4, (w // 2) % 2, w % 2
        self.pending = {}
    def dev(self, dz=0, fx=False, fy=False, fc=False):
        x = 1 - self.x if fx else self.x
        c = 1 - self.c if fc else self.c
        y = 1 - self.y if fy else self.y
        return ((self.z + dz) * 4 + x * 2 + c, y)
    def barrier(self):
        bar = pltpu.get_barrier_semaphore()
        def sig(**k): pl.semaphore_signal(bar, inc=1, device_id=self.dev(**k), device_id_type=MESH)
        sig(fx=True); sig(fy=True); sig(fc=True)
        @pl.when(self.z > 0)
        def _(): sig(dz=-1)
        @pl.when(self.z < 3)
        def _(): sig(dz=1)
        pl.semaphore_wait(bar, 3 + (self.z + 3) // 4 + (6 - self.z) // 4)
    def view(self, u, z=None, x=None, y=None, c=None):
        a, e, kind, r0, rn = self.units[u]
        o = self.outs[a]
        r, w = self.ins[a].shape[1:]
        zs = slice(None) if z is None else z
        xs = slice(None) if x is None else x
        cs = slice(None) if y is None else pl.ds(pl.multiple_of(y * w, 128), w)
        return o.at[e, zs, xs, pl.ds(pl.multiple_of((self.c if c is None else c) * r + r0, 16), rn), cs]
    def copy(self, u, sem, src, dst, dev):
        return pltpu.make_async_remote_copy(src_ref=src, dst_ref=dst, send_sem=self.send.at[u, sem], recv_sem=self.recv.at[u, sem], device_id=dev, device_id_type=MESH)
    def own_src(self, u):
        a, e, kind, r0, rn = self.units[u]
        return self.ins[a].at[e, pl.ds(r0, rn)]
    def zview(self, u, core, z):
        kind = self.units[u][2]
        if kind == "F": return self.view(u, z=z, x=self.x, y=self.y)
        if core == 0: return self.view(u, z=z, x=None, y=self.y)
        return self.view(u, z=z, x=self.x, y=None)
    def step(self, u, s):
        for core in (0, 1):
            pl.when(self.c == core)(lambda core=core: self._step(u, s, core))
    def A(self, core): return dict(fx=True) if core == 0 else dict(fy=True)
    def B(self, core): return dict(fy=True) if core == 0 else dict(fx=True)
    def a_src(self, u, core):
        kind = self.units[u][2]
        z = None if kind == "F" else self.z
        return self.view(u, z=z, x=self.x, y=self.y)
    def a_got(self, u, core):
        kind = self.units[u][2]
        z = None if kind == "F" else self.z
        return self.view(u, z=z, x=1 - self.x, y=self.y) if core == 0 else self.view(u, z=z, x=self.x, y=1 - self.y)
    def b_src(self, u, core):
        return self.view(u, x=None, y=self.y) if core == 0 else self.view(u, x=self.x, y=None)
    def b_got(self, u, core):
        return self.view(u, x=None, y=1 - self.y) if core == 0 else self.view(u, x=1 - self.x, y=None)
    def local(self, u, sem, ref):
        self.copy(u, sem, ref, ref, self.dev(fc=True)).start()
    def z_send(self, u, core, hop):
        z = self.z
        @pl.when((z - hop >= 0) & (z + 1 <= 3))
        def _():
            v = self.zview(u, core, z - hop)
            src = self.own_src(u) if (hop == 0 and self.units[u][2] == "F") else v
            self.copy(u, 2 + hop, src, v, self.dev(dz=1)).start()
        @pl.when((z + hop <= 3) & (z - 1 >= 0))
        def _():
            v = self.zview(u, core, z + hop)
            src = self.own_src(u) if (hop == 0 and self.units[u][2] == "F") else v
            self.copy(u, 5 + hop, src, v, self.dev(dz=-1)).start()
    def z_wait(self, u, core, hop):
        z = self.z
        @pl.when(z - 1 - hop >= 0)
        def _():
            v = self.zview(u, core, z - 1 - hop)
            self.copy(u, 2 + hop, v, v, self.dev(fc=True)).wait_recv()
            self.local(u, 11 + hop, v)
        @pl.when(z + 1 + hop <= 3)
        def _():
            v = self.zview(u, core, z + 1 + hop)
            self.copy(u, 5 + hop, v, v, self.dev(fc=True)).wait_recv()
            self.local(u, 14 + hop, v)
    def _step(self, u, s, core):
        F = self.units[u][2] == "F"
        own = self.view(u, z=self.z, x=self.x, y=self.y)
        if s == 0:
            src = self.own_src(u)
            self.copy(u, 8, src, own, self.dev(fc=True)).start()
            pltpu.make_async_copy(src, own, self.send.at[u, 17]).start()
            if F:
                self.z_send(u, core, 0)
            else:
                self.copy(u, 0, src, own, self.dev(**self.A(core))).start()
        if s == 1:
            pltpu.make_async_copy(self.own_src(u), own, self.send.at[u, 17]).wait()
            if F:
                self.z_wait(u, core, 0); self.z_send(u, core, 1)
            else:
                g = self.a_got(u, core)
                self.copy(u, 0, g, g, self.dev(fc=True)).wait_recv()
                self.z_send(u, core, 0)
                self.local(u, 9, g)
        if s == 2:
            if F: self.z_wait(u, core, 1); self.z_send(u, core, 2)
            else: self.z_wait(u, core, 0); self.z_send(u, core, 1)
        if s == 3:
            if F:
                self.z_wait(u, core, 2)
                v = self.a_src(u, core)
                self.copy(u, 0, v, v, self.dev(**self.A(core))).start()
            else:
                self.z_wait(u, core, 1); self.z_send(u, core, 2)
        if s == 4:
            if F:
                g = self.a_got(u, core)
                self.copy(u, 0, g, g, self.dev(fc=True)).wait_recv()
            else:
                self.z_wait(u, core, 2)
            v = self.b_src(u, core)
            self.copy(u, 1, v, v, self.dev(**self.B(core))).start()
            if F: self.local(u, 9, g)
        if s == 5:
            g = self.b_got(u, core)
            self.copy(u, 1, g, g, self.dev(fc=True)).wait_recv()
            self.local(u, 10, g)
        if s == 6:
            self.finish_recv(u, core); self.finish_send(u, core)
    def finish_recv(self, u, core):
        other = 1 - core
        c = 1 - self.c
        kind = self.units[u][2]
        def got(sem, v): self.copy(u, sem, v, v, self.dev(fc=True)).wait_recv()
        sv = lambda **k: self.view(u, c=c, **k)
        got(8, sv(z=self.z, x=self.x, y=self.y))
        za = None if kind == "F" else self.z
        got(9, sv(z=za, x=1 - self.x, y=self.y) if other == 0 else sv(z=za, x=self.x, y=1 - self.y))
        got(10, sv(x=None, y=1 - self.y) if other == 0 else sv(x=1 - self.x, y=None))
        def zv(z):
            if kind == "F": return sv(z=z, x=self.x, y=self.y)
            return sv(z=z, x=None, y=self.y) if other == 0 else sv(z=z, x=self.x, y=None)
        for hop in range(3):
            pl.when(self.z - 1 - hop >= 0)(lambda hop=hop: got(11 + hop, zv(self.z - 1 - hop)))
            pl.when(self.z + 1 + hop <= 3)(lambda hop=hop: got(14 + hop, zv(self.z + 1 + hop)))
    def finish_send(self, u, core):
        def sent(sem, v): self.copy(u, sem, v, v, self.dev(fc=True)).wait_send()
        own = self.view(u, z=self.z, x=self.x, y=self.y)
        sent(8, own)
        sent(0, self.a_src(u, core)); sent(1, self.b_src(u, core))
        sent(9, self.a_got(u, core)); sent(10, self.b_got(u, core))
        z = self.z
        for hop in range(3):
            pl.when((z - hop >= 0) & (z + 1 <= 3))(lambda hop=hop: sent(2 + hop, self.zview(u, core, z - hop)))
            pl.when((z + hop <= 3) & (z - 1 >= 0))(lambda hop=hop: sent(5 + hop, self.zview(u, core, z + hop)))
            pl.when(z - 1 - hop >= 0)(lambda hop=hop: sent(11 + hop, self.zview(u, core, z - 1 - hop)))
            pl.when(z + 1 + hop <= 3)(lambda hop=hop: sent(14 + hop, self.zview(u, core, z + 1 + hop)))

def gather_kernel(units, schedule, n, *refs):
    ins, outs, (send, recv) = refs[:n], refs[n:2*n], refs[2*n:]
    g = Gather(units, ins, outs, send, recv)
    g.barrier()
    for u, s in schedule: g.step(u, s)

def gather_call(arrays, units, schedule, name="gather"):
    n = len(arrays)
    shapes = [jax.ShapeDtypeStruct((a.shape[0], 4, 2, 2 * a.shape[1], 2 * a.shape[2]), a.dtype) for a in arrays]
    return pl.pallas_call(functools.partial(gather_kernel, units, schedule, n), out_shape=shapes,
        in_specs=[pl.BlockSpec(memory_space=pl.ANY)] * n, out_specs=[pl.BlockSpec(memory_space=pl.ANY)] * n,
        scratch_shapes=[pltpu.SemaphoreType.DMA((len(units), 18)), pltpu.SemaphoreType.DMA((len(units), 18))],
        compiler_params=pltpu.CompilerParams(collective_id=1, has_side_effects=True), name=name)(*arrays)


BLK=256
F32=jnp.float32; BF=jnp.bfloat16
NEG=-1e30; EPS=1e-12
def dot(a,b): return jnp.dot(a,b,preferred_element_type=F32)
def norm(u,g,b):
    c=u-jnp.mean(u,axis=-1,keepdims=True)
    s=jnp.mean(c*c,axis=-1,keepdims=True)
    return c*lax.rsqrt(s+EPS)*g+b
def pick(v):
    r=[v[i*64:i*64+1] for i in range(4)]
    return jnp.concatenate(r+[jnp.zeros_like(v[0:4])],axis=0)
def make_bias(bias_ref, slot, lens, slots):
    n=BLK//slots
    key=lax.broadcasted_iota(jnp.int32,(BLK,BLK),0)
    qry=lax.broadcasted_iota(jnp.int32,(BLK,BLK),1)
    ok=key<lens[0]
    if n>1:
        ok=ok&(qry<slots)
        for j in range(1,n):
            ok=ok|((key>=j*slots)&(key<j*slots+lens[j])&(qry>=j*slots)&(qry<(j+1)*slots))
    bias_ref[...]=jnp.where(ok,0.0,NEG)
def attend_block(row, x_ref, wqkv, vec, bias_ref, k_ref, v_ref, att_ref, q0_ref, b):
    x=x_ref[pl.ds(row,BLK),:]
    for g in range(3):
        cs=pl.ds(g*256,256)
        q4=dot(x,wqkv[:,g*256:g*256+256])+vec[0:1,g*256:g*256+256]
        q4=q4.astype(BF)
        k4=dot(x,wqkv[:,768+g*256:768+g*256+256]).astype(BF)
        v4=(dot(x,wqkv[:,1536+g*256:1536+g*256+256])+vec[1:2,g*256:g*256+256]).astype(BF)
        k_ref[pl.ds(row,BLK),cs]=k4
        v_ref[pl.ds(row,BLK),cs]=v4
        q0_ref[pl.ds(pl.multiple_of(b*8,8),8),cs]=pick(q4.astype(F32))
        qT=(q4.astype(F32)*0.125).T.astype(BF)
        vT=v4.astype(F32).T.astype(BF)
        lane=lax.broadcasted_iota(jnp.int32,(BLK,256),1)
        outs=[]
        for h in range(4):
            kh=jnp.where((lane>=64*h)&(lane<64*h+64),k4,jnp.zeros_like(k4))
            s=dot(kh,qT)+bias_ref[...]
            m=jnp.max(s,axis=0,keepdims=True)
            p=jnp.exp(s-m)
            l=jnp.sum(p,axis=0,keepdims=True)
            o=dot(vT[64*h:64*h+64,:],p.astype(BF))
            outs.append(o*(1.0/l))
        oT=jnp.concatenate(outs,axis=0)
        att_ref[pl.ds(row,BLK),cs]=oT.T.astype(BF)
def out_block(row, x_ref, att_ref, wo, vec, n_ref, a0_ref, p1_ref, b):
    att=att_ref[pl.ds(row,BLK),:]
    r8=pl.ds(pl.multiple_of(b*8,8),8)
    a0_ref[r8,:]=pick(att.astype(F32))
    pre=x_ref[pl.ds(row,BLK),:].astype(F32)+dot(att,wo[...])+vec[2:3,:]
    p1_ref[r8,:]=pick(pre)
    n_ref[pl.ds(row,BLK),:]=norm(pre,vec[3:4,:],vec[4:5,:])
def gelu(u):
    return 0.5*u*(1.0+jnp.tanh(0.7978845608028654*(u+0.044715*(u*u*u))))
def up_block(row, n_ref, wup, hb, act_ref, h0_ref, b, arow):
    nl=n_ref[pl.ds(row,BLK),:].astype(BF)
    r8=pl.ds(pl.multiple_of(b*8,8),8)
    for t in range(12):
        cs=slice(t*256,t*256+256)
        h=dot(nl,wup[:,cs])+hb[0:1,cs]
        h0_ref[r8,cs]=pick(h)
        act_ref[pl.ds(arow,BLK),cs]=gelu(h).astype(BF)
def down_block(row, n_ref, act_ref, wdown, vec, o_ref, p2_ref, b, arow):
    f=dot(act_ref[pl.ds(arow,BLK),:],wdown[...])+vec[5:6,:]
    pre=n_ref[pl.ds(row,BLK),:]+f
    p2_ref[pl.ds(pl.multiple_of(b*8,8),8),:]=pick(pre)
    o_ref[pl.ds(row,BLK),:]=norm(pre,vec[6:7,:],vec[7:8,:]).astype(BF)

def fw_kernel(phases, ql, pl_, qx, px, wqkv, wo, wup, wdn, vec, hb, qo, po, qk, qv, pk, pv, q0, a0, p1, h0, p2, bias, att, nrm, act):
    for e,(x,o,k,v,lens,nb,slots,base) in ((1,(px,po,pk,pv,pl_,6,256,2)),(0,(qx,qo,qk,qv,ql,2,64,0))):
        n=256//slots
        def body(i,_):
            row=pl.multiple_of(i*BLK,BLK); b=base+i; arow=0
            mrow=pl.multiple_of((base+i)*BLK,BLK)
            A=att.at[pl.ds(base*BLK,nb*BLK)]; N=nrm.at[pl.ds(base*BLK,nb*BLK)]
            if "1" in phases:
                make_bias(bias,0,[lens[i*n+j] for j in range(n)],slots)
                attend_block(row,x,wqkv.at[e],vec.at[e],bias,k,v,A,q0,b)
            if "2" in phases: out_block(row,x,A,wo.at[e],vec.at[e],N,a0,p1,b)
            if "3" in phases: up_block(row,N,wup.at[e],hb.at[e],act,h0,b,arow)
            if "4" in phases: down_block(row,N,act,wdn.at[e],vec.at[e],o,p2,b,arow)
            return _
        lax.fori_loop(0,nb,body,0)
def forward(ql,pl_,qx,px,wqkv,wo,wup,wdn,vec,hb,phases="1234"):
    S=jax.ShapeDtypeStruct
    V=pl.BlockSpec(memory_space=pltpu.VMEM); SM=pl.BlockSpec(memory_space=pltpu.SMEM)
    outs=[S(qx.shape,BF),S(px.shape,BF),S(qx.shape,BF),S(qx.shape,BF),S(px.shape,BF),S(px.shape,BF),S((64,768),F32),S((64,768),F32),S((64,768),F32),S((64,3072),F32),S((64,768),F32)]
    return pl.pallas_call(functools.partial(fw_kernel,phases),out_shape=outs,in_specs=[SM,SM]+[V]*8,out_specs=[V]*11,
      scratch_shapes=[pltpu.VMEM((256,256),F32),pltpu.VMEM((2048,768),BF),pltpu.VMEM((2048,768),F32),pltpu.VMEM((256,3072),BF)],
      compiler_params=pltpu.CompilerParams(vmem_limit_bytes=62*2**20),name="fw")(ql,pl_,qx,px,wqkv,wo,wup,wdn,vec,hb)


def small_tile(vectors, hidden_bias):
    tile = jnp.zeros((1, 16, 128), vectors.dtype)
    count, rows, width = vectors.shape
    tile = tile.at[0, : count * rows, :width].set(vectors.reshape(count * rows, width))
    return tile.at[0, count * rows : count * rows + count, : hidden_bias.shape[1]].set(hidden_bias)


def small_whole(tiles, vectors, hidden_bias):
    count, rows, width = vectors.shape
    tiles = tiles.reshape(16, 16, 2, 128)
    whole = tiles[:, : count * rows, :, :width].reshape(16, count, rows, 2, width)
    whole = whole.transpose(1, 3, 2, 0, 4).reshape(count, 2 * rows, 16 * width)
    bias = tiles[:, count * rows : count * rows + count, :, : hidden_bias.shape[1]]
    bias = bias.transpose(1, 0, 2, 3).reshape(count, -1)
    return (whole, bias)


GATHER_ORDER = ((4, 0), (0, 1), (0, 0), (1, 1), (1, 0), (2, 1), (3, 1), (2, 0), (3, 0))


def gather_weights_kernel(wqkv, wout, wup, wdown, vectors, hidden_bias):
    arrays = (wqkv, wout, wup, wdown, small_tile(vectors, hidden_bias))
    parts = (3, 1, 3, 3, 1)
    units = []
    for a, e in GATHER_ORDER:
        rows = arrays[a].shape[1] // parts[a]
        for j in range(parts[a]):
            units.append((a, e, "MFM"[len(units) % 3], j * rows, rows))
    schedule = ag_schedule(len(units), [i // 3 for i in range(len(units))])
    whole = gather_call(arrays, units, schedule)
    small = small_whole(whole[4], vectors, hidden_bias)
    return tuple(
        member.reshape(2, 16 * shard.shape[1], 2 * shard.shape[2])
        for member, shard in zip(whole[:4], arrays[:4])
    ) + small


def first_state(index, tokens_low, keys_low, values, lengths, rows_of, weights):
    queries, attended, pre_one, hidden_rows, pre_two = (
        rows_of(member) for member in index
    )
    seq_count, model_width = queries.shape
    seq_length = keys_low.shape[0] // seq_count
    vec_f32 = weights[4].astype(jnp.float32)
    scores = jnp.einsum(
        "shc,skhc->shk",
        queries.astype(jnp.bfloat16).reshape(seq_count, HEADS, -1),
        head_split(keys_low, seq_count),
        preferred_element_type=jnp.float32,
    ) * (model_width // HEADS) ** (-0.5)
    live = jnp.arange(seq_length)[None, :] < lengths[:, None]
    scores = jnp.where(live[:, None, :], scores, NEGATIVE)
    soft_first = jnp.exp(scores - jax.nn.logsumexp(scores, axis=-1, keepdims=True))
    normed_low = layer_norm(pre_one, vec_f32[3], vec_f32[4]).astype(jnp.bfloat16)
    return (
        queries.astype(jnp.bfloat16),
        keys_low,
        values,
        soft_first,
        attended.astype(jnp.bfloat16),
        pre_one,
        normed_low,
        hidden_rows,
        smooth_gate(hidden_rows).astype(jnp.bfloat16),
        pre_two,
    )


def kernels_fit(q_embed, p_embed, q_len, p_len):
    return (
        lax.axis_size("wq") == 16
        and lax.axis_size("np") == 2
        and q_embed.shape == (512, 768)
        and p_embed.shape == (1536, 768)
        and q_len.shape == (8,)
        and p_len.shape == (6,)
    )


def shards(
    q_embed,
    p_embed,
    q_len,
    p_len,
    q_set,
    p_set,
    gold,
    query_key_value_weight,
    attention_output_weight,
    up_weight,
    down_weight,
    vectors,
    hidden_bias,
):
    fast = kernels_fit(q_embed, p_embed, q_len, p_len)
    gathered = (gather_weights_kernel if fast else gather_weights)(
        query_key_value_weight,
        attention_output_weight,
        up_weight,
        down_weight,
        vectors,
        hidden_bias,
    )
    wq_size, np_size = lax.axis_size("wq"), lax.axis_size("np")
    both_axes = ("wq", "np")
    q_weights = tuple((member[0] for member in gathered))
    p_weights = tuple((member[1] for member in gathered))
    if fast:
        done = forward(
            q_len,
            p_len,
            q_embed,
            p_embed,
            *gathered[:4],
            gathered[4].astype(jnp.float32),
            gathered[5].astype(jnp.float32)[:, None, :],
        )
        q_encoded, p_encoded = done[0], done[1]
        q_stored = first_state(
            done[6:],
            q_embed,
            done[2],
            done[3],
            q_len,
            lambda m: m.reshape(8, 8, -1)[:2, :4].reshape(8, -1),
            q_weights,
        )
        p_stored = first_state(
            done[6:], p_embed, done[4], done[5], p_len, lambda m: m.reshape(8, 8, -1)[2:, 0], p_weights
        )
    else:
        p_encoded, p_stored = encode_forward(p_embed, p_len, p_weights)
        q_encoded, q_stored = encode_forward(q_embed, q_len, q_weights)
    model_width = q_embed.shape[1]
    ff_width = gathered[2].shape[2]
    q_count = q_len.shape[0]
    p_count = p_len.shape[0]
    own_heads = jnp.concatenate([first_rows(q_encoded, q_count), first_rows(p_encoded, p_count)])
    heads = lax.all_gather(own_heads, both_axes, axis=0)
    marks = lax.all_gather(jnp.concatenate([q_set, gold, p_set]), both_axes, axis=0)
    q_heads = heads[:, :q_count].reshape(-1, model_width)
    p_heads = heads[:, q_count:].reshape(-1, model_width)
    q_sets = marks[:, :q_count].reshape(-1)
    golds = marks[:, q_count : 2 * q_count].reshape(-1)
    p_sets = marks[:, 2 * q_count :].reshape(-1)
    scaling = model_width ** (-0.5)
    similar = (
        jnp.einsum("qd,pd->qp", q_heads, p_heads, preferred_element_type=jnp.float32) * scaling
    )
    is_gold = jnp.arange(p_heads.shape[0], dtype=jnp.int32)[None, :] == golds[:, None]
    usable = (q_sets[:, None] == p_sets[None, :]) | is_gold
    masked = jnp.where(usable, similar, NEGATIVE)
    highest = jnp.max(masked, axis=1)
    total = jnp.sum(jnp.where(usable, jnp.exp(masked - highest[:, None]), 0.0), axis=1)
    log_total = highest + jnp.log(total)
    gold_score = jnp.sum(jnp.where(is_gold, similar, 0.0), axis=1)
    loss = jnp.mean(log_total - gold_score)
    soft_rows = jnp.where(usable, jnp.exp(masked - log_total[:, None]), 0.0)
    grad_similar = (soft_rows - is_gold.astype(jnp.float32)).astype(jnp.bfloat16)
    me = lax.axis_index("wq") * np_size + lax.axis_index("np")
    grad_q_first = (
        jnp.einsum(
            "qp,pd->qd",
            lax.dynamic_slice_in_dim(grad_similar, me * q_count, q_count, 0),
            p_heads,
            preferred_element_type=jnp.float32,
        )
        * scaling
    )
    grad_p_first = (
        jnp.einsum(
            "qp,qd->pd",
            lax.dynamic_slice_in_dim(grad_similar, me * p_count, p_count, 1),
            q_heads,
            preferred_element_type=jnp.float32,
        )
        * scaling
    )
    q_back = encode_backward(q_embed, q_weights, q_stored, grad_q_first)
    p_back = encode_backward(p_embed, p_weights, p_stored, grad_p_first)
    left = jnp.concatenate(
        [left_message(member[1], wq_size, np_size) for member in (q_back, p_back)], axis=2
    )
    left = left.reshape((wq_size * np_size,) + left.shape[2:])
    left = lax.all_to_all(left, both_axes, 0, 0)
    right = jnp.concatenate([right_message(member[2], np_size) for member in (q_back, p_back)], axis=1)
    right = lax.all_gather(lax.all_to_all(right, "np", 0, 0), "wq", axis=0)
    right = right.reshape((wq_size * np_size,) + right.shape[2:])
    sums = jnp.concatenate(
        [
            jnp.stack([q_back[3], p_back[3]])
            .reshape(2, np_size, -1, wq_size, model_width // wq_size)
            .transpose(3, 1, 0, 2, 4)
            .reshape(wq_size * np_size, -1),
            jnp.stack([q_back[4], p_back[4]])
            .reshape(2, wq_size * np_size, -1)
            .transpose(1, 0, 2)
            .reshape(wq_size * np_size, -1),
        ],
        axis=1,
    )
    sums = jnp.sum(lax.all_to_all(sums, both_axes, 0, 0), axis=0)
    grad_vectors = sums[: sums.shape[0] - 2 * ff_width // (wq_size * np_size)].reshape(
        2, -1, model_width // wq_size
    )
    grad_b_in = sums[sums.shape[0] - 2 * ff_width // (wq_size * np_size) :].reshape(2, -1)
    q_weight_grads = weight_grads(
        left[:, :q_count].reshape(-1, left.shape[2]),
        right[:, :q_count].reshape(-1, right.shape[2]),
        model_width,
        ff_width,
        wq_size,
        np_size,
    )
    p_weight_grads = weight_grads(
        left[:, q_count:].reshape(-1, left.shape[2]),
        right[:, q_count:].reshape(-1, right.shape[2]),
        model_width,
        ff_width,
        wq_size,
        np_size,
    )
    shared = tuple(jnp.stack(pair) for pair in zip(q_weight_grads, p_weight_grads))
    return (
        loss,
        q_encoded,
        p_encoded,
        q_back[0],
        p_back[0],
        shared[0],
        shared[1],
        shared[2],
        shared[3],
        grad_vectors,
        grad_b_in,
    )


def solution(mesh):
    return jax.shard_map(
        shards,
        mesh=mesh,
        in_specs=(
            P(("wq", "np"), None),
            P(("wq", "np"), None),
            P(("wq", "np")),
            P(("wq", "np")),
            P(("wq", "np")),
            P(("wq", "np")),
            P(("wq", "np")),
            P(None, "wq", "np"),
            P(None, "wq", "np"),
            P(None, "wq", "np"),
            P(None, "wq", "np"),
            P(None, "np", "wq"),
            P(None, ("wq", "np")),
        ),
        out_specs=(
            P(),
            P(("wq", "np"), None),
            P(("wq", "np"), None),
            P(("wq", "np"), None),
            P(("wq", "np"), None),
            P(None, "wq", "np"),
            P(None, "wq", "np"),
            P(None, "wq", "np"),
            P(None, "wq", "np"),
            P(None, "np", "wq"),
            P(None, ("wq", "np")),
        ),
        check_vma=False,
    )
```

```python
import functools
import math

import jax
import jax.numpy as jnp
from jax import lax
from jax.experimental import pallas as pl
from jax.experimental.pallas import tpu as pltpu
from jax.sharding import PartitionSpec as P


HEADS = 12


EPSILON = 1e-12
NEGATIVE = -1e30


def layer_norm(inputs, gain_row, offset):
    centred = inputs - jnp.mean(inputs, axis=-1, keepdims=True)
    spread = jnp.mean(centred * centred, axis=-1, keepdims=True)
    return centred * lax.rsqrt(spread + EPSILON) * gain_row + offset


def smooth_gate(values):
    return jax.nn.gelu(values, approximate=True)


def gather_weights(
    query_key_value_weight, attention_output_weight, up_weight, down_weight, vectors, hidden_bias
):
    np_parts = (
        lax.all_gather(query_key_value_weight, "np", axis=2, tiled=True),
        lax.all_gather(attention_output_weight, "np", axis=2, tiled=True),
        lax.all_gather(up_weight, "np", axis=2, tiled=True),
        lax.all_gather(down_weight, "np", axis=2, tiled=True),
        lax.all_gather(vectors, "np", axis=1, tiled=True),
        lax.all_gather(hidden_bias, "np", axis=1, tiled=True),
    )
    return (
        lax.all_gather(np_parts[0], "wq", axis=1, tiled=True),
        lax.all_gather(np_parts[1], "wq", axis=1, tiled=True),
        lax.all_gather(np_parts[2], "wq", axis=1, tiled=True),
        lax.all_gather(np_parts[3], "wq", axis=1, tiled=True),
        lax.all_gather(np_parts[4], "wq", axis=2, tiled=True),
        lax.all_gather(np_parts[5], "wq", axis=1, tiled=True),
    )


def head_split(matrix, seq_count):
    row_count, model_width = matrix.shape
    return matrix.reshape(seq_count, row_count // seq_count, HEADS, model_width // HEADS)


def attention_scores(queries, keys_low, lengths):
    seq_count = lengths.shape[0]
    split_q = head_split(queries, seq_count)
    scores = jnp.einsum(
        "sqhc,skhc->shqk",
        split_q,
        head_split(keys_low, seq_count),
        preferred_element_type=jnp.float32,
    )
    scores = scores * split_q.shape[3] ** (-0.5)
    live_mask = jnp.arange(split_q.shape[1])[None, :] < lengths[:, None]
    return jnp.where(live_mask[:, None, None, :], scores, NEGATIVE)


def first_rows(matrix, seq_count):
    row_count, width = matrix.shape
    return matrix.reshape(seq_count, row_count // seq_count, width)[:, 0, :]


def encode_forward(token_rows, lengths, weights):
    (
        query_key_value_weight,
        attention_output_weight,
        up_weight,
        down_weight,
        vectors,
        hidden_bias,
    ) = weights
    row_count, model_width = token_rows.shape
    seq_count = lengths.shape[0]
    vec_f32 = vectors.astype(jnp.float32)
    projected_rows = jnp.dot(token_rows, query_key_value_weight, preferred_element_type=jnp.float32)
    queries = (projected_rows[:, :model_width] + vec_f32[0]).astype(jnp.bfloat16)
    keys_low = projected_rows[:, model_width : 2 * model_width].astype(jnp.bfloat16)
    values = (projected_rows[:, 2 * model_width :] + vec_f32[1]).astype(jnp.bfloat16)
    scores = attention_scores(queries, keys_low, lengths)
    totals = jax.nn.logsumexp(scores, axis=-1, keepdims=True)
    soft_low = jnp.exp(scores - totals).astype(jnp.bfloat16)
    attended_tokens = jnp.einsum(
        "shqk,skhc->sqhc",
        soft_low,
        head_split(values, seq_count),
        preferred_element_type=jnp.float32,
    )
    attended_tokens = attended_tokens.reshape(row_count, model_width).astype(jnp.bfloat16)
    residual_branch = (
        jnp.dot(attended_tokens, attention_output_weight, preferred_element_type=jnp.float32)
        + vec_f32[2]
    )
    pre_one = token_rows.astype(jnp.float32) + residual_branch
    first_normed = layer_norm(pre_one, vec_f32[3], vec_f32[4])
    normed_low = first_normed.astype(jnp.bfloat16)
    hidden_rows = jnp.dot(
        normed_low, up_weight, preferred_element_type=jnp.float32
    ) + hidden_bias.astype(jnp.float32)
    activated_hidden = smooth_gate(hidden_rows).astype(jnp.bfloat16)
    feedforward_output = (
        jnp.dot(activated_hidden, down_weight, preferred_element_type=jnp.float32) + vec_f32[5]
    )
    pre_two = first_normed + feedforward_output
    encoded_low = layer_norm(pre_two, vec_f32[6], vec_f32[7]).astype(jnp.bfloat16)
    soft_first = jnp.exp(scores[:, :, 0, :] - totals[:, :, 0, :])
    stored = (
        first_rows(queries, seq_count),
        keys_low,
        values,
        soft_first,
        first_rows(attended_tokens, seq_count),
        first_rows(pre_one, seq_count),
        first_rows(normed_low, seq_count),
        first_rows(hidden_rows, seq_count),
        first_rows(activated_hidden, seq_count),
        first_rows(pre_two, seq_count),
    )
    return (encoded_low, stored)


def norm_back(pre, gain_row, grad_out):
    centred = pre - jnp.mean(pre, axis=-1, keepdims=True)
    inverse = lax.rsqrt(jnp.mean(centred * centred, axis=-1, keepdims=True) + EPSILON)
    scaled = grad_out * gain_row
    inner = jnp.mean(scaled * centred, axis=-1, keepdims=True)
    grad_in = inverse * (
        scaled - jnp.mean(scaled, axis=-1, keepdims=True) - centred * (inverse * inverse * inner)
    )
    return (grad_in, jnp.sum(grad_out * centred * inverse, axis=0), jnp.sum(grad_out, axis=0))


def encode_backward(token_rows, weights, stored, grad_first):
    (
        query_key_value_weight,
        attention_output_weight,
        up_weight,
        down_weight,
        vectors,
        hidden_bias,
    ) = weights
    (
        queries,
        keys_low,
        values,
        soft_first,
        attended,
        pre_one,
        normed_low,
        hidden_rows,
        activated_hidden,
        pre_two,
    ) = stored
    seq_count, model_width = queries.shape
    seq_length = token_rows.shape[0] // seq_count
    head_width = model_width // HEADS
    scaling = head_width ** (-0.5)
    vec_f32 = vectors.astype(jnp.float32)
    grad_two, gain_two, shift_two = norm_back(pre_two, vec_f32[6], grad_first)
    grad_ffn = grad_two.astype(jnp.bfloat16)
    grad_activated = jnp.einsum(
        "rd,fd->rf", grad_ffn, down_weight, preferred_element_type=jnp.float32
    )
    grad_hidden = jax.vjp(smooth_gate, hidden_rows)[1](grad_activated)[0].astype(jnp.bfloat16)
    grad_normed = grad_two + jnp.einsum(
        "rf,df->rd", grad_hidden, up_weight, preferred_element_type=jnp.float32
    )
    grad_one, gain_one, shift_one = norm_back(pre_one, vec_f32[3], grad_normed)
    grad_branch = grad_one.astype(jnp.bfloat16)
    grad_attended = jnp.einsum(
        "re,de->rd", grad_branch, attention_output_weight, preferred_element_type=jnp.float32
    ).astype(jnp.bfloat16)
    grad_heads = grad_attended.reshape(seq_count, HEADS, head_width)
    grad_soft = jnp.einsum(
        "shc,skhc->shk",
        grad_heads,
        head_split(values, seq_count),
        preferred_element_type=jnp.float32,
    )
    row_inner = jnp.sum(soft_first * grad_soft, axis=-1, keepdims=True)
    grad_scores = (soft_first * (grad_soft - row_inner)).astype(jnp.bfloat16)
    soft_low = soft_first.astype(jnp.bfloat16)
    grad_queries = (
        jnp.einsum(
            "shk,skhc->shc",
            grad_scores,
            head_split(keys_low, seq_count),
            preferred_element_type=jnp.float32,
        )
        * scaling
    )
    grad_q_low = grad_queries.reshape(seq_count, model_width).astype(jnp.bfloat16)
    tokens = token_rows.reshape(seq_count, seq_length, model_width)
    both = jnp.concatenate([grad_scores, soft_low], axis=1)
    mixed = jnp.einsum("sgk,skd->sgd", both, tokens, preferred_element_type=jnp.float32).astype(
        jnp.bfloat16
    )
    scaled_queries = (queries.astype(jnp.float32) * scaling).astype(jnp.bfloat16)
    split_weight = query_key_value_weight.reshape(model_width, 3, HEADS, head_width)
    back_rows = jnp.concatenate(
        [
            jnp.einsum(
                "shc,dhc->shd",
                scaled_queries.reshape(seq_count, HEADS, head_width),
                split_weight[:, 1],
                preferred_element_type=jnp.float32,
            ),
            jnp.einsum(
                "shc,dhc->shd",
                grad_heads,
                split_weight[:, 2],
                preferred_element_type=jnp.float32,
            ),
        ],
        axis=1,
    ).astype(jnp.bfloat16)
    grad_tokens = jnp.einsum("sgk,sgd->skd", both, back_rows, preferred_element_type=jnp.float32)
    first_extra = grad_one + jnp.einsum(
        "se,de->sd",
        grad_q_low,
        query_key_value_weight[:, :model_width],
        preferred_element_type=jnp.float32,
    )
    is_first = (jnp.arange(seq_length) == 0)[None, :, None]
    grad_tokens = grad_tokens + jnp.where(is_first, first_extra[:, None, :], 0.0)
    soft_total = jnp.sum(soft_low.astype(jnp.float32), axis=-1, keepdims=True)
    vector_parts = jnp.stack(
        [
            jnp.sum(grad_q_low.astype(jnp.float32), axis=0),
            jnp.sum(grad_heads.astype(jnp.float32) * soft_total, axis=0).reshape(model_width),
            jnp.sum(grad_branch.astype(jnp.float32), axis=0),
            gain_one,
            shift_one,
            jnp.sum(grad_ffn.astype(jnp.float32), axis=0),
            gain_two,
            shift_two,
        ]
    )
    bias_part = jnp.sum(grad_hidden.astype(jnp.float32), axis=0)
    left = (
        activated_hidden,
        normed_low,
        attended,
        jnp.concatenate(
            [jnp.broadcast_to(tokens[:, :1, :], (seq_count, HEADS, model_width)), mixed], axis=1
        ),
    )
    right = (
        grad_ffn,
        grad_hidden,
        grad_branch,
        jnp.concatenate([grad_q_low, scaled_queries, grad_attended], axis=1),
    )
    return (
        grad_tokens.reshape(token_rows.shape),
        left,
        right,
        vector_parts,
        bias_part,
    )


def left_message(left, wq_size, np_size):
    activated, normed, attended, mixed = left
    rows, groups, model_width = mixed.shape
    part = model_width // wq_size
    columns = 3 * model_width // np_size
    head_width = model_width // HEADS
    group = math.gcd(head_width, columns)
    mixed = jnp.repeat(mixed, head_width // group, axis=1)
    mixed = mixed.reshape(rows, np_size, columns // group, wq_size, part)
    mixed = mixed.transpose(3, 1, 0, 2, 4).reshape(wq_size, np_size, rows, columns // group * part)

    def same(matrix):
        pieces = matrix.reshape(rows, wq_size, -1).transpose(1, 0, 2)
        return jnp.broadcast_to(pieces[:, None], (wq_size, np_size) + pieces.shape[1:])

    return jnp.concatenate([same(activated), same(normed), same(attended), mixed], axis=3)


def right_message(right, np_size):
    rows = right[0].shape[0]
    return jnp.concatenate(
        [member.reshape(rows, np_size, -1).transpose(1, 0, 2) for member in right], axis=2
    )


def weight_grads(left, right, model_width, ff_width, wq_size, np_size):
    rows = left.shape[0]
    part, ff_part = model_width // wq_size, ff_width // wq_size
    columns = 3 * model_width // np_size
    group = math.gcd(model_width // HEADS, columns)
    right_sizes = (model_width // np_size, ff_width // np_size, model_width // np_size)
    cut = [ff_part, ff_part + part, ff_part + 2 * part]
    activated, normed, attended, mixed = jnp.split(left, cut, axis=1)
    cut = [right_sizes[0], right_sizes[0] + right_sizes[1], sum(right_sizes)]
    grad_ffn, grad_hidden, grad_branch, grad_projected = jnp.split(right, cut, axis=1)

    def outer(one, two):
        return jnp.einsum("sd,se->de", one, two, preferred_element_type=jnp.float32)

    w_qkv = jnp.einsum(
        "sgd,sgc->dgc",
        mixed.reshape(rows, columns // group, part),
        grad_projected.reshape(rows, columns // group, group),
        preferred_element_type=jnp.float32,
    ).reshape(part, columns)
    return (
        w_qkv,
        outer(attended, grad_branch),
        outer(normed, grad_hidden),
        outer(activated, grad_ffn),
    )


BLK=256
F32=jnp.float32; BF=jnp.bfloat16
NEG=-1e30; EPS=1e-12
def dot(a,b): return jnp.dot(a,b,preferred_element_type=F32)
def norm(u,g,b):
    c=u-jnp.mean(u,axis=-1,keepdims=True)
    s=jnp.mean(c*c,axis=-1,keepdims=True)
    return c*lax.rsqrt(s+EPS)*g+b
def put_first(ref, e, i, cols, v):
    if e==1:
        ref[pl.ds(8+i,1),cols]=v[0:1]
    else:
        for j in range(4): ref[pl.ds(4*i+j,1),cols]=v[64*j:64*j+1]
def make_bias(bias_ref, slot, lens, slots):
    n=BLK//slots
    key=lax.broadcasted_iota(jnp.int32,(BLK,BLK),0)
    qry=lax.broadcasted_iota(jnp.int32,(BLK,BLK),1)
    ok=key<lens[0]
    if n>1:
        ok=ok&(qry<slots)
        for j in range(1,n):
            ok=ok|((key>=j*slots)&(key<j*slots+lens[j])&(qry>=j*slots)&(qry<(j+1)*slots))
    bias_ref[...]=jnp.where(ok,0.0,NEG)
def attend_block(row, x_ref, wqkv, vec, bias_ref, k_ref, v_ref, att_ref, q0_ref, e, i):
    x=x_ref[pl.ds(row,BLK),:]
    for g in range(3):
        cs=pl.ds(g*256,256)
        q4=dot(x,wqkv[:,g*256:g*256+256])+vec[0:1,g*256:g*256+256]
        q4=q4.astype(BF)
        k4=dot(x,wqkv[:,768+g*256:768+g*256+256]).astype(BF)
        v4=(dot(x,wqkv[:,1536+g*256:1536+g*256+256])+vec[1:2,g*256:g*256+256]).astype(BF)
        k_ref[pl.ds(row,BLK),cs]=k4
        v_ref[pl.ds(row,BLK),cs]=v4
        put_first(q0_ref,e,i,slice(g*256,g*256+256),q4.astype(F32))
        qT=(q4.astype(F32)*0.125).T.astype(BF)
        vT=v4.astype(F32).T.astype(BF)
        lane=lax.broadcasted_iota(jnp.int32,(BLK,256),1)
        outs=[]
        for h in range(4):
            kh=jnp.where((lane>=64*h)&(lane<64*h+64),k4,jnp.zeros_like(k4))
            s=dot(kh,qT)+bias_ref[...]
            m=jnp.max(s,axis=0,keepdims=True)
            p=jnp.exp(s-m)
            l=jnp.sum(p,axis=0,keepdims=True)
            o=dot(vT[64*h:64*h+64,:],p.astype(BF))
            outs.append(o*(1.0/l))
        oT=jnp.concatenate(outs,axis=0)
        att_ref[pl.ds(row,BLK),cs]=oT.T.astype(BF)
def out_block(row, x_ref, att_ref, wo, vec, n_ref, a0_ref, p1_ref, e, i):
    att=att_ref[pl.ds(row,BLK),:]
    put_first(a0_ref,e,i,slice(None),att.astype(F32))
    pre=x_ref[pl.ds(row,BLK),:].astype(F32)+dot(att,wo[...])+vec[2:3,:]
    put_first(p1_ref,e,i,slice(None),pre)
    n_ref[pl.ds(row,BLK),:]=norm(pre,vec[3:4,:],vec[4:5,:])
def gelu(u):
    return 0.5*u*(1.0+jnp.tanh(0.7978845608028654*(u+0.044715*(u*u*u))))
def up_block(row, n_ref, wup, hb, act_ref, h0_ref, e, i, arow):
    nl=n_ref[pl.ds(row,BLK),:].astype(BF)
    for t in range(12):
        cs=slice(t*256,t*256+256)
        h=dot(nl,wup[:,cs])+hb[0:1,cs]
        put_first(h0_ref,e,i,cs,h)
        act_ref[pl.ds(arow,BLK),cs]=gelu(h).astype(BF)
def down_block(row, n_ref, act_ref, wdown, vec, o_ref, p2_ref, hd_ref, e, i, arow):
    f=dot(act_ref[pl.ds(arow,BLK),:],wdown[...])+vec[5:6,:]
    pre=n_ref[pl.ds(row,BLK),:]+f
    put_first(p2_ref,e,i,slice(None),pre)
    enc=norm(pre,vec[6:7,:],vec[7:8,:])
    put_first(hd_ref,e,i,slice(None),enc)
    o_ref[pl.ds(row,BLK),:]=enc.astype(BF)

def fw_kernel(phases, ql, pl_, qx, px, wqkv, wo, wup, wdn, vec, hb, qo, po, qk, qv, pk, pv, q0, a0, p1, h0, p2, hd, bias, att, nrm, act):
    for ref in (q0,a0,p1,h0,p2,hd): ref[...]=jnp.zeros_like(ref)
    for e,(x,o,k,v,lens,nb,slots,base) in ((1,(px,po,pk,pv,pl_,6,256,2)),(0,(qx,qo,qk,qv,ql,2,64,0))):
        n=256//slots
        def body(i,_):
            row=pl.multiple_of(i*BLK,BLK); b=base+i; arow=0
            mrow=pl.multiple_of((base+i)*BLK,BLK)
            A=att.at[pl.ds(base*BLK,nb*BLK)]; N=nrm.at[pl.ds(base*BLK,nb*BLK)]
            if "1" in phases:
                make_bias(bias,0,[lens[i*n+j] for j in range(n)],slots)
                attend_block(row,x,wqkv.at[e],vec.at[e],bias,k,v,A,q0,e,i)
            if "2" in phases: out_block(row,x,A,wo.at[e],vec.at[e],N,a0,p1,e,i)
            if "3" in phases: up_block(row,N,wup.at[e],hb.at[e],act,h0,e,i,arow)
            if "4" in phases: down_block(row,N,act,wdn.at[e],vec.at[e],o,p2,hd,e,i,arow)
            return _
        lax.fori_loop(0,nb,body,0)
def forward(ql,pl_,qx,px,wqkv,wo,wup,wdn,vec,hb,phases="1234"):
    S=jax.ShapeDtypeStruct
    V=pl.BlockSpec(memory_space=pltpu.VMEM); SM=pl.BlockSpec(memory_space=pltpu.SMEM)
    outs=[S(qx.shape,BF),S(px.shape,BF),S(qx.shape,BF),S(qx.shape,BF),S(px.shape,BF),S(px.shape,BF),S((16,768),F32),S((16,768),F32),S((16,768),F32),S((16,3072),F32),S((16,768),F32),S((16,768),F32)]
    return pl.pallas_call(functools.partial(fw_kernel,phases),out_shape=outs,in_specs=[SM,SM]+[V]*8,out_specs=[V]*12,
      scratch_shapes=[pltpu.VMEM((256,256),F32),pltpu.VMEM((2048,768),BF),pltpu.VMEM((2048,768),F32),pltpu.VMEM((256,3072),BF)],
      compiler_params=pltpu.CompilerParams(vmem_limit_bytes=62*2**20),name="fw")(ql,pl_,qx,px,wqkv,wo,wup,wdn,vec,hb)


def dot_nt(a,b): return lax.dot_general(a,b,(((1,),(1,)),((),())),preferred_element_type=F32)
def gelu_slope(u):
    t=jnp.tanh(0.7978845608028654*(u+0.044715*(u*u*u)))
    return 0.5*(1.0+t)+0.5*u*(1.0-t*t)*(0.7978845608028654*(1.0+0.134145*(u*u)))
def norm_grad(u,g,gy):
    c=u-jnp.mean(u,axis=-1,keepdims=True)
    r=lax.rsqrt(jnp.mean(c*c,axis=-1,keepdims=True)+EPS)
    t=gy*g
    gu=r*(t-jnp.mean(t,axis=-1,keepdims=True)-c*(r*r)*jnp.mean(t*c,axis=-1,keepdims=True))
    return gu, jnp.sum(gy*c*r,axis=0,keepdims=True), jnp.sum(gy,axis=0,keepdims=True)
LEFT_ROWS=288
def heads_apart(rows, count):
    n=rows.shape[0]
    wide=jnp.concatenate([jnp.broadcast_to(rows[i:i+1],(16,768)) for i in range(n)],axis=0)
    r=lax.broadcasted_iota(jnp.int32,wide.shape,0)%16
    l=lax.broadcasted_iota(jnp.int32,wide.shape,1)//64
    return jnp.where(r==l,wide,0.0)
def back_one(e, base, nb, slots, lens, x, k, v, gtok, gr, q0, a0, p1, h0, p2, wqkv, wo, wup, wdn, vec, hb, ls, la, right, u_s, gq_s, sv_s, qa_s, ga_s):
    n=256//slots
    seqs=n*nb
    R=16*n
    rows=slice(8*e,8*e+8)
    W=lambda ref: ref.at[e]
    vv=vec[e]
    pre2=p2[rows,:]; pre1=p1[rows,:]; hid=h0[rows,:]
    g2,gain2,shift2=norm_grad(pre2,vv[6:7],gr[rows,:])
    gffn=g2.astype(BF)
    gact=dot_nt(gffn,wdn[e])
    gh=(gact*gelu_slope(hid)).astype(BF)
    act=gelu(hid)
    gn=g2+dot_nt(gh,wup[e])
    g1,gain1,shift1=norm_grad(pre1,vv[3:4],gn)
    nlow=norm(pre1,vv[3:4],vv[4:5])
    gb=g1.astype(BF)
    ga=dot_nt(gb,wo[e]).astype(BF).astype(F32)
    q0s=q0[rows,:]*0.125
    qa_s[...]=heads_apart(q0s,8).astype(BF)
    ga_s[...]=heads_apart(ga,8).astype(BF)
    u_s[0]=dot_nt(qa_s[...],wqkv[e,:,768:1536]).astype(BF)
    u_s[1]=dot_nt(ga_s[...],wqkv[e,:,1536:2304]).astype(BF)
    gq_s[...]=jnp.zeros_like(gq_s); sv_s[...]=jnp.zeros_like(sv_s)
    def block(i,_):
        row=i*256
        rr=i*R
        K=k[pl.ds(row,256),:]; V=v[pl.ds(row,256),:]; X=x[pl.ds(row,256),:]
        qa=qa_s[pl.ds(rr,R),:]; gab=ga_s[pl.ds(rr,R),:]
        s=dot_nt(qa,K)
        key=lax.broadcasted_iota(jnp.int32,(R,256),1)
        if n==1:
            ok=key<lens[i]
        else:
            grp=lax.broadcasted_iota(jnp.int32,(R,256),0)//16
            ok=(grp<0)
            for j in range(n):
                ok=ok|((grp==j)&(key>=j*slots)&(key<j*slots+lens[i*n+j]))
        s=jnp.where(ok,s,NEG)
        p=jnp.exp(s-jnp.max(s,axis=1,keepdims=True))
        p=p*(1.0/jnp.sum(p,axis=1,keepdims=True))
        gs=dot_nt(gab,V)
        gs=p*(gs-jnp.sum(p*gs,axis=1,keepdims=True))
        both=jnp.concatenate([gs,p],axis=0)
        bb=both.astype(BF)
        gq=dot(bb[:R],K)
        rr0=lax.broadcasted_iota(jnp.int32,(R,768),0); ll=lax.broadcasted_iota(jnp.int32,(R,768),1)//64
        gq=jnp.where(rr0%16==ll,gq,0.0)*0.125
        st=jnp.sum(bb[R:].astype(F32),axis=1,keepdims=True)
        sv_s[...]=sv_s[...]+jnp.sum(st*gab.astype(F32),axis=0,keepdims=True)
        mix=dot(bb,X)
        for j in range(n):
            slot=i*n+j
            gq_s[pl.ds(slot,1),:]=jnp.sum(gq[16*j:16*j+16],axis=0,keepdims=True)
            first=X[j*slots:j*slots+1].astype(F32)
            for c in range(6):
                cc=slice(128*c,128*c+128)
                ls[e,c,pl.ds(32+slot,12,stride=8),:]=mix[16*j:16*j+12,cc]
                ls[e,c,pl.ds(128+slot,12,stride=8),:]=mix[R+16*j:R+16*j+12,cc]
                ls[e,c,pl.ds(16+slot,1),:]=first[:,cc]
        uu=jnp.concatenate([u_s[0,pl.ds(rr,R),:],u_s[1,pl.ds(rr,R),:]],axis=0)
        gtok[pl.ds(row,256),:]=dot(both.T.astype(BF),uu)
        return _
    for i in range(nb): block(i,0)
    gql=gq_s[...].astype(BF)
    extra=g1+dot_nt(gql,wqkv[e,:,0:768])
    for i in range(seqs):
        gtok[i*slots:i*slots+1,:]=gtok[i*slots:i*slots+1,:]+extra[i:i+1]
    cs=lambda m: jnp.sum(m.astype(F32),axis=0,keepdims=True)
    sums=jnp.concatenate([cs(gql),sv_s[0:1],cs(gb),gain1,shift1,cs(gffn),gain2,shift2],axis=0)
    for c in range(6):
        cc=slice(128*c,128*c+128)
        ls[e,c,0:8,:]=nlow[:,cc]
        ls[e,c,8:16,:]=a0[rows,cc]
        ls[e,c,24:32,:]=sums[:,cc]
    la[e,0:8,:]=act
    la[e,8:16,:]=jnp.concatenate([cs(gh),jnp.zeros((7,3072),F32)],axis=0)
    rt=[(gffn.astype(F32)),gh.astype(F32),gb.astype(F32)]
    for half in range(2):
        o=0
        for m in rt:
            w=m.shape[1]//2
            right[half,rows,o:o+w]=m[:,half*w:half*w+w]; o+=w
        last=[gql.astype(F32),q0s[:,:384]] if half==0 else [q0s[:,384:],ga]
        for m in last:
            right[half,rows,o:o+m.shape[1]]=m; o+=m.shape[1]
def pick_matrix(off, lane0):
    r=lax.broadcasted_iota(jnp.int32,(256,128),0); l=lax.broadcasted_iota(jnp.int32,(256,128),1)
    return jnp.where((r-off==l-lane0)&(l>=lane0)&(l<lane0+48),1.0,0.0).astype(BF)
def left_messages(ls, la, left):
    two=lambda e,w: jnp.concatenate([ls[e,w//128],ls[e,w//128+1]],axis=1).astype(BF)
    aq=la[0].astype(BF); ap=la[1].astype(BF)
    def win(start, width):
        w=min(start//128*128, width-256); return w, start-w
    for j in range(16):
        w,off=win(48*j,768)
        m=dot(two(0,w),pick_matrix(off,0))+dot(two(1,w),pick_matrix(off,64))
        m=m.astype(BF)
        left[j,48:80,:]=m[0:32]; left[j,0:48,:]=m[32:80]; left[j,144:288,:]=m[80:224]
        for t in range(4):
            w,off=win(192*j+48*t,3072)
            left[j,80+16*t:96+16*t,:]=(dot(aq[:,w:w+256],pick_matrix(off,0))+dot(ap[:,w:w+256],pick_matrix(off,64))).astype(BF)
def back_kernel(ql,pln,gr,q0,a0,p1,h0,p2,qx,px,qk,qv,pk,pv,wqkv,wo,wup,wdn,vec,hb,gq_tok,gp_tok,left,right,ls,la,rs,u_s,gq_s,sv_s,qa_s,ga_s):
    ls[...]=jnp.zeros_like(ls)
    back_one(1,2,6,256,pln,px,pk,pv,gp_tok,gr,q0,a0,p1,h0,p2,wqkv,wo,wup,wdn,vec,hb,ls,la,rs,u_s,gq_s,sv_s,qa_s,ga_s)
    back_one(0,0,2,64,ql,qx,qk,qv,gq_tok,gr,q0,a0,p1,h0,p2,wqkv,wo,wup,wdn,vec,hb,ls,la,rs,u_s,gq_s,sv_s,qa_s,ga_s)
    right[...]=rs[...].astype(BF)
    left_messages(ls,la,left)
def backward(*a):
    S=jax.ShapeDtypeStruct
    V=pl.BlockSpec(memory_space=pltpu.VMEM); SM=pl.BlockSpec(memory_space=pltpu.SMEM)
    outs=[S((512,768),F32),S((1536,768),F32),S((16,LEFT_ROWS,128),BF),S((2,16,3456),BF)]
    VM=pltpu.VMEM
    return pl.pallas_call(back_kernel,out_shape=outs,in_specs=[SM,SM]+[V]*18,out_specs=[V]*4,
      scratch_shapes=[VM((2,6,224,128),F32),VM((2,16,3072),F32),VM((2,16,3456),F32),VM((2,128,768),BF),VM((8,768),F32),VM((8,768),F32),VM((128,768),BF),VM((128,768),BF)],
      compiler_params=pltpu.CompilerParams(vmem_limit_bytes=60*2**20),name="back")(*a)


MESH = pl.DeviceIdType.MESH

def ag_schedule(n_units, starts):
    out = []
    for t in range(max(starts) + 7):
        for u in sorted(range(n_units), key=lambda u: (starts[u], u)):
            s = t - starts[u]
            if 0 <= s <= 6: out.append((u, s))
    return out

class Gather:
    def __init__(self, units, ins, outs, send, recv):
        self.units, self.ins, self.outs, self.send, self.recv = units, ins, outs, send, recv
        w, self.y = lax.axis_index("wq"), lax.axis_index("np")
        self.w = w
        self.z, self.x, self.c = w // 4, (w // 2) % 2, w % 2
        self.pending = {}
    def dev(self, dz=0, fx=False, fy=False, fc=False):
        x = 1 - self.x if fx else self.x
        c = 1 - self.c if fc else self.c
        y = 1 - self.y if fy else self.y
        return ((self.z + dz) * 4 + x * 2 + c, y)
    def barrier(self):
        bar = pltpu.get_barrier_semaphore()
        def sig(**k): pl.semaphore_signal(bar, inc=1, device_id=self.dev(**k), device_id_type=MESH)
        sig(fx=True); sig(fy=True); sig(fc=True)
        @pl.when(self.z > 0)
        def _(): sig(dz=-1)
        @pl.when(self.z < 3)
        def _(): sig(dz=1)
        pl.semaphore_wait(bar, 3 + (self.z + 3) // 4 + (6 - self.z) // 4)
    def view(self, u, z=None, x=None, y=None, c=None):
        a, e, kind, r0, rn = self.units[u]
        o = self.outs[a]
        r, w = self.ins[a].shape[1:]
        zs = slice(None) if z is None else z
        xs = slice(None) if x is None else x
        cs = slice(None) if y is None else pl.ds(pl.multiple_of(y * w, 128), w)
        return o.at[e, zs, xs, pl.ds(pl.multiple_of((self.c if c is None else c) * r + r0, 16), rn), cs]
    def copy(self, u, sem, src, dst, dev):
        return pltpu.make_async_remote_copy(src_ref=src, dst_ref=dst, send_sem=self.send.at[u, sem], recv_sem=self.recv.at[u, sem], device_id=dev, device_id_type=MESH)
    def own_src(self, u):
        a, e, kind, r0, rn = self.units[u]
        return self.ins[a].at[e, pl.ds(r0, rn)]
    def zview(self, u, core, z):
        kind = self.units[u][2]
        if kind == "F": return self.view(u, z=z, x=self.x, y=self.y)
        if core == 0: return self.view(u, z=z, x=None, y=self.y)
        return self.view(u, z=z, x=self.x, y=None)
    def step(self, u, s):
        for core in (0, 1):
            pl.when(self.c == core)(lambda core=core: self._step(u, s, core))
    def A(self, core): return dict(fx=True) if core == 0 else dict(fy=True)
    def B(self, core): return dict(fy=True) if core == 0 else dict(fx=True)
    def a_src(self, u, core):
        kind = self.units[u][2]
        z = None if kind == "F" else self.z
        return self.view(u, z=z, x=self.x, y=self.y)
    def a_got(self, u, core):
        kind = self.units[u][2]
        z = None if kind == "F" else self.z
        return self.view(u, z=z, x=1 - self.x, y=self.y) if core == 0 else self.view(u, z=z, x=self.x, y=1 - self.y)
    def b_src(self, u, core):
        return self.view(u, x=None, y=self.y) if core == 0 else self.view(u, x=self.x, y=None)
    def b_got(self, u, core):
        return self.view(u, x=None, y=1 - self.y) if core == 0 else self.view(u, x=1 - self.x, y=None)
    def local(self, u, sem, ref):
        self.copy(u, sem, ref, ref, self.dev(fc=True)).start()
    def z_send(self, u, core, hop):
        z = self.z
        @pl.when((z - hop >= 0) & (z + 1 <= 3))
        def _():
            v = self.zview(u, core, z - hop)
            src = self.own_src(u) if (hop == 0 and self.units[u][2] == "F") else v
            self.copy(u, 2 + hop, src, v, self.dev(dz=1)).start()
        @pl.when((z + hop <= 3) & (z - 1 >= 0))
        def _():
            v = self.zview(u, core, z + hop)
            src = self.own_src(u) if (hop == 0 and self.units[u][2] == "F") else v
            self.copy(u, 5 + hop, src, v, self.dev(dz=-1)).start()
    def z_wait(self, u, core, hop):
        z = self.z
        @pl.when(z - 1 - hop >= 0)
        def _():
            v = self.zview(u, core, z - 1 - hop)
            self.copy(u, 2 + hop, v, v, self.dev(fc=True)).wait_recv()
            self.local(u, 11 + hop, v)
        @pl.when(z + 1 + hop <= 3)
        def _():
            v = self.zview(u, core, z + 1 + hop)
            self.copy(u, 5 + hop, v, v, self.dev(fc=True)).wait_recv()
            self.local(u, 14 + hop, v)
    def _step(self, u, s, core):
        F = self.units[u][2] == "F"
        own = self.view(u, z=self.z, x=self.x, y=self.y)
        if s == 0:
            src = self.own_src(u)
            self.copy(u, 8, src, own, self.dev(fc=True)).start()
            pltpu.make_async_copy(src, own, self.send.at[u, 17]).start()
            if F:
                self.z_send(u, core, 0)
            else:
                self.copy(u, 0, src, own, self.dev(**self.A(core))).start()
        if s == 1:
            pltpu.make_async_copy(self.own_src(u), own, self.send.at[u, 17]).wait()
            if F:
                self.z_wait(u, core, 0); self.z_send(u, core, 1)
            else:
                g = self.a_got(u, core)
                self.copy(u, 0, g, g, self.dev(fc=True)).wait_recv()
                self.z_send(u, core, 0)
                self.local(u, 9, g)
        if s == 2:
            if F: self.z_wait(u, core, 1); self.z_send(u, core, 2)
            else: self.z_wait(u, core, 0); self.z_send(u, core, 1)
        if s == 3:
            if F:
                self.z_wait(u, core, 2)
                v = self.a_src(u, core)
                self.copy(u, 0, v, v, self.dev(**self.A(core))).start()
            else:
                self.z_wait(u, core, 1); self.z_send(u, core, 2)
        if s == 4:
            if F:
                g = self.a_got(u, core)
                self.copy(u, 0, g, g, self.dev(fc=True)).wait_recv()
            else:
                self.z_wait(u, core, 2)
            v = self.b_src(u, core)
            self.copy(u, 1, v, v, self.dev(**self.B(core))).start()
            if F: self.local(u, 9, g)
        if s == 5:
            g = self.b_got(u, core)
            self.copy(u, 1, g, g, self.dev(fc=True)).wait_recv()
            self.local(u, 10, g)
        if s == 6:
            self.finish_recv(u, core); self.finish_send(u, core)
    def finish_recv(self, u, core):
        other = 1 - core
        c = 1 - self.c
        kind = self.units[u][2]
        def got(sem, v): self.copy(u, sem, v, v, self.dev(fc=True)).wait_recv()
        sv = lambda **k: self.view(u, c=c, **k)
        got(8, sv(z=self.z, x=self.x, y=self.y))
        za = None if kind == "F" else self.z
        got(9, sv(z=za, x=1 - self.x, y=self.y) if other == 0 else sv(z=za, x=self.x, y=1 - self.y))
        got(10, sv(x=None, y=1 - self.y) if other == 0 else sv(x=1 - self.x, y=None))
        def zv(z):
            if kind == "F": return sv(z=z, x=self.x, y=self.y)
            return sv(z=z, x=None, y=self.y) if other == 0 else sv(z=z, x=self.x, y=None)
        for hop in range(3):
            pl.when(self.z - 1 - hop >= 0)(lambda hop=hop: got(11 + hop, zv(self.z - 1 - hop)))
            pl.when(self.z + 1 + hop <= 3)(lambda hop=hop: got(14 + hop, zv(self.z + 1 + hop)))
    def finish_send(self, u, core):
        def sent(sem, v): self.copy(u, sem, v, v, self.dev(fc=True)).wait_send()
        own = self.view(u, z=self.z, x=self.x, y=self.y)
        sent(8, own)
        sent(0, self.a_src(u, core)); sent(1, self.b_src(u, core))
        sent(9, self.a_got(u, core)); sent(10, self.b_got(u, core))
        z = self.z
        for hop in range(3):
            pl.when((z - hop >= 0) & (z + 1 <= 3))(lambda hop=hop: sent(2 + hop, self.zview(u, core, z - hop)))
            pl.when((z + hop <= 3) & (z - 1 >= 0))(lambda hop=hop: sent(5 + hop, self.zview(u, core, z + hop)))
            pl.when(z - 1 - hop >= 0)(lambda hop=hop: sent(11 + hop, self.zview(u, core, z - 1 - hop)))
            pl.when(z + 1 + hop <= 3)(lambda hop=hop: sent(14 + hop, self.zview(u, core, z + 1 + hop)))

def gather_kernel(units, schedule, n, *refs):
    ins, outs, (send, recv) = refs[:n], refs[n:2*n], refs[2*n:]
    g = Gather(units, ins, outs, send, recv)
    g.barrier()
    for u, s in schedule: g.step(u, s)

def gather_call(arrays, units, schedule, name="gather"):
    n = len(arrays)
    shapes = [jax.ShapeDtypeStruct((a.shape[0], 4, 2, 2 * a.shape[1], 2 * a.shape[2]), a.dtype) for a in arrays]
    return pl.pallas_call(functools.partial(gather_kernel, units, schedule, n), out_shape=shapes,
        in_specs=[pl.BlockSpec(memory_space=pl.ANY)] * n, out_specs=[pl.BlockSpec(memory_space=pl.ANY)] * n,
        scratch_shapes=[pltpu.SemaphoreType.DMA((len(units), 18)), pltpu.SemaphoreType.DMA((len(units), 18))],
        compiler_params=pltpu.CompilerParams(collective_id=1, has_side_effects=True), name=name)(*arrays)


class Place:
    def __init__(self):
        self.w=lax.axis_index("wq"); self.y=lax.axis_index("np")
        self.z,self.x,self.c=self.w//4,(self.w//2)%2,self.w%2
        self.me=self.w*2+self.y
    def dev(self, z=None, fx=False, fy=False, fc=False):
        x=1-self.x if fx else self.x
        c=1-self.c if fc else self.c
        y=1-self.y if fy else self.y
        return ((self.z if z is None else z)*4+x*2+c, y)

def head_gather(pos, buf, send, recv):
    z,x,c,y=pos.z,pos.x,pos.c,pos.y
    def rc(sem,src,dev,dst=None):
        return pltpu.make_async_remote_copy(src_ref=src,dst_ref=src if dst is None else dst,send_sem=send.at[sem],recv_sem=recv.at[sem],device_id=dev,device_id_type=MESH)
    own=buf.at[z,x,c,y]
    for k in (1,2,3): rc(k-1,own,pos.dev(z=(z+k)%4)).start()
    def arrived(sem,ref): rc(sem,ref,pos.dev(fc=True)).wait_recv()
    for k in (1,2,3): arrived(k-1,buf.at[(z+4-k)%4,x,c,y])
    col=buf.at[:,x,c,y]
    def order(core):
        first=dict(fx=True) if core==0 else dict(fy=True)
        second=dict(fy=True) if core==0 else dict(fx=True)
        rc(3,col,pos.dev(**first)).start()
        rc(5,col,pos.dev(fc=True)).start()
        got=buf.at[:,1-x,c,y] if core==0 else buf.at[:,x,c,1-y]
        arrived(3,got)
        both=buf.at[:,:,c,y] if core==0 else buf.at[:,x,c,:]
        rc(4,both,pos.dev(**second)).start()
        rc(6,got,pos.dev(fc=True)).start()
        last=buf.at[:,:,c,1-y] if core==0 else buf.at[:,1-x,c,:]
        arrived(4,last)
        rc(7,last,pos.dev(fc=True)).start()
        o=1-c
        arrived(5,buf.at[:,x,o,y])
        arrived(6,buf.at[:,x,o,1-y] if core==0 else buf.at[:,1-x,o,y])
        arrived(7,buf.at[:,1-x,o,:] if core==0 else buf.at[:,:,o,1-y])
        for sem,ref in ((3,col),(4,both),(5,col),(6,got),(7,last)): rc(sem,ref,pos.dev(fc=True)).wait_send()
    for core in (0,1): pl.when(c==core)(functools.partial(order,core))
    for k in (1,2,3): rc(k-1,own,pos.dev(fc=True)).wait_send()

def similar_kernel(heads, marks, gr, loss, buf, gs_s, gt_s, send, recv):
    pos=Place()
    bar=pltpu.get_barrier_semaphore()
    for k in (1,2,3): pl.semaphore_signal(bar,inc=1,device_id=pos.dev(z=(pos.z+k)%4),device_id_type=MESH)
    for kw in (dict(fx=True),dict(fy=True),dict(fc=True)): pl.semaphore_signal(bar,inc=1,device_id=pos.dev(**kw),device_id_type=MESH)
    buf[pos.z,pos.x,pos.c,pos.y]=heads[...].astype(BF)
    pl.semaphore_wait(bar,6)
    head_gather(pos,buf,send,recv)
    g=buf[...].reshape(32,16,768).astype(F32)
    q=g[:,0:8].reshape(256,768).astype(BF); p=g[:,8:16].reshape(256,768).astype(BF)
    m=jnp.sum(marks[...].reshape(8,32,256),axis=0)
    m=m[0:16]+m[16:32]
    m=(m[:,0:128]+m[:,128:256]).astype(F32)
    row=lambda r: jnp.broadcast_to(jnp.concatenate([m[r:r+1],m[r+1:r+2]],axis=1),(256,256))
    qset=row(0).T; gold=row(2).T; pset=row(4)
    lane=lax.broadcasted_iota(jnp.int32,(256,256),1).astype(F32)
    is_gold=gold==lane
    usable=(qset==pset)|is_gold
    sim=dot_nt(q,p)*(768**-0.5)
    masked=jnp.where(usable,sim,NEG)
    high=jnp.max(masked,axis=1,keepdims=True)
    tot=high+jnp.log(jnp.sum(jnp.where(usable,jnp.exp(masked-high),0.0),axis=1,keepdims=True))
    gsc=jnp.sum(jnp.where(is_gold,sim,0.0),axis=1,keepdims=True)
    loss[...]=jnp.broadcast_to(jnp.sum(tot-gsc,axis=0,keepdims=True)*(1.0/256),loss.shape)
    soft=jnp.where(usable,jnp.exp(masked-tot),0.0)
    gsim=soft-jnp.where(is_gold,1.0,0.0)
    gs_s[...]=gsim; gt_s[...]=gsim.T
    me8=pl.ds(pl.multiple_of(pos.me*8,8),8)
    gr[0:8,:]=dot(gs_s[me8,:].astype(BF),p)*(768**-0.5)
    gr[8:16,:]=dot(gt_s[me8,:].astype(BF),q)*(768**-0.5)

def similar_call(heads,marks):
    V=pl.BlockSpec(memory_space=pltpu.VMEM)
    return pl.pallas_call(similar_kernel,out_shape=[jax.ShapeDtypeStruct((16,768),F32),jax.ShapeDtypeStruct((8,128),F32)],in_specs=[V,V],out_specs=[V,V],
      scratch_shapes=[pltpu.VMEM((4,2,2,2,16,768),BF),pltpu.VMEM((256,256),F32),pltpu.VMEM((256,256),F32),pltpu.SemaphoreType.DMA((8,)),pltpu.SemaphoreType.DMA((8,))],
      compiler_params=pltpu.CompilerParams(collective_id=2,has_side_effects=True,vmem_limit_bytes=40*2**20),name="similar")(heads,marks)

CHUNKS=3
class RightGather:
    def __init__(self,pos,src,buf,send,recv):
        self.pos,self.src,self.buf,self.send,self.recv=pos,src,buf,send,recv
        self.width=src.shape[2]//CHUNKS
    def rc(self,ch,sem,src,dst,dev):
        return pltpu.make_async_remote_copy(src_ref=src,dst_ref=dst,send_sem=self.send.at[ch,sem],recv_sem=self.recv.at[ch,sem],device_id=dev,device_id_type=MESH)
    def view(self,ch,z=None,x=None,c=None,y=None):
        p=self.pos
        f=lambda v: slice(None) if v is None else v
        return self.buf.at[f(z),p.x if x is None else x,p.c if c is None else c,f(y),:,ch*self.width:(ch+1)*self.width]
    def half(self,ch,y): return self.src.at[y,:,ch*self.width:(ch+1)*self.width]
    def step(self,ch,s):
        p=self.pos; z,y=p.z,p.y
        sib=p.dev(fc=True)
        def arrived(sem,v): self.rc(ch,sem,v,v,sib).wait_recv()
        def local(sem,v): self.rc(ch,sem,v,v,sib).start()
        def z_send(hop):
            @pl.when((z-hop>=0)&(z+1<=3))
            def _():
                v=self.view(ch,z=z-hop); self.rc(ch,2+hop,v,v,p.dev(z=z+1)).start()
            @pl.when((z+hop<=3)&(z-1>=0))
            def _():
                v=self.view(ch,z=z+hop); self.rc(ch,5+hop,v,v,p.dev(z=z-1)).start()
        def z_wait(hop):
            @pl.when(z-1-hop>=0)
            def _():
                v=self.view(ch,z=z-1-hop); arrived(2+hop,v); local(9+hop,v)
            @pl.when(z+1+hop<=3)
            def _():
                v=self.view(ch,z=z+1+hop); arrived(5+hop,v); local(12+hop,v)
        own=self.view(ch,z=z,y=y)
        if s==0:
            self.rc(ch,0,self.half(ch,1-y),own,p.dev(fy=True)).start()
            pltpu.make_async_copy(self.half(ch,y),own,self.send.at[ch,16]).start()
        if s==1:
            pltpu.make_async_copy(self.half(ch,y),own,self.send.at[ch,16]).wait()
            arrived(0,self.view(ch,z=z,y=1-y))
            z_send(0); local(8,self.view(ch,z=z))
        if s==2: z_wait(0); z_send(1)
        if s==3: z_wait(1); z_send(2)
        if s==4:
            z_wait(2)
            v=self.view(ch); self.rc(ch,1,v,v,p.dev(fx=True)).start()
        if s==5:
            g=self.view(ch,x=1-p.x); arrived(1,g); local(15,g)
        if s==6:
            o=1-p.c
            arrived(8,self.view(ch,z=z,c=o)); arrived(15,self.view(ch,x=1-p.x,c=o))
            def sent(sem,v): self.rc(ch,sem,v,v,sib).wait_send()
            sent(0,own); sent(1,self.view(ch)); sent(8,self.view(ch,z=z)); sent(15,self.view(ch,x=1-p.x))
            for hop in range(3):
                pl.when(z-1-hop>=0)(lambda hop=hop: arrived(9+hop,self.view(ch,z=z-1-hop,c=o)))
                pl.when(z+1+hop<=3)(lambda hop=hop: arrived(12+hop,self.view(ch,z=z+1+hop,c=o)))
                pl.when((z-hop>=0)&(z+1<=3))(lambda hop=hop: sent(2+hop,self.view(ch,z=z-hop)))
                pl.when((z+hop<=3)&(z-1>=0))(lambda hop=hop: sent(5+hop,self.view(ch,z=z+hop)))
                pl.when(z-1-hop>=0)(lambda hop=hop: sent(9+hop,self.view(ch,z=z-1-hop)))
                pl.when(z+1+hop<=3)(lambda hop=hop: sent(12+hop,self.view(ch,z=z+1+hop)))

def left_copies(pos,left,buf,send,recv):
    def to(d):
        t=(pos.me+d)%32
        return t//2,t%2
    def send_one(d,go):
        w,y=to(d)
        for half,(r0,n) in enumerate(((0,144),(48,240))):
            @pl.when(y==half)
            def _():
                go(pltpu.make_async_remote_copy(src_ref=left.at[w,pl.ds(r0,n)],dst_ref=buf.at[pos.me,pl.ds(0,n)],send_sem=send.at[d],recv_sem=recv.at[d],device_id=(w,y),device_id_type=MESH))
    def start():
        def lap(d,kept):
            send_one(d,lambda cp: cp.start()); return kept
        lax.fori_loop(1,32,lap,0)
    def finish():
        def lap(d,kept):
            send_one(d,lambda cp: cp.wait_send())
            s=(pos.me+32-d)%32
            for half,(r0,n) in enumerate(((0,144),(48,240))):
                @pl.when(pos.y==half)
                def _():
                    v=buf.at[s,pl.ds(0,n)]
                    pltpu.make_async_remote_copy(src_ref=v,dst_ref=v,send_sem=send.at[d],recv_sem=recv.at[d],device_id=(pos.w,pos.y),device_id_type=MESH).wait_recv()
            return kept
        lax.fori_loop(1,32,lap,0)
    def own():
        for half,(r0,n) in enumerate(((0,144),(48,240))):
            @pl.when(pos.y==half)
            def _(): buf[pos.me,0:n,:]=left[pos.w,r0:r0+n,:]
    return start,own,finish

def all_barrier(pos):
    bar=pltpu.get_barrier_semaphore()
    def lap(d,kept):
        t=(pos.me+d)%32
        pl.semaphore_signal(bar,inc=1,device_id=(t//2,t%2),device_id_type=MESH)
        return kept
    lax.fori_loop(1,32,lap,0)
    pl.semaphore_wait(bar,31)

def weight_products(pos,lbuf,rbuf,wqkv,wout,win,wback,gvec,gbin,bq,bp):
    r=rbuf[...].reshape(32,16,3456).astype(F32)
    bq[...]=r[:,0:8].reshape(256,3456).astype(BF)
    bp[...]=r[:,8:16].reshape(256,3456).astype(BF)
    def pair(r0):
        t=lbuf[:,r0:r0+16,:].astype(F32)
        return [t[:,8*i:8*i+8].reshape(256,128) for i in (0,1)]
    def put(out,rows,cols,tt,bcols):
        tt=tt.T.astype(BF)
        out[0,rows,cols]=dot(tt,bq[:,bcols])[0:48]
        out[1,rows,cols]=dot(tt,bp[:,bcols])[64:112]
    everything=slice(None)
    def common(base):
        nrm,att=pair(base)
        put(win,everything,everything,nrm,slice(384,1920))
        put(wout,everything,everything,att,slice(1920,2304))
        for k in range(4):
            put(wback,slice(48*k,48*k+48),everything,pair(base+32+16*k)[0],slice(0,384))
        x0,vs=pair(base+16)
        vs=jnp.sum(vs.reshape(32,8,128),axis=0)
        bs=[jnp.sum(pair(base+32+16*k)[1].reshape(32,8,128),axis=0)[0:1] for k in range(4)]
        return x0,vs,bs
    def mixed(r0,heads,col0,dst0):
        for h in range(0,heads,2):
            a,b=pair(r0+8*h)
            a=a.T.astype(BF); b=b.T.astype(BF)
            cs=slice(col0+64*h,col0+64*h+128); ds=slice(dst0+64*h,dst0+64*h+128)
            low=lax.broadcasted_iota(jnp.int32,(128,128),1)<64
            wqkv[0,:,ds]=jnp.where(low,dot(a,bq[:,cs]),dot(b,bq[:,cs]))[0:48]
            wqkv[1,:,ds]=jnp.where(low,dot(a,bp[:,cs]),dot(b,bp[:,cs]))[64:112]
    def sums(vs,bs,half):
        gvec[0]=vs[4*half:4*half+4,0:48]; gvec[1]=vs[4*half:4*half+4,64:112]
        for i in (0,1):
            gbin[0,i:i+1,:]=bs[2*half+i][:,0:48]; gbin[1,i:i+1,:]=bs[2*half+i][:,64:112]
    @pl.when(pos.y==0)
    def _():
        x0,vs,bs=common(48)
        put(wqkv,everything,slice(0,768),x0,slice(2304,3072))
        mixed(0,6,3072,768)
        sums(vs,bs,0)
    @pl.when(pos.y==1)
    def _():
        x0,vs,bs=common(0)
        mixed(96,6,2304,0)
        mixed(144,12,2688,384)
        sums(vs,bs,1)

def exchange_kernel(left,right,wqkv,wout,win,wback,gvec,gbin,lbuf,rbuf,bq,bp,lsend,lrecv,rsend,rrecv):
    pos=Place()
    all_barrier(pos)
    g=RightGather(pos,right,rbuf,rsend,rrecv)
    lstart,lown,lfinish=left_copies(pos,left,lbuf,lsend,lrecv)
    for ch in range(CHUNKS): g.step(ch,0)
    lstart()
    lown()
    for t in range(CHUNKS+6):
        for ch in range(CHUNKS):
            if 1<=t-ch<=6: g.step(ch,t-ch)
    lfinish()
    weight_products(pos,lbuf,rbuf,wqkv,wout,win,wback,gvec,gbin,bq,bp)

def exchange_call(left,right):
    V=pl.BlockSpec(memory_space=pltpu.VMEM); S=jax.ShapeDtypeStruct; VM=pltpu.VMEM; D=pltpu.SemaphoreType.DMA
    outs=[S((2,48,1152),F32),S((2,48,384),F32),S((2,48,1536),F32),S((2,192,384),F32),S((2,4,48),F32),S((2,2,48),F32)]
    return pl.pallas_call(exchange_kernel,out_shape=outs,in_specs=[V,V],out_specs=[V]*6,
      scratch_shapes=[VM((32,240,128),BF),VM((4,2,2,2,16,3456),BF),VM((256,3456),BF),VM((256,3456),BF),D((32,)),D((32,)),D((CHUNKS,17)),D((CHUNKS,17))],
      compiler_params=pltpu.CompilerParams(collective_id=3,has_side_effects=True,vmem_limit_bytes=50*2**20),name="exchange")(left,right)


def small_tile(vectors, hidden_bias):
    tile = jnp.zeros((1, 16, 128), vectors.dtype)
    count, rows, width = vectors.shape
    tile = tile.at[0, : count * rows, :width].set(vectors.reshape(count * rows, width))
    return tile.at[0, count * rows : count * rows + count, : hidden_bias.shape[1]].set(hidden_bias)


def small_whole(tiles, vectors, hidden_bias):
    count, rows, width = vectors.shape
    tiles = tiles.reshape(16, 16, 2, 128)
    whole = tiles[:, : count * rows, :, :width].reshape(16, count, rows, 2, width)
    whole = whole.transpose(1, 3, 2, 0, 4).reshape(count, 2 * rows, 16 * width)
    bias = tiles[:, count * rows : count * rows + count, :, : hidden_bias.shape[1]]
    bias = bias.transpose(1, 0, 2, 3).reshape(count, -1)
    return (whole, bias)


def mark_tile(q_set, gold, p_set):
    me = lax.axis_index("wq") * 2 + lax.axis_index("np")
    spare = jnp.full((8 - p_set.shape[0],), -1, jnp.int32)
    columns = gold // p_set.shape[0] * 8 + gold % p_set.shape[0]
    rows = jnp.stack([q_set, columns, jnp.concatenate([p_set, spare])])
    rows = jnp.where((jnp.arange(256) // 8 == me)[None, :], jnp.tile(rows, (1, 32)), 0)
    return jnp.zeros((1, 16, 128), jnp.int32).at[0, :6].set(rows.reshape(6, 128))


GATHER_ORDER = ((4, 0), (5, 0), (0, 1), (0, 0), (1, 1), (1, 0), (2, 1), (3, 1), (2, 0), (3, 0))


def gather_units(arrays):
    parts = (3, 1, 3, 3, 1, 1)
    units = []
    for a, e in GATHER_ORDER:
        rows = arrays[a].shape[1] // parts[a]
        for j in range(parts[a]):
            units.append((a, e, "MFM"[len(units) % 3], j * rows, rows))
    return units, ag_schedule(len(units), [max(i - 1, 0) // 3 for i in range(len(units))])


def kernel_shards(
    q_embed, p_embed, q_len, p_len, q_set, p_set, gold, wqkv, wout, wup, wdown, vectors, hidden_bias
):
    arrays = (
        wqkv, wout, wup, wdown, small_tile(vectors, hidden_bias), mark_tile(q_set, gold, p_set)
    )
    whole = gather_call(arrays, *gather_units(arrays))
    weights = tuple(
        member.reshape(2, 16 * shard.shape[1], 2 * shard.shape[2])
        for member, shard in zip(whole[:4], arrays[:4])
    )
    vec, bias = small_whole(whole[4], vectors, hidden_bias)
    vec, bias = vec.astype(jnp.float32), bias.astype(jnp.float32)[:, None, :]
    done = forward(q_len, p_len, q_embed, p_embed, *weights, vec, bias)
    q_out, p_out, q_keys, q_values, p_keys, p_values, q0, a0, p1, h0, p2, heads = done
    grad_first, loss = similar_call(heads, whole[5])
    grad_q, grad_p, left, right = backward(
        q_len, p_len, grad_first, q0, a0, p1, h0, p2, q_embed, p_embed,
        q_keys, q_values, p_keys, p_values, *weights, vec, bias,
    )
    grads = exchange_call(left, right)
    return (
        loss[0, 0], q_out, p_out, grad_q, grad_p, *grads[:5], grads[5].reshape(2, -1)
    )


def kernels_fit(q_embed, p_embed, q_len, p_len):
    return (
        lax.axis_size("wq") == 16
        and lax.axis_size("np") == 2
        and q_embed.shape == (512, 768)
        and p_embed.shape == (1536, 768)
        and q_len.shape == (8,)
        and p_len.shape == (6,)
    )


def shards(
    q_embed,
    p_embed,
    q_len,
    p_len,
    q_set,
    p_set,
    gold,
    query_key_value_weight,
    attention_output_weight,
    up_weight,
    down_weight,
    vectors,
    hidden_bias,
):
    if kernels_fit(q_embed, p_embed, q_len, p_len):
        return kernel_shards(
            q_embed,
            p_embed,
            q_len,
            p_len,
            q_set,
            p_set,
            gold,
            query_key_value_weight,
            attention_output_weight,
            up_weight,
            down_weight,
            vectors,
            hidden_bias,
        )
    gathered = gather_weights(
        query_key_value_weight,
        attention_output_weight,
        up_weight,
        down_weight,
        vectors,
        hidden_bias,
    )
    wq_size, np_size = lax.axis_size("wq"), lax.axis_size("np")
    both_axes = ("wq", "np")
    q_weights = tuple((member[0] for member in gathered))
    p_weights = tuple((member[1] for member in gathered))
    p_encoded, p_stored = encode_forward(p_embed, p_len, p_weights)
    q_encoded, q_stored = encode_forward(q_embed, q_len, q_weights)
    model_width = q_embed.shape[1]
    ff_width = gathered[2].shape[2]
    q_count = q_len.shape[0]
    p_count = p_len.shape[0]
    own_heads = jnp.concatenate([first_rows(q_encoded, q_count), first_rows(p_encoded, p_count)])
    heads = lax.all_gather(own_heads, both_axes, axis=0)
    marks = lax.all_gather(jnp.concatenate([q_set, gold, p_set]), both_axes, axis=0)
    q_heads = heads[:, :q_count].reshape(-1, model_width)
    p_heads = heads[:, q_count:].reshape(-1, model_width)
    q_sets = marks[:, :q_count].reshape(-1)
    golds = marks[:, q_count : 2 * q_count].reshape(-1)
    p_sets = marks[:, 2 * q_count :].reshape(-1)
    scaling = model_width ** (-0.5)
    similar = (
        jnp.einsum("qd,pd->qp", q_heads, p_heads, preferred_element_type=jnp.float32) * scaling
    )
    is_gold = jnp.arange(p_heads.shape[0], dtype=jnp.int32)[None, :] == golds[:, None]
    usable = (q_sets[:, None] == p_sets[None, :]) | is_gold
    masked = jnp.where(usable, similar, NEGATIVE)
    highest = jnp.max(masked, axis=1)
    total = jnp.sum(jnp.where(usable, jnp.exp(masked - highest[:, None]), 0.0), axis=1)
    log_total = highest + jnp.log(total)
    gold_score = jnp.sum(jnp.where(is_gold, similar, 0.0), axis=1)
    loss = jnp.mean(log_total - gold_score)
    soft_rows = jnp.where(usable, jnp.exp(masked - log_total[:, None]), 0.0)
    grad_similar = (soft_rows - is_gold.astype(jnp.float32)).astype(jnp.bfloat16)
    me = lax.axis_index("wq") * np_size + lax.axis_index("np")
    grad_q_first = (
        jnp.einsum(
            "qp,pd->qd",
            lax.dynamic_slice_in_dim(grad_similar, me * q_count, q_count, 0),
            p_heads,
            preferred_element_type=jnp.float32,
        )
        * scaling
    )
    grad_p_first = (
        jnp.einsum(
            "qp,qd->pd",
            lax.dynamic_slice_in_dim(grad_similar, me * p_count, p_count, 1),
            q_heads,
            preferred_element_type=jnp.float32,
        )
        * scaling
    )
    q_back = encode_backward(q_embed, q_weights, q_stored, grad_q_first)
    p_back = encode_backward(p_embed, p_weights, p_stored, grad_p_first)
    left = jnp.concatenate(
        [left_message(member[1], wq_size, np_size) for member in (q_back, p_back)], axis=2
    )
    left = left.reshape((wq_size * np_size,) + left.shape[2:])
    left = lax.all_to_all(left, both_axes, 0, 0)
    right = jnp.concatenate([right_message(member[2], np_size) for member in (q_back, p_back)], axis=1)
    right = lax.all_gather(lax.all_to_all(right, "np", 0, 0), "wq", axis=0)
    right = right.reshape((wq_size * np_size,) + right.shape[2:])
    sums = jnp.concatenate(
        [
            jnp.stack([q_back[3], p_back[3]])
            .reshape(2, np_size, -1, wq_size, model_width // wq_size)
            .transpose(3, 1, 0, 2, 4)
            .reshape(wq_size * np_size, -1),
            jnp.stack([q_back[4], p_back[4]])
            .reshape(2, wq_size * np_size, -1)
            .transpose(1, 0, 2)
            .reshape(wq_size * np_size, -1),
        ],
        axis=1,
    )
    sums = jnp.sum(lax.all_to_all(sums, both_axes, 0, 0), axis=0)
    grad_vectors = sums[: sums.shape[0] - 2 * ff_width // (wq_size * np_size)].reshape(
        2, -1, model_width // wq_size
    )
    grad_b_in = sums[sums.shape[0] - 2 * ff_width // (wq_size * np_size) :].reshape(2, -1)
    q_weight_grads = weight_grads(
        left[:, :q_count].reshape(-1, left.shape[2]),
        right[:, :q_count].reshape(-1, right.shape[2]),
        model_width,
        ff_width,
        wq_size,
        np_size,
    )
    p_weight_grads = weight_grads(
        left[:, q_count:].reshape(-1, left.shape[2]),
        right[:, q_count:].reshape(-1, right.shape[2]),
        model_width,
        ff_width,
        wq_size,
        np_size,
    )
    shared = tuple(jnp.stack(pair) for pair in zip(q_weight_grads, p_weight_grads))
    return (
        loss,
        q_encoded,
        p_encoded,
        q_back[0],
        p_back[0],
        shared[0],
        shared[1],
        shared[2],
        shared[3],
        grad_vectors,
        grad_b_in,
    )


def solution(mesh):
    return jax.shard_map(
        shards,
        mesh=mesh,
        in_specs=(
            P(("wq", "np"), None),
            P(("wq", "np"), None),
            P(("wq", "np")),
            P(("wq", "np")),
            P(("wq", "np")),
            P(("wq", "np")),
            P(("wq", "np")),
            P(None, "wq", "np"),
            P(None, "wq", "np"),
            P(None, "wq", "np"),
            P(None, "wq", "np"),
            P(None, "np", "wq"),
            P(None, ("wq", "np")),
        ),
        out_specs=(
            P(),
            P(("wq", "np"), None),
            P(("wq", "np"), None),
            P(("wq", "np"), None),
            P(("wq", "np"), None),
            P(None, "wq", "np"),
            P(None, "wq", "np"),
            P(None, "wq", "np"),
            P(None, "wq", "np"),
            P(None, "np", "wq"),
            P(None, ("wq", "np")),
        ),
        check_vma=False,
    )
```

```python
import functools
import math

import jax
import jax.numpy as jnp
from jax import lax
from jax.experimental import pallas as pl
from jax.experimental.pallas import tpu as pltpu
from jax.sharding import PartitionSpec as P


HEADS = 12


EPSILON = 1e-12
NEGATIVE = -1e30


def layer_norm(inputs, gain_row, offset):
    centred = inputs - jnp.mean(inputs, axis=-1, keepdims=True)
    spread = jnp.mean(centred * centred, axis=-1, keepdims=True)
    return centred * lax.rsqrt(spread + EPSILON) * gain_row + offset


def smooth_gate(values):
    return jax.nn.gelu(values, approximate=True)


def gather_weights(
    query_key_value_weight, attention_output_weight, up_weight, down_weight, vectors, hidden_bias
):
    np_parts = (
        lax.all_gather(query_key_value_weight, "np", axis=2, tiled=True),
        lax.all_gather(attention_output_weight, "np", axis=2, tiled=True),
        lax.all_gather(up_weight, "np", axis=2, tiled=True),
        lax.all_gather(down_weight, "np", axis=2, tiled=True),
        lax.all_gather(vectors, "np", axis=1, tiled=True),
        lax.all_gather(hidden_bias, "np", axis=1, tiled=True),
    )
    return (
        lax.all_gather(np_parts[0], "wq", axis=1, tiled=True),
        lax.all_gather(np_parts[1], "wq", axis=1, tiled=True),
        lax.all_gather(np_parts[2], "wq", axis=1, tiled=True),
        lax.all_gather(np_parts[3], "wq", axis=1, tiled=True),
        lax.all_gather(np_parts[4], "wq", axis=2, tiled=True),
        lax.all_gather(np_parts[5], "wq", axis=1, tiled=True),
    )


def head_split(matrix, seq_count):
    row_count, model_width = matrix.shape
    return matrix.reshape(seq_count, row_count // seq_count, HEADS, model_width // HEADS)


def attention_scores(queries, keys_low, lengths):
    seq_count = lengths.shape[0]
    split_q = head_split(queries, seq_count)
    scores = jnp.einsum(
        "sqhc,skhc->shqk",
        split_q,
        head_split(keys_low, seq_count),
        preferred_element_type=jnp.float32,
    )
    scores = scores * split_q.shape[3] ** (-0.5)
    live_mask = jnp.arange(split_q.shape[1])[None, :] < lengths[:, None]
    return jnp.where(live_mask[:, None, None, :], scores, NEGATIVE)


def first_rows(matrix, seq_count):
    row_count, width = matrix.shape
    return matrix.reshape(seq_count, row_count // seq_count, width)[:, 0, :]


def encode_forward(token_rows, lengths, weights):
    (
        query_key_value_weight,
        attention_output_weight,
        up_weight,
        down_weight,
        vectors,
        hidden_bias,
    ) = weights
    row_count, model_width = token_rows.shape
    seq_count = lengths.shape[0]
    vec_f32 = vectors.astype(jnp.float32)
    projected_rows = jnp.dot(token_rows, query_key_value_weight, preferred_element_type=jnp.float32)
    queries = (projected_rows[:, :model_width] + vec_f32[0]).astype(jnp.bfloat16)
    keys_low = projected_rows[:, model_width : 2 * model_width].astype(jnp.bfloat16)
    values = (projected_rows[:, 2 * model_width :] + vec_f32[1]).astype(jnp.bfloat16)
    scores = attention_scores(queries, keys_low, lengths)
    totals = jax.nn.logsumexp(scores, axis=-1, keepdims=True)
    soft_low = jnp.exp(scores - totals).astype(jnp.bfloat16)
    attended_tokens = jnp.einsum(
        "shqk,skhc->sqhc",
        soft_low,
        head_split(values, seq_count),
        preferred_element_type=jnp.float32,
    )
    attended_tokens = attended_tokens.reshape(row_count, model_width).astype(jnp.bfloat16)
    residual_branch = (
        jnp.dot(attended_tokens, attention_output_weight, preferred_element_type=jnp.float32)
        + vec_f32[2]
    )
    pre_one = token_rows.astype(jnp.float32) + residual_branch
    first_normed = layer_norm(pre_one, vec_f32[3], vec_f32[4])
    normed_low = first_normed.astype(jnp.bfloat16)
    hidden_rows = jnp.dot(
        normed_low, up_weight, preferred_element_type=jnp.float32
    ) + hidden_bias.astype(jnp.float32)
    activated_hidden = smooth_gate(hidden_rows).astype(jnp.bfloat16)
    feedforward_output = (
        jnp.dot(activated_hidden, down_weight, preferred_element_type=jnp.float32) + vec_f32[5]
    )
    pre_two = first_normed + feedforward_output
    encoded_low = layer_norm(pre_two, vec_f32[6], vec_f32[7]).astype(jnp.bfloat16)
    soft_first = jnp.exp(scores[:, :, 0, :] - totals[:, :, 0, :])
    stored = (
        first_rows(queries, seq_count),
        keys_low,
        values,
        soft_first,
        first_rows(attended_tokens, seq_count),
        first_rows(pre_one, seq_count),
        first_rows(normed_low, seq_count),
        first_rows(hidden_rows, seq_count),
        first_rows(activated_hidden, seq_count),
        first_rows(pre_two, seq_count),
    )
    return (encoded_low, stored)


def norm_back(pre, gain_row, grad_out):
    centred = pre - jnp.mean(pre, axis=-1, keepdims=True)
    inverse = lax.rsqrt(jnp.mean(centred * centred, axis=-1, keepdims=True) + EPSILON)
    scaled = grad_out * gain_row
    inner = jnp.mean(scaled * centred, axis=-1, keepdims=True)
    grad_in = inverse * (
        scaled - jnp.mean(scaled, axis=-1, keepdims=True) - centred * (inverse * inverse * inner)
    )
    return (grad_in, jnp.sum(grad_out * centred * inverse, axis=0), jnp.sum(grad_out, axis=0))


def encode_backward(token_rows, weights, stored, grad_first):
    (
        query_key_value_weight,
        attention_output_weight,
        up_weight,
        down_weight,
        vectors,
        hidden_bias,
    ) = weights
    (
        queries,
        keys_low,
        values,
        soft_first,
        attended,
        pre_one,
        normed_low,
        hidden_rows,
        activated_hidden,
        pre_two,
    ) = stored
    seq_count, model_width = queries.shape
    seq_length = token_rows.shape[0] // seq_count
    head_width = model_width // HEADS
    scaling = head_width ** (-0.5)
    vec_f32 = vectors.astype(jnp.float32)
    grad_two, gain_two, shift_two = norm_back(pre_two, vec_f32[6], grad_first)
    grad_ffn = grad_two.astype(jnp.bfloat16)
    grad_activated = jnp.einsum(
        "rd,fd->rf", grad_ffn, down_weight, preferred_element_type=jnp.float32
    )
    grad_hidden = jax.vjp(smooth_gate, hidden_rows)[1](grad_activated)[0].astype(jnp.bfloat16)
    grad_normed = grad_two + jnp.einsum(
        "rf,df->rd", grad_hidden, up_weight, preferred_element_type=jnp.float32
    )
    grad_one, gain_one, shift_one = norm_back(pre_one, vec_f32[3], grad_normed)
    grad_branch = grad_one.astype(jnp.bfloat16)
    grad_attended = jnp.einsum(
        "re,de->rd", grad_branch, attention_output_weight, preferred_element_type=jnp.float32
    ).astype(jnp.bfloat16)
    grad_heads = grad_attended.reshape(seq_count, HEADS, head_width)
    grad_soft = jnp.einsum(
        "shc,skhc->shk",
        grad_heads,
        head_split(values, seq_count),
        preferred_element_type=jnp.float32,
    )
    row_inner = jnp.sum(soft_first * grad_soft, axis=-1, keepdims=True)
    grad_scores = (soft_first * (grad_soft - row_inner)).astype(jnp.bfloat16)
    soft_low = soft_first.astype(jnp.bfloat16)
    grad_queries = (
        jnp.einsum(
            "shk,skhc->shc",
            grad_scores,
            head_split(keys_low, seq_count),
            preferred_element_type=jnp.float32,
        )
        * scaling
    )
    grad_q_low = grad_queries.reshape(seq_count, model_width).astype(jnp.bfloat16)
    tokens = token_rows.reshape(seq_count, seq_length, model_width)
    both = jnp.concatenate([grad_scores, soft_low], axis=1)
    mixed = jnp.einsum("sgk,skd->sgd", both, tokens, preferred_element_type=jnp.float32).astype(
        jnp.bfloat16
    )
    scaled_queries = (queries.astype(jnp.float32) * scaling).astype(jnp.bfloat16)
    split_weight = query_key_value_weight.reshape(model_width, 3, HEADS, head_width)
    back_rows = jnp.concatenate(
        [
            jnp.einsum(
                "shc,dhc->shd",
                scaled_queries.reshape(seq_count, HEADS, head_width),
                split_weight[:, 1],
                preferred_element_type=jnp.float32,
            ),
            jnp.einsum(
                "shc,dhc->shd",
                grad_heads,
                split_weight[:, 2],
                preferred_element_type=jnp.float32,
            ),
        ],
        axis=1,
    ).astype(jnp.bfloat16)
    grad_tokens = jnp.einsum("sgk,sgd->skd", both, back_rows, preferred_element_type=jnp.float32)
    first_extra = grad_one + jnp.einsum(
        "se,de->sd",
        grad_q_low,
        query_key_value_weight[:, :model_width],
        preferred_element_type=jnp.float32,
    )
    is_first = (jnp.arange(seq_length) == 0)[None, :, None]
    grad_tokens = grad_tokens + jnp.where(is_first, first_extra[:, None, :], 0.0)
    soft_total = jnp.sum(soft_low.astype(jnp.float32), axis=-1, keepdims=True)
    vector_parts = jnp.stack(
        [
            jnp.sum(grad_q_low.astype(jnp.float32), axis=0),
            jnp.sum(grad_heads.astype(jnp.float32) * soft_total, axis=0).reshape(model_width),
            jnp.sum(grad_branch.astype(jnp.float32), axis=0),
            gain_one,
            shift_one,
            jnp.sum(grad_ffn.astype(jnp.float32), axis=0),
            gain_two,
            shift_two,
        ]
    )
    bias_part = jnp.sum(grad_hidden.astype(jnp.float32), axis=0)
    left = (
        activated_hidden,
        normed_low,
        attended,
        jnp.concatenate(
            [jnp.broadcast_to(tokens[:, :1, :], (seq_count, HEADS, model_width)), mixed], axis=1
        ),
    )
    right = (
        grad_ffn,
        grad_hidden,
        grad_branch,
        jnp.concatenate([grad_q_low, scaled_queries, grad_attended], axis=1),
    )
    return (
        grad_tokens.reshape(token_rows.shape),
        left,
        right,
        vector_parts,
        bias_part,
    )


def left_message(left, wq_size, np_size):
    activated, normed, attended, mixed = left
    rows, groups, model_width = mixed.shape
    part = model_width // wq_size
    columns = 3 * model_width // np_size
    head_width = model_width // HEADS
    group = math.gcd(head_width, columns)
    mixed = jnp.repeat(mixed, head_width // group, axis=1)
    mixed = mixed.reshape(rows, np_size, columns // group, wq_size, part)
    mixed = mixed.transpose(3, 1, 0, 2, 4).reshape(wq_size, np_size, rows, columns // group * part)

    def same(matrix):
        pieces = matrix.reshape(rows, wq_size, -1).transpose(1, 0, 2)
        return jnp.broadcast_to(pieces[:, None], (wq_size, np_size) + pieces.shape[1:])

    return jnp.concatenate([same(activated), same(normed), same(attended), mixed], axis=3)


def right_message(right, np_size):
    rows = right[0].shape[0]
    return jnp.concatenate(
        [member.reshape(rows, np_size, -1).transpose(1, 0, 2) for member in right], axis=2
    )


def weight_grads(left, right, model_width, ff_width, wq_size, np_size):
    rows = left.shape[0]
    part, ff_part = model_width // wq_size, ff_width // wq_size
    columns = 3 * model_width // np_size
    group = math.gcd(model_width // HEADS, columns)
    right_sizes = (model_width // np_size, ff_width // np_size, model_width // np_size)
    cut = [ff_part, ff_part + part, ff_part + 2 * part]
    activated, normed, attended, mixed = jnp.split(left, cut, axis=1)
    cut = [right_sizes[0], right_sizes[0] + right_sizes[1], sum(right_sizes)]
    grad_ffn, grad_hidden, grad_branch, grad_projected = jnp.split(right, cut, axis=1)

    def outer(one, two):
        return jnp.einsum("sd,se->de", one, two, preferred_element_type=jnp.float32)

    w_qkv = jnp.einsum(
        "sgd,sgc->dgc",
        mixed.reshape(rows, columns // group, part),
        grad_projected.reshape(rows, columns // group, group),
        preferred_element_type=jnp.float32,
    ).reshape(part, columns)
    return (
        w_qkv,
        outer(attended, grad_branch),
        outer(normed, grad_hidden),
        outer(activated, grad_ffn),
    )


BLK=256
F32=jnp.float32; BF=jnp.bfloat16
NEG=-1e30; EPS=1e-12
def dot(a,b): return jnp.dot(a,b,preferred_element_type=F32)
def norm(u,g,b):
    c=u-jnp.mean(u,axis=-1,keepdims=True)
    s=jnp.mean(c*c,axis=-1,keepdims=True)
    return c*lax.rsqrt(s+EPS)*g+b
def put_first(ref, e, i, cols, v):
    if e==1:
        ref[pl.ds(8+i,1),cols]=v[0:1]
    else:
        for j in range(4): ref[pl.ds(4*i+j,1),cols]=v[64*j:64*j+1]
def make_bias(bias_ref, slot, lens, slots):
    n=BLK//slots
    key=lax.broadcasted_iota(jnp.int32,(BLK,BLK),0)
    qry=lax.broadcasted_iota(jnp.int32,(BLK,BLK),1)
    ok=key<lens[0]
    if n>1:
        ok=ok&(qry<slots)
        for j in range(1,n):
            ok=ok|((key>=j*slots)&(key<j*slots+lens[j])&(qry>=j*slots)&(qry<(j+1)*slots))
    bias_ref[...]=jnp.where(ok,0.0,NEG)
def attend_block(row, x_ref, wqkv, vec, bias_ref, k_ref, v_ref, att_ref, q0_ref, e, i):
    x=x_ref[pl.ds(row,BLK),:]
    for g in range(3):
        cs=pl.ds(g*256,256)
        q4=dot(x,wqkv[:,g*256:g*256+256])+vec[0:1,g*256:g*256+256]
        q4=q4.astype(BF)
        k4=dot(x,wqkv[:,768+g*256:768+g*256+256]).astype(BF)
        v4=(dot(x,wqkv[:,1536+g*256:1536+g*256+256])+vec[1:2,g*256:g*256+256]).astype(BF)
        k_ref[pl.ds(row,BLK),cs]=k4
        v_ref[pl.ds(row,BLK),cs]=v4
        put_first(q0_ref,e,i,slice(g*256,g*256+256),q4.astype(F32))
        qT=(q4.astype(F32)*0.125).T.astype(BF)
        vT=v4.astype(F32).T.astype(BF)
        lane=lax.broadcasted_iota(jnp.int32,(BLK,256),1)
        outs=[]
        for h in range(4):
            kh=jnp.where((lane>=64*h)&(lane<64*h+64),k4,jnp.zeros_like(k4))
            s=dot(kh,qT)+bias_ref[...]
            m=jnp.max(s,axis=0,keepdims=True)
            p=jnp.exp(s-m)
            l=jnp.sum(p,axis=0,keepdims=True)
            o=dot(vT[64*h:64*h+64,:],p.astype(BF))
            outs.append(o*(1.0/l))
        oT=jnp.concatenate(outs,axis=0)
        att_ref[pl.ds(row,BLK),cs]=oT.T.astype(BF)
def out_block(row, x_ref, att_ref, wo, vec, n_ref, a0_ref, p1_ref, e, i):
    att=att_ref[pl.ds(row,BLK),:]
    put_first(a0_ref,e,i,slice(None),att.astype(F32))
    pre=x_ref[pl.ds(row,BLK),:].astype(F32)+dot(att,wo[...])+vec[2:3,:]
    put_first(p1_ref,e,i,slice(None),pre)
    n_ref[pl.ds(row,BLK),:]=norm(pre,vec[3:4,:],vec[4:5,:])
def gelu(u):
    return 0.5*u*(1.0+jnp.tanh(0.7978845608028654*(u+0.044715*(u*u*u))))
def up_block(row, n_ref, wup, hb, act_ref, h0_ref, e, i, arow):
    nl=n_ref[pl.ds(row,BLK),:].astype(BF)
    for t in range(12):
        cs=slice(t*256,t*256+256)
        h=dot(nl,wup[:,cs])+hb[0:1,cs]
        put_first(h0_ref,e,i,cs,h)
        act_ref[pl.ds(arow,BLK),cs]=gelu(h).astype(BF)
def down_block(row, n_ref, act_ref, wdown, vec, o_ref, p2_ref, hd_ref, e, i, arow):
    f=dot(act_ref[pl.ds(arow,BLK),:],wdown[...])+vec[5:6,:]
    pre=n_ref[pl.ds(row,BLK),:]+f
    put_first(p2_ref,e,i,slice(None),pre)
    enc=norm(pre,vec[6:7,:],vec[7:8,:])
    put_first(hd_ref,e,i,slice(None),enc)
    o_ref[pl.ds(row,BLK),:]=enc.astype(BF)

def dot_nt(a,b): return lax.dot_general(a,b,(((1,),(1,)),((),())),preferred_element_type=F32)
def gelu_slope(u):
    t=jnp.tanh(0.7978845608028654*(u+0.044715*(u*u*u)))
    return 0.5*(1.0+t)+0.5*u*(1.0-t*t)*(0.7978845608028654*(1.0+0.134145*(u*u)))
def norm_grad(u,g,gy):
    c=u-jnp.mean(u,axis=-1,keepdims=True)
    r=lax.rsqrt(jnp.mean(c*c,axis=-1,keepdims=True)+EPS)
    t=gy*g
    gu=r*(t-jnp.mean(t,axis=-1,keepdims=True)-c*(r*r)*jnp.mean(t*c,axis=-1,keepdims=True))
    return gu, jnp.sum(gy*c*r,axis=0,keepdims=True), jnp.sum(gy,axis=0,keepdims=True)
LEFT_ROWS=288
def heads_apart(rows, count):
    n=rows.shape[0]
    wide=jnp.concatenate([jnp.broadcast_to(rows[i:i+1],(16,768)) for i in range(n)],axis=0)
    r=lax.broadcasted_iota(jnp.int32,wide.shape,0)%16
    l=lax.broadcasted_iota(jnp.int32,wide.shape,1)//64
    return jnp.where(r==l,wide,0.0)
def back_one(e, base, nb, slots, lens, x, k, v, gtok, gr, q0, a0, p1, h0, p2, wqkv, wo, wup, wdn, vec, hb, ls, la, right, u_s, gq_s, sv_s, qa_s, ga_s):
    n=256//slots
    seqs=n*nb
    R=16*n
    rows=slice(8*e,8*e+8)
    W=lambda ref: ref.at[e]
    vv=vec[e]
    pre2=p2[rows,:]; pre1=p1[rows,:]; hid=h0[rows,:]
    g2,gain2,shift2=norm_grad(pre2,vv[6:7],gr[rows,:])
    gffn=g2.astype(BF)
    gact=dot_nt(gffn,wdn[e])
    gh=(gact*gelu_slope(hid)).astype(BF)
    act=gelu(hid)
    gn=g2+dot_nt(gh,wup[e])
    g1,gain1,shift1=norm_grad(pre1,vv[3:4],gn)
    nlow=norm(pre1,vv[3:4],vv[4:5])
    gb=g1.astype(BF)
    ga=dot_nt(gb,wo[e]).astype(BF).astype(F32)
    q0s=q0[rows,:]*0.125
    qa_s[...]=heads_apart(q0s,8).astype(BF)
    ga_s[...]=heads_apart(ga,8).astype(BF)
    u_s[0]=dot_nt(qa_s[...],wqkv[e,:,768:1536]).astype(BF)
    u_s[1]=dot_nt(ga_s[...],wqkv[e,:,1536:2304]).astype(BF)
    gq_s[...]=jnp.zeros_like(gq_s); sv_s[...]=jnp.zeros_like(sv_s)
    def block(i,_):
        row=i*256
        rr=i*R
        K=k[pl.ds(row,256),:]; V=v[pl.ds(row,256),:]; X=x[pl.ds(row,256),:]
        qa=qa_s[pl.ds(rr,R),:]; gab=ga_s[pl.ds(rr,R),:]
        s=dot_nt(qa,K)
        key=lax.broadcasted_iota(jnp.int32,(R,256),1)
        if n==1:
            ok=key<lens[i]
        else:
            grp=lax.broadcasted_iota(jnp.int32,(R,256),0)//16
            ok=(grp<0)
            for j in range(n):
                ok=ok|((grp==j)&(key>=j*slots)&(key<j*slots+lens[i*n+j]))
        s=jnp.where(ok,s,NEG)
        p=jnp.exp(s-jnp.max(s,axis=1,keepdims=True))
        p=p*(1.0/jnp.sum(p,axis=1,keepdims=True))
        gs=dot_nt(gab,V)
        gs=p*(gs-jnp.sum(p*gs,axis=1,keepdims=True))
        both=jnp.concatenate([gs,p],axis=0)
        bb=both.astype(BF)
        gq=dot(bb[:R],K)
        rr0=lax.broadcasted_iota(jnp.int32,(R,768),0); ll=lax.broadcasted_iota(jnp.int32,(R,768),1)//64
        gq=jnp.where(rr0%16==ll,gq,0.0)*0.125
        st=jnp.sum(bb[R:].astype(F32),axis=1,keepdims=True)
        sv_s[...]=sv_s[...]+jnp.sum(st*gab.astype(F32),axis=0,keepdims=True)
        mix=dot(bb,X)
        for j in range(n):
            slot=i*n+j
            gq_s[pl.ds(slot,1),:]=jnp.sum(gq[16*j:16*j+16],axis=0,keepdims=True)
            first=X[j*slots:j*slots+1].astype(F32)
            for c in range(6):
                cc=slice(128*c,128*c+128)
                ls[e,c,pl.ds(32+slot,12,stride=8),:]=mix[16*j:16*j+12,cc]
                ls[e,c,pl.ds(128+slot,12,stride=8),:]=mix[R+16*j:R+16*j+12,cc]
                ls[e,c,pl.ds(16+slot,1),:]=first[:,cc]
        uu=jnp.concatenate([u_s[0,pl.ds(rr,R),:],u_s[1,pl.ds(rr,R),:]],axis=0)
        gtok[pl.ds(row,256),:]=dot(both.T.astype(BF),uu)
        return _
    for i in range(nb): block(i,0)
    gql=gq_s[...].astype(BF)
    extra=g1+dot_nt(gql,wqkv[e,:,0:768])
    for i in range(seqs):
        gtok[i*slots:i*slots+1,:]=gtok[i*slots:i*slots+1,:]+extra[i:i+1]
    cs=lambda m: jnp.sum(m.astype(F32),axis=0,keepdims=True)
    sums=jnp.concatenate([cs(gql),sv_s[0:1],cs(gb),gain1,shift1,cs(gffn),gain2,shift2],axis=0)
    for c in range(6):
        cc=slice(128*c,128*c+128)
        ls[e,c,0:8,:]=nlow[:,cc]
        ls[e,c,8:16,:]=a0[rows,cc]
        ls[e,c,24:32,:]=sums[:,cc]
    la[e,0:8,:]=act
    la[e,8:16,:]=jnp.concatenate([cs(gh),jnp.zeros((7,3072),F32)],axis=0)
    rt=[(gffn.astype(F32)),gh.astype(F32),gb.astype(F32)]
    for half in range(2):
        o=0
        for m in rt:
            w=m.shape[1]//2
            right[half,rows,o:o+w]=m[:,half*w:half*w+w]; o+=w
        last=[gql.astype(F32),q0s[:,:384]] if half==0 else [q0s[:,384:],ga]
        for m in last:
            right[half,rows,o:o+m.shape[1]]=m; o+=m.shape[1]
def pick_matrix(off, lane0):
    r=lax.broadcasted_iota(jnp.int32,(256,128),0); l=lax.broadcasted_iota(jnp.int32,(256,128),1)
    return jnp.where((r-off==l-lane0)&(l>=lane0)&(l<lane0+48),1.0,0.0).astype(BF)
def left_messages(ls, la, left):
    two=lambda e,w: jnp.concatenate([ls[e,w//128],ls[e,w//128+1]],axis=1).astype(BF)
    aq=la[0].astype(BF); ap=la[1].astype(BF)
    def win(start, width):
        w=min(start//128*128, width-256); return w, start-w
    for j in range(16):
        w,off=win(48*j,768)
        m=dot(two(0,w),pick_matrix(off,0))+dot(two(1,w),pick_matrix(off,64))
        m=m.astype(BF)
        left[j,48:80,:]=m[0:32]; left[j,0:48,:]=m[32:80]; left[j,144:288,:]=m[80:224]
        for t in range(4):
            w,off=win(192*j+48*t,3072)
            left[j,80+16*t:96+16*t,:]=(dot(aq[:,w:w+256],pick_matrix(off,0))+dot(ap[:,w:w+256],pick_matrix(off,64))).astype(BF)
def back_kernel(ql,pln,gr,q0,a0,p1,h0,p2,qx,px,qk,qv,pk,pv,wqkv,wo,wup,wdn,vec,hb,gq_tok,gp_tok,left,right,ls,la,rs,u_s,gq_s,sv_s,qa_s,ga_s):
    ls[...]=jnp.zeros_like(ls)
    back_one(1,2,6,256,pln,px,pk,pv,gp_tok,gr,q0,a0,p1,h0,p2,wqkv,wo,wup,wdn,vec,hb,ls,la,rs,u_s,gq_s,sv_s,qa_s,ga_s)
    back_one(0,0,2,64,ql,qx,qk,qv,gq_tok,gr,q0,a0,p1,h0,p2,wqkv,wo,wup,wdn,vec,hb,ls,la,rs,u_s,gq_s,sv_s,qa_s,ga_s)
    right[...]=rs[...].astype(BF)
    left_messages(ls,la,left)
def backward(*a):
    S=jax.ShapeDtypeStruct
    V=pl.BlockSpec(memory_space=pltpu.VMEM); SM=pl.BlockSpec(memory_space=pltpu.SMEM)
    outs=[S((512,768),F32),S((1536,768),F32),S((16,LEFT_ROWS,128),BF),S((2,16,3456),BF)]
    VM=pltpu.VMEM
    return pl.pallas_call(back_kernel,out_shape=outs,in_specs=[SM,SM]+[V]*18,out_specs=[V]*4,
      scratch_shapes=[VM((2,6,224,128),F32),VM((2,16,3072),F32),VM((2,16,3456),F32),VM((2,128,768),BF),VM((8,768),F32),VM((8,768),F32),VM((128,768),BF),VM((128,768),BF)],
      compiler_params=pltpu.CompilerParams(vmem_limit_bytes=60*2**20),name="back")(*a)


MESH = pl.DeviceIdType.MESH

class Gather:
    def __init__(self, units, ins, outs, send, recv):
        self.units, self.ins, self.outs, self.send, self.recv = units, ins, outs, send, recv
        w, self.y = lax.axis_index("wq"), lax.axis_index("np")
        self.w = w
        self.z, self.x, self.c = w // 4, (w // 2) % 2, w % 2
        self.pending = {}
    def dev(self, dz=0, fx=False, fy=False, fc=False):
        x = 1 - self.x if fx else self.x
        c = 1 - self.c if fc else self.c
        y = 1 - self.y if fy else self.y
        return ((self.z + dz) * 4 + x * 2 + c, y)
    def barrier(self):
        bar = pltpu.get_barrier_semaphore()
        def sig(**k): pl.semaphore_signal(bar, inc=1, device_id=self.dev(**k), device_id_type=MESH)
        sig(fx=True); sig(fy=True); sig(fc=True)
        @pl.when(self.z > 0)
        def _(): sig(dz=-1)
        @pl.when(self.z < 3)
        def _(): sig(dz=1)
        pl.semaphore_wait(bar, 3 + (self.z + 3) // 4 + (6 - self.z) // 4)
    def view(self, u, z=None, x=None, y=None, c=None):
        a, e, kind, r0, rn = self.units[u]
        o = self.outs[a]
        r, w = self.ins[a].shape[1:]
        zs = slice(None) if z is None else z
        xs = slice(None) if x is None else x
        cs = slice(None) if y is None else pl.ds(pl.multiple_of(y * w, 128), w)
        return o.at[e, zs, xs, pl.ds(pl.multiple_of((self.c if c is None else c) * r + r0, 16), rn), cs]
    def copy(self, u, sem, src, dst, dev):
        return pltpu.make_async_remote_copy(src_ref=src, dst_ref=dst, send_sem=self.send.at[u, sem], recv_sem=self.recv.at[u, sem], device_id=dev, device_id_type=MESH)
    def own_src(self, u):
        a, e, kind, r0, rn = self.units[u]
        return self.ins[a].at[e, pl.ds(r0, rn)]
    def zview(self, u, core, z):
        kind = self.units[u][2]
        if kind == "F": return self.view(u, z=z, x=self.x, y=self.y)
        if core == 0: return self.view(u, z=z, x=None, y=self.y)
        return self.view(u, z=z, x=self.x, y=None)
    def step(self, u, s):
        for core in (0, 1):
            pl.when(self.c == core)(lambda core=core: self._step(u, s, core))
    def A(self, core): return dict(fx=True) if core == 0 else dict(fy=True)
    def B(self, core): return dict(fy=True) if core == 0 else dict(fx=True)
    def a_src(self, u, core):
        kind = self.units[u][2]
        z = None if kind == "F" else self.z
        return self.view(u, z=z, x=self.x, y=self.y)
    def a_got(self, u, core):
        kind = self.units[u][2]
        z = None if kind == "F" else self.z
        return self.view(u, z=z, x=1 - self.x, y=self.y) if core == 0 else self.view(u, z=z, x=self.x, y=1 - self.y)
    def b_src(self, u, core):
        return self.view(u, x=None, y=self.y) if core == 0 else self.view(u, x=self.x, y=None)
    def b_got(self, u, core):
        return self.view(u, x=None, y=1 - self.y) if core == 0 else self.view(u, x=1 - self.x, y=None)
    def local(self, u, sem, ref):
        self.copy(u, sem, ref, ref, self.dev(fc=True)).start()
    def z_send(self, u, core, hop):
        z = self.z
        @pl.when((z - hop >= 0) & (z + 1 <= 3))
        def _():
            v = self.zview(u, core, z - hop)
            src = self.own_src(u) if (hop == 0 and self.units[u][2] == "F") else v
            self.copy(u, 2 + hop, src, v, self.dev(dz=1)).start()
        @pl.when((z + hop <= 3) & (z - 1 >= 0))
        def _():
            v = self.zview(u, core, z + hop)
            src = self.own_src(u) if (hop == 0 and self.units[u][2] == "F") else v
            self.copy(u, 5 + hop, src, v, self.dev(dz=-1)).start()
    def z_wait(self, u, core, hop):
        z = self.z
        @pl.when(z - 1 - hop >= 0)
        def _():
            v = self.zview(u, core, z - 1 - hop)
            self.copy(u, 2 + hop, v, v, self.dev(fc=True)).wait_recv()
            self.local(u, 11 + hop, v)
        @pl.when(z + 1 + hop <= 3)
        def _():
            v = self.zview(u, core, z + 1 + hop)
            self.copy(u, 5 + hop, v, v, self.dev(fc=True)).wait_recv()
            self.local(u, 14 + hop, v)
    def _step(self, u, s, core):
        F = self.units[u][2] == "F"
        own = self.view(u, z=self.z, x=self.x, y=self.y)
        if s == 0:
            src = self.own_src(u)
            self.copy(u, 8, src, own, self.dev(fc=True)).start()
            pltpu.make_async_copy(src, own, self.send.at[u, 17]).start()
            if F:
                self.z_send(u, core, 0)
            else:
                self.copy(u, 0, src, own, self.dev(**self.A(core))).start()
        if s == 1:
            pltpu.make_async_copy(self.own_src(u), own, self.send.at[u, 17]).wait()
            if F:
                self.z_wait(u, core, 0); self.z_send(u, core, 1)
            else:
                g = self.a_got(u, core)
                self.copy(u, 0, g, g, self.dev(fc=True)).wait_recv()
                self.z_send(u, core, 0)
                self.local(u, 9, g)
        if s == 2:
            if F: self.z_wait(u, core, 1); self.z_send(u, core, 2)
            else: self.z_wait(u, core, 0); self.z_send(u, core, 1)
        if s == 3:
            if F:
                self.z_wait(u, core, 2)
                v = self.a_src(u, core)
                self.copy(u, 0, v, v, self.dev(**self.A(core))).start()
            else:
                self.z_wait(u, core, 1); self.z_send(u, core, 2)
        if s == 4:
            if F:
                g = self.a_got(u, core)
                self.copy(u, 0, g, g, self.dev(fc=True)).wait_recv()
            else:
                self.z_wait(u, core, 2)
            v = self.b_src(u, core)
            self.copy(u, 1, v, v, self.dev(**self.B(core))).start()
            if F: self.local(u, 9, g)
        if s == 5:
            g = self.b_got(u, core)
            self.copy(u, 1, g, g, self.dev(fc=True)).wait_recv()
            self.local(u, 10, g)
        if s == 6:
            self.finish_recv(u, core); self.finish_send(u, core)
    def finish_recv(self, u, core):
        other = 1 - core
        c = 1 - self.c
        kind = self.units[u][2]
        def got(sem, v): self.copy(u, sem, v, v, self.dev(fc=True)).wait_recv()
        sv = lambda **k: self.view(u, c=c, **k)
        got(8, sv(z=self.z, x=self.x, y=self.y))
        za = None if kind == "F" else self.z
        got(9, sv(z=za, x=1 - self.x, y=self.y) if other == 0 else sv(z=za, x=self.x, y=1 - self.y))
        got(10, sv(x=None, y=1 - self.y) if other == 0 else sv(x=1 - self.x, y=None))
        def zv(z):
            if kind == "F": return sv(z=z, x=self.x, y=self.y)
            return sv(z=z, x=None, y=self.y) if other == 0 else sv(z=z, x=self.x, y=None)
        for hop in range(3):
            pl.when(self.z - 1 - hop >= 0)(lambda hop=hop: got(11 + hop, zv(self.z - 1 - hop)))
            pl.when(self.z + 1 + hop <= 3)(lambda hop=hop: got(14 + hop, zv(self.z + 1 + hop)))
    def finish_send(self, u, core):
        def sent(sem, v): self.copy(u, sem, v, v, self.dev(fc=True)).wait_send()
        own = self.view(u, z=self.z, x=self.x, y=self.y)
        sent(8, own)
        sent(0, self.a_src(u, core)); sent(1, self.b_src(u, core))
        sent(9, self.a_got(u, core)); sent(10, self.b_got(u, core))
        z = self.z
        for hop in range(3):
            pl.when((z - hop >= 0) & (z + 1 <= 3))(lambda hop=hop: sent(2 + hop, self.zview(u, core, z - hop)))
            pl.when((z + hop <= 3) & (z - 1 >= 0))(lambda hop=hop: sent(5 + hop, self.zview(u, core, z + hop)))
            pl.when(z - 1 - hop >= 0)(lambda hop=hop: sent(11 + hop, self.zview(u, core, z - 1 - hop)))
            pl.when(z + 1 + hop <= 3)(lambda hop=hop: sent(14 + hop, self.zview(u, core, z + 1 + hop)))

class Place:
    def __init__(self):
        self.w=lax.axis_index("wq"); self.y=lax.axis_index("np")
        self.z,self.x,self.c=self.w//4,(self.w//2)%2,self.w%2
        self.me=self.w*2+self.y
    def dev(self, z=None, fx=False, fy=False, fc=False):
        x=1-self.x if fx else self.x
        c=1-self.c if fc else self.c
        y=1-self.y if fy else self.y
        return ((self.z if z is None else z)*4+x*2+c, y)

def head_gather(pos, buf, send, recv):
    z,x,c,y=pos.z,pos.x,pos.c,pos.y
    def rc(sem,src,dev,dst=None):
        return pltpu.make_async_remote_copy(src_ref=src,dst_ref=src if dst is None else dst,send_sem=send.at[sem],recv_sem=recv.at[sem],device_id=dev,device_id_type=MESH)
    own=buf.at[z,x,c,y]
    for k in (1,2,3): rc(k-1,own,pos.dev(z=(z+k)%4)).start()
    def arrived(sem,ref): rc(sem,ref,pos.dev(fc=True)).wait_recv()
    for k in (1,2,3): arrived(k-1,buf.at[(z+4-k)%4,x,c,y])
    col=buf.at[:,x,c,y]
    def order(core):
        first=dict(fx=True) if core==0 else dict(fy=True)
        second=dict(fy=True) if core==0 else dict(fx=True)
        rc(3,col,pos.dev(**first)).start()
        rc(5,col,pos.dev(fc=True)).start()
        got=buf.at[:,1-x,c,y] if core==0 else buf.at[:,x,c,1-y]
        arrived(3,got)
        both=buf.at[:,:,c,y] if core==0 else buf.at[:,x,c,:]
        rc(4,both,pos.dev(**second)).start()
        rc(6,got,pos.dev(fc=True)).start()
        last=buf.at[:,:,c,1-y] if core==0 else buf.at[:,1-x,c,:]
        arrived(4,last)
        rc(7,last,pos.dev(fc=True)).start()
        o=1-c
        arrived(5,buf.at[:,x,o,y])
        arrived(6,buf.at[:,x,o,1-y] if core==0 else buf.at[:,1-x,o,y])
        arrived(7,buf.at[:,1-x,o,:] if core==0 else buf.at[:,:,o,1-y])
        for sem,ref in ((3,col),(4,both),(5,col),(6,got),(7,last)): rc(sem,ref,pos.dev(fc=True)).wait_send()
    for core in (0,1): pl.when(c==core)(functools.partial(order,core))
    for k in (1,2,3): rc(k-1,own,pos.dev(fc=True)).wait_send()

def similar_kernel(heads, marks, gr, loss, buf, gs_s, gt_s, send, recv):
    pos=Place()
    bar=pltpu.get_barrier_semaphore()
    for k in (1,2,3): pl.semaphore_signal(bar,inc=1,device_id=pos.dev(z=(pos.z+k)%4),device_id_type=MESH)
    for kw in (dict(fx=True),dict(fy=True),dict(fc=True)): pl.semaphore_signal(bar,inc=1,device_id=pos.dev(**kw),device_id_type=MESH)
    buf[pos.z,pos.x,pos.c,pos.y]=heads[...].astype(BF)
    pl.semaphore_wait(bar,6)
    head_gather(pos,buf,send,recv)
    g=buf[...].reshape(32,16,768).astype(F32)
    q=g[:,0:8].reshape(256,768).astype(BF); p=g[:,8:16].reshape(256,768).astype(BF)
    m=jnp.sum(marks[...].reshape(8,32,256),axis=0)
    m=m[0:16]+m[16:32]
    m=(m[:,0:128]+m[:,128:256]).astype(F32)
    row=lambda r: jnp.broadcast_to(jnp.concatenate([m[r:r+1],m[r+1:r+2]],axis=1),(256,256))
    qset=row(0).T; gold=row(2).T; pset=row(4)
    lane=lax.broadcasted_iota(jnp.int32,(256,256),1).astype(F32)
    is_gold=gold==lane
    usable=(qset==pset)|is_gold
    sim=dot_nt(q,p)*(768**-0.5)
    masked=jnp.where(usable,sim,NEG)
    high=jnp.max(masked,axis=1,keepdims=True)
    tot=high+jnp.log(jnp.sum(jnp.where(usable,jnp.exp(masked-high),0.0),axis=1,keepdims=True))
    gsc=jnp.sum(jnp.where(is_gold,sim,0.0),axis=1,keepdims=True)
    loss[...]=jnp.broadcast_to(jnp.sum(tot-gsc,axis=0,keepdims=True)*(1.0/256),loss.shape)
    soft=jnp.where(usable,jnp.exp(masked-tot),0.0)
    gsim=soft-jnp.where(is_gold,1.0,0.0)
    gs_s[...]=gsim; gt_s[...]=gsim.T
    me8=pl.ds(pl.multiple_of(pos.me*8,8),8)
    gr[0:8,:]=dot(gs_s[me8,:].astype(BF),p)*(768**-0.5)
    gr[8:16,:]=dot(gt_s[me8,:].astype(BF),q)*(768**-0.5)

def similar_call(heads,marks):
    V=pl.BlockSpec(memory_space=pltpu.VMEM)
    return pl.pallas_call(similar_kernel,out_shape=[jax.ShapeDtypeStruct((16,768),F32),jax.ShapeDtypeStruct((8,128),F32)],in_specs=[V,V],out_specs=[V,V],
      scratch_shapes=[pltpu.VMEM((4,2,2,2,16,768),BF),pltpu.VMEM((256,256),F32),pltpu.VMEM((256,256),F32),pltpu.SemaphoreType.DMA((8,)),pltpu.SemaphoreType.DMA((8,))],
      compiler_params=pltpu.CompilerParams(collective_id=2,has_side_effects=True,vmem_limit_bytes=40*2**20),name="similar")(heads,marks)

CHUNKS=3
class RightGather:
    def __init__(self,pos,src,buf,send,recv):
        self.pos,self.src,self.buf,self.send,self.recv=pos,src,buf,send,recv
        self.width=src.shape[2]//CHUNKS
    def rc(self,ch,sem,src,dst,dev):
        return pltpu.make_async_remote_copy(src_ref=src,dst_ref=dst,send_sem=self.send.at[ch,sem],recv_sem=self.recv.at[ch,sem],device_id=dev,device_id_type=MESH)
    def view(self,ch,z=None,x=None,c=None,y=None):
        p=self.pos
        f=lambda v: slice(None) if v is None else v
        return self.buf.at[f(z),p.x if x is None else x,p.c if c is None else c,f(y),:,ch*self.width:(ch+1)*self.width]
    def half(self,ch,y): return self.src.at[y,:,ch*self.width:(ch+1)*self.width]
    def step(self,ch,s):
        p=self.pos; z,y=p.z,p.y
        sib=p.dev(fc=True)
        def arrived(sem,v): self.rc(ch,sem,v,v,sib).wait_recv()
        def local(sem,v): self.rc(ch,sem,v,v,sib).start()
        def z_send(hop):
            @pl.when((z-hop>=0)&(z+1<=3))
            def _():
                v=self.view(ch,z=z-hop); self.rc(ch,2+hop,v,v,p.dev(z=z+1)).start()
            @pl.when((z+hop<=3)&(z-1>=0))
            def _():
                v=self.view(ch,z=z+hop); self.rc(ch,5+hop,v,v,p.dev(z=z-1)).start()
        def z_wait(hop):
            @pl.when(z-1-hop>=0)
            def _():
                v=self.view(ch,z=z-1-hop); arrived(2+hop,v); local(9+hop,v)
            @pl.when(z+1+hop<=3)
            def _():
                v=self.view(ch,z=z+1+hop); arrived(5+hop,v); local(12+hop,v)
        own=self.view(ch,z=z,y=y)
        if s==0:
            self.rc(ch,0,self.half(ch,1-y),own,p.dev(fy=True)).start()
            pltpu.make_async_copy(self.half(ch,y),own,self.send.at[ch,16]).start()
        if s==1:
            pltpu.make_async_copy(self.half(ch,y),own,self.send.at[ch,16]).wait()
            arrived(0,self.view(ch,z=z,y=1-y))
            z_send(0); local(8,self.view(ch,z=z))
        if s==2: z_wait(0); z_send(1)
        if s==3: z_wait(1); z_send(2)
        if s==4:
            z_wait(2)
            v=self.view(ch); self.rc(ch,1,v,v,p.dev(fx=True)).start()
        if s==5:
            g=self.view(ch,x=1-p.x); arrived(1,g); local(15,g)
        if s==6:
            o=1-p.c
            arrived(8,self.view(ch,z=z,c=o)); arrived(15,self.view(ch,x=1-p.x,c=o))
            def sent(sem,v): self.rc(ch,sem,v,v,sib).wait_send()
            sent(0,own); sent(1,self.view(ch)); sent(8,self.view(ch,z=z)); sent(15,self.view(ch,x=1-p.x))
            for hop in range(3):
                pl.when(z-1-hop>=0)(lambda hop=hop: arrived(9+hop,self.view(ch,z=z-1-hop,c=o)))
                pl.when(z+1+hop<=3)(lambda hop=hop: arrived(12+hop,self.view(ch,z=z+1+hop,c=o)))
                pl.when((z-hop>=0)&(z+1<=3))(lambda hop=hop: sent(2+hop,self.view(ch,z=z-hop)))
                pl.when((z+hop<=3)&(z-1>=0))(lambda hop=hop: sent(5+hop,self.view(ch,z=z+hop)))
                pl.when(z-1-hop>=0)(lambda hop=hop: sent(9+hop,self.view(ch,z=z-1-hop)))
                pl.when(z+1+hop<=3)(lambda hop=hop: sent(12+hop,self.view(ch,z=z+1+hop)))

def left_copies(pos,left,buf,send,recv):
    def to(d):
        t=(pos.me+d)%32
        return t//2,t%2
    def send_one(d,go):
        w,y=to(d)
        for half,(r0,n) in enumerate(((0,144),(48,240))):
            @pl.when(y==half)
            def _():
                go(pltpu.make_async_remote_copy(src_ref=left.at[w,pl.ds(r0,n)],dst_ref=buf.at[pos.me,pl.ds(0,n)],send_sem=send.at[d],recv_sem=recv.at[d],device_id=(w,y),device_id_type=MESH))
    def start():
        def lap(d,kept):
            send_one(d,lambda cp: cp.start()); return kept
        lax.fori_loop(1,32,lap,0)
    def finish():
        def lap(d,kept):
            send_one(d,lambda cp: cp.wait_send())
            s=(pos.me+32-d)%32
            for half,(r0,n) in enumerate(((0,144),(48,240))):
                @pl.when(pos.y==half)
                def _():
                    v=buf.at[s,pl.ds(0,n)]
                    pltpu.make_async_remote_copy(src_ref=v,dst_ref=v,send_sem=send.at[d],recv_sem=recv.at[d],device_id=(pos.w,pos.y),device_id_type=MESH).wait_recv()
            return kept
        lax.fori_loop(1,32,lap,0)
    def own():
        for half,(r0,n) in enumerate(((0,144),(48,240))):
            @pl.when(pos.y==half)
            def _(): buf[pos.me,0:n,:]=left[pos.w,r0:r0+n,:]
    return start,own,finish

def all_barrier(pos):
    bar=pltpu.get_barrier_semaphore()
    def lap(d,kept):
        t=(pos.me+d)%32
        pl.semaphore_signal(bar,inc=1,device_id=(t//2,t%2),device_id_type=MESH)
        return kept
    lax.fori_loop(1,32,lap,0)
    pl.semaphore_wait(bar,31)

def weight_products(pos,lbuf,rbuf,wqkv,wout,win,wback,gvec,gbin,bq,bp):
    r=rbuf[...].reshape(32,16,3456).astype(F32)
    bq[...]=r[:,0:8].reshape(256,3456).astype(BF)
    bp[...]=r[:,8:16].reshape(256,3456).astype(BF)
    def pair(r0):
        t=lbuf[:,r0:r0+16,:].astype(F32)
        return [t[:,8*i:8*i+8].reshape(256,128) for i in (0,1)]
    def put(out,rows,cols,tt,bcols):
        tt=tt.T.astype(BF)
        out[0,rows,cols]=dot(tt,bq[:,bcols])[0:48]
        out[1,rows,cols]=dot(tt,bp[:,bcols])[64:112]
    everything=slice(None)
    def common(base):
        nrm,att=pair(base)
        put(win,everything,everything,nrm,slice(384,1920))
        put(wout,everything,everything,att,slice(1920,2304))
        for k in range(4):
            put(wback,slice(48*k,48*k+48),everything,pair(base+32+16*k)[0],slice(0,384))
        x0,vs=pair(base+16)
        vs=jnp.sum(vs.reshape(32,8,128),axis=0)
        bs=[jnp.sum(pair(base+32+16*k)[1].reshape(32,8,128),axis=0)[0:1] for k in range(4)]
        return x0,vs,bs
    def mixed(r0,heads,col0,dst0):
        for h in range(0,heads,2):
            a,b=pair(r0+8*h)
            a=a.T.astype(BF); b=b.T.astype(BF)
            cs=slice(col0+64*h,col0+64*h+128); ds=slice(dst0+64*h,dst0+64*h+128)
            low=lax.broadcasted_iota(jnp.int32,(128,128),1)<64
            wqkv[0,:,ds]=jnp.where(low,dot(a,bq[:,cs]),dot(b,bq[:,cs]))[0:48]
            wqkv[1,:,ds]=jnp.where(low,dot(a,bp[:,cs]),dot(b,bp[:,cs]))[64:112]
    def sums(vs,bs,half):
        gvec[0]=vs[4*half:4*half+4,0:48]; gvec[1]=vs[4*half:4*half+4,64:112]
        for i in (0,1):
            gbin[0,i:i+1,:]=bs[2*half+i][:,0:48]; gbin[1,i:i+1,:]=bs[2*half+i][:,64:112]
    @pl.when(pos.y==0)
    def _():
        x0,vs,bs=common(48)
        put(wqkv,everything,slice(0,768),x0,slice(2304,3072))
        mixed(0,6,3072,768)
        sums(vs,bs,0)
    @pl.when(pos.y==1)
    def _():
        x0,vs,bs=common(0)
        mixed(96,6,2304,0)
        mixed(144,12,2688,384)
        sums(vs,bs,1)

def exchange_kernel(left,right,wqkv,wout,win,wback,gvec,gbin,lbuf,rbuf,bq,bp,lsend,lrecv,rsend,rrecv):
    pos=Place()
    all_barrier(pos)
    g=RightGather(pos,right,rbuf,rsend,rrecv)
    lstart,lown,lfinish=left_copies(pos,left,lbuf,lsend,lrecv)
    for ch in range(CHUNKS): g.step(ch,0)
    lstart()
    lown()
    for t in range(CHUNKS+6):
        for ch in range(CHUNKS):
            if 1<=t-ch<=6: g.step(ch,t-ch)
    lfinish()
    weight_products(pos,lbuf,rbuf,wqkv,wout,win,wback,gvec,gbin,bq,bp)

def exchange_call(left,right):
    V=pl.BlockSpec(memory_space=pltpu.VMEM); S=jax.ShapeDtypeStruct; VM=pltpu.VMEM; D=pltpu.SemaphoreType.DMA
    outs=[S((2,48,1152),F32),S((2,48,384),F32),S((2,48,1536),F32),S((2,192,384),F32),S((2,4,48),F32),S((2,2,48),F32)]
    return pl.pallas_call(exchange_kernel,out_shape=outs,in_specs=[V,V],out_specs=[V]*6,
      scratch_shapes=[VM((32,240,128),BF),VM((4,2,2,2,16,3456),BF),VM((256,3456),BF),VM((256,3456),BF),D((32,)),D((32,)),D((CHUNKS,17)),D((CHUNKS,17))],
      compiler_params=pltpu.CompilerParams(collective_id=3,has_side_effects=True,vmem_limit_bytes=50*2**20),name="exchange")(left,right)


def small_tile(vectors, hidden_bias):
    tile = jnp.zeros((1, 16, 128), vectors.dtype)
    count, rows, width = vectors.shape
    tile = tile.at[0, : count * rows, :width].set(vectors.reshape(count * rows, width))
    return tile.at[0, count * rows : count * rows + count, : hidden_bias.shape[1]].set(hidden_bias)


def mark_tile(q_set, gold, p_set):
    me = lax.axis_index("wq") * 2 + lax.axis_index("np")
    spare = jnp.full((8 - p_set.shape[0],), -1, jnp.int32)
    columns = gold // p_set.shape[0] * 8 + gold % p_set.shape[0]
    rows = jnp.stack([q_set, columns, jnp.concatenate([p_set, spare])])
    rows = jnp.where((jnp.arange(256) // 8 == me)[None, :], jnp.tile(rows, (1, 32)), 0)
    return jnp.zeros((1, 16, 128), jnp.int32).at[0, :6].set(rows.reshape(6, 128))


COSTS={"P1":4.1,"P2":0.6,"P3":1.75,"P4":1.4}
NEEDS={"P1":0,"P2":1,"P3":2,"P4":3}
WORK=(("P1",1),("P1",0),("P2",1),("P2",0),("P3",1),("P4",1),("P3",0),("P4",0))
BLOCKS={1:6,0:2}

def make_plan(units, starts, budget, lag=1, rank=(0,1,2,3,4,5,6), spread=True, piece=4.2):
    last={}
    for (a,e,*_),s in zip(units,starts): last[(a,e)]=max(last.get((a,e),0),s+6)
    todo=[(k,e,i) for k,e in WORK for i in range(BLOCKS[e])]
    plan=[]
    ticks=max(starts)+7
    for t in range(ticks):
        steps=[]
        for u,s in sorted(((u,t-starts[u]) for u in range(len(units))),key=lambda p:(rank.index(p[1]) if 0<=p[1]<=6 else 9,p[0])):
            if 0<=s<=6: steps.append(("comm",u,s))
        runs=[]; spent=0.0
        while todo and t+1<ticks:
            k,e,i=todo[0]
            if last[(NEEDS[k],e)]+lag>t or spent+COSTS[k]*0.5>budget: break
            todo.pop(0); spent+=COSTS[k]
            if runs and runs[-1][:2]==(k,e) and (runs[-1][3]-runs[-1][2]+1)*COSTS[k]<=piece: runs[-1]=(k,e,runs[-1][2],i+1)
            else: runs.append((k,e,i,i+1))
        n=len(steps)
        cut=[(m+1)*n//(len(runs)+1) if spread else n for m in range(len(runs))]
        for m in range(n+1):
            for c,r in zip(cut,runs):
                if c==m: plan.append(r)
            if m<n: plan.append(steps[m])
        for key,when in last.items():
            if when==t: plan.append(("load",)+key)
    for k,e,i in todo:
        if plan[-1][:2]==(k,e): plan[-1]=(k,e,plan[-1][2],i+1)
        else: plan.append((k,e,i,i+1))
    return plan

def spread_small(tiles, vec, hb):
    r=lax.broadcasted_iota(jnp.int32,(128,256),0); l=lax.broadcasted_iota(jnp.int32,(128,256),1)
    r4=lax.broadcasted_iota(jnp.int32,(128,384),0); l4=lax.broadcasted_iota(jnp.int32,(128,384),1)
    vec[...]=jnp.zeros_like(vec); hb[...]=jnp.zeros_like(hb)
    for w in range(16):
        for y in range(2):
            t=tiles[w//4,(w//2)%2,(w%2)*16:(w%2)*16+16,y*128:y*128+128]
            c=min(48*w//128*128,512); off=48*w-c
            v=dot(t,jnp.where((l-off==r)&(r<48),1.0,0.0).astype(BF))
            for e in (0,1): vec[e,4*y:4*y+4,c:c+256]+=v[4*e:4*e+4]
            c=min((192*w+96*y)//128*128,3072-384); off=192*w+96*y-c
            h=dot(t,jnp.where((l4-off==r4)&(r4<96),1.0,0.0).astype(BF))
            for e in (0,1): hb[e,0:1,c:c+384]+=h[8+e:9+e]

def fused_kernel(units, plan, *refs):
    ql,pln,qx,px=refs[0:4]; ins=refs[4:10]; outs=refs[10:16]
    vec,hb,qo,po,qk,qv,pk,pv,q0,a0,p1,h0,p2,hd=refs[16:30]
    wv=refs[30:34]; small,bias,att,nrm,act,send,recv,lsem=refs[34:]
    g=Gather(units,ins,outs,send,recv)
    g.barrier()
    for ref in (q0,a0,p1,h0,p2,hd): ref[...]=jnp.zeros_like(ref)
    X=(qx,px); O=(qo,po); K=(qk,pk); V=(qv,pv); LENS=(ql,pln); SLOTS=(64,256); BASE=(0,512); NB=(2,6)
    loaded=set()
    def load_copies(a,e):
        if a==5: return []
        if a==4: return [pltpu.make_async_copy(outs[4].at[0],small,lsem.at[a,e,0])]
        rows=outs[a].shape[3]
        return [pltpu.make_async_copy(outs[a].at[e,k//2,k%2],wv[a].at[e,pl.ds(k*rows,rows)],lsem.at[a,e,k]) for k in range(8)]
    def need(a,e):
        if (a,e) in loaded: return
        loaded.add((a,e))
        for cp in load_copies(a,e): cp.wait()
        if a==4: spread_small(small,vec,hb)
    for item in plan:
        if item[0]=="comm": g.step(item[1],item[2])
        elif item[0]=="load":
            for cp in load_copies(*item[1:]): cp.start()
        else:
            kind,e,lo,hi=item
            need(4,0); need(NEEDS[kind],e)
            n=256//SLOTS[e]
            A=att.at[pl.ds(BASE[e],NB[e]*BLK)]; N=nrm.at[pl.ds(BASE[e],NB[e]*BLK)]
            arow=0 if e==1 else 0
            def body(i,kept):
                row=pl.multiple_of(i*BLK,BLK)
                if kind=="P1":
                    make_bias(bias,0,[LENS[e][i*n+j] for j in range(n)],SLOTS[e])
                    attend_block(row,X[e],wv[0].at[e],vec.at[e],bias,K[e],V[e],A,q0,e,i)
                if kind=="P2": out_block(row,X[e],A,wv[1].at[e],vec.at[e],N,a0,p1,e,i)
                if kind=="P3": up_block(row,N,wv[2].at[e],hb.at[e],act,h0,e,i,row)
                if kind=="P4": down_block(row,N,act,wv[3].at[e],vec.at[e],O[e],p2,hd,e,i,row)
                return kept
            if hi-lo==1: body(lo,0)
            else: lax.fori_loop(lo,hi,body,0)

def fused_call(ql,pln,qx,px,arrays,units,plan):
    S=jax.ShapeDtypeStruct; VM=pltpu.VMEM; D=pltpu.SemaphoreType.DMA
    V=pl.BlockSpec(memory_space=pltpu.VMEM); SM=pl.BlockSpec(memory_space=pltpu.SMEM); A=pl.BlockSpec(memory_space=pl.ANY)
    outs=[S((a.shape[0],4,2,2*a.shape[1],2*a.shape[2]),a.dtype) for a in arrays]
    outs+=[S((2,8,768),F32),S((2,1,3072),F32),S(qx.shape,BF),S(px.shape,BF),S(qx.shape,BF),S(qx.shape,BF),S(px.shape,BF),S(px.shape,BF),S((16,768),F32),S((16,768),F32),S((16,768),F32),S((16,3072),F32),S((16,768),F32),S((16,768),F32)]
    return pl.pallas_call(functools.partial(fused_kernel,units,plan),out_shape=outs,in_specs=[SM,SM,V,V]+[A]*6,out_specs=[A]*6+[V]*14,
      scratch_shapes=[VM((2,768,2304),BF),VM((2,768,768),BF),VM((2,768,3072),BF),VM((2,3072,768),BF),VM((4,2,32,256),BF),VM((256,256),F32),VM((2048,768),BF),VM((2048,768),F32),VM((1536,3072),BF),D((len(units),18)),D((len(units),18)),D((6,2,8))],
      compiler_params=pltpu.CompilerParams(collective_id=1,has_side_effects=True,vmem_limit_bytes=63*2**20),name="fused")(ql,pln,qx,px,*arrays)


GATHER_ORDER = ((4, 0), (5, 0), (0, 1), (0, 0), (1, 1), (1, 0), (2, 1), (3, 1), (2, 0), (3, 0))
GATHER_PARTS = (3, 1, 3, 3, 1, 1)


def gather_units(arrays):
    units = []
    for a, e in GATHER_ORDER:
        rows = arrays[a].shape[1] // GATHER_PARTS[a]
        for j in range(GATHER_PARTS[a]):
            units.append((a, e, "MFM"[len(units) % 3], j * rows, rows))
    return units


def kernel_shards(
    q_embed, p_embed, q_len, p_len, q_set, p_set, gold, wqkv, wout, wup, wdown, vectors, hidden_bias
):
    arrays = (
        wqkv, wout, wup, wdown, small_tile(vectors, hidden_bias), mark_tile(q_set, gold, p_set)
    )
    units = gather_units(arrays)
    plan = make_plan(units, [max(i - 1, 0) // 2 for i in range(len(units))], 8.0)
    done = fused_call(q_len, p_len, q_embed, p_embed, arrays, units, plan)
    weights = tuple(
        member.reshape(2, 16 * shard.shape[1], 2 * shard.shape[2])
        for member, shard in zip(done[:4], arrays[:4])
    )
    vec, bias, q_out, p_out, q_keys, q_values, p_keys, p_values, q0, a0, p1, h0, p2, heads = done[6:]
    grad_first, loss = similar_call(heads, done[5])
    grad_q, grad_p, left, right = backward(
        q_len, p_len, grad_first, q0, a0, p1, h0, p2, q_embed, p_embed,
        q_keys, q_values, p_keys, p_values, *weights, vec, bias,
    )
    grads = exchange_call(left, right)
    return (
        loss[0, 0], q_out, p_out, grad_q, grad_p, *grads[:5], grads[5].reshape(2, -1)
    )


def kernels_fit(q_embed, p_embed, q_len, p_len):
    return (
        lax.axis_size("wq") == 16
        and lax.axis_size("np") == 2
        and q_embed.shape == (512, 768)
        and p_embed.shape == (1536, 768)
        and q_len.shape == (8,)
        and p_len.shape == (6,)
    )


def shards(
    q_embed,
    p_embed,
    q_len,
    p_len,
    q_set,
    p_set,
    gold,
    query_key_value_weight,
    attention_output_weight,
    up_weight,
    down_weight,
    vectors,
    hidden_bias,
):
    if kernels_fit(q_embed, p_embed, q_len, p_len):
        return kernel_shards(
            q_embed,
            p_embed,
            q_len,
            p_len,
            q_set,
            p_set,
            gold,
            query_key_value_weight,
            attention_output_weight,
            up_weight,
            down_weight,
            vectors,
            hidden_bias,
        )
    gathered = gather_weights(
        query_key_value_weight,
        attention_output_weight,
        up_weight,
        down_weight,
        vectors,
        hidden_bias,
    )
    wq_size, np_size = lax.axis_size("wq"), lax.axis_size("np")
    both_axes = ("wq", "np")
    q_weights = tuple((member[0] for member in gathered))
    p_weights = tuple((member[1] for member in gathered))
    p_encoded, p_stored = encode_forward(p_embed, p_len, p_weights)
    q_encoded, q_stored = encode_forward(q_embed, q_len, q_weights)
    model_width = q_embed.shape[1]
    ff_width = gathered[2].shape[2]
    q_count = q_len.shape[0]
    p_count = p_len.shape[0]
    own_heads = jnp.concatenate([first_rows(q_encoded, q_count), first_rows(p_encoded, p_count)])
    heads = lax.all_gather(own_heads, both_axes, axis=0)
    marks = lax.all_gather(jnp.concatenate([q_set, gold, p_set]), both_axes, axis=0)
    q_heads = heads[:, :q_count].reshape(-1, model_width)
    p_heads = heads[:, q_count:].reshape(-1, model_width)
    q_sets = marks[:, :q_count].reshape(-1)
    golds = marks[:, q_count : 2 * q_count].reshape(-1)
    p_sets = marks[:, 2 * q_count :].reshape(-1)
    scaling = model_width ** (-0.5)
    similar = (
        jnp.einsum("qd,pd->qp", q_heads, p_heads, preferred_element_type=jnp.float32) * scaling
    )
    is_gold = jnp.arange(p_heads.shape[0], dtype=jnp.int32)[None, :] == golds[:, None]
    usable = (q_sets[:, None] == p_sets[None, :]) | is_gold
    masked = jnp.where(usable, similar, NEGATIVE)
    highest = jnp.max(masked, axis=1)
    total = jnp.sum(jnp.where(usable, jnp.exp(masked - highest[:, None]), 0.0), axis=1)
    log_total = highest + jnp.log(total)
    gold_score = jnp.sum(jnp.where(is_gold, similar, 0.0), axis=1)
    loss = jnp.mean(log_total - gold_score)
    soft_rows = jnp.where(usable, jnp.exp(masked - log_total[:, None]), 0.0)
    grad_similar = (soft_rows - is_gold.astype(jnp.float32)).astype(jnp.bfloat16)
    me = lax.axis_index("wq") * np_size + lax.axis_index("np")
    grad_q_first = (
        jnp.einsum(
            "qp,pd->qd",
            lax.dynamic_slice_in_dim(grad_similar, me * q_count, q_count, 0),
            p_heads,
            preferred_element_type=jnp.float32,
        )
        * scaling
    )
    grad_p_first = (
        jnp.einsum(
            "qp,qd->pd",
            lax.dynamic_slice_in_dim(grad_similar, me * p_count, p_count, 1),
            q_heads,
            preferred_element_type=jnp.float32,
        )
        * scaling
    )
    q_back = encode_backward(q_embed, q_weights, q_stored, grad_q_first)
    p_back = encode_backward(p_embed, p_weights, p_stored, grad_p_first)
    left = jnp.concatenate(
        [left_message(member[1], wq_size, np_size) for member in (q_back, p_back)], axis=2
    )
    left = left.reshape((wq_size * np_size,) + left.shape[2:])
    left = lax.all_to_all(left, both_axes, 0, 0)
    right = jnp.concatenate([right_message(member[2], np_size) for member in (q_back, p_back)], axis=1)
    right = lax.all_gather(lax.all_to_all(right, "np", 0, 0), "wq", axis=0)
    right = right.reshape((wq_size * np_size,) + right.shape[2:])
    sums = jnp.concatenate(
        [
            jnp.stack([q_back[3], p_back[3]])
            .reshape(2, np_size, -1, wq_size, model_width // wq_size)
            .transpose(3, 1, 0, 2, 4)
            .reshape(wq_size * np_size, -1),
            jnp.stack([q_back[4], p_back[4]])
            .reshape(2, wq_size * np_size, -1)
            .transpose(1, 0, 2)
            .reshape(wq_size * np_size, -1),
        ],
        axis=1,
    )
    sums = jnp.sum(lax.all_to_all(sums, both_axes, 0, 0), axis=0)
    grad_vectors = sums[: sums.shape[0] - 2 * ff_width // (wq_size * np_size)].reshape(
        2, -1, model_width // wq_size
    )
    grad_b_in = sums[sums.shape[0] - 2 * ff_width // (wq_size * np_size) :].reshape(2, -1)
    q_weight_grads = weight_grads(
        left[:, :q_count].reshape(-1, left.shape[2]),
        right[:, :q_count].reshape(-1, right.shape[2]),
        model_width,
        ff_width,
        wq_size,
        np_size,
    )
    p_weight_grads = weight_grads(
        left[:, q_count:].reshape(-1, left.shape[2]),
        right[:, q_count:].reshape(-1, right.shape[2]),
        model_width,
        ff_width,
        wq_size,
        np_size,
    )
    shared = tuple(jnp.stack(pair) for pair in zip(q_weight_grads, p_weight_grads))
    return (
        loss,
        q_encoded,
        p_encoded,
        q_back[0],
        p_back[0],
        shared[0],
        shared[1],
        shared[2],
        shared[3],
        grad_vectors,
        grad_b_in,
    )


def solution(mesh):
    return jax.shard_map(
        shards,
        mesh=mesh,
        in_specs=(
            P(("wq", "np"), None),
            P(("wq", "np"), None),
            P(("wq", "np")),
            P(("wq", "np")),
            P(("wq", "np")),
            P(("wq", "np")),
            P(("wq", "np")),
            P(None, "wq", "np"),
            P(None, "wq", "np"),
            P(None, "wq", "np"),
            P(None, "wq", "np"),
            P(None, "np", "wq"),
            P(None, ("wq", "np")),
        ),
        out_specs=(
            P(),
            P(("wq", "np"), None),
            P(("wq", "np"), None),
            P(("wq", "np"), None),
            P(("wq", "np"), None),
            P(None, "wq", "np"),
            P(None, "wq", "np"),
            P(None, "wq", "np"),
            P(None, "wq", "np"),
            P(None, "np", "wq"),
            P(None, ("wq", "np")),
        ),
        check_vma=False,
    )
```

```python
import functools
import math

import jax
import jax.numpy as jnp
from jax import lax
from jax.experimental import pallas as pl
from jax.experimental.pallas import tpu as pltpu
from jax.sharding import PartitionSpec as P


HEADS = 12


EPSILON = 1e-12
NEGATIVE = -1e30


def layer_norm(inputs, gain_row, offset):
    centred = inputs - jnp.mean(inputs, axis=-1, keepdims=True)
    spread = jnp.mean(centred * centred, axis=-1, keepdims=True)
    return centred * lax.rsqrt(spread + EPSILON) * gain_row + offset


def smooth_gate(values):
    return jax.nn.gelu(values, approximate=True)


def gather_weights(
    query_key_value_weight, attention_output_weight, up_weight, down_weight, vectors, hidden_bias
):
    np_parts = (
        lax.all_gather(query_key_value_weight, "np", axis=2, tiled=True),
        lax.all_gather(attention_output_weight, "np", axis=2, tiled=True),
        lax.all_gather(up_weight, "np", axis=2, tiled=True),
        lax.all_gather(down_weight, "np", axis=2, tiled=True),
        lax.all_gather(vectors, "np", axis=1, tiled=True),
        lax.all_gather(hidden_bias, "np", axis=1, tiled=True),
    )
    return (
        lax.all_gather(np_parts[0], "wq", axis=1, tiled=True),
        lax.all_gather(np_parts[1], "wq", axis=1, tiled=True),
        lax.all_gather(np_parts[2], "wq", axis=1, tiled=True),
        lax.all_gather(np_parts[3], "wq", axis=1, tiled=True),
        lax.all_gather(np_parts[4], "wq", axis=2, tiled=True),
        lax.all_gather(np_parts[5], "wq", axis=1, tiled=True),
    )


def head_split(matrix, seq_count):
    row_count, model_width = matrix.shape
    return matrix.reshape(seq_count, row_count // seq_count, HEADS, model_width // HEADS)


def attention_scores(queries, keys_low, lengths):
    seq_count = lengths.shape[0]
    split_q = head_split(queries, seq_count)
    scores = jnp.einsum(
        "sqhc,skhc->shqk",
        split_q,
        head_split(keys_low, seq_count),
        preferred_element_type=jnp.float32,
    )
    scores = scores * split_q.shape[3] ** (-0.5)
    live_mask = jnp.arange(split_q.shape[1])[None, :] < lengths[:, None]
    return jnp.where(live_mask[:, None, None, :], scores, NEGATIVE)


def first_rows(matrix, seq_count):
    row_count, width = matrix.shape
    return matrix.reshape(seq_count, row_count // seq_count, width)[:, 0, :]


def encode_forward(token_rows, lengths, weights):
    (
        query_key_value_weight,
        attention_output_weight,
        up_weight,
        down_weight,
        vectors,
        hidden_bias,
    ) = weights
    row_count, model_width = token_rows.shape
    seq_count = lengths.shape[0]
    vec_f32 = vectors.astype(jnp.float32)
    projected_rows = jnp.dot(token_rows, query_key_value_weight, preferred_element_type=jnp.float32)
    queries = (projected_rows[:, :model_width] + vec_f32[0]).astype(jnp.bfloat16)
    keys_low = projected_rows[:, model_width : 2 * model_width].astype(jnp.bfloat16)
    values = (projected_rows[:, 2 * model_width :] + vec_f32[1]).astype(jnp.bfloat16)
    scores = attention_scores(queries, keys_low, lengths)
    totals = jax.nn.logsumexp(scores, axis=-1, keepdims=True)
    soft_low = jnp.exp(scores - totals).astype(jnp.bfloat16)
    attended_tokens = jnp.einsum(
        "shqk,skhc->sqhc",
        soft_low,
        head_split(values, seq_count),
        preferred_element_type=jnp.float32,
    )
    attended_tokens = attended_tokens.reshape(row_count, model_width).astype(jnp.bfloat16)
    residual_branch = (
        jnp.dot(attended_tokens, attention_output_weight, preferred_element_type=jnp.float32)
        + vec_f32[2]
    )
    pre_one = token_rows.astype(jnp.float32) + residual_branch
    first_normed = layer_norm(pre_one, vec_f32[3], vec_f32[4])
    normed_low = first_normed.astype(jnp.bfloat16)
    hidden_rows = jnp.dot(
        normed_low, up_weight, preferred_element_type=jnp.float32
    ) + hidden_bias.astype(jnp.float32)
    activated_hidden = smooth_gate(hidden_rows).astype(jnp.bfloat16)
    feedforward_output = (
        jnp.dot(activated_hidden, down_weight, preferred_element_type=jnp.float32) + vec_f32[5]
    )
    pre_two = first_normed + feedforward_output
    encoded_low = layer_norm(pre_two, vec_f32[6], vec_f32[7]).astype(jnp.bfloat16)
    soft_first = jnp.exp(scores[:, :, 0, :] - totals[:, :, 0, :])
    stored = (
        first_rows(queries, seq_count),
        keys_low,
        values,
        soft_first,
        first_rows(attended_tokens, seq_count),
        first_rows(pre_one, seq_count),
        first_rows(normed_low, seq_count),
        first_rows(hidden_rows, seq_count),
        first_rows(activated_hidden, seq_count),
        first_rows(pre_two, seq_count),
    )
    return (encoded_low, stored)


def norm_back(pre, gain_row, grad_out):
    centred = pre - jnp.mean(pre, axis=-1, keepdims=True)
    inverse = lax.rsqrt(jnp.mean(centred * centred, axis=-1, keepdims=True) + EPSILON)
    scaled = grad_out * gain_row
    inner = jnp.mean(scaled * centred, axis=-1, keepdims=True)
    grad_in = inverse * (
        scaled - jnp.mean(scaled, axis=-1, keepdims=True) - centred * (inverse * inverse * inner)
    )
    return (grad_in, jnp.sum(grad_out * centred * inverse, axis=0), jnp.sum(grad_out, axis=0))


def encode_backward(token_rows, weights, stored, grad_first):
    (
        query_key_value_weight,
        attention_output_weight,
        up_weight,
        down_weight,
        vectors,
        hidden_bias,
    ) = weights
    (
        queries,
        keys_low,
        values,
        soft_first,
        attended,
        pre_one,
        normed_low,
        hidden_rows,
        activated_hidden,
        pre_two,
    ) = stored
    seq_count, model_width = queries.shape
    seq_length = token_rows.shape[0] // seq_count
    head_width = model_width // HEADS
    scaling = head_width ** (-0.5)
    vec_f32 = vectors.astype(jnp.float32)
    grad_two, gain_two, shift_two = norm_back(pre_two, vec_f32[6], grad_first)
    grad_ffn = grad_two.astype(jnp.bfloat16)
    grad_activated = jnp.einsum(
        "rd,fd->rf", grad_ffn, down_weight, preferred_element_type=jnp.float32
    )
    grad_hidden = jax.vjp(smooth_gate, hidden_rows)[1](grad_activated)[0].astype(jnp.bfloat16)
    grad_normed = grad_two + jnp.einsum(
        "rf,df->rd", grad_hidden, up_weight, preferred_element_type=jnp.float32
    )
    grad_one, gain_one, shift_one = norm_back(pre_one, vec_f32[3], grad_normed)
    grad_branch = grad_one.astype(jnp.bfloat16)
    grad_attended = jnp.einsum(
        "re,de->rd", grad_branch, attention_output_weight, preferred_element_type=jnp.float32
    ).astype(jnp.bfloat16)
    grad_heads = grad_attended.reshape(seq_count, HEADS, head_width)
    grad_soft = jnp.einsum(
        "shc,skhc->shk",
        grad_heads,
        head_split(values, seq_count),
        preferred_element_type=jnp.float32,
    )
    row_inner = jnp.sum(soft_first * grad_soft, axis=-1, keepdims=True)
    grad_scores = (soft_first * (grad_soft - row_inner)).astype(jnp.bfloat16)
    soft_low = soft_first.astype(jnp.bfloat16)
    grad_queries = (
        jnp.einsum(
            "shk,skhc->shc",
            grad_scores,
            head_split(keys_low, seq_count),
            preferred_element_type=jnp.float32,
        )
        * scaling
    )
    grad_q_low = grad_queries.reshape(seq_count, model_width).astype(jnp.bfloat16)
    tokens = token_rows.reshape(seq_count, seq_length, model_width)
    both = jnp.concatenate([grad_scores, soft_low], axis=1)
    mixed = jnp.einsum("sgk,skd->sgd", both, tokens, preferred_element_type=jnp.float32).astype(
        jnp.bfloat16
    )
    scaled_queries = (queries.astype(jnp.float32) * scaling).astype(jnp.bfloat16)
    split_weight = query_key_value_weight.reshape(model_width, 3, HEADS, head_width)
    back_rows = jnp.concatenate(
        [
            jnp.einsum(
                "shc,dhc->shd",
                scaled_queries.reshape(seq_count, HEADS, head_width),
                split_weight[:, 1],
                preferred_element_type=jnp.float32,
            ),
            jnp.einsum(
                "shc,dhc->shd",
                grad_heads,
                split_weight[:, 2],
                preferred_element_type=jnp.float32,
            ),
        ],
        axis=1,
    ).astype(jnp.bfloat16)
    grad_tokens = jnp.einsum("sgk,sgd->skd", both, back_rows, preferred_element_type=jnp.float32)
    first_extra = grad_one + jnp.einsum(
        "se,de->sd",
        grad_q_low,
        query_key_value_weight[:, :model_width],
        preferred_element_type=jnp.float32,
    )
    is_first = (jnp.arange(seq_length) == 0)[None, :, None]
    grad_tokens = grad_tokens + jnp.where(is_first, first_extra[:, None, :], 0.0)
    soft_total = jnp.sum(soft_low.astype(jnp.float32), axis=-1, keepdims=True)
    vector_parts = jnp.stack(
        [
            jnp.sum(grad_q_low.astype(jnp.float32), axis=0),
            jnp.sum(grad_heads.astype(jnp.float32) * soft_total, axis=0).reshape(model_width),
            jnp.sum(grad_branch.astype(jnp.float32), axis=0),
            gain_one,
            shift_one,
            jnp.sum(grad_ffn.astype(jnp.float32), axis=0),
            gain_two,
            shift_two,
        ]
    )
    bias_part = jnp.sum(grad_hidden.astype(jnp.float32), axis=0)
    left = (
        activated_hidden,
        normed_low,
        attended,
        jnp.concatenate(
            [jnp.broadcast_to(tokens[:, :1, :], (seq_count, HEADS, model_width)), mixed], axis=1
        ),
    )
    right = (
        grad_ffn,
        grad_hidden,
        grad_branch,
        jnp.concatenate([grad_q_low, scaled_queries, grad_attended], axis=1),
    )
    return (
        grad_tokens.reshape(token_rows.shape),
        left,
        right,
        vector_parts,
        bias_part,
    )


def left_message(left, wq_size, np_size):
    activated, normed, attended, mixed = left
    rows, groups, model_width = mixed.shape
    part = model_width // wq_size
    columns = 3 * model_width // np_size
    head_width = model_width // HEADS
    group = math.gcd(head_width, columns)
    mixed = jnp.repeat(mixed, head_width // group, axis=1)
    mixed = mixed.reshape(rows, np_size, columns // group, wq_size, part)
    mixed = mixed.transpose(3, 1, 0, 2, 4).reshape(wq_size, np_size, rows, columns // group * part)

    def same(matrix):
        pieces = matrix.reshape(rows, wq_size, -1).transpose(1, 0, 2)
        return jnp.broadcast_to(pieces[:, None], (wq_size, np_size) + pieces.shape[1:])

    return jnp.concatenate([same(activated), same(normed), same(attended), mixed], axis=3)


def right_message(right, np_size):
    rows = right[0].shape[0]
    return jnp.concatenate(
        [member.reshape(rows, np_size, -1).transpose(1, 0, 2) for member in right], axis=2
    )


def weight_grads(left, right, model_width, ff_width, wq_size, np_size):
    rows = left.shape[0]
    part, ff_part = model_width // wq_size, ff_width // wq_size
    columns = 3 * model_width // np_size
    group = math.gcd(model_width // HEADS, columns)
    right_sizes = (model_width // np_size, ff_width // np_size, model_width // np_size)
    cut = [ff_part, ff_part + part, ff_part + 2 * part]
    activated, normed, attended, mixed = jnp.split(left, cut, axis=1)
    cut = [right_sizes[0], right_sizes[0] + right_sizes[1], sum(right_sizes)]
    grad_ffn, grad_hidden, grad_branch, grad_projected = jnp.split(right, cut, axis=1)

    def outer(one, two):
        return jnp.einsum("sd,se->de", one, two, preferred_element_type=jnp.float32)

    w_qkv = jnp.einsum(
        "sgd,sgc->dgc",
        mixed.reshape(rows, columns // group, part),
        grad_projected.reshape(rows, columns // group, group),
        preferred_element_type=jnp.float32,
    ).reshape(part, columns)
    return (
        w_qkv,
        outer(attended, grad_branch),
        outer(normed, grad_hidden),
        outer(activated, grad_ffn),
    )


BLK=256
F32=jnp.float32; BF=jnp.bfloat16
NEG=-1e30; EPS=1e-12
def dot(a,b): return jnp.dot(a,b,preferred_element_type=F32)
def norm(u,g,b):
    c=u-jnp.mean(u,axis=-1,keepdims=True)
    s=jnp.mean(c*c,axis=-1,keepdims=True)
    return c*lax.rsqrt(s+EPS)*g+b
def put_first(ref, e, i, cols, v):
    if e==1:
        ref[pl.ds(8+i,1),cols]=v[0:1]
    else:
        for j in range(4): ref[pl.ds(4*i+j,1),cols]=v[64*j:64*j+1]
def make_bias(bias_ref, slot, lens, slots):
    n=BLK//slots
    key=lax.broadcasted_iota(jnp.int32,(BLK,BLK),0)
    qry=lax.broadcasted_iota(jnp.int32,(BLK,BLK),1)
    ok=key<lens[0]
    if n>1:
        ok=ok&(qry<slots)
        for j in range(1,n):
            ok=ok|((key>=j*slots)&(key<j*slots+lens[j])&(qry>=j*slots)&(qry<(j+1)*slots))
    bias_ref[...]=jnp.where(ok,0.0,NEG)
def attend_block(row, x_ref, wqkv, vec, bias_ref, k_ref, v_ref, att_ref, q0_ref, e, i):
    x=x_ref[pl.ds(row,BLK),:]
    for g in range(3):
        cs=pl.ds(g*256,256)
        q4=dot(x,wqkv[:,g*256:g*256+256])+vec[0:1,g*256:g*256+256]
        q4=q4.astype(BF)
        k4=dot(x,wqkv[:,768+g*256:768+g*256+256]).astype(BF)
        v4=(dot(x,wqkv[:,1536+g*256:1536+g*256+256])+vec[1:2,g*256:g*256+256]).astype(BF)
        k_ref[pl.ds(row,BLK),cs]=k4
        v_ref[pl.ds(row,BLK),cs]=v4
        put_first(q0_ref,e,i,slice(g*256,g*256+256),q4.astype(F32))
        qT=(q4.astype(F32)*0.125).T.astype(BF)
        vT=v4.astype(F32).T.astype(BF)
        lane=lax.broadcasted_iota(jnp.int32,(BLK,256),1)
        outs=[]
        for h in range(4):
            kh=jnp.where((lane>=64*h)&(lane<64*h+64),k4,jnp.zeros_like(k4))
            s=dot(kh,qT)+bias_ref[...]
            m=jnp.max(s,axis=0,keepdims=True)
            p=jnp.exp(s-m)
            l=jnp.sum(p,axis=0,keepdims=True)
            o=dot(vT[64*h:64*h+64,:],p.astype(BF))
            outs.append(o*(1.0/l))
        oT=jnp.concatenate(outs,axis=0)
        att_ref[pl.ds(row,BLK),cs]=oT.T.astype(BF)
def out_block(row, x_ref, att_ref, wo, vec, n_ref, a0_ref, p1_ref, e, i):
    att=att_ref[pl.ds(row,BLK),:]
    put_first(a0_ref,e,i,slice(None),att.astype(F32))
    pre=x_ref[pl.ds(row,BLK),:].astype(F32)+dot(att,wo[...])+vec[2:3,:]
    put_first(p1_ref,e,i,slice(None),pre)
    n_ref[pl.ds(row,BLK),:]=norm(pre,vec[3:4,:],vec[4:5,:])
def gelu(u):
    return 0.5*u*(1.0+jnp.tanh(0.7978845608028654*(u+0.044715*(u*u*u))))
def up_block(row, n_ref, wup, hb, act_ref, h0_ref, e, i, arow):
    nl=n_ref[pl.ds(row,BLK),:].astype(BF)
    for t in range(12):
        cs=slice(t*256,t*256+256)
        h=dot(nl,wup[:,cs])+hb[0:1,cs]
        put_first(h0_ref,e,i,cs,h)
        act_ref[pl.ds(arow,BLK),cs]=gelu(h).astype(BF)
def down_block(row, n_ref, act_ref, wdown, vec, o_ref, p2_ref, hd_ref, e, i, arow):
    f=dot(act_ref[pl.ds(arow,BLK),:],wdown[...])+vec[5:6,:]
    pre=n_ref[pl.ds(row,BLK),:]+f
    put_first(p2_ref,e,i,slice(None),pre)
    enc=norm(pre,vec[6:7,:],vec[7:8,:])
    put_first(hd_ref,e,i,slice(None),enc)
    o_ref[pl.ds(row,BLK),:]=enc.astype(BF)

def dot_nt(a,b): return lax.dot_general(a,b,(((1,),(1,)),((),())),preferred_element_type=F32)
def gelu_slope(u):
    t=jnp.tanh(0.7978845608028654*(u+0.044715*(u*u*u)))
    return 0.5*(1.0+t)+0.5*u*(1.0-t*t)*(0.7978845608028654*(1.0+0.134145*(u*u)))
def norm_grad(u,g,gy):
    c=u-jnp.mean(u,axis=-1,keepdims=True)
    r=lax.rsqrt(jnp.mean(c*c,axis=-1,keepdims=True)+EPS)
    t=gy*g
    gu=r*(t-jnp.mean(t,axis=-1,keepdims=True)-c*(r*r)*jnp.mean(t*c,axis=-1,keepdims=True))
    return gu, jnp.sum(gy*c*r,axis=0,keepdims=True), jnp.sum(gy,axis=0,keepdims=True)
def heads_apart(rows, count):
    n=rows.shape[0]
    wide=jnp.concatenate([jnp.broadcast_to(rows[i:i+1],(16,768)) for i in range(n)],axis=0)
    r=lax.broadcasted_iota(jnp.int32,wide.shape,0)%16
    l=lax.broadcasted_iota(jnp.int32,wide.shape,1)//64
    return jnp.where(r==l,wide,0.0)
def pick_matrix(off, lane0):
    r=lax.broadcasted_iota(jnp.int32,(256,128),0); l=lax.broadcasted_iota(jnp.int32,(256,128),1)
    return jnp.where((r-off==l-lane0)&(l>=lane0)&(l<lane0+48),1.0,0.0).astype(BF)
MESH = pl.DeviceIdType.MESH

class Gather:
    def __init__(self, units, ins, outs, send, recv):
        self.units, self.ins, self.outs, self.send, self.recv = units, ins, outs, send, recv
        w, self.y = lax.axis_index("wq"), lax.axis_index("np")
        self.w = w
        self.z, self.x, self.c = w // 4, (w // 2) % 2, w % 2
        self.pending = {}
    def dev(self, dz=0, fx=False, fy=False, fc=False):
        x = 1 - self.x if fx else self.x
        c = 1 - self.c if fc else self.c
        y = 1 - self.y if fy else self.y
        return ((self.z + dz) * 4 + x * 2 + c, y)
    def barrier(self):
        bar = pltpu.get_barrier_semaphore()
        def sig(**k): pl.semaphore_signal(bar, inc=1, device_id=self.dev(**k), device_id_type=MESH)
        sig(fx=True); sig(fy=True); sig(fc=True)
        @pl.when(self.z > 0)
        def _(): sig(dz=-1)
        @pl.when(self.z < 3)
        def _(): sig(dz=1)
        pl.semaphore_wait(bar, 3 + (self.z + 3) // 4 + (6 - self.z) // 4)
    def view(self, u, z=None, x=None, y=None, c=None):
        a, e, kind, r0, rn = self.units[u]
        o = self.outs[a]
        r, w = self.ins[a].shape[1:]
        zs = slice(None) if z is None else z
        xs = slice(None) if x is None else x
        cs = slice(None) if y is None else pl.ds(pl.multiple_of(y * w, 128), w)
        return o.at[e, zs, xs, pl.ds(pl.multiple_of((self.c if c is None else c) * r + r0, 16), rn), cs]
    def copy(self, u, sem, src, dst, dev):
        return pltpu.make_async_remote_copy(src_ref=src, dst_ref=dst, send_sem=self.send.at[u, sem], recv_sem=self.recv.at[u, sem], device_id=dev, device_id_type=MESH)
    def own_src(self, u):
        a, e, kind, r0, rn = self.units[u]
        return self.ins[a].at[e, pl.ds(r0, rn)]
    def zview(self, u, core, z):
        kind = self.units[u][2]
        if kind == "F": return self.view(u, z=z, x=self.x, y=self.y)
        if core == 0: return self.view(u, z=z, x=None, y=self.y)
        return self.view(u, z=z, x=self.x, y=None)
    def step(self, u, s):
        for core in (0, 1):
            pl.when(self.c == core)(lambda core=core: self._step(u, s, core))
    def A(self, core): return dict(fx=True) if core == 0 else dict(fy=True)
    def B(self, core): return dict(fy=True) if core == 0 else dict(fx=True)
    def a_src(self, u, core):
        kind = self.units[u][2]
        z = None if kind == "F" else self.z
        return self.view(u, z=z, x=self.x, y=self.y)
    def a_got(self, u, core):
        kind = self.units[u][2]
        z = None if kind == "F" else self.z
        return self.view(u, z=z, x=1 - self.x, y=self.y) if core == 0 else self.view(u, z=z, x=self.x, y=1 - self.y)
    def b_src(self, u, core):
        return self.view(u, x=None, y=self.y) if core == 0 else self.view(u, x=self.x, y=None)
    def b_got(self, u, core):
        return self.view(u, x=None, y=1 - self.y) if core == 0 else self.view(u, x=1 - self.x, y=None)
    def local(self, u, sem, ref):
        self.copy(u, sem, ref, ref, self.dev(fc=True)).start()
    def z_send(self, u, core, hop):
        z = self.z
        @pl.when((z - hop >= 0) & (z + 1 <= 3))
        def _():
            v = self.zview(u, core, z - hop)
            src = self.own_src(u) if (hop == 0 and self.units[u][2] == "F") else v
            self.copy(u, 2 + hop, src, v, self.dev(dz=1)).start()
        @pl.when((z + hop <= 3) & (z - 1 >= 0))
        def _():
            v = self.zview(u, core, z + hop)
            src = self.own_src(u) if (hop == 0 and self.units[u][2] == "F") else v
            self.copy(u, 5 + hop, src, v, self.dev(dz=-1)).start()
    def z_wait(self, u, core, hop):
        z = self.z
        @pl.when(z - 1 - hop >= 0)
        def _():
            v = self.zview(u, core, z - 1 - hop)
            self.copy(u, 2 + hop, v, v, self.dev(fc=True)).wait_recv()
            self.local(u, 11 + hop, v)
        @pl.when(z + 1 + hop <= 3)
        def _():
            v = self.zview(u, core, z + 1 + hop)
            self.copy(u, 5 + hop, v, v, self.dev(fc=True)).wait_recv()
            self.local(u, 14 + hop, v)
    def _step(self, u, s, core):
        F = self.units[u][2] == "F"
        own = self.view(u, z=self.z, x=self.x, y=self.y)
        if s == 0:
            src = self.own_src(u)
            self.copy(u, 8, src, own, self.dev(fc=True)).start()
            pltpu.make_async_copy(src, own, self.send.at[u, 17]).start()
            if F:
                self.z_send(u, core, 0)
            else:
                self.copy(u, 0, src, own, self.dev(**self.A(core))).start()
        if s == 1:
            pltpu.make_async_copy(self.own_src(u), own, self.send.at[u, 17]).wait()
            if F:
                self.z_wait(u, core, 0); self.z_send(u, core, 1)
            else:
                g = self.a_got(u, core)
                self.copy(u, 0, g, g, self.dev(fc=True)).wait_recv()
                self.z_send(u, core, 0)
                self.local(u, 9, g)
        if s == 2:
            if F: self.z_wait(u, core, 1); self.z_send(u, core, 2)
            else: self.z_wait(u, core, 0); self.z_send(u, core, 1)
        if s == 3:
            if F:
                self.z_wait(u, core, 2)
                v = self.a_src(u, core)
                self.copy(u, 0, v, v, self.dev(**self.A(core))).start()
            else:
                self.z_wait(u, core, 1); self.z_send(u, core, 2)
        if s == 4:
            if F:
                g = self.a_got(u, core)
                self.copy(u, 0, g, g, self.dev(fc=True)).wait_recv()
            else:
                self.z_wait(u, core, 2)
            v = self.b_src(u, core)
            self.copy(u, 1, v, v, self.dev(**self.B(core))).start()
            if F: self.local(u, 9, g)
        if s == 5:
            g = self.b_got(u, core)
            self.copy(u, 1, g, g, self.dev(fc=True)).wait_recv()
            self.local(u, 10, g)
        if s == 6:
            self.finish_recv(u, core); self.finish_send(u, core)
    def finish_recv(self, u, core):
        other = 1 - core
        c = 1 - self.c
        kind = self.units[u][2]
        def got(sem, v): self.copy(u, sem, v, v, self.dev(fc=True)).wait_recv()
        sv = lambda **k: self.view(u, c=c, **k)
        got(8, sv(z=self.z, x=self.x, y=self.y))
        za = None if kind == "F" else self.z
        got(9, sv(z=za, x=1 - self.x, y=self.y) if other == 0 else sv(z=za, x=self.x, y=1 - self.y))
        got(10, sv(x=None, y=1 - self.y) if other == 0 else sv(x=1 - self.x, y=None))
        def zv(z):
            if kind == "F": return sv(z=z, x=self.x, y=self.y)
            return sv(z=z, x=None, y=self.y) if other == 0 else sv(z=z, x=self.x, y=None)
        for hop in range(3):
            pl.when(self.z - 1 - hop >= 0)(lambda hop=hop: got(11 + hop, zv(self.z - 1 - hop)))
            pl.when(self.z + 1 + hop <= 3)(lambda hop=hop: got(14 + hop, zv(self.z + 1 + hop)))
    def finish_send(self, u, core):
        def sent(sem, v): self.copy(u, sem, v, v, self.dev(fc=True)).wait_send()
        own = self.view(u, z=self.z, x=self.x, y=self.y)
        sent(8, own)
        sent(0, self.a_src(u, core)); sent(1, self.b_src(u, core))
        sent(9, self.a_got(u, core)); sent(10, self.b_got(u, core))
        z = self.z
        for hop in range(3):
            pl.when((z - hop >= 0) & (z + 1 <= 3))(lambda hop=hop: sent(2 + hop, self.zview(u, core, z - hop)))
            pl.when((z + hop <= 3) & (z - 1 >= 0))(lambda hop=hop: sent(5 + hop, self.zview(u, core, z + hop)))
            pl.when(z - 1 - hop >= 0)(lambda hop=hop: sent(11 + hop, self.zview(u, core, z - 1 - hop)))
            pl.when(z + 1 + hop <= 3)(lambda hop=hop: sent(14 + hop, self.zview(u, core, z + 1 + hop)))

class Place:
    def __init__(self):
        self.w=lax.axis_index("wq"); self.y=lax.axis_index("np")
        self.z,self.x,self.c=self.w//4,(self.w//2)%2,self.w%2
        self.me=self.w*2+self.y
    def dev(self, z=None, fx=False, fy=False, fc=False):
        x=1-self.x if fx else self.x
        c=1-self.c if fc else self.c
        y=1-self.y if fy else self.y
        return ((self.z if z is None else z)*4+x*2+c, y)

class HeadGather:
    def __init__(self,pos,buf,send,recv):
        self.pos,self.buf,self.send,self.recv=pos,buf,send,recv
    def rc(self,sem,ref,dev):
        return pltpu.make_async_remote_copy(src_ref=ref,dst_ref=ref,send_sem=self.send.at[sem],recv_sem=self.recv.at[sem],device_id=dev,device_id_type=MESH)
    def phase(self,s):
        for core in (0,1): pl.when(self.pos.c==core)(functools.partial(self.core_phase,s,core))
    def core_phase(self,s,core):
        pos,buf=self.pos,self.buf
        z,x,c,y=pos.z,pos.x,pos.c,pos.y
        sib=pos.dev(fc=True)
        def arrived(sem,ref): self.rc(sem,ref,sib).wait_recv()
        own=buf.at[z,x,c,y]; col=buf.at[:,x,c,y]
        got=buf.at[:,1-x,c,y] if core==0 else buf.at[:,x,c,1-y]
        both=buf.at[:,:,c,y] if core==0 else buf.at[:,x,c,:]
        last=buf.at[:,:,c,1-y] if core==0 else buf.at[:,1-x,c,:]
        first=dict(fx=True) if core==0 else dict(fy=True)
        second=dict(fy=True) if core==0 else dict(fx=True)
        if s==0:
            for k in (1,2,3): self.rc(k-1,own,pos.dev(z=(z+k)%4)).start()
        if s==1:
            for k in (1,2,3): arrived(k-1,buf.at[(z+4-k)%4,x,c,y])
            self.rc(3,col,pos.dev(**first)).start(); self.rc(5,col,sib).start()
        if s==2:
            arrived(3,got)
            self.rc(4,both,pos.dev(**second)).start(); self.rc(6,got,sib).start()
        if s==3:
            arrived(4,last); self.rc(7,last,sib).start()
            o=1-c
            arrived(5,buf.at[:,x,o,y])
            arrived(6,buf.at[:,x,o,1-y] if core==0 else buf.at[:,1-x,o,y])
            arrived(7,buf.at[:,1-x,o,:] if core==0 else buf.at[:,:,o,1-y])
            for sem,ref in ((0,own),(1,own),(2,own),(3,col),(4,both),(5,col),(6,got),(7,last)): self.rc(sem,ref,sib).wait_send()

CHUNKS=((0,1024),(1024,896),(1920,768),(2688,768))
class RightGather:
    def __init__(self,pos,src,buf,send,recv):
        self.pos,self.src,self.buf,self.send,self.recv=pos,src,buf,send,recv
    def rc(self,ch,sem,src,dst,dev):
        return pltpu.make_async_remote_copy(src_ref=src,dst_ref=dst,send_sem=self.send.at[ch,sem],recv_sem=self.recv.at[ch,sem],device_id=dev,device_id_type=MESH)
    def view(self,ch,z=None,x=None,c=None,y=None):
        p=self.pos; c0,w=CHUNKS[ch]
        f=lambda v: slice(None) if v is None else v
        return self.buf.at[f(z),p.x if x is None else x,p.c if c is None else c,f(y),:,c0:c0+w]
    def half(self,ch,y):
        c0,w=CHUNKS[ch]
        return self.src.at[y,:,c0:c0+w]
    def step(self,ch,s):
        p=self.pos; z,y=p.z,p.y
        sib=p.dev(fc=True)
        def arrived(sem,v): self.rc(ch,sem,v,v,sib).wait_recv()
        def local(sem,v): self.rc(ch,sem,v,v,sib).start()
        def z_send(hop):
            @pl.when((z-hop>=0)&(z+1<=3))
            def _():
                v=self.view(ch,z=z-hop); self.rc(ch,2+hop,v,v,p.dev(z=z+1)).start()
            @pl.when((z+hop<=3)&(z-1>=0))
            def _():
                v=self.view(ch,z=z+hop); self.rc(ch,5+hop,v,v,p.dev(z=z-1)).start()
        def z_wait(hop):
            @pl.when(z-1-hop>=0)
            def _():
                v=self.view(ch,z=z-1-hop); arrived(2+hop,v); local(9+hop,v)
            @pl.when(z+1+hop<=3)
            def _():
                v=self.view(ch,z=z+1+hop); arrived(5+hop,v); local(12+hop,v)
        own=self.view(ch,z=z,y=y)
        if s==0:
            self.rc(ch,0,self.half(ch,1-y),own,p.dev(fy=True)).start()
            pltpu.make_async_copy(self.half(ch,y),own,self.send.at[ch,16]).start()
        if s==1:
            pltpu.make_async_copy(self.half(ch,y),own,self.send.at[ch,16]).wait()
            arrived(0,self.view(ch,z=z,y=1-y))
            z_send(0); local(8,self.view(ch,z=z))
        if s==2: z_wait(0); z_send(1)
        if s==3: z_wait(1); z_send(2)
        if s==4:
            z_wait(2)
            v=self.view(ch); self.rc(ch,1,v,v,p.dev(fx=True)).start()
        if s==5:
            g=self.view(ch,x=1-p.x); arrived(1,g); local(15,g)
        if s==6:
            o=1-p.c
            arrived(8,self.view(ch,z=z,c=o)); arrived(15,self.view(ch,x=1-p.x,c=o))
            def sent(sem,v): self.rc(ch,sem,v,v,sib).wait_send()
            sent(0,own); sent(1,self.view(ch)); sent(8,self.view(ch,z=z)); sent(15,self.view(ch,x=1-p.x))
            for hop in range(3):
                pl.when(z-1-hop>=0)(lambda hop=hop: arrived(9+hop,self.view(ch,z=z-1-hop,c=o)))
                pl.when(z+1+hop<=3)(lambda hop=hop: arrived(12+hop,self.view(ch,z=z+1+hop,c=o)))
                pl.when((z-hop>=0)&(z+1<=3))(lambda hop=hop: sent(2+hop,self.view(ch,z=z-hop)))
                pl.when((z+hop<=3)&(z-1>=0))(lambda hop=hop: sent(5+hop,self.view(ch,z=z+hop)))
                pl.when(z-1-hop>=0)(lambda hop=hop: sent(9+hop,self.view(ch,z=z-1-hop)))
                pl.when(z+1+hop<=3)(lambda hop=hop: sent(12+hop,self.view(ch,z=z+1+hop)))

class LeftCopies:
    def __init__(self,pos,left,buf,spans,send,recv):
        self.pos,self.left,self.buf,self.spans,self.send,self.recv=pos,left,buf,spans,send,recv
    def each(self,d,go):
        t=(self.pos.me+d)%32
        w,y=t//2,t%2
        for half,(r0,n) in enumerate(self.spans):
            @pl.when(y==half)
            def _():
                go(pltpu.make_async_remote_copy(src_ref=self.left.at[w,pl.ds(r0,n)],dst_ref=self.buf.at[self.pos.me,pl.ds(0,n)],send_sem=self.send.at[d],recv_sem=self.recv.at[d],device_id=(w,y),device_id_type=MESH))
    def start(self):
        def lap(d,kept):
            self.each(d,lambda cp: cp.start()); return kept
        lax.fori_loop(1,32,lap,0)
        for half,(r0,n) in enumerate(self.spans):
            @pl.when(self.pos.y==half)
            def _(): self.buf[self.pos.me,0:n,:]=self.left[self.pos.w,r0:r0+n,:]
    def finish(self):
        def lap(d,kept):
            self.each(d,lambda cp: cp.wait_send())
            s=(self.pos.me+32-d)%32
            for half,(r0,n) in enumerate(self.spans):
                @pl.when(self.pos.y==half)
                def _():
                    v=self.buf.at[s,pl.ds(0,n)]
                    pltpu.make_async_remote_copy(src_ref=v,dst_ref=v,send_sem=self.send.at[d],recv_sem=self.recv.at[d],device_id=(self.pos.w,self.pos.y),device_id_type=MESH).wait_recv()
            return kept
        lax.fori_loop(1,32,lap,0)

def similarity(pos,buf,marks,loss,gr,gs_s,gt_s):
    g=buf[...].reshape(32,16,768).astype(F32)
    q=g[:,0:8].reshape(256,768).astype(BF); p=g[:,8:16].reshape(256,768).astype(BF)
    m=jnp.sum(marks[...].reshape(8,32,256),axis=0)
    m=m[0:16]+m[16:32]
    m=(m[:,0:128]+m[:,128:256]).astype(F32)
    row=lambda r: jnp.broadcast_to(jnp.concatenate([m[r:r+1],m[r+1:r+2]],axis=1),(256,256))
    qset=row(0).T; gold=row(2).T; pset=row(4)
    lane=lax.broadcasted_iota(jnp.int32,(256,256),1).astype(F32)
    is_gold=gold==lane
    usable=(qset==pset)|is_gold
    sim=dot_nt(q,p)*(768**-0.5)
    masked=jnp.where(usable,sim,NEG)
    high=jnp.max(masked,axis=1,keepdims=True)
    tot=high+jnp.log(jnp.sum(jnp.where(usable,jnp.exp(masked-high),0.0),axis=1,keepdims=True))
    gsc=jnp.sum(jnp.where(is_gold,sim,0.0),axis=1,keepdims=True)
    loss[...]=jnp.broadcast_to(jnp.sum(tot-gsc,axis=0,keepdims=True)*(1.0/256),loss.shape)
    soft=jnp.where(usable,jnp.exp(masked-tot),0.0)
    gsim=soft-jnp.where(is_gold,1.0,0.0)
    gs_s[...]=gsim; gt_s[...]=gsim.T
    me8=pl.ds(pl.multiple_of(pos.me*8,8),8)
    gr[0:8,:]=dot(gs_s[me8,:].astype(BF),p)*(768**-0.5)
    gr[8:16,:]=dot(gt_s[me8,:].astype(BF),q)*(768**-0.5)

EARLY=((0,64),(16,144)); LATE=((0,64),(48,64))
SLOTS=(64,256); NB=(2,6)
def window(s):
    w=min(48*s//128*128,128)
    return w,48*s-w
def two(ref,e,w): return jnp.concatenate([ref[e,w//128],ref[e,w//128+1]],axis=1)
def select_rows(ref,s):
    w,off=window(s)
    cat=lambda e: jnp.concatenate([two(ref,e,w),two(ref,e,w+384)],axis=0).astype(BF)
    m=dot(cat(0),pick_matrix(off,0))+dot(cat(1),pick_matrix(off,64))
    n=ref.shape[2]
    return m[0:n],m[n:2*n]
def select_wide(ref,s):
    w,off=window(s)
    cat=lambda e: jnp.concatenate([ref[e,:,384*m+w:384*m+w+256] for m in range(8)],axis=0).astype(BF)
    m=dot(cat(0),pick_matrix(off,0))+dot(cat(1),pick_matrix(off,64))
    return [m[8*k:8*k+8] for k in range(8)]
def early_messages(ls,la,stage,left):
    for s in range(8):
        for k,r in enumerate(select_rows(ls,s)):
            left[s+8*k,0:32,:]=r[0:32].astype(BF); left[s+8*k,64:160,:]=r[32:128].astype(BF)
        for m,r in enumerate(select_wide(la,s)):
            n=8*m+s
            stage[n//4,8*(n%4):8*(n%4)+8,:]=r
    for j in range(16): left[j,32:64,:]=stage[j].astype(BF)
def late_messages(ll,lb,stage,left):
    for j in range(16): stage[j,0:8,:]=jnp.zeros((8,128),F32)
    for s in range(8):
        for m,r in enumerate(select_wide(lb,s)):
            n=8*m+s
            stage[n//4,n%4:n%4+1,:]=r[0:1]
    for s in range(8):
        for k,r in enumerate(select_rows(ll,s)):
            j=s+8*k
            left[j,0:48,:]=r[0:48].astype(BF); left[j,64:112,:]=r[48:96].astype(BF)
            left[j,48:64,:]=jnp.concatenate([r[96:104],stage[j,0:8]],axis=0).astype(BF)

def early_block(e,i,lens,K,X,qa_s,P_s,ls):
    slots=SLOTS[e]; n=256//slots; R=16*n; row=i*256; pr=(96 if e==0 else 0)+i*R
    k=K[row:row+256,:]; x=X[row:row+256,:]
    s=dot_nt(qa_s[e,i*R:i*R+R,:],k)
    key=lax.broadcasted_iota(jnp.int32,(R,256),1)
    if n==1: ok=key<lens[i]
    else:
        grp=lax.broadcasted_iota(jnp.int32,(R,256),0)//16
        ok=(grp<0)
        for j in range(n): ok=ok|((grp==j)&(key>=j*slots)&(key<j*slots+lens[i*n+j]))
    s=jnp.where(ok,s,NEG)
    p=jnp.exp(s-jnp.max(s,axis=1,keepdims=True))
    p=p*(1.0/jnp.sum(p,axis=1,keepdims=True))
    P_s[pr:pr+R,:]=p
    mix=dot(p.astype(BF),x)
    for j in range(n):
        slot=i*n+j
        first=x[j*slots:j*slots+1].astype(F32)
        for c in range(6):
            cc=slice(128*c,128*c+128)
            ls[e,c,pl.ds(32+slot,12,stride=8),:]=mix[16*j:16*j+12,cc]
            ls[e,c,slot:slot+1,:]=first[:,cc]
def late_block(e,i,K,V,X,ga_s,P_s,ll,gq_s,sv_s,tmix):
    slots=SLOTS[e]; n=256//slots; R=16*n; row=i*256; pr=(96 if e==0 else 0)+i*R
    gab=ga_s[e,i*R:i*R+R,:]
    p=P_s[pr:pr+R,:]
    gs=dot_nt(gab,V[row:row+256,:])
    gs=p*(gs-jnp.sum(p*gs,axis=1,keepdims=True))
    gsb=gs.astype(BF); pb=p.astype(BF)
    tmix[i,0:R,:]=gsb; tmix[i,R:2*R,:]=pb
    gq=dot(gsb,K[row:row+256,:])
    r0=lax.broadcasted_iota(jnp.int32,(R,768),0); hl=lax.broadcasted_iota(jnp.int32,(R,768),1)//64
    gq=jnp.where(r0%16==hl,gq,0.0)*0.125
    st=jnp.sum(pb.astype(F32),axis=1,keepdims=True)
    sv_s[e]=sv_s[e]+jnp.sum(st*gab.astype(F32),axis=0,keepdims=True)
    mix=dot(gsb,X[row:row+256,:])
    for j in range(n):
        slot=i*n+j
        gq_s[e,slot:slot+1,:]=jnp.sum(gq[16*j:16*j+16],axis=0,keepdims=True)
        for c in range(6): ll[e,c,pl.ds(slot,12,stride=8),:]=mix[16*j:16*j+12,128*c:128*c+128]

def colsum(m): return jnp.sum(m.astype(F32),axis=0,keepdims=True)

class Products:
    def __init__(self,pos,eb,lb,rbuf,bq,bp,wqkv,wout,win,wback,gvec,gbin):
        self.__dict__.update(locals())
    def right(self,c0,w):
        r=self.rbuf[:,:,:,:,:,c0:c0+w].reshape(32,16,w).astype(F32)
        self.bq[:,c0:c0+w]=r[:,0:8].reshape(256,w).astype(BF)
        self.bp[:,c0:c0+w]=r[:,8:16].reshape(256,w).astype(BF)
    def pair(self,buf,r0):
        t=buf[:,r0:r0+16,:].astype(F32)
        return [t[:,8*i:8*i+8].reshape(256,128) for i in (0,1)]
    def put(self,out,rows,cols,tt,c0,w):
        tt=tt.T.astype(BF)
        out[0,rows,cols]=dot(tt,self.bq[:,c0:c0+w])[0:48]
        out[1,rows,cols]=dot(tt,self.bp[:,c0:c0+w])[64:112]
    def mixed(self,buf,r0,heads,col0,dst0):
        low=lax.broadcasted_iota(jnp.int32,(128,128),1)<64
        for h in range(0,heads,2):
            a,b=[v.T.astype(BF) for v in self.pair(buf,r0+8*h)]
            cs=slice(col0+64*h,col0+64*h+128); ds=slice(dst0+64*h,dst0+64*h+128)
            self.wqkv[0,:,ds]=jnp.where(low,dot(a,self.bq[:,cs]),dot(b,self.bq[:,cs]))[0:48]
            self.wqkv[1,:,ds]=jnp.where(low,dot(a,self.bp[:,cs]),dot(b,self.bp[:,cs]))[64:112]
    def first(self):
        al=slice(None)
        def go(base):
            nrm,att=self.pair(self.eb,base)
            self.put(self.win,al,al,nrm,384,1536)
            for k in range(0,4,2):
                for i,a in enumerate(self.pair(self.eb,base+16+8*k)):
                    self.put(self.wback,slice(48*(k+i),48*(k+i)+48),al,a,0,384)
        pl.when(self.pos.y==0)(lambda: go(16))
        pl.when(self.pos.y==1)(lambda: go(0))
    def second(self):
        al=slice(None)
        def sums(r0,half):
            vs,bs=[jnp.sum(v.reshape(32,8,128),axis=0) for v in self.pair(self.lb,r0)]
            for e in (0,1):
                ls=slice(64*e,64*e+48)
                self.gvec[e]=vs[4*half:4*half+4,ls]
                self.gbin[e]=bs[2*half:2*half+2,ls]
        @pl.when(self.pos.y==0)
        def _():
            self.put(self.wout,al,al,self.pair(self.eb,16)[1],1920,384)
            self.put(self.wqkv,al,slice(0,768),self.pair(self.eb,0)[0],2304,768)
            self.mixed(self.lb,0,6,3072,768)
            sums(48,0)
        @pl.when(self.pos.y==1)
        def _():
            self.put(self.wout,al,al,self.pair(self.eb,0)[1],1920,384)
            self.mixed(self.lb,16,6,2304,0)
            self.mixed(self.eb,48,12,2688,384)
            sums(0,1)

def tail_kernel(*refs):
    (ql,pln,qx_h,px_h,qk_h,qv_h,pk_h,pv_h,wqkv_h,wo_h,wup_h,wdn_h,q0,a0,p1,h0,p2,heads,marks,vec,
     loss,tq,tp,uq,up_,extra,wqkv,wout,win,wback,gvec,gbin,
     kv_q,kv_p,w_qkv,w_o,w_up,w_dn,hbuf,gr,gs_s,gt_s,qa_s,ga_s,P_s,ls,la,ll,lb,stage,left_e,left_l,ebuf,lbuf,rs,rb,rbuf,bq,bp,gq_s,sv_s,
     msem,hsend,hrecv,esend,erecv,lsend,lrecv,rsend,rrecv)=refs
    pos=Place()
    bar=pltpu.get_barrier_semaphore()
    def lap(d,kept):
        t=(pos.me+d)%32
        pl.semaphore_signal(bar,inc=1,device_id=(t//2,t%2),device_id_type=MESH)
        return kept
    lax.fori_loop(1,32,lap,0)
    moves={}
    def move(name,src,dst): moves[name]=pltpu.make_async_copy(src,dst,msem.at[len(moves)]); moves[name].start()
    for n,(h,d) in enumerate(((pk_h,kv_p),(px_h,kv_p),(pv_h,kv_p),(qk_h,kv_q),(qx_h,kv_q),(qv_h,kv_q))): move("kxv"[n%3]+"pq"[n//3],h,d.at[n%3])
    for nm,h,d in (("dn",wdn_h,w_dn),("up",wup_h,w_up),("o",wo_h,w_o),("qkv",wqkv_h,w_qkv)):
        for e in (1,0): move(nm+str(e),h.at[e],d.at[e])
    def need(*names):
        for nm in names:
            if nm in moves: moves.pop(nm).wait()
    hbuf[pos.z,pos.x,pos.c,pos.y]=heads[...].astype(BF)
    for ref in (ls,ll,lb,gq_s,sv_s): ref[...]=jnp.zeros_like(ref)
    pl.semaphore_wait(bar,31)
    hg=HeadGather(pos,hbuf,hsend,hrecv)
    hg.phase(0)
    KXV={1:kv_p,0:kv_q}; LENS=(ql,pln)
    vv=lambda e: vec[e]
    for e in (1,0):
        rows=slice(8*e,8*e+8)
        qa_s[e]=heads_apart(q0[rows,:]*0.125,8).astype(BF)
        nlow=norm(p1[rows,:],vv(e)[3:4],vv(e)[4:5])
        for c in range(6):
            cc=slice(128*c,128*c+128)
            ls[e,c,16:24,:]=nlow[:,cc]; ls[e,c,24:32,:]=a0[rows,cc]
        la[e]=gelu(h0[rows,:])
    need("kp","xp")
    for i in range(2): early_block(1,i,pln,kv_p.at[0],kv_p.at[1],qa_s,P_s,ls)
    hg.phase(1)
    for i in range(2,6): early_block(1,i,pln,kv_p.at[0],kv_p.at[1],qa_s,P_s,ls)
    hg.phase(2)
    need("kq","xq")
    for i in range(2): early_block(0,i,ql,kv_q.at[0],kv_q.at[1],qa_s,P_s,ls)
    early_messages(ls,la,stage,left_e)
    hg.phase(3)
    ec=LeftCopies(pos,left_e,ebuf,EARLY,esend,erecv)
    ec.start()
    similarity(pos,hbuf,marks,loss,gr,gs_s,gt_s)
    g2,sums,gn={}, {}, {}
    need("dn1","dn0","up1","up0")
    for e in (1,0):
        rows=slice(8*e,8*e+8)
        g2[e],gain2,shift2=norm_grad(p2[rows,:],vv(e)[6:7],gr[rows,:])
        gffn=g2[e].astype(BF)
        gh=(dot_nt(gffn,w_dn[e])*gelu_slope(h0[rows,:])).astype(BF)
        for half in (0,1):
            rs[half,rows,0:384]=gffn[:,384*half:384*half+384].astype(F32)
            rs[half,rows,384:1920]=gh[:,1536*half:1536*half+1536].astype(F32)
        lb[e,0:1,:]=colsum(gh)
        gn[e]=g2[e]+dot_nt(gh,w_up[e])
        sums[e]=(colsum(gffn),gain2,shift2)
    rg=RightGather(pos,rb,rbuf,rsend,rrecv)
    rb[:,:,0:1920]=rs[:,:,0:1920].astype(BF)
    rg.step(0,0); rg.step(1,0)
    need("o1","o0","qkv1","qkv0","vp","vq")
    g1,gb,sums1={}, {}, {}
    for e in (1,0):
        rows=slice(8*e,8*e+8)
        g1[e],gain1,shift1=norm_grad(p1[rows,:],vv(e)[3:4],gn[e])
        gb[e]=g1[e].astype(BF)
        sums1[e]=(colsum(gb[e]),gain1,shift1)
        ga=dot_nt(gb[e],w_o[e]).astype(BF).astype(F32)
        ga_s[e]=heads_apart(ga,8).astype(BF)
        q0s=q0[rows,:]*0.125
        for half in (0,1): rs[half,rows,1920:2304]=gb[e][:,384*half:384*half+384].astype(F32)
        rs[0,rows,3072:3456]=q0s[:,0:384]; rs[1,rows,2304:2688]=q0s[:,384:768]; rs[1,rows,2688:3456]=ga
    rg.step(0,1); rg.step(1,1)
    for i in range(0,3): late_block(1,i,kv_p.at[0],kv_p.at[2],kv_p.at[1],ga_s,P_s,ll,gq_s,sv_s,tp)
    rg.step(0,2); rg.step(1,2)
    for i in range(3,6): late_block(1,i,kv_p.at[0],kv_p.at[2],kv_p.at[1],ga_s,P_s,ll,gq_s,sv_s,tp)
    rg.step(0,3); rg.step(1,3)
    for i in range(2): late_block(0,i,kv_q.at[0],kv_q.at[2],kv_q.at[1],ga_s,P_s,ll,gq_s,sv_s,tq)
    for e in (1,0):
        rows=slice(8*e,8*e+8)
        gql=gq_s[e].astype(BF)
        rs[0,rows,2304:3072]=gql.astype(F32)
        vs=jnp.concatenate([colsum(gql),sv_s[e,0:1],*sums1[e],*sums[e]],axis=0)
        for c in range(6): ll[e,c,96:104,:]=vs[:,128*c:128*c+128]
    rb[:,:,1920:3456]=rs[:,:,1920:3456].astype(BF)
    rg.step(2,0); rg.step(3,0)
    rg.step(0,4); rg.step(1,4)
    late_messages(ll,lb,stage,left_l)
    lc=LeftCopies(pos,left_l,lbuf,LATE,lsend,lrecv)
    lc.start()
    rg.step(2,1); rg.step(3,1)
    for e in (1,0):
        uk=dot_nt(qa_s[e],w_qkv[e,:,768:1536]).astype(BF); uv=dot_nt(ga_s[e],w_qkv[e,:,1536:2304]).astype(BF)
        out=(uq,up_)[e]; R=16*256//SLOTS[e]
        for i in range(NB[e]):
            out[i,0:R,:]=uk[i*R:i*R+R]; out[i,R:2*R,:]=uv[i*R:i*R+R]
        extra[8*e:8*e+8,:]=g1[e]+dot_nt(gq_s[e].astype(BF),w_qkv[e,:,0:768])
    rg.step(2,2); rg.step(3,2)
    rg.step(0,5); rg.step(1,5)
    pr=Products(pos,ebuf,lbuf,rbuf,bq,bp,wqkv,wout,win,wback,gvec,gbin)
    ec.finish()
    rg.step(2,3); rg.step(3,3)
    rg.step(0,6); rg.step(1,6)
    pr.right(0,1920)
    rg.step(2,4); rg.step(3,4)
    pr.first()
    rg.step(2,5); rg.step(3,5)
    rg.step(2,6); rg.step(3,6)
    pr.right(1920,1536)
    lc.finish()
    pr.second()

def tail_call(*a):
    S=jax.ShapeDtypeStruct; VM=pltpu.VMEM; D=pltpu.SemaphoreType.DMA
    V=pl.BlockSpec(memory_space=pltpu.VMEM); SM=pl.BlockSpec(memory_space=pltpu.SMEM); A=pl.BlockSpec(memory_space=pl.ANY)
    outs=[S((8,128),F32),S((2,128,256),BF),S((6,32,256),BF),S((2,128,768),BF),S((6,32,768),BF),S((16,768),F32),
          S((2,48,1152),F32),S((2,48,384),F32),S((2,48,1536),F32),S((2,192,384),F32),S((2,4,48),F32),S((2,2,48),F32)]
    scratch=[VM((3,512,768),BF),VM((3,1536,768),BF),VM((2,768,2304),BF),VM((2,768,768),BF),VM((2,768,3072),BF),VM((2,3072,768),BF),
      VM((4,2,2,2,16,768),BF),VM((16,768),F32),VM((256,256),F32),VM((256,256),F32),VM((2,128,768),BF),VM((2,128,768),BF),VM((224,256),F32),
      VM((2,6,128,128),F32),VM((2,8,3072),F32),VM((2,6,112,128),F32),VM((2,8,3072),F32),VM((16,32,128),F32),VM((16,160,128),BF),VM((16,112,128),BF),
      VM((32,144,128),BF),VM((32,64,128),BF),VM((2,16,3456),F32),VM((2,16,3456),BF),VM((4,2,2,2,16,3456),BF),VM((256,3456),BF),VM((256,3456),BF),VM((2,8,768),F32),VM((2,8,768),F32),
      D((14,)),D((8,)),D((8,)),D((32,)),D((32,)),D((32,)),D((32,)),D((4,17)),D((4,17))]
    return pl.pallas_call(tail_kernel,out_shape=outs,in_specs=[SM,SM]+[A]*10+[V]*8,out_specs=[V]*12,scratch_shapes=scratch,
      compiler_params=pltpu.CompilerParams(collective_id=2,has_side_effects=True,vmem_limit_bytes=62*2**20),name="tail")(*a)

def token_kernel(e,mix,u,extra,out):
    i=pl.program_id(0)
    slots=SLOTS[e]; n=256//slots
    out[...]=dot(mix[0].astype(F32).T.astype(BF),u[0])
    for j in range(n): out[j*slots:j*slots+1,:]+=extra[pl.ds(8*e+i*n+j,1),:]
def token_call(e,mix,u,extra):
    nb,r2,_=mix.shape
    return pl.pallas_call(functools.partial(token_kernel,e),grid=(nb,),out_shape=jax.ShapeDtypeStruct((nb*256,768),F32),
      in_specs=[pl.BlockSpec((1,r2,256),lambda i:(i,0,0)),pl.BlockSpec((1,r2,768),lambda i:(i,0,0)),pl.BlockSpec((16,768),lambda i:(0,0))],
      out_specs=pl.BlockSpec((256,768),lambda i:(i,0)),name="tokens")(mix,u,extra)

def small_tile(vectors, hidden_bias):
    tile = jnp.zeros((1, 16, 128), vectors.dtype)
    count, rows, width = vectors.shape
    tile = tile.at[0, : count * rows, :width].set(vectors.reshape(count * rows, width))
    return tile.at[0, count * rows : count * rows + count, : hidden_bias.shape[1]].set(hidden_bias)


def mark_tile(q_set, gold, p_set):
    me = lax.axis_index("wq") * 2 + lax.axis_index("np")
    spare = jnp.full((8 - p_set.shape[0],), -1, jnp.int32)
    columns = gold // p_set.shape[0] * 8 + gold % p_set.shape[0]
    rows = jnp.stack([q_set, columns, jnp.concatenate([p_set, spare])])
    rows = jnp.where((jnp.arange(256) // 8 == me)[None, :], jnp.tile(rows, (1, 32)), 0)
    return jnp.zeros((1, 16, 128), jnp.int32).at[0, :6].set(rows.reshape(6, 128))


COSTS={"P1":4.1,"P2":0.6,"P3":1.75,"P4":1.4}
NEEDS={"P1":0,"P2":1,"P3":2,"P4":3}
WORK=(("P1",1),("P1",0),("P2",1),("P2",0),("P3",1),("P4",1),("P3",0),("P4",0))
BLOCKS={1:6,0:2}

def make_plan(units, starts, budget, lag=1, rank=(0,1,2,3,4,5,6), spread=True, piece=4.2):
    last={}
    for (a,e,*_),s in zip(units,starts): last[(a,e)]=max(last.get((a,e),0),s+6)
    todo=[(k,e,i) for k,e in WORK for i in range(BLOCKS[e])]
    plan=[]
    ticks=max(starts)+7
    for t in range(ticks):
        steps=[]
        for u,s in sorted(((u,t-starts[u]) for u in range(len(units))),key=lambda p:(rank.index(p[1]) if 0<=p[1]<=6 else 9,p[0])):
            if 0<=s<=6: steps.append(("comm",u,s))
        runs=[]; spent=0.0
        while todo and t+1<ticks:
            k,e,i=todo[0]
            if last[(NEEDS[k],e)]+lag>t or spent+COSTS[k]*0.5>budget: break
            todo.pop(0); spent+=COSTS[k]
            if runs and runs[-1][:2]==(k,e) and (runs[-1][3]-runs[-1][2]+1)*COSTS[k]<=piece: runs[-1]=(k,e,runs[-1][2],i+1)
            else: runs.append((k,e,i,i+1))
        n=len(steps)
        cut=[(m+1)*n//(len(runs)+1) if spread else n for m in range(len(runs))]
        for m in range(n+1):
            for c,r in zip(cut,runs):
                if c==m: plan.append(r)
            if m<n: plan.append(steps[m])
        for key,when in last.items():
            if when==t: plan.append(("load",)+key)
    for k,e,i in todo:
        if plan[-1][:2]==(k,e): plan[-1]=(k,e,plan[-1][2],i+1)
        else: plan.append((k,e,i,i+1))
    return plan

def spread_small(tiles, vec, hb):
    r=lax.broadcasted_iota(jnp.int32,(128,256),0); l=lax.broadcasted_iota(jnp.int32,(128,256),1)
    r4=lax.broadcasted_iota(jnp.int32,(128,384),0); l4=lax.broadcasted_iota(jnp.int32,(128,384),1)
    vec[...]=jnp.zeros_like(vec); hb[...]=jnp.zeros_like(hb)
    for w in range(16):
        for y in range(2):
            t=tiles[w//4,(w//2)%2,(w%2)*16:(w%2)*16+16,y*128:y*128+128]
            c=min(48*w//128*128,512); off=48*w-c
            v=dot(t,jnp.where((l-off==r)&(r<48),1.0,0.0).astype(BF))
            for e in (0,1): vec[e,4*y:4*y+4,c:c+256]+=v[4*e:4*e+4]
            c=min((192*w+96*y)//128*128,3072-384); off=192*w+96*y-c
            h=dot(t,jnp.where((l4-off==r4)&(r4<96),1.0,0.0).astype(BF))
            for e in (0,1): hb[e,0:1,c:c+384]+=h[8+e:9+e]

def fused_kernel(units, plan, *refs):
    ql,pln,qx,px=refs[0:4]; ins=refs[4:10]; outs=refs[10:16]
    vec,hb,qo,po,qk,qv,pk,pv,q0,a0,p1,h0,p2,hd=refs[16:30]
    wv=refs[30:34]; small,bias,att,nrm,act,send,recv,lsem=refs[34:]
    g=Gather(units,ins,outs,send,recv)
    g.barrier()
    for ref in (q0,a0,p1,h0,p2,hd): ref[...]=jnp.zeros_like(ref)
    X=(qx,px); O=(qo,po); K=(qk,pk); V=(qv,pv); LENS=(ql,pln); SLOTS=(64,256); BASE=(0,512); NB=(2,6)
    loaded=set()
    def load_copies(a,e):
        if a==5: return []
        if a==4: return [pltpu.make_async_copy(outs[4].at[0],small,lsem.at[a,e,0])]
        rows=outs[a].shape[3]
        return [pltpu.make_async_copy(outs[a].at[e,k//2,k%2],wv[a].at[e,pl.ds(k*rows,rows)],lsem.at[a,e,k]) for k in range(8)]
    def need(a,e):
        if (a,e) in loaded: return
        loaded.add((a,e))
        for cp in load_copies(a,e): cp.wait()
        if a==4: spread_small(small,vec,hb)
    for item in plan:
        if item[0]=="comm": g.step(item[1],item[2])
        elif item[0]=="load":
            for cp in load_copies(*item[1:]): cp.start()
        else:
            kind,e,lo,hi=item
            need(4,0); need(NEEDS[kind],e)
            n=256//SLOTS[e]
            A=att.at[pl.ds(BASE[e],NB[e]*BLK)]; N=nrm.at[pl.ds(BASE[e],NB[e]*BLK)]
            arow=0 if e==1 else 0
            def body(i,kept):
                row=pl.multiple_of(i*BLK,BLK)
                if kind=="P1":
                    make_bias(bias,0,[LENS[e][i*n+j] for j in range(n)],SLOTS[e])
                    attend_block(row,X[e],wv[0].at[e],vec.at[e],bias,K[e],V[e],A,q0,e,i)
                if kind=="P2": out_block(row,X[e],A,wv[1].at[e],vec.at[e],N,a0,p1,e,i)
                if kind=="P3": up_block(row,N,wv[2].at[e],hb.at[e],act,h0,e,i,row)
                if kind=="P4": down_block(row,N,act,wv[3].at[e],vec.at[e],O[e],p2,hd,e,i,row)
                return kept
            if hi-lo==1: body(lo,0)
            else: lax.fori_loop(lo,hi,body,0)

def fused_call(ql,pln,qx,px,arrays,units,plan):
    S=jax.ShapeDtypeStruct; VM=pltpu.VMEM; D=pltpu.SemaphoreType.DMA
    V=pl.BlockSpec(memory_space=pltpu.VMEM); SM=pl.BlockSpec(memory_space=pltpu.SMEM); A=pl.BlockSpec(memory_space=pl.ANY)
    outs=[S((a.shape[0],4,2,2*a.shape[1],2*a.shape[2]),a.dtype) for a in arrays]
    outs+=[S((2,8,768),F32),S((2,1,3072),F32),S(qx.shape,BF),S(px.shape,BF),S(qx.shape,BF),S(qx.shape,BF),S(px.shape,BF),S(px.shape,BF),S((16,768),F32),S((16,768),F32),S((16,768),F32),S((16,3072),F32),S((16,768),F32),S((16,768),F32)]
    return pl.pallas_call(functools.partial(fused_kernel,units,plan),out_shape=outs,in_specs=[SM,SM,V,V]+[A]*6,out_specs=[A]*6+[V]*14,
      scratch_shapes=[VM((2,768,2304),BF),VM((2,768,768),BF),VM((2,768,3072),BF),VM((2,3072,768),BF),VM((4,2,32,256),BF),VM((256,256),F32),VM((2048,768),BF),VM((2048,768),F32),VM((1536,3072),BF),D((len(units),18)),D((len(units),18)),D((6,2,8))],
      compiler_params=pltpu.CompilerParams(collective_id=1,has_side_effects=True,vmem_limit_bytes=63*2**20),name="fused")(ql,pln,qx,px,*arrays)


GATHER_ORDER = ((4, 0), (5, 0), (0, 1), (0, 0), (1, 1), (1, 0), (2, 1), (3, 1), (2, 0), (3, 0))
GATHER_PARTS = (3, 1, 3, 3, 1, 1)


def gather_units(arrays):
    units = []
    for a, e in GATHER_ORDER:
        rows = arrays[a].shape[1] // GATHER_PARTS[a]
        for j in range(GATHER_PARTS[a]):
            units.append((a, e, "MFM"[len(units) % 3], j * rows, rows))
    return units


def kernel_shards(
    q_embed, p_embed, q_len, p_len, q_set, p_set, gold, wqkv, wout, wup, wdown, vectors, hidden_bias
):
    arrays = (
        wqkv, wout, wup, wdown, small_tile(vectors, hidden_bias), mark_tile(q_set, gold, p_set)
    )
    units = gather_units(arrays)
    plan = make_plan(units, [max(i - 1, 0) // 2 for i in range(len(units))], 8.0)
    done = fused_call(q_len, p_len, q_embed, p_embed, arrays, units, plan)
    weights = tuple(
        member.reshape(2, 16 * shard.shape[1], 2 * shard.shape[2])
        for member, shard in zip(done[:4], arrays[:4])
    )
    vec, bias, q_out, p_out, q_keys, q_values, p_keys, p_values, q0, a0, p1, h0, p2, heads = done[6:]
    loss, tq, tp, uq, up, extra, *grads = tail_call(
        q_len, p_len, q_embed, p_embed, q_keys, q_values, p_keys, p_values, *weights,
        q0, a0, p1, h0, p2, heads, done[5], vec,
    )
    grad_q, grad_p = token_call(0, tq, uq, extra), token_call(1, tp, up, extra)
    return (
        loss[0, 0], q_out, p_out, grad_q, grad_p, *grads[:5], grads[5].reshape(2, -1)
    )


def kernels_fit(q_embed, p_embed, q_len, p_len):
    return (
        lax.axis_size("wq") == 16
        and lax.axis_size("np") == 2
        and q_embed.shape == (512, 768)
        and p_embed.shape == (1536, 768)
        and q_len.shape == (8,)
        and p_len.shape == (6,)
    )


def shards(
    q_embed,
    p_embed,
    q_len,
    p_len,
    q_set,
    p_set,
    gold,
    query_key_value_weight,
    attention_output_weight,
    up_weight,
    down_weight,
    vectors,
    hidden_bias,
):
    if kernels_fit(q_embed, p_embed, q_len, p_len):
        return kernel_shards(
            q_embed,
            p_embed,
            q_len,
            p_len,
            q_set,
            p_set,
            gold,
            query_key_value_weight,
            attention_output_weight,
            up_weight,
            down_weight,
            vectors,
            hidden_bias,
        )
    gathered = gather_weights(
        query_key_value_weight,
        attention_output_weight,
        up_weight,
        down_weight,
        vectors,
        hidden_bias,
    )
    wq_size, np_size = lax.axis_size("wq"), lax.axis_size("np")
    both_axes = ("wq", "np")
    q_weights = tuple((member[0] for member in gathered))
    p_weights = tuple((member[1] for member in gathered))
    p_encoded, p_stored = encode_forward(p_embed, p_len, p_weights)
    q_encoded, q_stored = encode_forward(q_embed, q_len, q_weights)
    model_width = q_embed.shape[1]
    ff_width = gathered[2].shape[2]
    q_count = q_len.shape[0]
    p_count = p_len.shape[0]
    own_heads = jnp.concatenate([first_rows(q_encoded, q_count), first_rows(p_encoded, p_count)])
    heads = lax.all_gather(own_heads, both_axes, axis=0)
    marks = lax.all_gather(jnp.concatenate([q_set, gold, p_set]), both_axes, axis=0)
    q_heads = heads[:, :q_count].reshape(-1, model_width)
    p_heads = heads[:, q_count:].reshape(-1, model_width)
    q_sets = marks[:, :q_count].reshape(-1)
    golds = marks[:, q_count : 2 * q_count].reshape(-1)
    p_sets = marks[:, 2 * q_count :].reshape(-1)
    scaling = model_width ** (-0.5)
    similar = (
        jnp.einsum("qd,pd->qp", q_heads, p_heads, preferred_element_type=jnp.float32) * scaling
    )
    is_gold = jnp.arange(p_heads.shape[0], dtype=jnp.int32)[None, :] == golds[:, None]
    usable = (q_sets[:, None] == p_sets[None, :]) | is_gold
    masked = jnp.where(usable, similar, NEGATIVE)
    highest = jnp.max(masked, axis=1)
    total = jnp.sum(jnp.where(usable, jnp.exp(masked - highest[:, None]), 0.0), axis=1)
    log_total = highest + jnp.log(total)
    gold_score = jnp.sum(jnp.where(is_gold, similar, 0.0), axis=1)
    loss = jnp.mean(log_total - gold_score)
    soft_rows = jnp.where(usable, jnp.exp(masked - log_total[:, None]), 0.0)
    grad_similar = (soft_rows - is_gold.astype(jnp.float32)).astype(jnp.bfloat16)
    me = lax.axis_index("wq") * np_size + lax.axis_index("np")
    grad_q_first = (
        jnp.einsum(
            "qp,pd->qd",
            lax.dynamic_slice_in_dim(grad_similar, me * q_count, q_count, 0),
            p_heads,
            preferred_element_type=jnp.float32,
        )
        * scaling
    )
    grad_p_first = (
        jnp.einsum(
            "qp,qd->pd",
            lax.dynamic_slice_in_dim(grad_similar, me * p_count, p_count, 1),
            q_heads,
            preferred_element_type=jnp.float32,
        )
        * scaling
    )
    q_back = encode_backward(q_embed, q_weights, q_stored, grad_q_first)
    p_back = encode_backward(p_embed, p_weights, p_stored, grad_p_first)
    left = jnp.concatenate(
        [left_message(member[1], wq_size, np_size) for member in (q_back, p_back)], axis=2
    )
    left = left.reshape((wq_size * np_size,) + left.shape[2:])
    left = lax.all_to_all(left, both_axes, 0, 0)
    right = jnp.concatenate([right_message(member[2], np_size) for member in (q_back, p_back)], axis=1)
    right = lax.all_gather(lax.all_to_all(right, "np", 0, 0), "wq", axis=0)
    right = right.reshape((wq_size * np_size,) + right.shape[2:])
    sums = jnp.concatenate(
        [
            jnp.stack([q_back[3], p_back[3]])
            .reshape(2, np_size, -1, wq_size, model_width // wq_size)
            .transpose(3, 1, 0, 2, 4)
            .reshape(wq_size * np_size, -1),
            jnp.stack([q_back[4], p_back[4]])
            .reshape(2, wq_size * np_size, -1)
            .transpose(1, 0, 2)
            .reshape(wq_size * np_size, -1),
        ],
        axis=1,
    )
    sums = jnp.sum(lax.all_to_all(sums, both_axes, 0, 0), axis=0)
    grad_vectors = sums[: sums.shape[0] - 2 * ff_width // (wq_size * np_size)].reshape(
        2, -1, model_width // wq_size
    )
    grad_b_in = sums[sums.shape[0] - 2 * ff_width // (wq_size * np_size) :].reshape(2, -1)
    q_weight_grads = weight_grads(
        left[:, :q_count].reshape(-1, left.shape[2]),
        right[:, :q_count].reshape(-1, right.shape[2]),
        model_width,
        ff_width,
        wq_size,
        np_size,
    )
    p_weight_grads = weight_grads(
        left[:, q_count:].reshape(-1, left.shape[2]),
        right[:, q_count:].reshape(-1, right.shape[2]),
        model_width,
        ff_width,
        wq_size,
        np_size,
    )
    shared = tuple(jnp.stack(pair) for pair in zip(q_weight_grads, p_weight_grads))
    return (
        loss,
        q_encoded,
        p_encoded,
        q_back[0],
        p_back[0],
        shared[0],
        shared[1],
        shared[2],
        shared[3],
        grad_vectors,
        grad_b_in,
    )


def solution(mesh):
    return jax.shard_map(
        shards,
        mesh=mesh,
        in_specs=(
            P(("wq", "np"), None),
            P(("wq", "np"), None),
            P(("wq", "np")),
            P(("wq", "np")),
            P(("wq", "np")),
            P(("wq", "np")),
            P(("wq", "np")),
            P(None, "wq", "np"),
            P(None, "wq", "np"),
            P(None, "wq", "np"),
            P(None, "wq", "np"),
            P(None, "np", "wq"),
            P(None, ("wq", "np")),
        ),
        out_specs=(
            P(),
            P(("wq", "np"), None),
            P(("wq", "np"), None),
            P(("wq", "np"), None),
            P(("wq", "np"), None),
            P(None, "wq", "np"),
            P(None, "wq", "np"),
            P(None, "wq", "np"),
            P(None, "wq", "np"),
            P(None, "np", "wq"),
            P(None, ("wq", "np")),
        ),
        check_vma=False,
    )
```

```python
import functools
import math

import jax
import jax.numpy as jnp
from jax import lax
from jax.experimental import pallas as pl
from jax.experimental.pallas import tpu as pltpu
from jax.sharding import PartitionSpec as P


HEADS = 12


EPSILON = 1e-12
NEGATIVE = -1e30


def layer_norm(inputs, gain_row, offset):
    centred = inputs - jnp.mean(inputs, axis=-1, keepdims=True)
    spread = jnp.mean(centred * centred, axis=-1, keepdims=True)
    return centred * lax.rsqrt(spread + EPSILON) * gain_row + offset


def smooth_gate(values):
    return jax.nn.gelu(values, approximate=True)


def gather_weights(
    query_key_value_weight, attention_output_weight, up_weight, down_weight, vectors, hidden_bias
):
    np_parts = (
        lax.all_gather(query_key_value_weight, "np", axis=2, tiled=True),
        lax.all_gather(attention_output_weight, "np", axis=2, tiled=True),
        lax.all_gather(up_weight, "np", axis=2, tiled=True),
        lax.all_gather(down_weight, "np", axis=2, tiled=True),
        lax.all_gather(vectors, "np", axis=1, tiled=True),
        lax.all_gather(hidden_bias, "np", axis=1, tiled=True),
    )
    return (
        lax.all_gather(np_parts[0], "wq", axis=1, tiled=True),
        lax.all_gather(np_parts[1], "wq", axis=1, tiled=True),
        lax.all_gather(np_parts[2], "wq", axis=1, tiled=True),
        lax.all_gather(np_parts[3], "wq", axis=1, tiled=True),
        lax.all_gather(np_parts[4], "wq", axis=2, tiled=True),
        lax.all_gather(np_parts[5], "wq", axis=1, tiled=True),
    )


def head_split(matrix, seq_count):
    row_count, model_width = matrix.shape
    return matrix.reshape(seq_count, row_count // seq_count, HEADS, model_width // HEADS)


def attention_scores(queries, keys_low, lengths):
    seq_count = lengths.shape[0]
    split_q = head_split(queries, seq_count)
    scores = jnp.einsum(
        "sqhc,skhc->shqk",
        split_q,
        head_split(keys_low, seq_count),
        preferred_element_type=jnp.float32,
    )
    scores = scores * split_q.shape[3] ** (-0.5)
    live_mask = jnp.arange(split_q.shape[1])[None, :] < lengths[:, None]
    return jnp.where(live_mask[:, None, None, :], scores, NEGATIVE)


def first_rows(matrix, seq_count):
    row_count, width = matrix.shape
    return matrix.reshape(seq_count, row_count // seq_count, width)[:, 0, :]


def encode_forward(token_rows, lengths, weights):
    (
        query_key_value_weight,
        attention_output_weight,
        up_weight,
        down_weight,
        vectors,
        hidden_bias,
    ) = weights
    row_count, model_width = token_rows.shape
    seq_count = lengths.shape[0]
    vec_f32 = vectors.astype(jnp.float32)
    projected_rows = jnp.dot(token_rows, query_key_value_weight, preferred_element_type=jnp.float32)
    queries = (projected_rows[:, :model_width] + vec_f32[0]).astype(jnp.bfloat16)
    keys_low = projected_rows[:, model_width : 2 * model_width].astype(jnp.bfloat16)
    values = (projected_rows[:, 2 * model_width :] + vec_f32[1]).astype(jnp.bfloat16)
    scores = attention_scores(queries, keys_low, lengths)
    totals = jax.nn.logsumexp(scores, axis=-1, keepdims=True)
    soft_low = jnp.exp(scores - totals).astype(jnp.bfloat16)
    attended_tokens = jnp.einsum(
        "shqk,skhc->sqhc",
        soft_low,
        head_split(values, seq_count),
        preferred_element_type=jnp.float32,
    )
    attended_tokens = attended_tokens.reshape(row_count, model_width).astype(jnp.bfloat16)
    residual_branch = (
        jnp.dot(attended_tokens, attention_output_weight, preferred_element_type=jnp.float32)
        + vec_f32[2]
    )
    pre_one = token_rows.astype(jnp.float32) + residual_branch
    first_normed = layer_norm(pre_one, vec_f32[3], vec_f32[4])
    normed_low = first_normed.astype(jnp.bfloat16)
    hidden_rows = jnp.dot(
        normed_low, up_weight, preferred_element_type=jnp.float32
    ) + hidden_bias.astype(jnp.float32)
    activated_hidden = smooth_gate(hidden_rows).astype(jnp.bfloat16)
    feedforward_output = (
        jnp.dot(activated_hidden, down_weight, preferred_element_type=jnp.float32) + vec_f32[5]
    )
    pre_two = first_normed + feedforward_output
    encoded_low = layer_norm(pre_two, vec_f32[6], vec_f32[7]).astype(jnp.bfloat16)
    soft_first = jnp.exp(scores[:, :, 0, :] - totals[:, :, 0, :])
    stored = (
        first_rows(queries, seq_count),
        keys_low,
        values,
        soft_first,
        first_rows(attended_tokens, seq_count),
        first_rows(pre_one, seq_count),
        first_rows(normed_low, seq_count),
        first_rows(hidden_rows, seq_count),
        first_rows(activated_hidden, seq_count),
        first_rows(pre_two, seq_count),
    )
    return (encoded_low, stored)


def norm_back(pre, gain_row, grad_out):
    centred = pre - jnp.mean(pre, axis=-1, keepdims=True)
    inverse = lax.rsqrt(jnp.mean(centred * centred, axis=-1, keepdims=True) + EPSILON)
    scaled = grad_out * gain_row
    inner = jnp.mean(scaled * centred, axis=-1, keepdims=True)
    grad_in = inverse * (
        scaled - jnp.mean(scaled, axis=-1, keepdims=True) - centred * (inverse * inverse * inner)
    )
    return (grad_in, jnp.sum(grad_out * centred * inverse, axis=0), jnp.sum(grad_out, axis=0))


def encode_backward(token_rows, weights, stored, grad_first):
    (
        query_key_value_weight,
        attention_output_weight,
        up_weight,
        down_weight,
        vectors,
        hidden_bias,
    ) = weights
    (
        queries,
        keys_low,
        values,
        soft_first,
        attended,
        pre_one,
        normed_low,
        hidden_rows,
        activated_hidden,
        pre_two,
    ) = stored
    seq_count, model_width = queries.shape
    seq_length = token_rows.shape[0] // seq_count
    head_width = model_width // HEADS
    scaling = head_width ** (-0.5)
    vec_f32 = vectors.astype(jnp.float32)
    grad_two, gain_two, shift_two = norm_back(pre_two, vec_f32[6], grad_first)
    grad_ffn = grad_two.astype(jnp.bfloat16)
    grad_activated = jnp.einsum(
        "rd,fd->rf", grad_ffn, down_weight, preferred_element_type=jnp.float32
    )
    grad_hidden = jax.vjp(smooth_gate, hidden_rows)[1](grad_activated)[0].astype(jnp.bfloat16)
    grad_normed = grad_two + jnp.einsum(
        "rf,df->rd", grad_hidden, up_weight, preferred_element_type=jnp.float32
    )
    grad_one, gain_one, shift_one = norm_back(pre_one, vec_f32[3], grad_normed)
    grad_branch = grad_one.astype(jnp.bfloat16)
    grad_attended = jnp.einsum(
        "re,de->rd", grad_branch, attention_output_weight, preferred_element_type=jnp.float32
    ).astype(jnp.bfloat16)
    grad_heads = grad_attended.reshape(seq_count, HEADS, head_width)
    grad_soft = jnp.einsum(
        "shc,skhc->shk",
        grad_heads,
        head_split(values, seq_count),
        preferred_element_type=jnp.float32,
    )
    row_inner = jnp.sum(soft_first * grad_soft, axis=-1, keepdims=True)
    grad_scores = (soft_first * (grad_soft - row_inner)).astype(jnp.bfloat16)
    soft_low = soft_first.astype(jnp.bfloat16)
    grad_queries = (
        jnp.einsum(
            "shk,skhc->shc",
            grad_scores,
            head_split(keys_low, seq_count),
            preferred_element_type=jnp.float32,
        )
        * scaling
    )
    grad_q_low = grad_queries.reshape(seq_count, model_width).astype(jnp.bfloat16)
    tokens = token_rows.reshape(seq_count, seq_length, model_width)
    both = jnp.concatenate([grad_scores, soft_low], axis=1)
    mixed = jnp.einsum("sgk,skd->sgd", both, tokens, preferred_element_type=jnp.float32).astype(
        jnp.bfloat16
    )
    scaled_queries = (queries.astype(jnp.float32) * scaling).astype(jnp.bfloat16)
    split_weight = query_key_value_weight.reshape(model_width, 3, HEADS, head_width)
    back_rows = jnp.concatenate(
        [
            jnp.einsum(
                "shc,dhc->shd",
                scaled_queries.reshape(seq_count, HEADS, head_width),
                split_weight[:, 1],
                preferred_element_type=jnp.float32,
            ),
            jnp.einsum(
                "shc,dhc->shd",
                grad_heads,
                split_weight[:, 2],
                preferred_element_type=jnp.float32,
            ),
        ],
        axis=1,
    ).astype(jnp.bfloat16)
    grad_tokens = jnp.einsum("sgk,sgd->skd", both, back_rows, preferred_element_type=jnp.float32)
    first_extra = grad_one + jnp.einsum(
        "se,de->sd",
        grad_q_low,
        query_key_value_weight[:, :model_width],
        preferred_element_type=jnp.float32,
    )
    is_first = (jnp.arange(seq_length) == 0)[None, :, None]
    grad_tokens = grad_tokens + jnp.where(is_first, first_extra[:, None, :], 0.0)
    soft_total = jnp.sum(soft_low.astype(jnp.float32), axis=-1, keepdims=True)
    vector_parts = jnp.stack(
        [
            jnp.sum(grad_q_low.astype(jnp.float32), axis=0),
            jnp.sum(grad_heads.astype(jnp.float32) * soft_total, axis=0).reshape(model_width),
            jnp.sum(grad_branch.astype(jnp.float32), axis=0),
            gain_one,
            shift_one,
            jnp.sum(grad_ffn.astype(jnp.float32), axis=0),
            gain_two,
            shift_two,
        ]
    )
    bias_part = jnp.sum(grad_hidden.astype(jnp.float32), axis=0)
    left = (
        activated_hidden,
        normed_low,
        attended,
        jnp.concatenate(
            [jnp.broadcast_to(tokens[:, :1, :], (seq_count, HEADS, model_width)), mixed], axis=1
        ),
    )
    right = (
        grad_ffn,
        grad_hidden,
        grad_branch,
        jnp.concatenate([grad_q_low, scaled_queries, grad_attended], axis=1),
    )
    return (
        grad_tokens.reshape(token_rows.shape),
        left,
        right,
        vector_parts,
        bias_part,
    )


def left_message(left, wq_size, np_size):
    activated, normed, attended, mixed = left
    rows, groups, model_width = mixed.shape
    part = model_width // wq_size
    columns = 3 * model_width // np_size
    head_width = model_width // HEADS
    group = math.gcd(head_width, columns)
    mixed = jnp.repeat(mixed, head_width // group, axis=1)
    mixed = mixed.reshape(rows, np_size, columns // group, wq_size, part)
    mixed = mixed.transpose(3, 1, 0, 2, 4).reshape(wq_size, np_size, rows, columns // group * part)

    def same(matrix):
        pieces = matrix.reshape(rows, wq_size, -1).transpose(1, 0, 2)
        return jnp.broadcast_to(pieces[:, None], (wq_size, np_size) + pieces.shape[1:])

    return jnp.concatenate([same(activated), same(normed), same(attended), mixed], axis=3)


def right_message(right, np_size):
    rows = right[0].shape[0]
    return jnp.concatenate(
        [member.reshape(rows, np_size, -1).transpose(1, 0, 2) for member in right], axis=2
    )


def weight_grads(left, right, model_width, ff_width, wq_size, np_size):
    rows = left.shape[0]
    part, ff_part = model_width // wq_size, ff_width // wq_size
    columns = 3 * model_width // np_size
    group = math.gcd(model_width // HEADS, columns)
    right_sizes = (model_width // np_size, ff_width // np_size, model_width // np_size)
    cut = [ff_part, ff_part + part, ff_part + 2 * part]
    activated, normed, attended, mixed = jnp.split(left, cut, axis=1)
    cut = [right_sizes[0], right_sizes[0] + right_sizes[1], sum(right_sizes)]
    grad_ffn, grad_hidden, grad_branch, grad_projected = jnp.split(right, cut, axis=1)

    def outer(one, two):
        return jnp.einsum("sd,se->de", one, two, preferred_element_type=jnp.float32)

    w_qkv = jnp.einsum(
        "sgd,sgc->dgc",
        mixed.reshape(rows, columns // group, part),
        grad_projected.reshape(rows, columns // group, group),
        preferred_element_type=jnp.float32,
    ).reshape(part, columns)
    return (
        w_qkv,
        outer(attended, grad_branch),
        outer(normed, grad_hidden),
        outer(activated, grad_ffn),
    )


BLK=256
F32=jnp.float32; BF=jnp.bfloat16
NEG=-1e30; EPS=1e-12
def dot(a,b): return jnp.dot(a,b,preferred_element_type=F32)
def norm(u,g,b):
    c=u-jnp.mean(u,axis=-1,keepdims=True)
    s=jnp.mean(c*c,axis=-1,keepdims=True)
    return c*lax.rsqrt(s+EPS)*g+b
def put_first(ref, e, i, cols, v):
    if e==1:
        ref[pl.ds(8+i,1),cols]=v[0:1]
    else:
        for j in range(4): ref[pl.ds(4*i+j,1),cols]=v[64*j:64*j+1]
def make_bias(bias_ref, slot, lens, slots):
    n=BLK//slots
    key=lax.broadcasted_iota(jnp.int32,(BLK,BLK),0)
    qry=lax.broadcasted_iota(jnp.int32,(BLK,BLK),1)
    ok=key<lens[0]
    if n>1:
        ok=ok&(qry<slots)
        for j in range(1,n):
            ok=ok|((key>=j*slots)&(key<j*slots+lens[j])&(qry>=j*slots)&(qry<(j+1)*slots))
    bias_ref[...]=jnp.where(ok,0.0,NEG)
def attend_block(row, x_ref, wqkv, vec, bias_ref, k_ref, v_ref, att_ref, q0_ref, e, i):
    x=x_ref[pl.ds(row,BLK),:]
    for g in range(3):
        cs=pl.ds(g*256,256)
        q4=dot(x,wqkv[:,g*256:g*256+256])+vec[0:1,g*256:g*256+256]
        q4=q4.astype(BF)
        k4=dot(x,wqkv[:,768+g*256:768+g*256+256]).astype(BF)
        v4=(dot(x,wqkv[:,1536+g*256:1536+g*256+256])+vec[1:2,g*256:g*256+256]).astype(BF)
        k_ref[pl.ds(row,BLK),cs]=k4
        v_ref[pl.ds(row,BLK),cs]=v4
        put_first(q0_ref,e,i,slice(g*256,g*256+256),q4.astype(F32))
        qT=(q4.astype(F32)*0.125).T.astype(BF)
        vT=v4.astype(F32).T.astype(BF)
        lane=lax.broadcasted_iota(jnp.int32,(BLK,256),1)
        outs=[]
        for h in range(4):
            kh=jnp.where((lane>=64*h)&(lane<64*h+64),k4,jnp.zeros_like(k4))
            s=dot(kh,qT)+bias_ref[...]
            m=jnp.max(s,axis=0,keepdims=True)
            p=jnp.exp(s-m)
            l=jnp.sum(p,axis=0,keepdims=True)
            o=dot(vT[64*h:64*h+64,:],p.astype(BF))
            outs.append(o*(1.0/l))
        oT=jnp.concatenate(outs,axis=0)
        att_ref[pl.ds(row,BLK),cs]=oT.T.astype(BF)
def out_block(row, x_ref, att_ref, wo, vec, n_ref, a0_ref, p1_ref, e, i):
    att=att_ref[pl.ds(row,BLK),:]
    put_first(a0_ref,e,i,slice(None),att.astype(F32))
    pre=x_ref[pl.ds(row,BLK),:].astype(F32)+dot(att,wo[...])+vec[2:3,:]
    put_first(p1_ref,e,i,slice(None),pre)
    n_ref[pl.ds(row,BLK),:]=norm(pre,vec[3:4,:],vec[4:5,:])
def gelu(u):
    return 0.5*u*(1.0+jnp.tanh(0.7978845608028654*(u+0.044715*(u*u*u))))
def up_block(row, n_ref, wup, hb, act_ref, h0_ref, e, i, arow):
    nl=n_ref[pl.ds(row,BLK),:].astype(BF)
    for t in range(12):
        cs=slice(t*256,t*256+256)
        h=dot(nl,wup[:,cs])+hb[0:1,cs]
        put_first(h0_ref,e,i,cs,h)
        act_ref[pl.ds(arow,BLK),cs]=gelu(h).astype(BF)
def down_block(row, n_ref, act_ref, wdown, vec, o_ref, p2_ref, hd_ref, e, i, arow):
    f=dot(act_ref[pl.ds(arow,BLK),:],wdown[...])+vec[5:6,:]
    pre=n_ref[pl.ds(row,BLK),:]+f
    put_first(p2_ref,e,i,slice(None),pre)
    enc=norm(pre,vec[6:7,:],vec[7:8,:])
    put_first(hd_ref,e,i,slice(None),enc)
    o_ref[pl.ds(row,BLK),:]=enc.astype(BF)

def dot_nt(a,b): return lax.dot_general(a,b,(((1,),(1,)),((),())),preferred_element_type=F32)
def gelu_slope(u):
    t=jnp.tanh(0.7978845608028654*(u+0.044715*(u*u*u)))
    return 0.5*(1.0+t)+0.5*u*(1.0-t*t)*(0.7978845608028654*(1.0+0.134145*(u*u)))
def norm_grad(u,g,gy):
    c=u-jnp.mean(u,axis=-1,keepdims=True)
    r=lax.rsqrt(jnp.mean(c*c,axis=-1,keepdims=True)+EPS)
    t=gy*g
    gu=r*(t-jnp.mean(t,axis=-1,keepdims=True)-c*(r*r)*jnp.mean(t*c,axis=-1,keepdims=True))
    return gu, jnp.sum(gy*c*r,axis=0,keepdims=True), jnp.sum(gy,axis=0,keepdims=True)
def heads_apart(rows, count):
    n=rows.shape[0]
    wide=jnp.concatenate([jnp.broadcast_to(rows[i:i+1],(16,768)) for i in range(n)],axis=0)
    r=lax.broadcasted_iota(jnp.int32,wide.shape,0)%16
    l=lax.broadcasted_iota(jnp.int32,wide.shape,1)//64
    return jnp.where(r==l,wide,0.0)
def pick_matrix(off, lane0):
    r=lax.broadcasted_iota(jnp.int32,(256,128),0); l=lax.broadcasted_iota(jnp.int32,(256,128),1)
    return jnp.where((r-off==l-lane0)&(l>=lane0)&(l<lane0+48),1.0,0.0).astype(BF)
MESH = pl.DeviceIdType.MESH

class Gather:
    def __init__(self, units, ins, outs, send, recv):
        self.units, self.ins, self.outs, self.send, self.recv = units, ins, outs, send, recv
        w, self.y = lax.axis_index("wq"), lax.axis_index("np")
        self.w = w
        self.z, self.x, self.c = w // 4, (w // 2) % 2, w % 2
        self.pending = {}
    def dev(self, dz=0, fx=False, fy=False, fc=False):
        x = 1 - self.x if fx else self.x
        c = 1 - self.c if fc else self.c
        y = 1 - self.y if fy else self.y
        return ((self.z + dz) * 4 + x * 2 + c, y)
    def barrier(self):
        bar = pltpu.get_barrier_semaphore()
        def sig(**k): pl.semaphore_signal(bar, inc=1, device_id=self.dev(**k), device_id_type=MESH)
        sig(fx=True); sig(fy=True); sig(fc=True)
        @pl.when(self.z > 0)
        def _(): sig(dz=-1)
        @pl.when(self.z < 3)
        def _(): sig(dz=1)
        pl.semaphore_wait(bar, 3 + (self.z + 3) // 4 + (6 - self.z) // 4)
    def view(self, u, z=None, x=None, y=None, c=None):
        a, e, kind, r0, rn = self.units[u]
        o = self.outs[a]
        r, w = self.ins[a].shape[1:]
        zs = slice(None) if z is None else z
        xs = slice(None) if x is None else x
        cs = slice(None) if y is None else pl.ds(pl.multiple_of(y * w, 128), w)
        return o.at[e, zs, xs, pl.ds(pl.multiple_of((self.c if c is None else c) * r + r0, 16), rn), cs]
    def copy(self, u, sem, src, dst, dev):
        return pltpu.make_async_remote_copy(src_ref=src, dst_ref=dst, send_sem=self.send.at[u, sem], recv_sem=self.recv.at[u, sem], device_id=dev, device_id_type=MESH)
    def own_src(self, u):
        a, e, kind, r0, rn = self.units[u]
        return self.ins[a].at[e, pl.ds(r0, rn)]
    def zview(self, u, core, z):
        kind = self.units[u][2]
        if not kind: return self.view(u, z=z, x=self.x, y=self.y)
        if core == 0: return self.view(u, z=z, x=None, y=self.y)
        return self.view(u, z=z, x=self.x, y=None)
    def step(self, u, s):
        for core in (0, 1):
            pl.when(self.c == core)(lambda core=core: self._step(u, s, core))
    def A(self, core): return dict(fx=True) if core == 0 else dict(fy=True)
    def B(self, core): return dict(fy=True) if core == 0 else dict(fx=True)
    def a_src(self, u, core):
        kind = self.units[u][2]
        z = None if not kind else self.z
        return self.view(u, z=z, x=self.x, y=self.y)
    def a_got(self, u, core):
        kind = self.units[u][2]
        z = None if not kind else self.z
        return self.view(u, z=z, x=1 - self.x, y=self.y) if core == 0 else self.view(u, z=z, x=self.x, y=1 - self.y)
    def b_src(self, u, core):
        return self.view(u, x=None, y=self.y) if core == 0 else self.view(u, x=self.x, y=None)
    def b_got(self, u, core):
        return self.view(u, x=None, y=1 - self.y) if core == 0 else self.view(u, x=1 - self.x, y=None)
    def local(self, u, sem, ref):
        self.copy(u, sem, ref, ref, self.dev(fc=True)).start()
    def z_send(self, u, core, hop):
        z = self.z
        @pl.when((z - hop >= 0) & (z + 1 <= 3))
        def _():
            v = self.zview(u, core, z - hop)
            src = self.own_src(u) if (hop == 0 and not self.units[u][2]) else v
            self.copy(u, 2 + hop, src, v, self.dev(dz=1)).start()
        @pl.when((z + hop <= 3) & (z - 1 >= 0))
        def _():
            v = self.zview(u, core, z + hop)
            src = self.own_src(u) if (hop == 0 and not self.units[u][2]) else v
            self.copy(u, 5 + hop, src, v, self.dev(dz=-1)).start()
    def z_wait(self, u, core, hop):
        z = self.z
        @pl.when(z - 1 - hop >= 0)
        def _():
            v = self.zview(u, core, z - 1 - hop)
            self.copy(u, 2 + hop, v, v, self.dev(fc=True)).wait_recv()
            self.local(u, 11 + hop, v)
        @pl.when(z + 1 + hop <= 3)
        def _():
            v = self.zview(u, core, z + 1 + hop)
            self.copy(u, 5 + hop, v, v, self.dev(fc=True)).wait_recv()
            self.local(u, 14 + hop, v)
    def _step(self, u, s, core):
        F = not self.units[u][2]
        own = self.view(u, z=self.z, x=self.x, y=self.y)
        if s == 0:
            src = self.own_src(u)
            self.copy(u, 8, src, own, self.dev(fc=True)).start()
            pltpu.make_async_copy(src, own, self.send.at[u, 17]).start()
            if F:
                self.z_send(u, core, 0)
            else:
                self.copy(u, 0, src, own, self.dev(**self.A(core))).start()
        if s == 1:
            pltpu.make_async_copy(self.own_src(u), own, self.send.at[u, 17]).wait()
            if F:
                self.z_wait(u, core, 0); self.z_send(u, core, 1)
            else:
                g = self.a_got(u, core)
                self.copy(u, 0, g, g, self.dev(fc=True)).wait_recv()
                self.z_send(u, core, 0)
                self.local(u, 9, g)
        if s == 2:
            if F: self.z_wait(u, core, 1); self.z_send(u, core, 2)
            else: self.z_wait(u, core, 0); self.z_send(u, core, 1)
        if s == 3:
            if F:
                self.z_wait(u, core, 2)
                v = self.a_src(u, core)
                self.copy(u, 0, v, v, self.dev(**self.A(core))).start()
            else:
                self.z_wait(u, core, 1); self.z_send(u, core, 2)
        if s == 4:
            if F:
                g = self.a_got(u, core)
                self.copy(u, 0, g, g, self.dev(fc=True)).wait_recv()
            else:
                self.z_wait(u, core, 2)
            v = self.b_src(u, core)
            self.copy(u, 1, v, v, self.dev(**self.B(core))).start()
            if F: self.local(u, 9, g)
        if s == 5:
            g = self.b_got(u, core)
            self.copy(u, 1, g, g, self.dev(fc=True)).wait_recv()
            self.local(u, 10, g)
        if s == 6:
            self.finish_recv(u, core); self.finish_send(u, core)
    def finish_recv(self, u, core):
        other = 1 - core
        c = 1 - self.c
        kind = self.units[u][2]
        def got(sem, v): self.copy(u, sem, v, v, self.dev(fc=True)).wait_recv()
        sv = lambda **k: self.view(u, c=c, **k)
        got(8, sv(z=self.z, x=self.x, y=self.y))
        za = None if not kind else self.z
        got(9, sv(z=za, x=1 - self.x, y=self.y) if other == 0 else sv(z=za, x=self.x, y=1 - self.y))
        got(10, sv(x=None, y=1 - self.y) if other == 0 else sv(x=1 - self.x, y=None))
        def zv(z):
            if not kind: return sv(z=z, x=self.x, y=self.y)
            return sv(z=z, x=None, y=self.y) if other == 0 else sv(z=z, x=self.x, y=None)
        for hop in range(3):
            pl.when(self.z - 1 - hop >= 0)(lambda hop=hop: got(11 + hop, zv(self.z - 1 - hop)))
            pl.when(self.z + 1 + hop <= 3)(lambda hop=hop: got(14 + hop, zv(self.z + 1 + hop)))
    def finish_send(self, u, core):
        def sent(sem, v): self.copy(u, sem, v, v, self.dev(fc=True)).wait_send()
        own = self.view(u, z=self.z, x=self.x, y=self.y)
        sent(8, own)
        sent(0, self.a_src(u, core)); sent(1, self.b_src(u, core))
        sent(9, self.a_got(u, core)); sent(10, self.b_got(u, core))
        z = self.z
        for hop in range(3):
            pl.when((z - hop >= 0) & (z + 1 <= 3))(lambda hop=hop: sent(2 + hop, self.zview(u, core, z - hop)))
            pl.when((z + hop <= 3) & (z - 1 >= 0))(lambda hop=hop: sent(5 + hop, self.zview(u, core, z + hop)))
            pl.when(z - 1 - hop >= 0)(lambda hop=hop: sent(11 + hop, self.zview(u, core, z - 1 - hop)))
            pl.when(z + 1 + hop <= 3)(lambda hop=hop: sent(14 + hop, self.zview(u, core, z + 1 + hop)))

class Place:
    def __init__(self):
        self.w=lax.axis_index("wq"); self.y=lax.axis_index("np")
        self.z,self.x,self.c=self.w//4,(self.w//2)%2,self.w%2
        self.me=self.w*2+self.y
    def dev(self, z=None, fx=False, fy=False, fc=False):
        x=1-self.x if fx else self.x
        c=1-self.c if fc else self.c
        y=1-self.y if fy else self.y
        return ((self.z if z is None else z)*4+x*2+c, y)

class HeadGather:
    def __init__(self,pos,buf,send,recv):
        self.pos,self.buf,self.send,self.recv=pos,buf,send,recv
    def rc(self,sem,ref,dev):
        return pltpu.make_async_remote_copy(src_ref=ref,dst_ref=ref,send_sem=self.send.at[sem],recv_sem=self.recv.at[sem],device_id=dev,device_id_type=MESH)
    def phase(self,s):
        pos,buf=self.pos,self.buf
        z,x,c,y=pos.z,pos.x,pos.c,pos.y
        sib=pos.dev(fc=True)
        def arrived(sem,ref): self.rc(sem,ref,sib).wait_recv()
        own=buf.at[z,x,c,y]
        col=lambda fx,fy,core: buf.at[:,1-x if fx else x,core,1-y if fy else y]
        ways=((3,True,True),(4,True,False),(5,False,True))
        if s==0:
            for k in (1,2,3): self.rc(k-1,own,pos.dev(z=(z+k)%4)).start()
        if s==1:
            for k in (1,2,3): arrived(k-1,buf.at[(z+4-k)%4,x,c,y])
            for sem,fx,fy in ways: self.rc(sem,col(False,False,c),pos.dev(fx=fx,fy=fy)).start()
            self.rc(6,col(False,False,c),sib).start()
        if s==2:
            for sem,fx,fy in ways[1:]+ways[:1]:
                arrived(sem,col(fx,fy,c)); self.rc(sem+4,col(fx,fy,c),sib).start()
        if s==3:
            o=1-c
            arrived(6,col(False,False,o))
            for sem,fx,fy in ways: arrived(sem+4,col(fx,fy,o))
            for k in (1,2,3): self.rc(k-1,own,sib).wait_send()
            for sem in (3,4,5,6): self.rc(sem,col(False,False,c),sib).wait_send()
            for sem,fx,fy in ways: self.rc(sem+4,col(fx,fy,c),sib).wait_send()

CHUNKS=((0,1152,False),(1152,512,False),(1664,256,True),(1920,768,False),(2688,384,True))
class RightGather:
    def __init__(self,pos,src,buf,send,recv):
        self.pos,self.src,self.buf,self.send,self.recv=pos,src,buf,send,recv
    def rc(self,ch,sem,src,dst,dev):
        return pltpu.make_async_remote_copy(src_ref=src,dst_ref=dst,send_sem=self.send.at[ch,sem],recv_sem=self.recv.at[ch,sem],device_id=dev,device_id_type=MESH)
    def view(self,ch,z=None,x=None,c=None,y=None):
        p=self.pos; c0,w,_=CHUNKS[ch]
        f=lambda v: slice(None) if v is None else v
        return self.buf.at[f(z),p.x if x is None else x,p.c if c is None else c,f(y),:,c0:c0+w]
    def half(self,ch,y):
        c0,w,_=CHUNKS[ch]
        return self.src.at[y,:,c0:c0+w]
    def column(self,ch,z,c=None):
        p=self.pos; c0,w,x_first=CHUNKS[ch]
        return self.buf.at[z,slice(None) if x_first else p.x,p.c if c is None else c,:,:,c0:c0+w]
    def across(self,ch,x,c=None):
        p=self.pos
        return self.view(ch,z=p.z if CHUNKS[ch][2] else None,x=x,c=c)
    def step(self,ch,s):
        p=self.pos; z,y=p.z,p.y; x_first=CHUNKS[ch][2]
        sib=p.dev(fc=True)
        def arrived(sem,v): self.rc(ch,sem,v,v,sib).wait_recv()
        def local(sem,v): self.rc(ch,sem,v,v,sib).start()
        def z_send(hop):
            @pl.when((z-hop>=0)&(z+1<=3))
            def _():
                v=self.column(ch,z-hop); self.rc(ch,2+hop,v,v,p.dev(z=z+1)).start()
            @pl.when((z+hop<=3)&(z-1>=0))
            def _():
                v=self.column(ch,z+hop); self.rc(ch,5+hop,v,v,p.dev(z=z-1)).start()
        def z_wait(hop):
            @pl.when(z-1-hop>=0)
            def _():
                v=self.column(ch,z-1-hop); arrived(2+hop,v); local(9+hop,v)
            @pl.when(z+1+hop<=3)
            def _():
                v=self.column(ch,z+1+hop); arrived(5+hop,v); local(12+hop,v)
        def x_send():
            v=self.across(ch,p.x); self.rc(ch,1,v,v,p.dev(fx=True)).start()
        def x_wait():
            g=self.across(ch,1-p.x); arrived(1,g); local(15,g)
        own=self.view(ch,z=z,y=y)
        if s==0:
            self.rc(ch,0,self.half(ch,1-y),own,p.dev(fy=True)).start()
            pltpu.make_async_copy(self.half(ch,y),own,self.send.at[ch,16]).start()
        if s==1:
            pltpu.make_async_copy(self.half(ch,y),own,self.send.at[ch,16]).wait()
            arrived(0,self.view(ch,z=z,y=1-y))
            if x_first: x_send()
            else: z_send(0)
            local(8,self.view(ch,z=z))
        if x_first:
            if s==2: x_wait(); z_send(0)
            if s==3: z_wait(0); z_send(1)
            if s==4: z_wait(1); z_send(2)
            if s==5: z_wait(2)
        else:
            if s==2: z_wait(0); z_send(1)
            if s==3: z_wait(1); z_send(2)
            if s==4: z_wait(2); x_send()
            if s==5: x_wait()
        if s==6:
            o=1-p.c
            arrived(8,self.view(ch,z=z,c=o)); arrived(15,self.across(ch,1-p.x,c=o))
            def sent(sem,v): self.rc(ch,sem,v,v,sib).wait_send()
            sent(0,own); sent(1,self.across(ch,p.x)); sent(8,self.view(ch,z=z)); sent(15,self.across(ch,1-p.x))
            for hop in range(3):
                pl.when(z-1-hop>=0)(lambda hop=hop: arrived(9+hop,self.column(ch,z-1-hop,c=o)))
                pl.when(z+1+hop<=3)(lambda hop=hop: arrived(12+hop,self.column(ch,z+1+hop,c=o)))
                pl.when((z-hop>=0)&(z+1<=3))(lambda hop=hop: sent(2+hop,self.column(ch,z-hop)))
                pl.when((z+hop<=3)&(z-1>=0))(lambda hop=hop: sent(5+hop,self.column(ch,z+hop)))
                pl.when(z-1-hop>=0)(lambda hop=hop: sent(9+hop,self.column(ch,z-1-hop)))
                pl.when(z+1+hop<=3)(lambda hop=hop: sent(12+hop,self.column(ch,z+1+hop)))

class LeftCopies:
    def __init__(self,pos,left,buf,spans,send,recv):
        self.pos,self.left,self.buf,self.spans,self.send,self.recv=pos,left,buf,spans,send,recv
    def each(self,d,go):
        t=(self.pos.me+d)%32
        w,y=t//2,t%2
        for half,(r0,n) in enumerate(self.spans):
            @pl.when(y==half)
            def _():
                go(pltpu.make_async_remote_copy(src_ref=self.left.at[w,pl.ds(r0,n)],dst_ref=self.buf.at[self.pos.me,pl.ds(0,n)],send_sem=self.send.at[d],recv_sem=self.recv.at[d],device_id=(w,y),device_id_type=MESH))
    def start(self,batch):
        def lap(k,kept):
            self.each(4*k+batch,lambda cp: cp.start()); return kept
        lax.fori_loop(0 if batch else 1,8,lap,0)
        if batch: return
        for half,(r0,n) in enumerate(self.spans):
            @pl.when(self.pos.y==half)
            def _(): self.buf[self.pos.me,0:n,:]=self.left[self.pos.w,r0:r0+n,:]
    def finish(self):
        def lap(d,kept):
            self.each(d,lambda cp: cp.wait_send())
            s=(self.pos.me+32-d)%32
            for half,(r0,n) in enumerate(self.spans):
                @pl.when(self.pos.y==half)
                def _():
                    v=self.buf.at[s,pl.ds(0,n)]
                    pltpu.make_async_remote_copy(src_ref=v,dst_ref=v,send_sem=self.send.at[d],recv_sem=self.recv.at[d],device_id=(self.pos.w,self.pos.y),device_id_type=MESH).wait_recv()
            return kept
        lax.fori_loop(1,32,lap,0)

def similarity(pos,buf,marks,loss,gr,gs_s,gt_s):
    g=buf[...].reshape(32,16,768).astype(F32)
    q=g[:,0:8].reshape(256,768).astype(BF); p=g[:,8:16].reshape(256,768).astype(BF)
    m=jnp.sum(marks[...].reshape(8,32,256),axis=0)
    m=m[0:16]+m[16:32]
    m=(m[:,0:128]+m[:,128:256]).astype(F32)
    row=lambda r: jnp.broadcast_to(jnp.concatenate([m[r:r+1],m[r+1:r+2]],axis=1),(256,256))
    qset=row(0).T; gold=row(2).T; pset=row(4)
    lane=lax.broadcasted_iota(jnp.int32,(256,256),1).astype(F32)
    is_gold=gold==lane
    usable=(qset==pset)|is_gold
    sim=dot_nt(q,p)*(768**-0.5)
    masked=jnp.where(usable,sim,NEG)
    high=jnp.max(masked,axis=1,keepdims=True)
    tot=high+jnp.log(jnp.sum(jnp.where(usable,jnp.exp(masked-high),0.0),axis=1,keepdims=True))
    gsc=jnp.sum(jnp.where(is_gold,sim,0.0),axis=1,keepdims=True)
    loss[0,0]=jnp.sum(tot-gsc)*(1.0/256)
    soft=jnp.where(usable,jnp.exp(masked-tot),0.0)
    gsim=soft-jnp.where(is_gold,1.0,0.0)
    gs_s[...]=gsim; gt_s[...]=gsim.T
    me8=pl.ds(pl.multiple_of(pos.me*8,8),8)
    gr[0:8,:]=dot(gs_s[me8,:].astype(BF),p)*(768**-0.5)
    gr[8:16,:]=dot(gt_s[me8,:].astype(BF),q)*(768**-0.5)

EARLY=((0,16),(0,112)); LATE=((0,64),(48,64))
SLOTS=(64,256); NB=(2,6)
def window(s):
    w=min(48*s//128*128,128)
    return w,48*s-w
def two(ref,e,w): return jnp.concatenate([ref[e,w//128],ref[e,w//128+1]],axis=1)
def select_rows(ref,s):
    w,off=window(s)
    cat=lambda e: jnp.concatenate([two(ref,e,w),two(ref,e,w+384)],axis=0).astype(BF)
    m=dot(cat(0),pick_matrix(off,0))+dot(cat(1),pick_matrix(off,64))
    n=ref.shape[2]
    return m[0:n],m[n:2*n]
def select_wide(ref,s):
    w,off=window(s)
    cat=lambda e: jnp.concatenate([ref[e,:,384*m+w:384*m+w+256] for m in range(8)],axis=0).astype(BF)
    m=dot(cat(0),pick_matrix(off,0))+dot(cat(1),pick_matrix(off,64))
    return [m[8*k:8*k+8] for k in range(8)]
def early_messages(ls,left):
    for s in range(8):
        for k,r in enumerate(select_rows(ls,s)): left[s+8*k]=r.astype(BF)
def late_messages(ll,lb,stage,left):
    for j in range(16): stage[j,0:8,:]=jnp.zeros((8,128),F32)
    for s in range(8):
        for m,r in enumerate(select_wide(lb,s)):
            n=8*m+s
            stage[n//4,n%4:n%4+1,:]=r[0:1]
    for s in range(8):
        for k,r in enumerate(select_rows(ll,s)):
            j=s+8*k
            left[j,0:48,:]=r[0:48].astype(BF); left[j,64:112,:]=r[48:96].astype(BF)
            left[j,48:64,:]=jnp.concatenate([r[96:104],stage[j,0:8]],axis=0).astype(BF)

def early_block(e,i,lens,K,X,qa_s,P_s,ls):
    slots=SLOTS[e]; n=256//slots; R=16*n; row=i*256; pr=(96 if e==0 else 0)+i*R
    k=K[row:row+256,:]; x=X[row:row+256,:]
    s=dot_nt(qa_s[e,i*R:i*R+R,:],k)
    key=lax.broadcasted_iota(jnp.int32,(R,256),1)
    if n==1: ok=key<lens[i]
    else:
        grp=lax.broadcasted_iota(jnp.int32,(R,256),0)//16
        ok=(grp<0)
        for j in range(n): ok=ok|((grp==j)&(key>=j*slots)&(key<j*slots+lens[i*n+j]))
    s=jnp.where(ok,s,NEG)
    p=jnp.exp(s-jnp.max(s,axis=1,keepdims=True))
    p=p*(1.0/jnp.sum(p,axis=1,keepdims=True))
    P_s[pr:pr+R,:]=p
    mix=dot(p.astype(BF),x)
    for j in range(n):
        slot=i*n+j
        first=x[j*slots:j*slots+1].astype(F32)
        for c in range(6):
            cc=slice(128*c,128*c+128)
            ls[e,c,pl.ds(16+slot,12,stride=8),:]=mix[16*j:16*j+12,cc]
            ls[e,c,slot:slot+1,:]=first[:,cc]
def late_block(e,i,K,V,X,ga_s,P_s,ll,gq_s,sv_s,tmix):
    slots=SLOTS[e]; n=256//slots; R=16*n; row=i*256; pr=(96 if e==0 else 0)+i*R
    gab=ga_s[e,i*R:i*R+R,:]
    p=P_s[pr:pr+R,:]
    gs=dot_nt(gab,V[row:row+256,:])
    gs=p*(gs-jnp.sum(p*gs,axis=1,keepdims=True))
    gsb=gs.astype(BF); pb=p.astype(BF)
    tmix[i,0:R,:]=gsb; tmix[i,R:2*R,:]=pb
    gq=dot(gsb,K[row:row+256,:])
    r0=lax.broadcasted_iota(jnp.int32,(R,768),0); hl=lax.broadcasted_iota(jnp.int32,(R,768),1)//64
    gq=jnp.where(r0%16==hl,gq,0.0)*0.125
    st=jnp.sum(pb.astype(F32),axis=1,keepdims=True)
    sv_s[e]=sv_s[e]+jnp.sum(st*gab.astype(F32),axis=0,keepdims=True)
    mix=dot(gsb,X[row:row+256,:])
    for j in range(n):
        slot=i*n+j
        gq_s[e,slot:slot+1,:]=jnp.sum(gq[16*j:16*j+16],axis=0,keepdims=True)
        for c in range(6): ll[e,c,pl.ds(slot,12,stride=8),:]=mix[16*j:16*j+12,128*c:128*c+128]

def colsum(m): return jnp.sum(m.astype(F32),axis=0,keepdims=True)

class Products:
    def __init__(self,pos,eb,lb,rbuf,bq,bp,wqkv,wout,win,wback,gvec,gbin,w_up,w_dn,hb):
        self.__dict__.update(locals())
    def right(self,c0,w):
        r=self.rbuf[:,:,:,:,:,c0:c0+w].reshape(32,16,w).astype(F32)
        self.bq[:,c0:c0+w]=r[:,0:8].reshape(256,w).astype(BF)
        self.bp[:,c0:c0+w]=r[:,8:16].reshape(256,w).astype(BF)
    def pair(self,buf,r0):
        t=buf[:,r0:r0+16,:].astype(F32)
        return [t[:,8*i:8*i+8].reshape(256,128) for i in (0,1)]
    def put(self,out,rows,cols,tt,c0,w):
        tt=tt.T.astype(BF)
        out[0,rows,cols]=dot(tt,self.bq[:,c0:c0+w])[0:48]
        out[1,rows,cols]=dot(tt,self.bp[:,c0:c0+w])[64:112]
    def mixed(self,buf,r0,heads,col0,dst0):
        low=lax.broadcasted_iota(jnp.int32,(128,128),1)<64
        for h in range(0,heads,2):
            a,b=[v.T.astype(BF) for v in self.pair(buf,r0+8*h)]
            cs=slice(col0+64*h,col0+64*h+128); ds=slice(dst0+64*h,dst0+64*h+128)
            self.wqkv[0,:,ds]=jnp.where(low,dot(a,self.bq[:,cs]),dot(b,self.bq[:,cs]))[0:48]
            self.wqkv[1,:,ds]=jnp.where(low,dot(a,self.bp[:,cs]),dot(b,self.bp[:,cs]))[64:112]
    def feed_forward(self,e):
        b=(self.bq,self.bp)[e]; w,y=self.pos.w,self.pos.y
        nl=b[:,0:768]
        r=lax.broadcasted_iota(jnp.int32,(768,128),0); l=lax.broadcasted_iota(jnp.int32,(768,128),1)
        mine=dot(nl,jnp.where((r==48*w+l)&(l<48),1.0,0.0).astype(BF)).T[0:48].astype(BF)
        for t in range(4):
            cols=pl.ds(pl.multiple_of(y*1536+384*t,128),384)
            hid=dot(nl,self.w_up[e,:,cols])+self.hb[e,:,cols]
            gh=(dot_nt(b[:,1152:1920],self.w_dn[e,cols,:])*gelu_slope(hid)).astype(BF)
            self.win[e,:,384*t:384*t+384]=dot(mine,gh)
        cols=pl.ds(pl.multiple_of(192*w//128*128,128),256)
        act=gelu(dot(nl,self.w_up[e,:,cols])+self.hb[e,:,cols]).astype(BF).astype(F32).T.astype(BF)
        back=dot(act,b[:,pl.ds(pl.multiple_of(1152+y*384,128),384)])
        self.wback[e]=jnp.where(w%2==1,back[64:256],back[0:192])
    def second(self):
        al=slice(None)
        x0,att=self.pair(self.eb,0)
        self.put(self.wout,al,al,att,1920,384)
        @pl.when(self.pos.y==0)
        def _(): self.put(self.wqkv,al,slice(0,768),x0,2304,768)
        @pl.when(self.pos.y==1)
        def _(): self.mixed(self.eb,16,12,2304,384)
    def third(self):
        def sums(r0,half):
            vs,bs=[jnp.sum(v.reshape(32,8,128),axis=0) for v in self.pair(self.lb,r0)]
            for e in (0,1):
                ls=slice(64*e,64*e+48)
                self.gvec[e]=vs[4*half:4*half+4,ls]
                for k in (0,1): self.gbin[e:e+1,48*k:48*k+48]=bs[2*half+k:2*half+k+1,ls]
        @pl.when(self.pos.y==0)
        def _():
            self.mixed(self.lb,0,6,768,768)
            sums(48,0)
        @pl.when(self.pos.y==1)
        def _():
            self.mixed(self.lb,16,6,768,0)
            sums(0,1)

def tail_kernel(*refs):
    (ql,pln,qx_h,px_h,qk_h,qv_h,pk_h,pv_h,wqkv_h,wo_h,wup_h,wdn_h,q0,a0,p1,h0,p2,heads,marks,vec,hb,
     loss,tq,tp,uq,up_,extra,wqkv,wout,win,wback,gvec,gbin,
     kv_q,kv_p,w_qkv,w_o,w_up,w_dn,hbuf,gr,gs_s,gt_s,qa_s,ga_s,P_s,ls,ll,lb,stage,left_e,left_l,ebuf,lbuf,rs,rb,rbuf,bq,bp,gq_s,sv_s,
     msem,hsend,hrecv,esend,erecv,lsend,lrecv,rsend,rrecv)=refs
    pos=Place()
    bar=pltpu.get_barrier_semaphore()
    def lap(d,kept):
        t=(pos.me+d)%32
        pl.semaphore_signal(bar,inc=1,device_id=(t//2,t%2),device_id_type=MESH)
        return kept
    lax.fori_loop(1,32,lap,0)
    moves={}
    def move(name,src,dst): moves[name]=pltpu.make_async_copy(src,dst,msem.at[len(moves)]); moves[name].start()
    for n,(h,d) in enumerate(((pk_h,kv_p),(px_h,kv_p),(pv_h,kv_p),(qk_h,kv_q),(qx_h,kv_q),(qv_h,kv_q))): move("kxv"[n%3]+"pq"[n//3],h,d.at[n%3])
    for nm,h,d in (("dn",wdn_h,w_dn),("up",wup_h,w_up),("o",wo_h,w_o),("qkv",wqkv_h,w_qkv)):
        for e in (1,0): move(nm+str(e),h.at[e],d.at[e])
    def need(*names):
        for nm in names:
            if nm in moves: moves.pop(nm).wait()
    hbuf[pos.z,pos.x,pos.c,pos.y]=heads[...].astype(BF)
    for ref in (ls,ll,lb,gq_s,sv_s): ref[...]=jnp.zeros_like(ref)
    pl.semaphore_wait(bar,31)
    hg=HeadGather(pos,hbuf,hsend,hrecv)
    hg.phase(0)
    vv=lambda e: vec[e]
    for e in (1,0):
        rows=slice(8*e,8*e+8)
        q0s=q0[rows,:]*0.125
        qa_s[e]=heads_apart(q0s,8).astype(BF)
        nlow=norm(p1[rows,:],vv(e)[3:4],vv(e)[4:5])
        for c in range(6): ls[e,c,8:16,:]=a0[rows,128*c:128*c+128]
        for half in (0,1):
            rs[half,rows,0:768]=nlow; rs[half,rows,768:1152]=q0s[:,384*half:384*half+384]
    rb[:,:,0:1152]=rs[:,:,0:1152].astype(BF)
    rg=RightGather(pos,rb,rbuf,rsend,rrecv)
    rg.step(0,0)
    need("kp","xp")
    for i in range(2): early_block(1,i,pln,kv_p.at[0],kv_p.at[1],qa_s,P_s,ls)
    hg.phase(1)
    rg.step(0,1)
    for i in range(2,6): early_block(1,i,pln,kv_p.at[0],kv_p.at[1],qa_s,P_s,ls)
    hg.phase(2)
    need("kq","xq")
    for i in range(2): early_block(0,i,ql,kv_q.at[0],kv_q.at[1],qa_s,P_s,ls)
    early_messages(ls,left_e)
    hg.phase(3)
    rg.step(0,2)
    ec=LeftCopies(pos,left_e,ebuf,EARLY,esend,erecv)
    for k in range(4): ec.start(k)
    similarity(pos,hbuf,marks,loss,gr,gs_s,gt_s)
    rg.step(0,3)
    g2,sums,gn={}, {}, {}
    need("dn1","dn0")
    for e in (1,0):
        rows=slice(8*e,8*e+8)
        g2[e],gain2,shift2=norm_grad(p2[rows,:],vv(e)[6:7],gr[rows,:])
        gffn=g2[e].astype(BF).astype(F32)
        for half in (0,1): rs[half,rows,1152:1920]=gffn
        sums[e]=(colsum(gffn),gain2,shift2)
    rb[:,:,1152:1920]=rs[:,:,1152:1920].astype(BF)
    rg.step(1,0); rg.step(2,0)
    need("up1","up0")
    for e in (1,0):
        gh=(dot_nt(g2[e].astype(BF),w_dn[e])*gelu_slope(h0[8*e:8*e+8,:])).astype(BF)
        lb[e,0:1,:]=colsum(gh)
        gn[e]=g2[e]+dot_nt(gh,w_up[e])
    rg.step(1,1); rg.step(2,1); rg.step(0,4)
    need("o1","o0","qkv1","qkv0","vp","vq")
    g1,sums1={}, {}
    for e in (1,0):
        rows=slice(8*e,8*e+8)
        g1[e],gain1,shift1=norm_grad(p1[rows,:],vv(e)[3:4],gn[e])
        gb=g1[e].astype(BF)
        sums1[e]=(colsum(gb),gain1,shift1)
        ga=dot_nt(gb,w_o[e]).astype(BF).astype(F32)
        ga_s[e]=heads_apart(ga,8).astype(BF)
        for half in (0,1): rs[half,rows,1920:2304]=gb[:,384*half:384*half+384].astype(F32)
        rs[1,rows,2304:3072]=ga
    rg.step(1,2); rg.step(2,2)
    for i in range(0,3): late_block(1,i,kv_p.at[0],kv_p.at[2],kv_p.at[1],ga_s,P_s,ll,gq_s,sv_s,tp)
    rg.step(1,3); rg.step(2,3); rg.step(0,5)
    for i in range(3,6): late_block(1,i,kv_p.at[0],kv_p.at[2],kv_p.at[1],ga_s,P_s,ll,gq_s,sv_s,tp)
    rg.step(1,4); rg.step(2,4)
    for i in range(2): late_block(0,i,kv_q.at[0],kv_q.at[2],kv_q.at[1],ga_s,P_s,ll,gq_s,sv_s,tq)
    for e in (1,0):
        rows=slice(8*e,8*e+8)
        gql=gq_s[e].astype(BF)
        rs[0,rows,2304:3072]=gql.astype(F32)
        vs=jnp.concatenate([colsum(gql),sv_s[e,0:1],*sums1[e],*sums[e]],axis=0)
        for c in range(6): ll[e,c,96:104,:]=vs[:,128*c:128*c+128]
    rb[:,:,1920:3072]=rs[:,:,1920:3072].astype(BF)
    rg.step(3,0); rg.step(4,0)
    late_messages(ll,lb,stage,left_l)
    rg.step(3,1); rg.step(4,1)
    lc=LeftCopies(pos,left_l,lbuf,LATE,lsend,lrecv)
    lc.start(1); lc.start(3)
    rg.step(1,5); rg.step(2,5)
    for e in (1,0):
        uk=dot_nt(qa_s[e],w_qkv[e,:,768:1536]).astype(BF); uv=dot_nt(ga_s[e],w_qkv[e,:,1536:2304]).astype(BF)
        out=(uq,up_)[e]; R=16*256//SLOTS[e]
        for i in range(NB[e]):
            out[i,0:R,:]=uk[i*R:i*R+R]; out[i,R:2*R,:]=uv[i*R:i*R+R]
        extra[8*e:8*e+8,:]=g1[e]+dot_nt(gq_s[e].astype(BF),w_qkv[e,:,0:768])
    rg.step(3,2); rg.step(4,2)
    lc.start(2)
    rg.step(0,6); rg.step(1,6); rg.step(2,6)
    pr=Products(pos,ebuf,lbuf,rbuf,bq,bp,wqkv,wout,win,wback,gvec,gbin,w_up,w_dn,hb)
    pr.right(0,1920)
    rg.step(3,3); rg.step(4,3)
    lc.start(0)
    pr.feed_forward(1)
    rg.step(3,4); rg.step(4,4)
    pr.feed_forward(0)
    rg.step(3,5); rg.step(4,5)
    rg.step(3,6); rg.step(4,6)
    pr.right(1920,1152)
    ec.finish()
    pr.second()
    lc.finish()
    pr.third()

def tail_call(*a):
    S=jax.ShapeDtypeStruct; VM=pltpu.VMEM; D=pltpu.SemaphoreType.DMA
    V=pl.BlockSpec(memory_space=pltpu.VMEM); SM=pl.BlockSpec(memory_space=pltpu.SMEM); A=pl.BlockSpec(memory_space=pl.ANY)
    outs=[S((1,1),F32),S((2,128,256),BF),S((6,32,256),BF),S((2,128,768),BF),S((6,32,768),BF),S((16,768),F32),
          S((2,48,1152),F32),S((2,48,384),F32),S((2,48,1536),F32),S((2,192,384),F32),S((2,4,48),F32),S((2,96),F32)]
    scratch=[VM((3,512,768),BF),VM((3,1536,768),BF),VM((2,768,2304),BF),VM((2,768,768),BF),VM((2,768,3072),BF),VM((2,3072,768),BF),
      VM((4,2,2,2,16,768),BF),VM((16,768),F32),VM((256,256),F32),VM((256,256),F32),VM((2,128,768),BF),VM((2,128,768),BF),VM((224,256),F32),
      VM((2,6,112,128),F32),VM((2,6,112,128),F32),VM((2,8,3072),F32),VM((16,8,128),F32),VM((16,112,128),BF),VM((16,112,128),BF),
      VM((32,112,128),BF),VM((32,64,128),BF),VM((2,16,3072),F32),VM((2,16,3072),BF),VM((4,2,2,2,16,3072),BF),VM((256,3072),BF),VM((256,3072),BF),VM((2,8,768),F32),VM((2,8,768),F32),
      D((14,)),D((10,)),D((10,)),D((32,)),D((32,)),D((32,)),D((32,)),D((5,17)),D((5,17))]
    return pl.pallas_call(tail_kernel,out_shape=outs,in_specs=[SM,SM]+[A]*10+[V]*9,out_specs=[SM]+[V]*11,scratch_shapes=scratch,
      compiler_params=pltpu.CompilerParams(collective_id=2,has_side_effects=True,vmem_limit_bytes=62*2**20),name="tail")(*a)

def finish_kernel(loss_in,q_in,p_in,wqkv_in,wout_in,win_in,wback_in,gvec_in,gbin_in,tq,tp,uq,up_,extra,
                  loss,q_out,p_out,gq,gp,wqkv,wout,win,wback,gvec,gbin,slots,sem,osem):
    copies=[pltpu.make_async_copy(a,b,sem.at[k]) for k,(a,b) in enumerate(((p_in,p_out),(q_in,q_out),(win_in,win),(wqkv_in,wqkv),(wback_in,wback),(wout_in,wout)))]
    for cp in copies: cp.start()
    loss[0,0]=loss_in[0,0]
    gvec[...]=gvec_in[...]; gbin[...]=gbin_in[...]
    flying={}
    for b in range(8):
        e,i=(1,b) if b<6 else (0,b-6)
        mix,u,out=((tq,uq,gq),(tp,up_,gp))[e]
        slot=b%4
        if slot in flying: flying[slot].wait()
        slots[slot]=dot(mix[i].astype(F32).T.astype(BF),u[i])
        n=256//SLOTS[e]
        for j in range(n): slots[slot,j*SLOTS[e]:j*SLOTS[e]+1,:]+=extra[8*e+i*n+j:8*e+i*n+j+1,:]
        flying[slot]=pltpu.make_async_copy(slots.at[slot],out.at[pl.ds(i*256,256)],osem.at[slot])
        flying[slot].start()
    for cp in flying.values(): cp.wait()
    for cp in copies: cp.wait()
def finish_call(loss,q_out,p_out,grads,tq,tp,uq,up_,extra):
    S=jax.ShapeDtypeStruct; VM=pltpu.VMEM; D=pltpu.SemaphoreType.DMA
    V=pl.BlockSpec(memory_space=pltpu.VMEM); SM=pl.BlockSpec(memory_space=pltpu.SMEM); A=pl.BlockSpec(memory_space=pl.ANY)
    ins=(loss,q_out,p_out,*grads,tq,tp,uq,up_,extra)
    shape=lambda a: S(a.shape,a.dtype)
    outs=[shape(loss),shape(q_out),shape(p_out),S(q_out.shape,F32),S(p_out.shape,F32)]+[shape(g) for g in grads]
    return pl.pallas_call(finish_kernel,out_shape=outs,in_specs=[SM]+[A]*6+[V]*7,out_specs=[SM]+[A]*8+[V]*2,
      scratch_shapes=[VM((4,256,768),F32),D((6,)),D((4,))],compiler_params=pltpu.CompilerParams(vmem_limit_bytes=32*2**20),name="finish")(*ins)

STEP, LOAD, P1, P2, P3, P4 = range(6)
NEEDS={P1:0,P2:1,P3:2,P4:3}

def spread_small(tiles, vec, hb):
    r=lax.broadcasted_iota(jnp.int32,(128,256),0); l=lax.broadcasted_iota(jnp.int32,(128,256),1)
    r4=lax.broadcasted_iota(jnp.int32,(128,384),0); l4=lax.broadcasted_iota(jnp.int32,(128,384),1)
    vec[...]=jnp.zeros_like(vec); hb[...]=jnp.zeros_like(hb)
    for w in range(16):
        for y in range(2):
            t=tiles[w//4,(w//2)%2,(w%2)*16:(w%2)*16+16,y*128:y*128+128]
            c=min(48*w//128*128,512); off=48*w-c
            v=dot(t,jnp.where((l-off==r)&(r<48),1.0,0.0).astype(BF))
            for e in (0,1): vec[e,4*y:4*y+4,c:c+256]+=v[4*e:4*e+4]
            c=min((192*w+96*y)//128*128,3072-384); off=192*w+96*y-c
            h=dot(t,jnp.where((l4-off==r4)&(r4<96),1.0,0.0).astype(BF))
            for e in (0,1): hb[e,0:1,c:c+384]+=h[8+e:9+e]

def own_tiles(vectors, hidden_bias, q_set, gold, p_set, stage, small, marks):
    stage[...]=jnp.zeros_like(stage)
    for e in (0,1):
        stage[4*e:4*e+4,0:48]=vectors[e].astype(F32)
        stage[8+e:9+e,0:96]=hidden_bias[e:e+1,:].astype(F32)
    small[0]=stage[...].astype(BF)
    me=lax.axis_index("wq")*2+lax.axis_index("np")
    r=lax.broadcasted_iota(jnp.int32,(16,128),0); place=(r%2)*128+lax.broadcasted_iota(jnp.int32,(16,128),1)-me*8
    count=p_set.shape[0]
    tile=jnp.zeros((16,128),jnp.int32)
    for k in range(8):
        here=place==k
        tile=jnp.where(here&(r//2==0),q_set[k],tile)
        tile=jnp.where(here&(r//2==1),gold[k]//count*8+gold[k]%count,tile)
        tile=jnp.where(here&(r//2==2),p_set[k] if k<count else -1,tile)
    marks[0]=tile

def fused_kernel(units, plan, *refs):
    (ql,pln,q_set,gold,p_set,qx_h,px_h,vectors,hidden_bias)=refs[0:9]; ins=list(refs[9:13]); outs=refs[13:19]
    vec,hb,qo_h,po_h,qk_h,qv_h,pk_h,pv_h,q0,a0,p1,h0,p2,hd=refs[19:33]
    wv=refs[33:37]; qx,px,qo,po,qk,qv,pk,pv,stage,small_src,mark_src,small,bias,att,nrm,act,send,recv,lsem,xsem=refs[37:]
    moves={}
    def move(name,src,dst):
        moves[name]=pltpu.make_async_copy(src,dst,xsem.at[len(moves)]); moves[name].start()
    move("x1",px_h,px); move("x0",qx_h,qx)
    own_tiles(vectors,hidden_bias,q_set,gold,p_set,stage,small_src,mark_src)
    ins+=[small_src,mark_src]
    g=Gather(units,ins,outs,send,recv)
    g.barrier()
    for ref in (q0,a0,p1,h0,p2,hd): ref[...]=jnp.zeros_like(ref)
    X=(qx,px); O=(qo,po); K=(qk,pk); V=(qv,pv); LENS=(ql,pln); SLOTS=(64,256); BASE=(0,512); NB=(2,6)
    HBM=((qk_h,qv_h,qo_h),(pk_h,pv_h,po_h))
    loaded=set()
    def load_copies(a,e):
        if a==5: return []
        if a==4: return [pltpu.make_async_copy(outs[4].at[0],small,lsem.at[a,e,0])]
        rows=outs[a].shape[3]
        return [pltpu.make_async_copy(outs[a].at[e,k//2,k%2],wv[a].at[e,pl.ds(k*rows,rows)],lsem.at[a,e,k]) for k in range(8)]
    def need(a,e):
        if (a,e) in loaded: return
        loaded.add((a,e))
        for cp in load_copies(a,e): cp.wait()
        if a==4: spread_small(small,vec,hb)
        if a==0: moves["x%d"%e].wait()
    for item in plan:
        if item[0]==STEP: g.step(item[1],item[2])
        elif item[0]==LOAD:
            for cp in load_copies(*item[1:]): cp.start()
        else:
            kind,e,lo,hi=item
            need(4,0); need(NEEDS[kind],e)
            n=256//SLOTS[e]
            A=att.at[pl.ds(BASE[e],NB[e]*BLK)]; N=nrm.at[pl.ds(BASE[e],NB[e]*BLK)]
            def body(i,kept):
                row=pl.multiple_of(i*BLK,BLK)
                if kind==P1:
                    make_bias(bias,0,[LENS[e][i*n+j] for j in range(n)],SLOTS[e])
                    attend_block(row,X[e],wv[0].at[e],vec.at[e],bias,K[e],V[e],A,q0,e,i)
                if kind==P2: out_block(row,X[e],A,wv[1].at[e],vec.at[e],N,a0,p1,e,i)
                if kind==P3: up_block(row,N,wv[2].at[e],hb.at[e],act,h0,e,i,row)
                if kind==P4: down_block(row,N,act,wv[3].at[e],vec.at[e],O[e],p2,hd,e,i,row)
                return kept
            if hi-lo==1: body(lo,0)
            else: lax.fori_loop(lo,hi,body,0)
            if hi==NB[e]:
                if kind==P1:
                    move("k%d"%e,K[e],HBM[e][0]); move("v%d"%e,V[e],HBM[e][1])
                if kind==P4: move("o%d"%e,O[e],HBM[e][2])
    for name in moves:
        if name[0]!="x": moves[name].wait()

def fused_call(ql,pln,q_set,gold,p_set,qx,px,vectors,hidden_bias,arrays,units,plan):
    S=jax.ShapeDtypeStruct; VM=pltpu.VMEM; D=pltpu.SemaphoreType.DMA
    V=pl.BlockSpec(memory_space=pltpu.VMEM); SM=pl.BlockSpec(memory_space=pltpu.SMEM); A=pl.BlockSpec(memory_space=pl.ANY)
    outs=[S((a.shape[0],4,2,2*a.shape[1],2*a.shape[2]),a.dtype) for a in arrays]+[S((1,4,2,32,256),BF),S((1,4,2,32,256),jnp.int32)]
    outs+=[S((2,8,768),F32),S((2,1,3072),F32),S(qx.shape,BF),S(px.shape,BF),S(qx.shape,BF),S(qx.shape,BF),S(px.shape,BF),S(px.shape,BF),S((16,768),F32),S((16,768),F32),S((16,768),F32),S((16,3072),F32),S((16,768),F32),S((16,768),F32)]
    big=[VM(qx.shape,BF),VM(px.shape,BF)]+[VM(qx.shape,BF),VM(px.shape,BF)]+[VM(qx.shape,BF)]*2+[VM(px.shape,BF)]*2
    return pl.pallas_call(functools.partial(fused_kernel,units,plan),out_shape=outs,in_specs=[SM]*5+[A,A,V,V]+[A]*4,out_specs=[A]*6+[V,V]+[A]*6+[V]*6,
      scratch_shapes=[VM((2,768,2304),BF),VM((2,768,768),BF),VM((2,768,3072),BF),VM((2,3072,768),BF)]+big+[VM((16,128),F32),VM((1,16,128),BF),VM((1,16,128),jnp.int32),VM((4,2,32,256),BF),VM((256,256),F32),VM((2048,768),BF),VM((2048,768),F32),VM((1536,3072),BF),D((len(units),18)),D((len(units),18)),D((6,2,8)),D((8,))],
      compiler_params=pltpu.CompilerParams(collective_id=1,has_side_effects=True,vmem_limit_bytes=63*2**20),name="fused")(ql,pln,q_set,gold,p_set,qx,px,vectors,hidden_bias,*arrays)


GATHER_UNITS = (
    (4, 0, False, 0, 16), (5, 0, False, 0, 16), (0, 1, False, 0, 16), (0, 1, False, 16, 16),
    (0, 1, False, 32, 16), (1, 1, True, 0, 16), (1, 1, True, 16, 16), (1, 1, True, 32, 16),
    (0, 0, False, 0, 48), (2, 1, False, 0, 48), (1, 0, True, 0, 48), (3, 1, True, 0, 64),
    (3, 1, True, 64, 64), (3, 1, True, 128, 64), (2, 0, True, 0, 48), (3, 0, True, 0, 64),
    (3, 0, True, 64, 64), (3, 0, True, 128, 64),
)
GATHER_PLAN = (
    (STEP, 0, 0), (STEP, 1, 0), (STEP, 2, 0), (STEP, 3, 0), (STEP, 4, 0), (STEP, 5, 0),
    (STEP, 6, 0), (STEP, 7, 0), (STEP, 0, 1), (STEP, 1, 1), (STEP, 2, 1), (STEP, 5, 1),
    (STEP, 3, 1), (STEP, 0, 2), (STEP, 6, 1), (STEP, 7, 1), (STEP, 1, 2), (STEP, 4, 1),
    (STEP, 2, 2), (STEP, 5, 2), (STEP, 0, 3), (STEP, 3, 2), (STEP, 6, 2), (STEP, 1, 3),
    (STEP, 7, 2), (STEP, 0, 4), (STEP, 4, 2), (STEP, 2, 3), (STEP, 1, 4), (STEP, 5, 3),
    (STEP, 0, 5), (STEP, 8, 0), (STEP, 3, 3), (STEP, 6, 3), (STEP, 0, 6), (LOAD, 4, 0),
    (STEP, 7, 3), (STEP, 2, 4), (STEP, 4, 3), (STEP, 5, 4), (STEP, 1, 5), (STEP, 9, 0),
    (STEP, 1, 6), (LOAD, 5, 0), (STEP, 3, 4), (STEP, 8, 1), (STEP, 6, 4), (STEP, 7, 4),
    (STEP, 2, 5), (STEP, 10, 0), (STEP, 2, 6), (STEP, 4, 4), (STEP, 9, 1), (STEP, 5, 5),
    (STEP, 11, 0), (STEP, 5, 6), (STEP, 8, 2), (STEP, 3, 5), (STEP, 12, 0), (STEP, 6, 5),
    (STEP, 13, 0), (STEP, 3, 6), (STEP, 9, 2), (STEP, 7, 5), (STEP, 14, 0), (STEP, 6, 6),
    (STEP, 10, 1), (STEP, 7, 6), (LOAD, 1, 1), (STEP, 8, 3), (STEP, 4, 5), (STEP, 15, 0),
    (STEP, 11, 1), (STEP, 12, 1), (STEP, 9, 3), (STEP, 4, 6), (LOAD, 0, 1), (STEP, 13, 1),
    (STEP, 10, 2), (STEP, 14, 1), (STEP, 11, 2), (P1, 1, 0, 1), (STEP, 8, 4), (STEP, 12, 2),
    (STEP, 15, 1), (STEP, 13, 2), (P1, 1, 1, 2), (STEP, 10, 3), (STEP, 9, 4), (P1, 1, 2, 3),
    (STEP, 14, 2), (STEP, 11, 3), (P1, 1, 3, 4), (STEP, 12, 3), (STEP, 8, 5), (STEP, 16, 0),
    (STEP, 15, 2), (P1, 1, 4, 5), (STEP, 8, 6), (LOAD, 0, 0), (STEP, 13, 3), (STEP, 10, 4),
    (P1, 1, 5, 6), (STEP, 14, 3), (P1, 0, 0, 1), (STEP, 9, 5), (STEP, 17, 0), (STEP, 11, 4),
    (STEP, 12, 4), (STEP, 16, 1), (P1, 0, 1, 2), (STEP, 10, 5), (STEP, 9, 6), (LOAD, 2, 1),
    (STEP, 15, 3), (STEP, 17, 1), (STEP, 13, 4), (P2, 1, 0, 1), (STEP, 10, 6), (LOAD, 1, 0),
    (STEP, 11, 5), (P2, 1, 1, 4), (STEP, 11, 6), (P2, 1, 4, 6), (STEP, 12, 5), (STEP, 14, 4),
    (P2, 0, 0, 2), (STEP, 12, 6), (STEP, 16, 2), (P3, 1, 0, 1), (P3, 1, 1, 2), (STEP, 13, 5),
    (STEP, 15, 4), (P3, 1, 2, 3), (STEP, 13, 6), (LOAD, 3, 1), (STEP, 17, 2), (STEP, 16, 3),
    (P3, 1, 3, 4), (P3, 1, 4, 5), (STEP, 17, 3), (P3, 1, 5, 6), (P4, 1, 0, 2), (STEP, 14, 5),
    (STEP, 16, 4), (STEP, 17, 4), (P4, 1, 2, 4), (STEP, 14, 6), (LOAD, 2, 0), (P4, 1, 4, 5),
    (STEP, 15, 5), (P4, 1, 5, 6), (P3, 0, 0, 1), (STEP, 15, 6), (STEP, 16, 5), (P3, 0, 1, 2),
    (STEP, 16, 6), (STEP, 17, 5), (STEP, 17, 6), (LOAD, 3, 0), (P4, 0, 0, 2),
)


def kernel_shards(
    q_embed, p_embed, q_len, p_len, q_set, p_set, gold, wqkv, wout, wup, wdown, vectors, hidden_bias
):
    arrays = (wqkv, wout, wup, wdown)
    done = fused_call(
        q_len, p_len, q_set, gold, p_set, q_embed, p_embed, vectors, hidden_bias, arrays, GATHER_UNITS, GATHER_PLAN
    )
    weights = tuple(
        member.reshape(2, 16 * shard.shape[1], 2 * shard.shape[2])
        for member, shard in zip(done[:4], arrays)
    )
    vec, bias, q_out, p_out, q_keys, q_values, p_keys, p_values, q0, a0, p1, h0, p2, heads = done[6:]
    loss, tq, tp, uq, up, extra, *grads = tail_call(
        q_len, p_len, q_embed, p_embed, q_keys, q_values, p_keys, p_values, *weights,
        q0, a0, p1, h0, p2, heads, done[5], vec, bias,
    )
    loss, *rest = finish_call(loss, q_out, p_out, grads, tq, tp, uq, up, extra)
    return (loss[0, 0], *rest)


def kernels_fit(q_embed, p_embed, q_len, p_len):
    return (
        lax.axis_size("wq") == 16
        and lax.axis_size("np") == 2
        and q_embed.shape == (512, 768)
        and p_embed.shape == (1536, 768)
        and q_len.shape == (8,)
        and p_len.shape == (6,)
    )


def shards(
    q_embed,
    p_embed,
    q_len,
    p_len,
    q_set,
    p_set,
    gold,
    query_key_value_weight,
    attention_output_weight,
    up_weight,
    down_weight,
    vectors,
    hidden_bias,
):
    if kernels_fit(q_embed, p_embed, q_len, p_len):
        return kernel_shards(
            q_embed,
            p_embed,
            q_len,
            p_len,
            q_set,
            p_set,
            gold,
            query_key_value_weight,
            attention_output_weight,
            up_weight,
            down_weight,
            vectors,
            hidden_bias,
        )
    gathered = gather_weights(
        query_key_value_weight,
        attention_output_weight,
        up_weight,
        down_weight,
        vectors,
        hidden_bias,
    )
    wq_size, np_size = lax.axis_size("wq"), lax.axis_size("np")
    both_axes = ("wq", "np")
    q_weights = tuple((member[0] for member in gathered))
    p_weights = tuple((member[1] for member in gathered))
    p_encoded, p_stored = encode_forward(p_embed, p_len, p_weights)
    q_encoded, q_stored = encode_forward(q_embed, q_len, q_weights)
    model_width = q_embed.shape[1]
    ff_width = gathered[2].shape[2]
    q_count = q_len.shape[0]
    p_count = p_len.shape[0]
    own_heads = jnp.concatenate([first_rows(q_encoded, q_count), first_rows(p_encoded, p_count)])
    heads = lax.all_gather(own_heads, both_axes, axis=0)
    marks = lax.all_gather(jnp.concatenate([q_set, gold, p_set]), both_axes, axis=0)
    q_heads = heads[:, :q_count].reshape(-1, model_width)
    p_heads = heads[:, q_count:].reshape(-1, model_width)
    q_sets = marks[:, :q_count].reshape(-1)
    golds = marks[:, q_count : 2 * q_count].reshape(-1)
    p_sets = marks[:, 2 * q_count :].reshape(-1)
    scaling = model_width ** (-0.5)
    similar = (
        jnp.einsum("qd,pd->qp", q_heads, p_heads, preferred_element_type=jnp.float32) * scaling
    )
    is_gold = jnp.arange(p_heads.shape[0], dtype=jnp.int32)[None, :] == golds[:, None]
    usable = (q_sets[:, None] == p_sets[None, :]) | is_gold
    masked = jnp.where(usable, similar, NEGATIVE)
    highest = jnp.max(masked, axis=1)
    total = jnp.sum(jnp.where(usable, jnp.exp(masked - highest[:, None]), 0.0), axis=1)
    log_total = highest + jnp.log(total)
    gold_score = jnp.sum(jnp.where(is_gold, similar, 0.0), axis=1)
    loss = jnp.mean(log_total - gold_score)
    soft_rows = jnp.where(usable, jnp.exp(masked - log_total[:, None]), 0.0)
    grad_similar = (soft_rows - is_gold.astype(jnp.float32)).astype(jnp.bfloat16)
    me = lax.axis_index("wq") * np_size + lax.axis_index("np")
    grad_q_first = (
        jnp.einsum(
            "qp,pd->qd",
            lax.dynamic_slice_in_dim(grad_similar, me * q_count, q_count, 0),
            p_heads,
            preferred_element_type=jnp.float32,
        )
        * scaling
    )
    grad_p_first = (
        jnp.einsum(
            "qp,qd->pd",
            lax.dynamic_slice_in_dim(grad_similar, me * p_count, p_count, 1),
            q_heads,
            preferred_element_type=jnp.float32,
        )
        * scaling
    )
    q_back = encode_backward(q_embed, q_weights, q_stored, grad_q_first)
    p_back = encode_backward(p_embed, p_weights, p_stored, grad_p_first)
    left = jnp.concatenate(
        [left_message(member[1], wq_size, np_size) for member in (q_back, p_back)], axis=2
    )
    left = left.reshape((wq_size * np_size,) + left.shape[2:])
    left = lax.all_to_all(left, both_axes, 0, 0)
    right = jnp.concatenate([right_message(member[2], np_size) for member in (q_back, p_back)], axis=1)
    right = lax.all_gather(lax.all_to_all(right, "np", 0, 0), "wq", axis=0)
    right = right.reshape((wq_size * np_size,) + right.shape[2:])
    sums = jnp.concatenate(
        [
            jnp.stack([q_back[3], p_back[3]])
            .reshape(2, np_size, -1, wq_size, model_width // wq_size)
            .transpose(3, 1, 0, 2, 4)
            .reshape(wq_size * np_size, -1),
            jnp.stack([q_back[4], p_back[4]])
            .reshape(2, wq_size * np_size, -1)
            .transpose(1, 0, 2)
            .reshape(wq_size * np_size, -1),
        ],
        axis=1,
    )
    sums = jnp.sum(lax.all_to_all(sums, both_axes, 0, 0), axis=0)
    grad_vectors = sums[: sums.shape[0] - 2 * ff_width // (wq_size * np_size)].reshape(
        2, -1, model_width // wq_size
    )
    grad_b_in = sums[sums.shape[0] - 2 * ff_width // (wq_size * np_size) :].reshape(2, -1)
    q_weight_grads = weight_grads(
        left[:, :q_count].reshape(-1, left.shape[2]),
        right[:, :q_count].reshape(-1, right.shape[2]),
        model_width,
        ff_width,
        wq_size,
        np_size,
    )
    p_weight_grads = weight_grads(
        left[:, q_count:].reshape(-1, left.shape[2]),
        right[:, q_count:].reshape(-1, right.shape[2]),
        model_width,
        ff_width,
        wq_size,
        np_size,
    )
    shared = tuple(jnp.stack(pair) for pair in zip(q_weight_grads, p_weight_grads))
    return (
        loss,
        q_encoded,
        p_encoded,
        q_back[0],
        p_back[0],
        shared[0],
        shared[1],
        shared[2],
        shared[3],
        grad_vectors,
        grad_b_in,
    )


def solution(mesh):
    return jax.shard_map(
        shards,
        mesh=mesh,
        in_specs=(
            P(("wq", "np"), None),
            P(("wq", "np"), None),
            P(("wq", "np")),
            P(("wq", "np")),
            P(("wq", "np")),
            P(("wq", "np")),
            P(("wq", "np")),
            P(None, "wq", "np"),
            P(None, "wq", "np"),
            P(None, "wq", "np"),
            P(None, "wq", "np"),
            P(None, "np", "wq"),
            P(None, ("wq", "np")),
        ),
        out_specs=(
            P(),
            P(("wq", "np"), None),
            P(("wq", "np"), None),
            P(("wq", "np"), None),
            P(("wq", "np"), None),
            P(None, "wq", "np"),
            P(None, "wq", "np"),
            P(None, "wq", "np"),
            P(None, "wq", "np"),
            P(None, "np", "wq"),
            P(None, ("wq", "np")),
        ),
        check_vma=False,
    )
```

```python
import functools
import math

import jax
import jax.numpy as jnp
from jax import lax
from jax.experimental import pallas as pl
from jax.experimental.pallas import tpu as pltpu
from jax.sharding import PartitionSpec as P


HEADS = 12


EPSILON = 1e-12
NEGATIVE = -1e30


def layer_norm(inputs, gain_row, offset):
    centred = inputs - jnp.mean(inputs, axis=-1, keepdims=True)
    spread = jnp.mean(centred * centred, axis=-1, keepdims=True)
    return centred * lax.rsqrt(spread + EPSILON) * gain_row + offset


def smooth_gate(values):
    return jax.nn.gelu(values, approximate=True)


def gather_weights(
    query_key_value_weight, attention_output_weight, up_weight, down_weight, vectors, hidden_bias
):
    np_parts = (
        lax.all_gather(query_key_value_weight, "np", axis=2, tiled=True),
        lax.all_gather(attention_output_weight, "np", axis=2, tiled=True),
        lax.all_gather(up_weight, "np", axis=2, tiled=True),
        lax.all_gather(down_weight, "np", axis=2, tiled=True),
        lax.all_gather(vectors, "np", axis=1, tiled=True),
        lax.all_gather(hidden_bias, "np", axis=1, tiled=True),
    )
    return (
        lax.all_gather(np_parts[0], "wq", axis=1, tiled=True),
        lax.all_gather(np_parts[1], "wq", axis=1, tiled=True),
        lax.all_gather(np_parts[2], "wq", axis=1, tiled=True),
        lax.all_gather(np_parts[3], "wq", axis=1, tiled=True),
        lax.all_gather(np_parts[4], "wq", axis=2, tiled=True),
        lax.all_gather(np_parts[5], "wq", axis=1, tiled=True),
    )


def head_split(matrix, seq_count):
    row_count, model_width = matrix.shape
    return matrix.reshape(seq_count, row_count // seq_count, HEADS, model_width // HEADS)


def attention_scores(queries, keys_low, lengths):
    seq_count = lengths.shape[0]
    split_q = head_split(queries, seq_count)
    scores = jnp.einsum(
        "sqhc,skhc->shqk",
        split_q,
        head_split(keys_low, seq_count),
        preferred_element_type=jnp.float32,
    )
    scores = scores * split_q.shape[3] ** (-0.5)
    live_mask = jnp.arange(split_q.shape[1])[None, :] < lengths[:, None]
    return jnp.where(live_mask[:, None, None, :], scores, NEGATIVE)


def first_rows(matrix, seq_count):
    row_count, width = matrix.shape
    return matrix.reshape(seq_count, row_count // seq_count, width)[:, 0, :]


def encode_forward(token_rows, lengths, weights):
    (
        query_key_value_weight,
        attention_output_weight,
        up_weight,
        down_weight,
        vectors,
        hidden_bias,
    ) = weights
    row_count, model_width = token_rows.shape
    seq_count = lengths.shape[0]
    vec_f32 = vectors.astype(jnp.float32)
    projected_rows = jnp.dot(token_rows, query_key_value_weight, preferred_element_type=jnp.float32)
    queries = (projected_rows[:, :model_width] + vec_f32[0]).astype(jnp.bfloat16)
    keys_low = projected_rows[:, model_width : 2 * model_width].astype(jnp.bfloat16)
    values = (projected_rows[:, 2 * model_width :] + vec_f32[1]).astype(jnp.bfloat16)
    scores = attention_scores(queries, keys_low, lengths)
    totals = jax.nn.logsumexp(scores, axis=-1, keepdims=True)
    soft_low = jnp.exp(scores - totals).astype(jnp.bfloat16)
    attended_tokens = jnp.einsum(
        "shqk,skhc->sqhc",
        soft_low,
        head_split(values, seq_count),
        preferred_element_type=jnp.float32,
    )
    attended_tokens = attended_tokens.reshape(row_count, model_width).astype(jnp.bfloat16)
    residual_branch = (
        jnp.dot(attended_tokens, attention_output_weight, preferred_element_type=jnp.float32)
        + vec_f32[2]
    )
    pre_one = token_rows.astype(jnp.float32) + residual_branch
    first_normed = layer_norm(pre_one, vec_f32[3], vec_f32[4])
    normed_low = first_normed.astype(jnp.bfloat16)
    hidden_rows = jnp.dot(
        normed_low, up_weight, preferred_element_type=jnp.float32
    ) + hidden_bias.astype(jnp.float32)
    activated_hidden = smooth_gate(hidden_rows).astype(jnp.bfloat16)
    feedforward_output = (
        jnp.dot(activated_hidden, down_weight, preferred_element_type=jnp.float32) + vec_f32[5]
    )
    pre_two = first_normed + feedforward_output
    encoded_low = layer_norm(pre_two, vec_f32[6], vec_f32[7]).astype(jnp.bfloat16)
    soft_first = jnp.exp(scores[:, :, 0, :] - totals[:, :, 0, :])
    stored = (
        first_rows(queries, seq_count),
        keys_low,
        values,
        soft_first,
        first_rows(attended_tokens, seq_count),
        first_rows(pre_one, seq_count),
        first_rows(normed_low, seq_count),
        first_rows(hidden_rows, seq_count),
        first_rows(activated_hidden, seq_count),
        first_rows(pre_two, seq_count),
    )
    return (encoded_low, stored)


def norm_back(pre, gain_row, grad_out):
    centred = pre - jnp.mean(pre, axis=-1, keepdims=True)
    inverse = lax.rsqrt(jnp.mean(centred * centred, axis=-1, keepdims=True) + EPSILON)
    scaled = grad_out * gain_row
    inner = jnp.mean(scaled * centred, axis=-1, keepdims=True)
    grad_in = inverse * (
        scaled - jnp.mean(scaled, axis=-1, keepdims=True) - centred * (inverse * inverse * inner)
    )
    return (grad_in, jnp.sum(grad_out * centred * inverse, axis=0), jnp.sum(grad_out, axis=0))


def encode_backward(token_rows, weights, stored, grad_first):
    (
        query_key_value_weight,
        attention_output_weight,
        up_weight,
        down_weight,
        vectors,
        hidden_bias,
    ) = weights
    (
        queries,
        keys_low,
        values,
        soft_first,
        attended,
        pre_one,
        normed_low,
        hidden_rows,
        activated_hidden,
        pre_two,
    ) = stored
    seq_count, model_width = queries.shape
    seq_length = token_rows.shape[0] // seq_count
    head_width = model_width // HEADS
    scaling = head_width ** (-0.5)
    vec_f32 = vectors.astype(jnp.float32)
    grad_two, gain_two, shift_two = norm_back(pre_two, vec_f32[6], grad_first)
    grad_ffn = grad_two.astype(jnp.bfloat16)
    grad_activated = jnp.einsum(
        "rd,fd->rf", grad_ffn, down_weight, preferred_element_type=jnp.float32
    )
    grad_hidden = jax.vjp(smooth_gate, hidden_rows)[1](grad_activated)[0].astype(jnp.bfloat16)
    grad_normed = grad_two + jnp.einsum(
        "rf,df->rd", grad_hidden, up_weight, preferred_element_type=jnp.float32
    )
    grad_one, gain_one, shift_one = norm_back(pre_one, vec_f32[3], grad_normed)
    grad_branch = grad_one.astype(jnp.bfloat16)
    grad_attended = jnp.einsum(
        "re,de->rd", grad_branch, attention_output_weight, preferred_element_type=jnp.float32
    ).astype(jnp.bfloat16)
    grad_heads = grad_attended.reshape(seq_count, HEADS, head_width)
    grad_soft = jnp.einsum(
        "shc,skhc->shk",
        grad_heads,
        head_split(values, seq_count),
        preferred_element_type=jnp.float32,
    )
    row_inner = jnp.sum(soft_first * grad_soft, axis=-1, keepdims=True)
    grad_scores = (soft_first * (grad_soft - row_inner)).astype(jnp.bfloat16)
    soft_low = soft_first.astype(jnp.bfloat16)
    grad_queries = (
        jnp.einsum(
            "shk,skhc->shc",
            grad_scores,
            head_split(keys_low, seq_count),
            preferred_element_type=jnp.float32,
        )
        * scaling
    )
    grad_q_low = grad_queries.reshape(seq_count, model_width).astype(jnp.bfloat16)
    tokens = token_rows.reshape(seq_count, seq_length, model_width)
    both = jnp.concatenate([grad_scores, soft_low], axis=1)
    mixed = jnp.einsum("sgk,skd->sgd", both, tokens, preferred_element_type=jnp.float32).astype(
        jnp.bfloat16
    )
    scaled_queries = (queries.astype(jnp.float32) * scaling).astype(jnp.bfloat16)
    split_weight = query_key_value_weight.reshape(model_width, 3, HEADS, head_width)
    back_rows = jnp.concatenate(
        [
            jnp.einsum(
                "shc,dhc->shd",
                scaled_queries.reshape(seq_count, HEADS, head_width),
                split_weight[:, 1],
                preferred_element_type=jnp.float32,
            ),
            jnp.einsum(
                "shc,dhc->shd",
                grad_heads,
                split_weight[:, 2],
                preferred_element_type=jnp.float32,
            ),
        ],
        axis=1,
    ).astype(jnp.bfloat16)
    grad_tokens = jnp.einsum("sgk,sgd->skd", both, back_rows, preferred_element_type=jnp.float32)
    first_extra = grad_one + jnp.einsum(
        "se,de->sd",
        grad_q_low,
        query_key_value_weight[:, :model_width],
        preferred_element_type=jnp.float32,
    )
    is_first = (jnp.arange(seq_length) == 0)[None, :, None]
    grad_tokens = grad_tokens + jnp.where(is_first, first_extra[:, None, :], 0.0)
    soft_total = jnp.sum(soft_low.astype(jnp.float32), axis=-1, keepdims=True)
    vector_parts = jnp.stack(
        [
            jnp.sum(grad_q_low.astype(jnp.float32), axis=0),
            jnp.sum(grad_heads.astype(jnp.float32) * soft_total, axis=0).reshape(model_width),
            jnp.sum(grad_branch.astype(jnp.float32), axis=0),
            gain_one,
            shift_one,
            jnp.sum(grad_ffn.astype(jnp.float32), axis=0),
            gain_two,
            shift_two,
        ]
    )
    bias_part = jnp.sum(grad_hidden.astype(jnp.float32), axis=0)
    left = (
        activated_hidden,
        normed_low,
        attended,
        jnp.concatenate(
            [jnp.broadcast_to(tokens[:, :1, :], (seq_count, HEADS, model_width)), mixed], axis=1
        ),
    )
    right = (
        grad_ffn,
        grad_hidden,
        grad_branch,
        jnp.concatenate([grad_q_low, scaled_queries, grad_attended], axis=1),
    )
    return (
        grad_tokens.reshape(token_rows.shape),
        left,
        right,
        vector_parts,
        bias_part,
    )


def left_message(left, wq_size, np_size):
    activated, normed, attended, mixed = left
    rows, groups, model_width = mixed.shape
    part = model_width // wq_size
    columns = 3 * model_width // np_size
    head_width = model_width // HEADS
    group = math.gcd(head_width, columns)
    mixed = jnp.repeat(mixed, head_width // group, axis=1)
    mixed = mixed.reshape(rows, np_size, columns // group, wq_size, part)
    mixed = mixed.transpose(3, 1, 0, 2, 4).reshape(wq_size, np_size, rows, columns // group * part)

    def same(matrix):
        pieces = matrix.reshape(rows, wq_size, -1).transpose(1, 0, 2)
        return jnp.broadcast_to(pieces[:, None], (wq_size, np_size) + pieces.shape[1:])

    return jnp.concatenate([same(activated), same(normed), same(attended), mixed], axis=3)


def right_message(right, np_size):
    rows = right[0].shape[0]
    return jnp.concatenate(
        [member.reshape(rows, np_size, -1).transpose(1, 0, 2) for member in right], axis=2
    )


def weight_grads(left, right, model_width, ff_width, wq_size, np_size):
    rows = left.shape[0]
    part, ff_part = model_width // wq_size, ff_width // wq_size
    columns = 3 * model_width // np_size
    group = math.gcd(model_width // HEADS, columns)
    right_sizes = (model_width // np_size, ff_width // np_size, model_width // np_size)
    cut = [ff_part, ff_part + part, ff_part + 2 * part]
    activated, normed, attended, mixed = jnp.split(left, cut, axis=1)
    cut = [right_sizes[0], right_sizes[0] + right_sizes[1], sum(right_sizes)]
    grad_ffn, grad_hidden, grad_branch, grad_projected = jnp.split(right, cut, axis=1)

    def outer(one, two):
        return jnp.einsum("sd,se->de", one, two, preferred_element_type=jnp.float32)

    w_qkv = jnp.einsum(
        "sgd,sgc->dgc",
        mixed.reshape(rows, columns // group, part),
        grad_projected.reshape(rows, columns // group, group),
        preferred_element_type=jnp.float32,
    ).reshape(part, columns)
    return (
        w_qkv,
        outer(attended, grad_branch),
        outer(normed, grad_hidden),
        outer(activated, grad_ffn),
    )


BLK=256
F32=jnp.float32; BF=jnp.bfloat16
NEG=-1e30; EPS=1e-12
def dot(a,b): return jnp.dot(a,b,preferred_element_type=F32)
def norm(u,g,b):
    c=u-jnp.mean(u,axis=-1,keepdims=True)
    s=jnp.mean(c*c,axis=-1,keepdims=True)
    return c*lax.rsqrt(s+EPS)*g+b
def put_first(ref, e, i, cols, v):
    if e==1:
        ref[pl.ds(8+i,1),cols]=v[0:1]
    else:
        for j in range(4): ref[pl.ds(4*i+j,1),cols]=v[64*j:64*j+1]
def make_bias(bias_ref, slot, lens, slots):
    n=BLK//slots
    key=lax.broadcasted_iota(jnp.int32,(BLK,BLK),0)
    qry=lax.broadcasted_iota(jnp.int32,(BLK,BLK),1)
    ok=key<lens[0]
    if n>1:
        ok=ok&(qry<slots)
        for j in range(1,n):
            ok=ok|((key>=j*slots)&(key<j*slots+lens[j])&(qry>=j*slots)&(qry<(j+1)*slots))
    bias_ref[...]=jnp.where(ok,0.0,NEG)
def attend_block(row, x_ref, wqkv, vec, bias_ref, k_ref, v_ref, att_ref, q0_ref, e, i):
    x=x_ref[pl.ds(row,BLK),:]
    for g in range(3):
        cs=pl.ds(g*256,256)
        q4=dot(x,wqkv[:,g*256:g*256+256])+vec[0:1,g*256:g*256+256]
        q4=q4.astype(BF)
        k4=dot(x,wqkv[:,768+g*256:768+g*256+256]).astype(BF)
        v4=(dot(x,wqkv[:,1536+g*256:1536+g*256+256])+vec[1:2,g*256:g*256+256]).astype(BF)
        k_ref[pl.ds(row,BLK),cs]=k4
        v_ref[pl.ds(row,BLK),cs]=v4
        put_first(q0_ref,e,i,slice(g*256,g*256+256),q4.astype(F32))
        qT=(q4.astype(F32)*0.125).T.astype(BF)
        vT=v4.astype(F32).T.astype(BF)
        lane=lax.broadcasted_iota(jnp.int32,(BLK,256),1)
        outs=[]
        for h in range(4):
            kh=jnp.where((lane>=64*h)&(lane<64*h+64),k4,jnp.zeros_like(k4))
            s=dot(kh,qT)+bias_ref[...]
            m=jnp.max(s,axis=0,keepdims=True)
            p=jnp.exp(s-m)
            l=jnp.sum(p,axis=0,keepdims=True)
            o=dot(vT[64*h:64*h+64,:],p.astype(BF))
            outs.append(o*(1.0/l))
        oT=jnp.concatenate(outs,axis=0)
        att_ref[pl.ds(row,BLK),cs]=oT.T.astype(BF)
def out_block(row, x_ref, att_ref, wo, vec, n_ref, a0_ref, p1_ref, e, i):
    att=att_ref[pl.ds(row,BLK),:]
    put_first(a0_ref,e,i,slice(None),att.astype(F32))
    pre=x_ref[pl.ds(row,BLK),:].astype(F32)+dot(att,wo[...])+vec[2:3,:]
    put_first(p1_ref,e,i,slice(None),pre)
    n_ref[pl.ds(row,BLK),:]=norm(pre,vec[3:4,:],vec[4:5,:])
def gelu(u):
    return 0.5*u*(1.0+jnp.tanh(0.7978845608028654*(u+0.044715*(u*u*u))))
def up_block(row, n_ref, wup, hb, act_ref, h0_ref, e, i, arow):
    nl=n_ref[pl.ds(row,BLK),:].astype(BF)
    for t in range(12):
        cs=slice(t*256,t*256+256)
        h=dot(nl,wup[:,cs])+hb[0:1,cs]
        put_first(h0_ref,e,i,cs,h)
        act_ref[pl.ds(arow,BLK),cs]=gelu(h).astype(BF)
def down_block(row, n_ref, act_ref, wdown, vec, o_ref, p2_ref, hd_ref, e, i, arow):
    f=dot(act_ref[pl.ds(arow,BLK),:],wdown[...])+vec[5:6,:]
    pre=n_ref[pl.ds(row,BLK),:]+f
    put_first(p2_ref,e,i,slice(None),pre)
    enc=norm(pre,vec[6:7,:],vec[7:8,:])
    put_first(hd_ref,e,i,slice(None),enc)
    o_ref[pl.ds(row,BLK),:]=enc.astype(BF)

def dot_nt(a,b): return lax.dot_general(a,b,(((1,),(1,)),((),())),preferred_element_type=F32)
def gelu_slope(u):
    t=jnp.tanh(0.7978845608028654*(u+0.044715*(u*u*u)))
    return 0.5*(1.0+t)+0.5*u*(1.0-t*t)*(0.7978845608028654*(1.0+0.134145*(u*u)))
def norm_grad(u,g,gy):
    c=u-jnp.mean(u,axis=-1,keepdims=True)
    r=lax.rsqrt(jnp.mean(c*c,axis=-1,keepdims=True)+EPS)
    t=gy*g
    gu=r*(t-jnp.mean(t,axis=-1,keepdims=True)-c*(r*r)*jnp.mean(t*c,axis=-1,keepdims=True))
    return gu, jnp.sum(gy*c*r,axis=0,keepdims=True), jnp.sum(gy,axis=0,keepdims=True)
def heads_apart(rows, count):
    n=rows.shape[0]
    wide=jnp.concatenate([jnp.broadcast_to(rows[i:i+1],(16,768)) for i in range(n)],axis=0)
    r=lax.broadcasted_iota(jnp.int32,wide.shape,0)%16
    l=lax.broadcasted_iota(jnp.int32,wide.shape,1)//64
    return jnp.where(r==l,wide,0.0)
def pick_matrix(off, lane0):
    r=lax.broadcasted_iota(jnp.int32,(256,128),0); l=lax.broadcasted_iota(jnp.int32,(256,128),1)
    return jnp.where((r-off==l-lane0)&(l>=lane0)&(l<lane0+48),1.0,0.0).astype(BF)
MESH = pl.DeviceIdType.MESH

class Gather:
    def __init__(self, units, ins, outs, send, recv):
        self.units, self.ins, self.outs, self.send, self.recv = units, ins, outs, send, recv
        w, self.y = lax.axis_index("wq"), lax.axis_index("np")
        self.w = w
        self.z, self.x, self.c = w // 4, (w // 2) % 2, w % 2
        self.pending = {}
    def dev(self, dz=0, fx=False, fy=False, fc=False):
        x = 1 - self.x if fx else self.x
        c = 1 - self.c if fc else self.c
        y = 1 - self.y if fy else self.y
        return ((self.z + dz) * 4 + x * 2 + c, y)
    def barrier(self):
        bar = pltpu.get_barrier_semaphore()
        def sig(**k): pl.semaphore_signal(bar, inc=1, device_id=self.dev(**k), device_id_type=MESH)
        sig(fx=True); sig(fy=True); sig(fc=True)
        @pl.when(self.z > 0)
        def _(): sig(dz=-1)
        @pl.when(self.z < 3)
        def _(): sig(dz=1)
        pl.semaphore_wait(bar, 3 + (self.z + 3) // 4 + (6 - self.z) // 4)
    def view(self, u, z=None, x=None, y=None, c=None):
        a, e, kind, r0, rn = self.units[u]
        o = self.outs[a]
        r, w = self.ins[a].shape[1:]
        zs = slice(None) if z is None else z
        xs = slice(None) if x is None else x
        cs = slice(None) if y is None else pl.ds(pl.multiple_of(y * w, 128), w)
        return o.at[e, zs, xs, pl.ds(pl.multiple_of((self.c if c is None else c) * r + r0, 16), rn), cs]
    def copy(self, u, sem, src, dst, dev):
        return pltpu.make_async_remote_copy(src_ref=src, dst_ref=dst, send_sem=self.send.at[u, sem], recv_sem=self.recv.at[u, sem], device_id=dev, device_id_type=MESH)
    def own_src(self, u):
        a, e, kind, r0, rn = self.units[u]
        return self.ins[a].at[e, pl.ds(r0, rn)]
    def zview(self, u, core, z):
        kind = self.units[u][2]
        if not kind: return self.view(u, z=z, x=self.x, y=self.y)
        if core == 0: return self.view(u, z=z, x=None, y=self.y)
        return self.view(u, z=z, x=self.x, y=None)
    def step(self, u, s):
        for core in (0, 1):
            pl.when(self.c == core)(lambda core=core: self._step(u, s, core))
    def A(self, core): return dict(fx=True) if core == 0 else dict(fy=True)
    def B(self, core): return dict(fy=True) if core == 0 else dict(fx=True)
    def a_src(self, u, core):
        kind = self.units[u][2]
        z = None if not kind else self.z
        return self.view(u, z=z, x=self.x, y=self.y)
    def a_got(self, u, core):
        kind = self.units[u][2]
        z = None if not kind else self.z
        return self.view(u, z=z, x=1 - self.x, y=self.y) if core == 0 else self.view(u, z=z, x=self.x, y=1 - self.y)
    def b_src(self, u, core):
        return self.view(u, x=None, y=self.y) if core == 0 else self.view(u, x=self.x, y=None)
    def b_got(self, u, core):
        return self.view(u, x=None, y=1 - self.y) if core == 0 else self.view(u, x=1 - self.x, y=None)
    def local(self, u, sem, ref):
        self.copy(u, sem, ref, ref, self.dev(fc=True)).start()
    def z_send(self, u, core, hop):
        z = self.z
        @pl.when((z - hop >= 0) & (z + 1 <= 3))
        def _():
            v = self.zview(u, core, z - hop)
            src = self.own_src(u) if (hop == 0 and not self.units[u][2]) else v
            self.copy(u, 2 + hop, src, v, self.dev(dz=1)).start()
        @pl.when((z + hop <= 3) & (z - 1 >= 0))
        def _():
            v = self.zview(u, core, z + hop)
            src = self.own_src(u) if (hop == 0 and not self.units[u][2]) else v
            self.copy(u, 5 + hop, src, v, self.dev(dz=-1)).start()
    def z_wait(self, u, core, hop):
        z = self.z
        @pl.when(z - 1 - hop >= 0)
        def _():
            v = self.zview(u, core, z - 1 - hop)
            self.copy(u, 2 + hop, v, v, self.dev(fc=True)).wait_recv()
            self.local(u, 11 + hop, v)
        @pl.when(z + 1 + hop <= 3)
        def _():
            v = self.zview(u, core, z + 1 + hop)
            self.copy(u, 5 + hop, v, v, self.dev(fc=True)).wait_recv()
            self.local(u, 14 + hop, v)
    def _step(self, u, s, core):
        F = not self.units[u][2]
        own = self.view(u, z=self.z, x=self.x, y=self.y)
        if s == 0:
            src = self.own_src(u)
            self.copy(u, 8, src, own, self.dev(fc=True)).start()
            pltpu.make_async_copy(src, own, self.send.at[u, 17]).start()
            if F:
                self.z_send(u, core, 0)
            else:
                self.copy(u, 0, src, own, self.dev(**self.A(core))).start()
        if s == 1:
            pltpu.make_async_copy(self.own_src(u), own, self.send.at[u, 17]).wait()
            if F:
                self.z_wait(u, core, 0); self.z_send(u, core, 1)
            else:
                g = self.a_got(u, core)
                self.copy(u, 0, g, g, self.dev(fc=True)).wait_recv()
                self.z_send(u, core, 0)
                self.local(u, 9, g)
        if s == 2:
            if F: self.z_wait(u, core, 1); self.z_send(u, core, 2)
            else: self.z_wait(u, core, 0); self.z_send(u, core, 1)
        if s == 3:
            if F:
                self.z_wait(u, core, 2)
                v = self.a_src(u, core)
                self.copy(u, 0, v, v, self.dev(**self.A(core))).start()
            else:
                self.z_wait(u, core, 1); self.z_send(u, core, 2)
        if s == 4:
            if F:
                g = self.a_got(u, core)
                self.copy(u, 0, g, g, self.dev(fc=True)).wait_recv()
            else:
                self.z_wait(u, core, 2)
            v = self.b_src(u, core)
            self.copy(u, 1, v, v, self.dev(**self.B(core))).start()
            if F: self.local(u, 9, g)
        if s == 5:
            g = self.b_got(u, core)
            self.copy(u, 1, g, g, self.dev(fc=True)).wait_recv()
            self.local(u, 10, g)
        if s == 6:
            self.finish_recv(u, core); self.finish_send(u, core)
    def finish_recv(self, u, core):
        other = 1 - core
        c = 1 - self.c
        kind = self.units[u][2]
        def got(sem, v): self.copy(u, sem, v, v, self.dev(fc=True)).wait_recv()
        sv = lambda **k: self.view(u, c=c, **k)
        got(8, sv(z=self.z, x=self.x, y=self.y))
        za = None if not kind else self.z
        got(9, sv(z=za, x=1 - self.x, y=self.y) if other == 0 else sv(z=za, x=self.x, y=1 - self.y))
        got(10, sv(x=None, y=1 - self.y) if other == 0 else sv(x=1 - self.x, y=None))
        def zv(z):
            if not kind: return sv(z=z, x=self.x, y=self.y)
            return sv(z=z, x=None, y=self.y) if other == 0 else sv(z=z, x=self.x, y=None)
        for hop in range(3):
            pl.when(self.z - 1 - hop >= 0)(lambda hop=hop: got(11 + hop, zv(self.z - 1 - hop)))
            pl.when(self.z + 1 + hop <= 3)(lambda hop=hop: got(14 + hop, zv(self.z + 1 + hop)))
    def finish_send(self, u, core):
        def sent(sem, v): self.copy(u, sem, v, v, self.dev(fc=True)).wait_send()
        own = self.view(u, z=self.z, x=self.x, y=self.y)
        sent(8, own)
        sent(0, self.a_src(u, core)); sent(1, self.b_src(u, core))
        sent(9, self.a_got(u, core)); sent(10, self.b_got(u, core))
        z = self.z
        for hop in range(3):
            pl.when((z - hop >= 0) & (z + 1 <= 3))(lambda hop=hop: sent(2 + hop, self.zview(u, core, z - hop)))
            pl.when((z + hop <= 3) & (z - 1 >= 0))(lambda hop=hop: sent(5 + hop, self.zview(u, core, z + hop)))
            pl.when(z - 1 - hop >= 0)(lambda hop=hop: sent(11 + hop, self.zview(u, core, z - 1 - hop)))
            pl.when(z + 1 + hop <= 3)(lambda hop=hop: sent(14 + hop, self.zview(u, core, z + 1 + hop)))

class Place:
    def __init__(self):
        self.w=lax.axis_index("wq"); self.y=lax.axis_index("np")
        self.z,self.x,self.c=self.w//4,(self.w//2)%2,self.w%2
        self.me=self.w*2+self.y
    def dev(self, z=None, fx=False, fy=False, fc=False):
        x=1-self.x if fx else self.x
        c=1-self.c if fc else self.c
        y=1-self.y if fy else self.y
        return ((self.z if z is None else z)*4+x*2+c, y)

class HeadGather:
    def __init__(self,pos,buf,send,recv):
        self.pos,self.buf,self.send,self.recv=pos,buf,send,recv
    def rc(self,sem,ref,dev):
        return pltpu.make_async_remote_copy(src_ref=ref,dst_ref=ref,send_sem=self.send.at[sem],recv_sem=self.recv.at[sem],device_id=dev,device_id_type=MESH)
    def phase(self,s):
        pos,buf=self.pos,self.buf
        z,x,c,y=pos.z,pos.x,pos.c,pos.y
        sib=pos.dev(fc=True)
        def arrived(sem,ref): self.rc(sem,ref,sib).wait_recv()
        own=buf.at[z,x,c,y]
        col=lambda fx,fy,core: buf.at[:,1-x if fx else x,core,1-y if fy else y]
        ways=((3,True,True),(4,True,False),(5,False,True))
        if s==0:
            for k in (1,2,3): self.rc(k-1,own,pos.dev(z=(z+k)%4)).start()
        if s==1:
            for k in (1,2,3): arrived(k-1,buf.at[(z+4-k)%4,x,c,y])
            for sem,fx,fy in ways: self.rc(sem,col(False,False,c),pos.dev(fx=fx,fy=fy)).start()
            self.rc(6,col(False,False,c),sib).start()
        if s==2:
            for sem,fx,fy in ways[1:]+ways[:1]:
                arrived(sem,col(fx,fy,c)); self.rc(sem+4,col(fx,fy,c),sib).start()
        if s==3:
            o=1-c
            arrived(6,col(False,False,o))
            for sem,fx,fy in ways: arrived(sem+4,col(fx,fy,o))
            for k in (1,2,3): self.rc(k-1,own,sib).wait_send()
            for sem in (3,4,5,6): self.rc(sem,col(False,False,c),sib).wait_send()
            for sem,fx,fy in ways: self.rc(sem+4,col(fx,fy,c),sib).wait_send()

CHUNKS=((0,1152,False),(1152,512,False),(1664,256,True),(1920,768,False),(2688,384,True))
class RightGather:
    def __init__(self,pos,src,buf,send,recv):
        self.pos,self.src,self.buf,self.send,self.recv=pos,src,buf,send,recv
    def rc(self,ch,sem,src,dst,dev):
        return pltpu.make_async_remote_copy(src_ref=src,dst_ref=dst,send_sem=self.send.at[ch,sem],recv_sem=self.recv.at[ch,sem],device_id=dev,device_id_type=MESH)
    def view(self,ch,z=None,x=None,c=None,y=None):
        p=self.pos; c0,w,_=CHUNKS[ch]
        f=lambda v: slice(None) if v is None else v
        return self.buf.at[f(z),p.x if x is None else x,p.c if c is None else c,f(y),:,c0:c0+w]
    def half(self,ch,y):
        c0,w,_=CHUNKS[ch]
        return self.src.at[y,:,c0:c0+w]
    def column(self,ch,z,c=None):
        p=self.pos; c0,w,x_first=CHUNKS[ch]
        return self.buf.at[z,slice(None) if x_first else p.x,p.c if c is None else c,:,:,c0:c0+w]
    def across(self,ch,x,c=None):
        p=self.pos
        return self.view(ch,z=p.z if CHUNKS[ch][2] else None,x=x,c=c)
    def step(self,ch,s):
        p=self.pos; z,y=p.z,p.y; x_first=CHUNKS[ch][2]
        sib=p.dev(fc=True)
        def arrived(sem,v): self.rc(ch,sem,v,v,sib).wait_recv()
        def local(sem,v): self.rc(ch,sem,v,v,sib).start()
        def z_send(hop):
            @pl.when((z-hop>=0)&(z+1<=3))
            def _():
                v=self.column(ch,z-hop); self.rc(ch,2+hop,v,v,p.dev(z=z+1)).start()
            @pl.when((z+hop<=3)&(z-1>=0))
            def _():
                v=self.column(ch,z+hop); self.rc(ch,5+hop,v,v,p.dev(z=z-1)).start()
        def z_wait(hop):
            @pl.when(z-1-hop>=0)
            def _():
                v=self.column(ch,z-1-hop); arrived(2+hop,v); local(9+hop,v)
            @pl.when(z+1+hop<=3)
            def _():
                v=self.column(ch,z+1+hop); arrived(5+hop,v); local(12+hop,v)
        def x_send():
            v=self.across(ch,p.x); self.rc(ch,1,v,v,p.dev(fx=True)).start()
        def x_wait():
            g=self.across(ch,1-p.x); arrived(1,g); local(15,g)
        own=self.view(ch,z=z,y=y)
        if s==0:
            self.rc(ch,0,self.half(ch,1-y),own,p.dev(fy=True)).start()
            pltpu.make_async_copy(self.half(ch,y),own,self.send.at[ch,16]).start()
        if s==1:
            pltpu.make_async_copy(self.half(ch,y),own,self.send.at[ch,16]).wait()
            arrived(0,self.view(ch,z=z,y=1-y))
            if x_first: x_send()
            else: z_send(0)
            local(8,self.view(ch,z=z))
        if x_first:
            if s==2: x_wait(); z_send(0)
            if s==3: z_wait(0); z_send(1)
            if s==4: z_wait(1); z_send(2)
            if s==5: z_wait(2)
        else:
            if s==2: z_wait(0); z_send(1)
            if s==3: z_wait(1); z_send(2)
            if s==4: z_wait(2); x_send()
            if s==5: x_wait()
        if s==6:
            o=1-p.c
            arrived(8,self.view(ch,z=z,c=o)); arrived(15,self.across(ch,1-p.x,c=o))
            def sent(sem,v): self.rc(ch,sem,v,v,sib).wait_send()
            sent(0,own); sent(1,self.across(ch,p.x)); sent(8,self.view(ch,z=z)); sent(15,self.across(ch,1-p.x))
            for hop in range(3):
                pl.when(z-1-hop>=0)(lambda hop=hop: arrived(9+hop,self.column(ch,z-1-hop,c=o)))
                pl.when(z+1+hop<=3)(lambda hop=hop: arrived(12+hop,self.column(ch,z+1+hop,c=o)))
                pl.when((z-hop>=0)&(z+1<=3))(lambda hop=hop: sent(2+hop,self.column(ch,z-hop)))
                pl.when((z+hop<=3)&(z-1>=0))(lambda hop=hop: sent(5+hop,self.column(ch,z+hop)))
                pl.when(z-1-hop>=0)(lambda hop=hop: sent(9+hop,self.column(ch,z-1-hop)))
                pl.when(z+1+hop<=3)(lambda hop=hop: sent(12+hop,self.column(ch,z+1+hop)))

class LeftCopies:
    def __init__(self,pos,left,buf,spans,send,recv):
        self.pos,self.left,self.buf,self.spans,self.send,self.recv=pos,left,buf,spans,send,recv
    def each(self,d,go):
        t=(self.pos.me+d)%32
        w,y=t//2,t%2
        for half,(r0,n) in enumerate(self.spans):
            @pl.when(y==half)
            def _():
                go(pltpu.make_async_remote_copy(src_ref=self.left.at[w,pl.ds(r0,n)],dst_ref=self.buf.at[self.pos.me,pl.ds(0,n)],send_sem=self.send.at[d],recv_sem=self.recv.at[d],device_id=(w,y),device_id_type=MESH))
    def start(self,batch):
        def lap(k,kept):
            self.each(4*k+batch,lambda cp: cp.start()); return kept
        lax.fori_loop(0 if batch else 1,8,lap,0)
        if batch: return
        for half,(r0,n) in enumerate(self.spans):
            @pl.when(self.pos.y==half)
            def _(): self.buf[self.pos.me,0:n,:]=self.left[self.pos.w,r0:r0+n,:]
    def finish(self):
        def lap(d,kept):
            self.each(d,lambda cp: cp.wait_send())
            s=(self.pos.me+32-d)%32
            for half,(r0,n) in enumerate(self.spans):
                @pl.when(self.pos.y==half)
                def _():
                    v=self.buf.at[s,pl.ds(0,n)]
                    pltpu.make_async_remote_copy(src_ref=v,dst_ref=v,send_sem=self.send.at[d],recv_sem=self.recv.at[d],device_id=(self.pos.w,self.pos.y),device_id_type=MESH).wait_recv()
            return kept
        lax.fori_loop(1,32,lap,0)

def similarity(pos,buf,marks,loss,gr,gs_s,gt_s):
    g=buf[...].reshape(32,16,768).astype(F32)
    q=g[:,0:8].reshape(256,768).astype(BF); p=g[:,8:16].reshape(256,768).astype(BF)
    m=jnp.sum(marks[...].reshape(8,32,256),axis=0)
    m=m[0:16]+m[16:32]
    m=(m[:,0:128]+m[:,128:256]).astype(F32)
    row=lambda r: jnp.broadcast_to(jnp.concatenate([m[r:r+1],m[r+1:r+2]],axis=1),(256,256))
    qset=row(0).T; gold=row(2).T; pset=row(4)
    lane=lax.broadcasted_iota(jnp.int32,(256,256),1).astype(F32)
    is_gold=gold==lane
    usable=(qset==pset)|is_gold
    sim=dot_nt(q,p)*(768**-0.5)
    masked=jnp.where(usable,sim,NEG)
    high=jnp.max(masked,axis=1,keepdims=True)
    tot=high+jnp.log(jnp.sum(jnp.where(usable,jnp.exp(masked-high),0.0),axis=1,keepdims=True))
    gsc=jnp.sum(jnp.where(is_gold,sim,0.0),axis=1,keepdims=True)
    loss[0,0]=jnp.sum(tot-gsc)*(1.0/256)
    soft=jnp.where(usable,jnp.exp(masked-tot),0.0)
    gsim=soft-jnp.where(is_gold,1.0,0.0)
    gs_s[...]=gsim; gt_s[...]=gsim.T
    me8=pl.ds(pl.multiple_of(pos.me*8,8),8)
    gr[0:8,:]=dot(gs_s[me8,:].astype(BF),p)*(768**-0.5)
    gr[8:16,:]=dot(gt_s[me8,:].astype(BF),q)*(768**-0.5)

EARLY=((0,16),(0,112)); LATE=((0,64),(48,64))
SLOTS=(64,256); NB=(2,6)
def window(s):
    w=min(48*s//128*128,128)
    return w,48*s-w
def two(ref,e,w): return jnp.concatenate([ref[e,w//128],ref[e,w//128+1]],axis=1)
def select_rows(ref,s):
    w,off=window(s)
    cat=lambda e: jnp.concatenate([two(ref,e,w),two(ref,e,w+384)],axis=0).astype(BF)
    m=dot(cat(0),pick_matrix(off,0))+dot(cat(1),pick_matrix(off,64))
    n=ref.shape[2]
    return m[0:n],m[n:2*n]
def select_wide(ref,s):
    w,off=window(s)
    cat=lambda e: jnp.concatenate([ref[e,:,384*m+w:384*m+w+256] for m in range(8)],axis=0).astype(BF)
    m=dot(cat(0),pick_matrix(off,0))+dot(cat(1),pick_matrix(off,64))
    return [m[8*k:8*k+8] for k in range(8)]
def early_messages(ls,left):
    for s in range(8):
        for k,r in enumerate(select_rows(ls,s)): left[s+8*k]=r.astype(BF)
def late_messages(ll,lb,stage,left):
    for j in range(16): stage[j,0:8,:]=jnp.zeros((8,128),F32)
    for s in range(8):
        for m,r in enumerate(select_wide(lb,s)):
            n=8*m+s
            stage[n//4,n%4:n%4+1,:]=r[0:1]
    for s in range(8):
        for k,r in enumerate(select_rows(ll,s)):
            j=s+8*k
            left[j,0:48,:]=r[0:48].astype(BF); left[j,64:112,:]=r[48:96].astype(BF)
            left[j,48:64,:]=jnp.concatenate([r[96:104],stage[j,0:8]],axis=0).astype(BF)

def early_block(e,i,lens,K,X,qa_s,P_s,ls):
    slots=SLOTS[e]; n=256//slots; R=16*n; row=i*256; pr=(96 if e==0 else 0)+i*R
    k=K[row:row+256,:]; x=X[row:row+256,:]
    s=dot_nt(qa_s[e,i*R:i*R+R,:],k)
    key=lax.broadcasted_iota(jnp.int32,(R,256),1)
    if n==1: ok=key<lens[i]
    else:
        grp=lax.broadcasted_iota(jnp.int32,(R,256),0)//16
        ok=(grp<0)
        for j in range(n): ok=ok|((grp==j)&(key>=j*slots)&(key<j*slots+lens[i*n+j]))
    s=jnp.where(ok,s,NEG)
    p=jnp.exp(s-jnp.max(s,axis=1,keepdims=True))
    p=p*(1.0/jnp.sum(p,axis=1,keepdims=True))
    P_s[pr:pr+R,:]=p
    mix=dot(p.astype(BF),x)
    for j in range(n):
        slot=i*n+j
        first=x[j*slots:j*slots+1].astype(F32)
        for c in range(6):
            cc=slice(128*c,128*c+128)
            ls[e,c,pl.ds(16+slot,12,stride=8),:]=mix[16*j:16*j+12,cc]
            ls[e,c,slot:slot+1,:]=first[:,cc]
def late_block(e,i,K,V,X,ga_s,P_s,ll,gq_s,sv_s,tmix):
    slots=SLOTS[e]; n=256//slots; R=16*n; row=i*256; pr=(96 if e==0 else 0)+i*R
    gab=ga_s[e,i*R:i*R+R,:]
    p=P_s[pr:pr+R,:]
    gs=dot_nt(gab,V[row:row+256,:])
    gs=p*(gs-jnp.sum(p*gs,axis=1,keepdims=True))
    gsb=gs.astype(BF); pb=p.astype(BF)
    tmix[i,0:R,:]=gsb; tmix[i,R:2*R,:]=pb
    gq=dot(gsb,K[row:row+256,:])
    r0=lax.broadcasted_iota(jnp.int32,(R,768),0); hl=lax.broadcasted_iota(jnp.int32,(R,768),1)//64
    gq=jnp.where(r0%16==hl,gq,0.0)*0.125
    st=jnp.sum(pb.astype(F32),axis=1,keepdims=True)
    sv_s[e]=sv_s[e]+jnp.sum(st*gab.astype(F32),axis=0,keepdims=True)
    mix=dot(gsb,X[row:row+256,:])
    for j in range(n):
        slot=i*n+j
        gq_s[e,slot:slot+1,:]=jnp.sum(gq[16*j:16*j+16],axis=0,keepdims=True)
        for c in range(6): ll[e,c,pl.ds(slot,12,stride=8),:]=mix[16*j:16*j+12,128*c:128*c+128]

def colsum(m): return jnp.sum(m.astype(F32),axis=0,keepdims=True)

class Products:
    def __init__(self,pos,eb,lb,rbuf,bq,bp,wqkv,wout,win,wback,gvec,gbin,w_up,w_dn,hb):
        self.__dict__.update(locals())
    def right(self,c0,w):
        r=self.rbuf[:,:,:,:,:,c0:c0+w].reshape(32,16,w).astype(F32)
        self.bq[:,c0:c0+w]=r[:,0:8].reshape(256,w).astype(BF)
        self.bp[:,c0:c0+w]=r[:,8:16].reshape(256,w).astype(BF)
    def pair(self,buf,r0):
        t=buf[:,r0:r0+16,:].astype(F32)
        return [t[:,8*i:8*i+8].reshape(256,128) for i in (0,1)]
    def put(self,out,rows,cols,tt,c0,w):
        tt=tt.T.astype(BF)
        out[0,rows,cols]=dot(tt,self.bq[:,c0:c0+w])[0:48]
        out[1,rows,cols]=dot(tt,self.bp[:,c0:c0+w])[64:112]
    def mixed(self,buf,r0,heads,col0,dst0):
        low=lax.broadcasted_iota(jnp.int32,(128,128),1)<64
        for h in range(0,heads,2):
            a,b=[v.T.astype(BF) for v in self.pair(buf,r0+8*h)]
            cs=slice(col0+64*h,col0+64*h+128); ds=slice(dst0+64*h,dst0+64*h+128)
            self.wqkv[0,:,ds]=jnp.where(low,dot(a,self.bq[:,cs]),dot(b,self.bq[:,cs]))[0:48]
            self.wqkv[1,:,ds]=jnp.where(low,dot(a,self.bp[:,cs]),dot(b,self.bp[:,cs]))[64:112]
    def feed_forward(self,e):
        b=(self.bq,self.bp)[e]; w,y=self.pos.w,self.pos.y
        nl=b[:,0:768]
        r=lax.broadcasted_iota(jnp.int32,(768,128),0); l=lax.broadcasted_iota(jnp.int32,(768,128),1)
        mine=dot(nl,jnp.where((r==48*w+l)&(l<48),1.0,0.0).astype(BF)).T[0:48].astype(BF)
        for t in range(4):
            cols=pl.ds(pl.multiple_of(y*1536+384*t,128),384)
            hid=dot(nl,self.w_up[e,:,cols])+self.hb[e,:,cols]
            gh=(dot_nt(b[:,1152:1920],self.w_dn[e,cols,:])*gelu_slope(hid)).astype(BF)
            self.win[e,:,384*t:384*t+384]=dot(mine,gh)
        cols=pl.ds(pl.multiple_of(192*w//128*128,128),256)
        act=gelu(dot(nl,self.w_up[e,:,cols])+self.hb[e,:,cols]).astype(BF).astype(F32).T.astype(BF)
        back=dot(act,b[:,pl.ds(pl.multiple_of(1152+y*384,128),384)])
        self.wback[e]=jnp.where(w%2==1,back[64:256],back[0:192])
    def second(self):
        al=slice(None)
        x0,att=self.pair(self.eb,0)
        self.put(self.wout,al,al,att,1920,384)
        @pl.when(self.pos.y==0)
        def _(): self.put(self.wqkv,al,slice(0,768),x0,2304,768)
        @pl.when(self.pos.y==1)
        def _(): self.mixed(self.eb,16,12,2304,384)
    def third(self):
        def sums(r0,half):
            vs,bs=[jnp.sum(v.reshape(32,8,128),axis=0) for v in self.pair(self.lb,r0)]
            for e in (0,1):
                ls=slice(64*e,64*e+48)
                self.gvec[e]=vs[4*half:4*half+4,ls]
                for k in (0,1): self.gbin[e:e+1,48*k:48*k+48]=bs[2*half+k:2*half+k+1,ls]
        @pl.when(self.pos.y==0)
        def _():
            self.mixed(self.lb,0,6,768,768)
            sums(48,0)
        @pl.when(self.pos.y==1)
        def _():
            self.mixed(self.lb,16,6,768,0)
            sums(0,1)

def tail_kernel(*refs):
    (ql,pln,qx_h,px_h,qk_h,qv_h,pk_h,pv_h,wqkv_h,wo_h,wup_h,wdn_h,q0,a0,p1,h0,p2,heads,marks,vec,hb,
     loss,tq,tp,uq,up_,extra,wqkv,wout,win,wback,gvec,gbin,
     kv_q,kv_p,w_qkv,w_o,w_up,w_dn,hbuf,gr,gs_s,gt_s,qa_s,ga_s,P_s,ls,ll,lb,stage,left_e,left_l,ebuf,lbuf,rs,rb,rbuf,bq,bp,gq_s,sv_s,
     msem,hsend,hrecv,esend,erecv,lsend,lrecv,rsend,rrecv)=refs
    pos=Place()
    bar=pltpu.get_barrier_semaphore()
    def lap(d,kept):
        t=(pos.me+d)%32
        pl.semaphore_signal(bar,inc=1,device_id=(t//2,t%2),device_id_type=MESH)
        return kept
    lax.fori_loop(1,32,lap,0)
    moves={}
    def move(name,src,dst): moves[name]=pltpu.make_async_copy(src,dst,msem.at[len(moves)]); moves[name].start()
    for n,(h,d) in enumerate(((pk_h,kv_p),(px_h,kv_p),(pv_h,kv_p),(qk_h,kv_q),(qx_h,kv_q),(qv_h,kv_q))): move("kxv"[n%3]+"pq"[n//3],h,d.at[n%3])
    for nm,h,d in (("dn",wdn_h,w_dn),("up",wup_h,w_up),("o",wo_h,w_o),("qkv",wqkv_h,w_qkv)):
        for e in (1,0): move(nm+str(e),h.at[e],d.at[e])
    def need(*names):
        for nm in names:
            if nm in moves: moves.pop(nm).wait()
    hbuf[pos.z,pos.x,pos.c,pos.y]=heads[...].astype(BF)
    for ref in (ls,ll,lb,gq_s,sv_s): ref[...]=jnp.zeros_like(ref)
    pl.semaphore_wait(bar,31)
    hg=HeadGather(pos,hbuf,hsend,hrecv)
    hg.phase(0)
    vv=lambda e: vec[e]
    for e in (1,0):
        rows=slice(8*e,8*e+8)
        q0s=q0[rows,:]*0.125
        qa_s[e]=heads_apart(q0s,8).astype(BF)
        nlow=norm(p1[rows,:],vv(e)[3:4],vv(e)[4:5])
        for c in range(6): ls[e,c,8:16,:]=a0[rows,128*c:128*c+128]
        for half in (0,1):
            rs[half,rows,0:768]=nlow; rs[half,rows,768:1152]=q0s[:,384*half:384*half+384]
    rb[:,:,0:1152]=rs[:,:,0:1152].astype(BF)
    rg=RightGather(pos,rb,rbuf,rsend,rrecv)
    rg.step(0,0)
    need("kp","xp")
    for i in range(2): early_block(1,i,pln,kv_p.at[0],kv_p.at[1],qa_s,P_s,ls)
    hg.phase(1)
    rg.step(0,1)
    for i in range(2,6): early_block(1,i,pln,kv_p.at[0],kv_p.at[1],qa_s,P_s,ls)
    hg.phase(2)
    need("kq","xq")
    for i in range(2): early_block(0,i,ql,kv_q.at[0],kv_q.at[1],qa_s,P_s,ls)
    early_messages(ls,left_e)
    hg.phase(3)
    rg.step(0,2)
    ec=LeftCopies(pos,left_e,ebuf,EARLY,esend,erecv)
    for k in range(4): ec.start(k)
    similarity(pos,hbuf,marks,loss,gr,gs_s,gt_s)
    rg.step(0,3)
    g2,sums,gn={}, {}, {}
    need("dn1","dn0")
    for e in (1,0):
        rows=slice(8*e,8*e+8)
        g2[e],gain2,shift2=norm_grad(p2[rows,:],vv(e)[6:7],gr[rows,:])
        gffn=g2[e].astype(BF).astype(F32)
        for half in (0,1): rs[half,rows,1152:1920]=gffn
        sums[e]=(colsum(gffn),gain2,shift2)
    rb[:,:,1152:1920]=rs[:,:,1152:1920].astype(BF)
    rg.step(1,0); rg.step(2,0)
    need("up1","up0")
    for e in (1,0):
        gh=(dot_nt(g2[e].astype(BF),w_dn[e])*gelu_slope(h0[8*e:8*e+8,:])).astype(BF)
        lb[e,0:1,:]=colsum(gh)
        gn[e]=g2[e]+dot_nt(gh,w_up[e])
    rg.step(1,1); rg.step(2,1); rg.step(0,4)
    need("o1","o0","qkv1","qkv0","vp","vq")
    g1,sums1={}, {}
    for e in (1,0):
        rows=slice(8*e,8*e+8)
        g1[e],gain1,shift1=norm_grad(p1[rows,:],vv(e)[3:4],gn[e])
        gb=g1[e].astype(BF)
        sums1[e]=(colsum(gb),gain1,shift1)
        ga=dot_nt(gb,w_o[e]).astype(BF).astype(F32)
        ga_s[e]=heads_apart(ga,8).astype(BF)
        for half in (0,1): rs[half,rows,1920:2304]=gb[:,384*half:384*half+384].astype(F32)
        rs[1,rows,2304:3072]=ga
    rg.step(1,2); rg.step(2,2)
    for i in range(0,3): late_block(1,i,kv_p.at[0],kv_p.at[2],kv_p.at[1],ga_s,P_s,ll,gq_s,sv_s,tp)
    rg.step(1,3); rg.step(2,3); rg.step(0,5)
    for i in range(3,6): late_block(1,i,kv_p.at[0],kv_p.at[2],kv_p.at[1],ga_s,P_s,ll,gq_s,sv_s,tp)
    rg.step(1,4); rg.step(2,4)
    for i in range(2): late_block(0,i,kv_q.at[0],kv_q.at[2],kv_q.at[1],ga_s,P_s,ll,gq_s,sv_s,tq)
    for e in (1,0):
        rows=slice(8*e,8*e+8)
        gql=gq_s[e].astype(BF)
        rs[0,rows,2304:3072]=gql.astype(F32)
        vs=jnp.concatenate([colsum(gql),sv_s[e,0:1],*sums1[e],*sums[e]],axis=0)
        for c in range(6): ll[e,c,96:104,:]=vs[:,128*c:128*c+128]
    rb[:,:,1920:3072]=rs[:,:,1920:3072].astype(BF)
    rg.step(3,0); rg.step(4,0)
    late_messages(ll,lb,stage,left_l)
    rg.step(3,1); rg.step(4,1)
    lc=LeftCopies(pos,left_l,lbuf,LATE,lsend,lrecv)
    lc.start(1); lc.start(3)
    rg.step(1,5); rg.step(2,5)
    for e in (1,0):
        uk=dot_nt(qa_s[e],w_qkv[e,:,768:1536]).astype(BF); uv=dot_nt(ga_s[e],w_qkv[e,:,1536:2304]).astype(BF)
        out=(uq,up_)[e]; R=16*256//SLOTS[e]
        for i in range(NB[e]):
            out[i,0:R,:]=uk[i*R:i*R+R]; out[i,R:2*R,:]=uv[i*R:i*R+R]
        extra[8*e:8*e+8,:]=g1[e]+dot_nt(gq_s[e].astype(BF),w_qkv[e,:,0:768])
    rg.step(3,2); rg.step(4,2)
    lc.start(2)
    rg.step(0,6); rg.step(1,6); rg.step(2,6)
    pr=Products(pos,ebuf,lbuf,rbuf,bq,bp,wqkv,wout,win,wback,gvec,gbin,w_up,w_dn,hb)
    pr.right(0,1920)
    rg.step(3,3); rg.step(4,3)
    lc.start(0)
    pr.feed_forward(1)
    rg.step(3,4); rg.step(4,4)
    pr.feed_forward(0)
    rg.step(3,5); rg.step(4,5)
    rg.step(3,6); rg.step(4,6)
    pr.right(1920,1152)
    ec.finish()
    pr.second()
    lc.finish()
    pr.third()

def tail_call(*a):
    S=jax.ShapeDtypeStruct; VM=pltpu.VMEM; D=pltpu.SemaphoreType.DMA
    V=pl.BlockSpec(memory_space=pltpu.VMEM); SM=pl.BlockSpec(memory_space=pltpu.SMEM); A=pl.BlockSpec(memory_space=pl.ANY)
    outs=[S((1,1),F32),S((2,128,256),BF),S((6,32,256),BF),S((2,128,768),BF),S((6,32,768),BF),S((16,768),F32),
          S((2,48,1152),F32),S((2,48,384),F32),S((2,48,1536),F32),S((2,192,384),F32),S((2,4,48),F32),S((2,96),F32)]
    scratch=[VM((3,512,768),BF),VM((3,1536,768),BF),VM((2,768,2304),BF),VM((2,768,768),BF),VM((2,768,3072),BF),VM((2,3072,768),BF),
      VM((4,2,2,2,16,768),BF),VM((16,768),F32),VM((256,256),F32),VM((256,256),F32),VM((2,128,768),BF),VM((2,128,768),BF),VM((224,256),F32),
      VM((2,6,112,128),F32),VM((2,6,112,128),F32),VM((2,8,3072),F32),VM((16,8,128),F32),VM((16,112,128),BF),VM((16,112,128),BF),
      VM((32,112,128),BF),VM((32,64,128),BF),VM((2,16,3072),F32),VM((2,16,3072),BF),VM((4,2,2,2,16,3072),BF),VM((256,3072),BF),VM((256,3072),BF),VM((2,8,768),F32),VM((2,8,768),F32),
      D((14,)),D((10,)),D((10,)),D((32,)),D((32,)),D((32,)),D((32,)),D((5,17)),D((5,17))]
    return pl.pallas_call(tail_kernel,out_shape=outs,in_specs=[SM,SM]+[A]*10+[V]*9,out_specs=[SM]+[V]*11,scratch_shapes=scratch,
      compiler_params=pltpu.CompilerParams(collective_id=2,has_side_effects=True,vmem_limit_bytes=62*2**20),name="tail")(*a)

def finish_kernel(loss_in,q_in,p_in,wqkv_in,wout_in,win_in,wback_in,gvec_in,gbin_in,tq,tp,uq,up_,extra,
                  loss,q_out,p_out,gq,gp,wqkv,wout,win,wback,gvec,gbin,slots,sem,osem,*held):
    ways=((p_in,p_out),(q_in,q_out),(win_in,win),(wqkv_in,wqkv),(wback_in,wback),(wout_in,wout))
    loads=[pltpu.make_async_copy(a,h,sem.at[0,k]) for k,((a,b),h) in enumerate(zip(ways,held))]
    stores=[pltpu.make_async_copy(h,b,sem.at[1,k]) for k,((a,b),h) in enumerate(zip(ways,held))]
    for cp in loads: cp.start()
    loss[0,0]=loss_in[0,0]
    gvec[...]=gvec_in[...]; gbin[...]=gbin_in[...]
    flying={}
    for b in range(8):
        e,i=(1,b) if b<6 else (0,b-6)
        mix,u,out=((tq,uq,gq),(tp,up_,gp))[e]
        slot=b%4
        if slot in flying: flying[slot].wait()
        slots[slot]=dot(mix[i].astype(F32).T.astype(BF),u[i])
        n=256//SLOTS[e]
        for j in range(n): slots[slot,j*SLOTS[e]:j*SLOTS[e]+1,:]+=extra[8*e+i*n+j:8*e+i*n+j+1,:]
        flying[slot]=pltpu.make_async_copy(slots.at[slot],out.at[pl.ds(i*256,256)],osem.at[slot])
        flying[slot].start()
        if 1<=b<=6:
            loads[b-1].wait(); stores[b-1].start()
    for cp in flying.values(): cp.wait()
    for cp in stores: cp.wait()
def finish_call(loss,q_out,p_out,grads,tq,tp,uq,up_,extra):
    S=jax.ShapeDtypeStruct; VM=pltpu.VMEM; D=pltpu.SemaphoreType.DMA
    V=pl.BlockSpec(memory_space=pltpu.VMEM); SM=pl.BlockSpec(memory_space=pltpu.SMEM); A=pl.BlockSpec(memory_space=pl.ANY)
    ins=(loss,q_out,p_out,*grads,tq,tp,uq,up_,extra)
    shape=lambda a: S(a.shape,a.dtype)
    outs=[shape(loss),shape(q_out),shape(p_out),S(q_out.shape,F32),S(p_out.shape,F32)]+[shape(g) for g in grads]
    return pl.pallas_call(finish_kernel,out_shape=outs,in_specs=[SM]+[A]*6+[V]*7,out_specs=[SM]+[A]*8+[V]*2,
      scratch_shapes=[VM((4,256,768),F32),D((2,6)),D((4,))]+[VM(a.shape,a.dtype) for a in (p_out,q_out,grads[2],grads[0],grads[3],grads[1])],compiler_params=pltpu.CompilerParams(vmem_limit_bytes=63*2**20),name="finish")(*ins)

STEP, LOAD, P1, P2, P3, P4 = range(6)
NEEDS={P1:0,P2:1,P3:2,P4:3}

def spread_small(tiles, vec, hb):
    r=lax.broadcasted_iota(jnp.int32,(128,256),0); l=lax.broadcasted_iota(jnp.int32,(128,256),1)
    r4=lax.broadcasted_iota(jnp.int32,(128,384),0); l4=lax.broadcasted_iota(jnp.int32,(128,384),1)
    vec[...]=jnp.zeros_like(vec); hb[...]=jnp.zeros_like(hb)
    for w in range(16):
        for y in range(2):
            t=tiles[w//4,(w//2)%2,(w%2)*16:(w%2)*16+16,y*128:y*128+128]
            c=min(48*w//128*128,512); off=48*w-c
            v=dot(t,jnp.where((l-off==r)&(r<48),1.0,0.0).astype(BF))
            for e in (0,1): vec[e,4*y:4*y+4,c:c+256]+=v[4*e:4*e+4]
            c=min((192*w+96*y)//128*128,3072-384); off=192*w+96*y-c
            h=dot(t,jnp.where((l4-off==r4)&(r4<96),1.0,0.0).astype(BF))
            for e in (0,1): hb[e,0:1,c:c+384]+=h[8+e:9+e]

def own_tiles(vectors, hidden_bias, q_set, gold, p_set, stage, small, marks):
    stage[...]=jnp.zeros_like(stage)
    for e in (0,1):
        stage[4*e:4*e+4,0:48]=vectors[e].astype(F32)
        stage[8+e:9+e,0:96]=hidden_bias[e:e+1,:].astype(F32)
    small[0]=stage[...].astype(BF)
    me=lax.axis_index("wq")*2+lax.axis_index("np")
    r=lax.broadcasted_iota(jnp.int32,(16,128),0); place=(r%2)*128+lax.broadcasted_iota(jnp.int32,(16,128),1)-me*8
    count=p_set.shape[0]
    tile=jnp.zeros((16,128),jnp.int32)
    for k in range(8):
        here=place==k
        tile=jnp.where(here&(r//2==0),q_set[k],tile)
        tile=jnp.where(here&(r//2==1),gold[k]//count*8+gold[k]%count,tile)
        tile=jnp.where(here&(r//2==2),p_set[k] if k<count else -1,tile)
    marks[0]=tile

def fused_kernel(units, plan, *refs):
    (ql,pln,q_set,gold,p_set,qx_h,px_h,vectors,hidden_bias)=refs[0:9]; ins=list(refs[9:13]); outs=refs[13:19]
    vec,hb,qo_h,po_h,qk_h,qv_h,pk_h,pv_h,q0,a0,p1,h0,p2,hd=refs[19:33]
    wv=refs[33:37]; qx,px,qo,po,qk,qv,pk,pv,stage,small_src,mark_src,small,bias,att,nrm,act,send,recv,lsem,xsem=refs[37:]
    moves={}
    def move(name,src,dst):
        moves[name]=pltpu.make_async_copy(src,dst,xsem.at[len(moves)]); moves[name].start()
    move("x1",px_h,px); move("x0",qx_h,qx)
    own_tiles(vectors,hidden_bias,q_set,gold,p_set,stage,small_src,mark_src)
    ins+=[small_src,mark_src]
    g=Gather(units,ins,outs,send,recv)
    g.barrier()
    for ref in (q0,a0,p1,h0,p2,hd): ref[...]=jnp.zeros_like(ref)
    X=(qx,px); O=(qo,po); K=(qk,pk); V=(qv,pv); LENS=(ql,pln); SLOTS=(64,256); BASE=(0,512); NB=(2,6)
    HBM=((qk_h,qv_h,qo_h),(pk_h,pv_h,po_h))
    loaded=set()
    def load_copies(a,e):
        if a==5: return []
        if a==4: return [pltpu.make_async_copy(outs[4].at[0],small,lsem.at[a,e,0])]
        rows=outs[a].shape[3]
        return [pltpu.make_async_copy(outs[a].at[e,k//2,k%2],wv[a].at[e,pl.ds(k*rows,rows)],lsem.at[a,e,k]) for k in range(8)]
    def need(a,e):
        if (a,e) in loaded: return
        loaded.add((a,e))
        for cp in load_copies(a,e): cp.wait()
        if a==4: spread_small(small,vec,hb)
        if a==0: moves["x%d"%e].wait()
    for item in plan:
        if item[0]==STEP: g.step(item[1],item[2])
        elif item[0]==LOAD:
            for cp in load_copies(*item[1:]): cp.start()
        else:
            kind,e,lo,hi=item
            need(4,0); need(NEEDS[kind],e)
            n=256//SLOTS[e]
            A=att.at[pl.ds(BASE[e],NB[e]*BLK)]; N=nrm.at[pl.ds(BASE[e],NB[e]*BLK)]
            def body(i,kept):
                row=pl.multiple_of(i*BLK,BLK)
                if kind==P1:
                    make_bias(bias,0,[LENS[e][i*n+j] for j in range(n)],SLOTS[e])
                    attend_block(row,X[e],wv[0].at[e],vec.at[e],bias,K[e],V[e],A,q0,e,i)
                if kind==P2: out_block(row,X[e],A,wv[1].at[e],vec.at[e],N,a0,p1,e,i)
                if kind==P3: up_block(row,N,wv[2].at[e],hb.at[e],act,h0,e,i,row)
                if kind==P4: down_block(row,N,act,wv[3].at[e],vec.at[e],O[e],p2,hd,e,i,row)
                return kept
            if hi-lo==1: body(lo,0)
            else: lax.fori_loop(lo,hi,body,0)
            if hi==NB[e]:
                if kind==P1:
                    move("k%d"%e,K[e],HBM[e][0]); move("v%d"%e,V[e],HBM[e][1])
                if kind==P4: move("o%d"%e,O[e],HBM[e][2])
    for name in moves:
        if name[0]!="x": moves[name].wait()

def fused_call(ql,pln,q_set,gold,p_set,qx,px,vectors,hidden_bias,arrays,units,plan):
    S=jax.ShapeDtypeStruct; VM=pltpu.VMEM; D=pltpu.SemaphoreType.DMA
    V=pl.BlockSpec(memory_space=pltpu.VMEM); SM=pl.BlockSpec(memory_space=pltpu.SMEM); A=pl.BlockSpec(memory_space=pl.ANY)
    outs=[S((a.shape[0],4,2,2*a.shape[1],2*a.shape[2]),a.dtype) for a in arrays]+[S((1,4,2,32,256),BF),S((1,4,2,32,256),jnp.int32)]
    outs+=[S((2,8,768),F32),S((2,1,3072),F32),S(qx.shape,BF),S(px.shape,BF),S(qx.shape,BF),S(qx.shape,BF),S(px.shape,BF),S(px.shape,BF),S((16,768),F32),S((16,768),F32),S((16,768),F32),S((16,3072),F32),S((16,768),F32),S((16,768),F32)]
    big=[VM(qx.shape,BF),VM(px.shape,BF)]+[VM(qx.shape,BF),VM(px.shape,BF)]+[VM(qx.shape,BF)]*2+[VM(px.shape,BF)]*2
    return pl.pallas_call(functools.partial(fused_kernel,units,plan),out_shape=outs,in_specs=[SM]*5+[A,A,V,V]+[A]*4,out_specs=[A]*6+[V,V]+[A]*6+[V]*6,
      scratch_shapes=[VM((2,768,2304),BF),VM((2,768,768),BF),VM((2,768,3072),BF),VM((2,3072,768),BF)]+big+[VM((16,128),F32),VM((1,16,128),BF),VM((1,16,128),jnp.int32),VM((4,2,32,256),BF),VM((256,256),F32),VM((2048,768),BF),VM((2048,768),F32),VM((1536,3072),BF),D((len(units),18)),D((len(units),18)),D((6,2,8)),D((8,))],
      compiler_params=pltpu.CompilerParams(collective_id=1,has_side_effects=True,vmem_limit_bytes=63*2**20),name="fused")(ql,pln,q_set,gold,p_set,qx,px,vectors,hidden_bias,*arrays)


GATHER_UNITS = (
    (4, 0, False, 0, 16), (5, 0, False, 0, 16), (0, 1, False, 0, 16), (0, 1, False, 16, 16),
    (0, 1, False, 32, 16), (1, 1, True, 0, 16), (1, 1, True, 16, 16), (1, 1, True, 32, 16),
    (0, 0, False, 0, 48), (2, 1, False, 0, 48), (1, 0, True, 0, 48), (3, 1, True, 0, 64),
    (3, 1, True, 64, 64), (3, 1, True, 128, 64), (2, 0, True, 0, 48), (3, 0, True, 0, 64),
    (3, 0, True, 64, 64), (3, 0, True, 128, 64),
)
GATHER_PLAN = (
    (STEP, 0, 0), (STEP, 1, 0), (STEP, 2, 0), (STEP, 3, 0), (STEP, 4, 0), (STEP, 5, 0),
    (STEP, 6, 0), (STEP, 7, 0), (STEP, 0, 1), (STEP, 1, 1), (STEP, 2, 1), (STEP, 5, 1),
    (STEP, 3, 1), (STEP, 0, 2), (STEP, 6, 1), (STEP, 7, 1), (STEP, 1, 2), (STEP, 4, 1),
    (STEP, 2, 2), (STEP, 5, 2), (STEP, 0, 3), (STEP, 3, 2), (STEP, 6, 2), (STEP, 1, 3),
    (STEP, 7, 2), (STEP, 0, 4), (STEP, 4, 2), (STEP, 2, 3), (STEP, 1, 4), (STEP, 5, 3),
    (STEP, 0, 5), (STEP, 8, 0), (STEP, 3, 3), (STEP, 6, 3), (STEP, 0, 6), (LOAD, 4, 0),
    (STEP, 7, 3), (STEP, 2, 4), (STEP, 4, 3), (STEP, 5, 4), (STEP, 1, 5), (STEP, 9, 0),
    (STEP, 1, 6), (LOAD, 5, 0), (STEP, 3, 4), (STEP, 8, 1), (STEP, 6, 4), (STEP, 7, 4),
    (STEP, 2, 5), (STEP, 10, 0), (STEP, 2, 6), (STEP, 4, 4), (STEP, 9, 1), (STEP, 5, 5),
    (STEP, 11, 0), (STEP, 5, 6), (STEP, 8, 2), (STEP, 3, 5), (STEP, 12, 0), (STEP, 6, 5),
    (STEP, 13, 0), (STEP, 3, 6), (STEP, 9, 2), (STEP, 7, 5), (STEP, 14, 0), (STEP, 6, 6),
    (STEP, 10, 1), (STEP, 7, 6), (LOAD, 1, 1), (STEP, 8, 3), (STEP, 4, 5), (STEP, 15, 0),
    (STEP, 11, 1), (STEP, 12, 1), (STEP, 9, 3), (STEP, 4, 6), (LOAD, 0, 1), (STEP, 13, 1),
    (STEP, 10, 2), (STEP, 14, 1), (STEP, 11, 2), (P1, 1, 0, 1), (STEP, 8, 4), (STEP, 12, 2),
    (STEP, 15, 1), (STEP, 13, 2), (P1, 1, 1, 2), (STEP, 10, 3), (STEP, 9, 4), (P1, 1, 2, 3),
    (STEP, 14, 2), (STEP, 11, 3), (P1, 1, 3, 4), (STEP, 12, 3), (STEP, 8, 5), (STEP, 16, 0),
    (STEP, 15, 2), (P1, 1, 4, 5), (STEP, 8, 6), (LOAD, 0, 0), (STEP, 13, 3), (STEP, 10, 4),
    (P1, 1, 5, 6), (STEP, 14, 3), (P1, 0, 0, 1), (STEP, 9, 5), (STEP, 17, 0), (STEP, 11, 4),
    (STEP, 12, 4), (STEP, 16, 1), (P1, 0, 1, 2), (STEP, 10, 5), (STEP, 9, 6), (LOAD, 2, 1),
    (STEP, 15, 3), (STEP, 17, 1), (STEP, 13, 4), (P2, 1, 0, 1), (STEP, 10, 6), (LOAD, 1, 0),
    (STEP, 11, 5), (P2, 1, 1, 4), (STEP, 11, 6), (P2, 1, 4, 6), (STEP, 12, 5), (STEP, 14, 4),
    (P2, 0, 0, 2), (STEP, 12, 6), (STEP, 16, 2), (P3, 1, 0, 1), (P3, 1, 1, 2), (STEP, 13, 5),
    (STEP, 15, 4), (P3, 1, 2, 3), (STEP, 13, 6), (LOAD, 3, 1), (STEP, 17, 2), (STEP, 16, 3),
    (P3, 1, 3, 4), (P3, 1, 4, 5), (STEP, 17, 3), (P3, 1, 5, 6), (P4, 1, 0, 2), (STEP, 14, 5),
    (STEP, 16, 4), (STEP, 17, 4), (P4, 1, 2, 4), (STEP, 14, 6), (LOAD, 2, 0), (P4, 1, 4, 5),
    (STEP, 15, 5), (P4, 1, 5, 6), (P3, 0, 0, 1), (STEP, 15, 6), (STEP, 16, 5), (P3, 0, 1, 2),
    (STEP, 16, 6), (STEP, 17, 5), (STEP, 17, 6), (LOAD, 3, 0), (P4, 0, 0, 2),
)


def kernel_shards(
    q_embed, p_embed, q_len, p_len, q_set, p_set, gold, wqkv, wout, wup, wdown, vectors, hidden_bias
):
    arrays = (wqkv, wout, wup, wdown)
    done = fused_call(
        q_len, p_len, q_set, gold, p_set, q_embed, p_embed, vectors, hidden_bias, arrays, GATHER_UNITS, GATHER_PLAN
    )
    weights = tuple(
        member.reshape(2, 16 * shard.shape[1], 2 * shard.shape[2])
        for member, shard in zip(done[:4], arrays)
    )
    vec, bias, q_out, p_out, q_keys, q_values, p_keys, p_values, q0, a0, p1, h0, p2, heads = done[6:]
    loss, tq, tp, uq, up, extra, *grads = tail_call(
        q_len, p_len, q_embed, p_embed, q_keys, q_values, p_keys, p_values, *weights,
        q0, a0, p1, h0, p2, heads, done[5], vec, bias,
    )
    loss, *rest = finish_call(loss, q_out, p_out, grads, tq, tp, uq, up, extra)
    return (loss[0, 0], *rest)


def kernels_fit(q_embed, p_embed, q_len, p_len):
    return (
        lax.axis_size("wq") == 16
        and lax.axis_size("np") == 2
        and q_embed.shape == (512, 768)
        and p_embed.shape == (1536, 768)
        and q_len.shape == (8,)
        and p_len.shape == (6,)
    )


def shards(
    q_embed,
    p_embed,
    q_len,
    p_len,
    q_set,
    p_set,
    gold,
    query_key_value_weight,
    attention_output_weight,
    up_weight,
    down_weight,
    vectors,
    hidden_bias,
):
    if kernels_fit(q_embed, p_embed, q_len, p_len):
        return kernel_shards(
            q_embed,
            p_embed,
            q_len,
            p_len,
            q_set,
            p_set,
            gold,
            query_key_value_weight,
            attention_output_weight,
            up_weight,
            down_weight,
            vectors,
            hidden_bias,
        )
    gathered = gather_weights(
        query_key_value_weight,
        attention_output_weight,
        up_weight,
        down_weight,
        vectors,
        hidden_bias,
    )
    wq_size, np_size = lax.axis_size("wq"), lax.axis_size("np")
    both_axes = ("wq", "np")
    q_weights = tuple((member[0] for member in gathered))
    p_weights = tuple((member[1] for member in gathered))
    p_encoded, p_stored = encode_forward(p_embed, p_len, p_weights)
    q_encoded, q_stored = encode_forward(q_embed, q_len, q_weights)
    model_width = q_embed.shape[1]
    ff_width = gathered[2].shape[2]
    q_count = q_len.shape[0]
    p_count = p_len.shape[0]
    own_heads = jnp.concatenate([first_rows(q_encoded, q_count), first_rows(p_encoded, p_count)])
    heads = lax.all_gather(own_heads, both_axes, axis=0)
    marks = lax.all_gather(jnp.concatenate([q_set, gold, p_set]), both_axes, axis=0)
    q_heads = heads[:, :q_count].reshape(-1, model_width)
    p_heads = heads[:, q_count:].reshape(-1, model_width)
    q_sets = marks[:, :q_count].reshape(-1)
    golds = marks[:, q_count : 2 * q_count].reshape(-1)
    p_sets = marks[:, 2 * q_count :].reshape(-1)
    scaling = model_width ** (-0.5)
    similar = (
        jnp.einsum("qd,pd->qp", q_heads, p_heads, preferred_element_type=jnp.float32) * scaling
    )
    is_gold = jnp.arange(p_heads.shape[0], dtype=jnp.int32)[None, :] == golds[:, None]
    usable = (q_sets[:, None] == p_sets[None, :]) | is_gold
    masked = jnp.where(usable, similar, NEGATIVE)
    highest = jnp.max(masked, axis=1)
    total = jnp.sum(jnp.where(usable, jnp.exp(masked - highest[:, None]), 0.0), axis=1)
    log_total = highest + jnp.log(total)
    gold_score = jnp.sum(jnp.where(is_gold, similar, 0.0), axis=1)
    loss = jnp.mean(log_total - gold_score)
    soft_rows = jnp.where(usable, jnp.exp(masked - log_total[:, None]), 0.0)
    grad_similar = (soft_rows - is_gold.astype(jnp.float32)).astype(jnp.bfloat16)
    me = lax.axis_index("wq") * np_size + lax.axis_index("np")
    grad_q_first = (
        jnp.einsum(
            "qp,pd->qd",
            lax.dynamic_slice_in_dim(grad_similar, me * q_count, q_count, 0),
            p_heads,
            preferred_element_type=jnp.float32,
        )
        * scaling
    )
    grad_p_first = (
        jnp.einsum(
            "qp,qd->pd",
            lax.dynamic_slice_in_dim(grad_similar, me * p_count, p_count, 1),
            q_heads,
            preferred_element_type=jnp.float32,
        )
        * scaling
    )
    q_back = encode_backward(q_embed, q_weights, q_stored, grad_q_first)
    p_back = encode_backward(p_embed, p_weights, p_stored, grad_p_first)
    left = jnp.concatenate(
        [left_message(member[1], wq_size, np_size) for member in (q_back, p_back)], axis=2
    )
    left = left.reshape((wq_size * np_size,) + left.shape[2:])
    left = lax.all_to_all(left, both_axes, 0, 0)
    right = jnp.concatenate([right_message(member[2], np_size) for member in (q_back, p_back)], axis=1)
    right = lax.all_gather(lax.all_to_all(right, "np", 0, 0), "wq", axis=0)
    right = right.reshape((wq_size * np_size,) + right.shape[2:])
    sums = jnp.concatenate(
        [
            jnp.stack([q_back[3], p_back[3]])
            .reshape(2, np_size, -1, wq_size, model_width // wq_size)
            .transpose(3, 1, 0, 2, 4)
            .reshape(wq_size * np_size, -1),
            jnp.stack([q_back[4], p_back[4]])
            .reshape(2, wq_size * np_size, -1)
            .transpose(1, 0, 2)
            .reshape(wq_size * np_size, -1),
        ],
        axis=1,
    )
    sums = jnp.sum(lax.all_to_all(sums, both_axes, 0, 0), axis=0)
    grad_vectors = sums[: sums.shape[0] - 2 * ff_width // (wq_size * np_size)].reshape(
        2, -1, model_width // wq_size
    )
    grad_b_in = sums[sums.shape[0] - 2 * ff_width // (wq_size * np_size) :].reshape(2, -1)
    q_weight_grads = weight_grads(
        left[:, :q_count].reshape(-1, left.shape[2]),
        right[:, :q_count].reshape(-1, right.shape[2]),
        model_width,
        ff_width,
        wq_size,
        np_size,
    )
    p_weight_grads = weight_grads(
        left[:, q_count:].reshape(-1, left.shape[2]),
        right[:, q_count:].reshape(-1, right.shape[2]),
        model_width,
        ff_width,
        wq_size,
        np_size,
    )
    shared = tuple(jnp.stack(pair) for pair in zip(q_weight_grads, p_weight_grads))
    return (
        loss,
        q_encoded,
        p_encoded,
        q_back[0],
        p_back[0],
        shared[0],
        shared[1],
        shared[2],
        shared[3],
        grad_vectors,
        grad_b_in,
    )


def solution(mesh):
    return jax.shard_map(
        shards,
        mesh=mesh,
        in_specs=(
            P(("wq", "np"), None),
            P(("wq", "np"), None),
            P(("wq", "np")),
            P(("wq", "np")),
            P(("wq", "np")),
            P(("wq", "np")),
            P(("wq", "np")),
            P(None, "wq", "np"),
            P(None, "wq", "np"),
            P(None, "wq", "np"),
            P(None, "wq", "np"),
            P(None, "np", "wq"),
            P(None, ("wq", "np")),
        ),
        out_specs=(
            P(),
            P(("wq", "np"), None),
            P(("wq", "np"), None),
            P(("wq", "np"), None),
            P(("wq", "np"), None),
            P(None, "wq", "np"),
            P(None, "wq", "np"),
            P(None, "wq", "np"),
            P(None, "wq", "np"),
            P(None, "np", "wq"),
            P(None, ("wq", "np")),
        ),
        check_vma=False,
    )
```

```python
import functools
import math

import jax
import jax.numpy as jnp
from jax import lax
from jax.experimental import pallas as pl
from jax.experimental.pallas import tpu as pltpu
from jax.sharding import PartitionSpec as P


HEADS = 12


EPSILON = 1e-12
NEGATIVE = -1e30


def layer_norm(inputs, gain_row, offset):
    centred = inputs - jnp.mean(inputs, axis=-1, keepdims=True)
    spread = jnp.mean(centred * centred, axis=-1, keepdims=True)
    return centred * lax.rsqrt(spread + EPSILON) * gain_row + offset


def smooth_gate(values):
    return jax.nn.gelu(values, approximate=True)


def gather_weights(
    query_key_value_weight, attention_output_weight, up_weight, down_weight, vectors, hidden_bias
):
    np_parts = (
        lax.all_gather(query_key_value_weight, "np", axis=2, tiled=True),
        lax.all_gather(attention_output_weight, "np", axis=2, tiled=True),
        lax.all_gather(up_weight, "np", axis=2, tiled=True),
        lax.all_gather(down_weight, "np", axis=2, tiled=True),
        lax.all_gather(vectors, "np", axis=1, tiled=True),
        lax.all_gather(hidden_bias, "np", axis=1, tiled=True),
    )
    return (
        lax.all_gather(np_parts[0], "wq", axis=1, tiled=True),
        lax.all_gather(np_parts[1], "wq", axis=1, tiled=True),
        lax.all_gather(np_parts[2], "wq", axis=1, tiled=True),
        lax.all_gather(np_parts[3], "wq", axis=1, tiled=True),
        lax.all_gather(np_parts[4], "wq", axis=2, tiled=True),
        lax.all_gather(np_parts[5], "wq", axis=1, tiled=True),
    )


def head_split(matrix, seq_count):
    row_count, model_width = matrix.shape
    return matrix.reshape(seq_count, row_count // seq_count, HEADS, model_width // HEADS)


def attention_scores(queries, keys_low, lengths):
    seq_count = lengths.shape[0]
    split_q = head_split(queries, seq_count)
    scores = jnp.einsum(
        "sqhc,skhc->shqk",
        split_q,
        head_split(keys_low, seq_count),
        preferred_element_type=jnp.float32,
    )
    scores = scores * split_q.shape[3] ** (-0.5)
    live_mask = jnp.arange(split_q.shape[1])[None, :] < lengths[:, None]
    return jnp.where(live_mask[:, None, None, :], scores, NEGATIVE)


def first_rows(matrix, seq_count):
    row_count, width = matrix.shape
    return matrix.reshape(seq_count, row_count // seq_count, width)[:, 0, :]


def encode_forward(token_rows, lengths, weights):
    (
        query_key_value_weight,
        attention_output_weight,
        up_weight,
        down_weight,
        vectors,
        hidden_bias,
    ) = weights
    row_count, model_width = token_rows.shape
    seq_count = lengths.shape[0]
    vec_f32 = vectors.astype(jnp.float32)
    projected_rows = jnp.dot(token_rows, query_key_value_weight, preferred_element_type=jnp.float32)
    queries = (projected_rows[:, :model_width] + vec_f32[0]).astype(jnp.bfloat16)
    keys_low = projected_rows[:, model_width : 2 * model_width].astype(jnp.bfloat16)
    values = (projected_rows[:, 2 * model_width :] + vec_f32[1]).astype(jnp.bfloat16)
    scores = attention_scores(queries, keys_low, lengths)
    totals = jax.nn.logsumexp(scores, axis=-1, keepdims=True)
    soft_low = jnp.exp(scores - totals).astype(jnp.bfloat16)
    attended_tokens = jnp.einsum(
        "shqk,skhc->sqhc",
        soft_low,
        head_split(values, seq_count),
        preferred_element_type=jnp.float32,
    )
    attended_tokens = attended_tokens.reshape(row_count, model_width).astype(jnp.bfloat16)
    residual_branch = (
        jnp.dot(attended_tokens, attention_output_weight, preferred_element_type=jnp.float32)
        + vec_f32[2]
    )
    pre_one = token_rows.astype(jnp.float32) + residual_branch
    first_normed = layer_norm(pre_one, vec_f32[3], vec_f32[4])
    normed_low = first_normed.astype(jnp.bfloat16)
    hidden_rows = jnp.dot(
        normed_low, up_weight, preferred_element_type=jnp.float32
    ) + hidden_bias.astype(jnp.float32)
    activated_hidden = smooth_gate(hidden_rows).astype(jnp.bfloat16)
    feedforward_output = (
        jnp.dot(activated_hidden, down_weight, preferred_element_type=jnp.float32) + vec_f32[5]
    )
    pre_two = first_normed + feedforward_output
    encoded_low = layer_norm(pre_two, vec_f32[6], vec_f32[7]).astype(jnp.bfloat16)
    soft_first = jnp.exp(scores[:, :, 0, :] - totals[:, :, 0, :])
    stored = (
        first_rows(queries, seq_count),
        keys_low,
        values,
        soft_first,
        first_rows(attended_tokens, seq_count),
        first_rows(pre_one, seq_count),
        first_rows(normed_low, seq_count),
        first_rows(hidden_rows, seq_count),
        first_rows(activated_hidden, seq_count),
        first_rows(pre_two, seq_count),
    )
    return (encoded_low, stored)


def norm_back(pre, gain_row, grad_out):
    centred = pre - jnp.mean(pre, axis=-1, keepdims=True)
    inverse = lax.rsqrt(jnp.mean(centred * centred, axis=-1, keepdims=True) + EPSILON)
    scaled = grad_out * gain_row
    inner = jnp.mean(scaled * centred, axis=-1, keepdims=True)
    grad_in = inverse * (
        scaled - jnp.mean(scaled, axis=-1, keepdims=True) - centred * (inverse * inverse * inner)
    )
    return (grad_in, jnp.sum(grad_out * centred * inverse, axis=0), jnp.sum(grad_out, axis=0))


def encode_backward(token_rows, weights, stored, grad_first):
    (
        query_key_value_weight,
        attention_output_weight,
        up_weight,
        down_weight,
        vectors,
        hidden_bias,
    ) = weights
    (
        queries,
        keys_low,
        values,
        soft_first,
        attended,
        pre_one,
        normed_low,
        hidden_rows,
        activated_hidden,
        pre_two,
    ) = stored
    seq_count, model_width = queries.shape
    seq_length = token_rows.shape[0] // seq_count
    head_width = model_width // HEADS
    scaling = head_width ** (-0.5)
    vec_f32 = vectors.astype(jnp.float32)
    grad_two, gain_two, shift_two = norm_back(pre_two, vec_f32[6], grad_first)
    grad_ffn = grad_two.astype(jnp.bfloat16)
    grad_activated = jnp.einsum(
        "rd,fd->rf", grad_ffn, down_weight, preferred_element_type=jnp.float32
    )
    grad_hidden = jax.vjp(smooth_gate, hidden_rows)[1](grad_activated)[0].astype(jnp.bfloat16)
    grad_normed = grad_two + jnp.einsum(
        "rf,df->rd", grad_hidden, up_weight, preferred_element_type=jnp.float32
    )
    grad_one, gain_one, shift_one = norm_back(pre_one, vec_f32[3], grad_normed)
    grad_branch = grad_one.astype(jnp.bfloat16)
    grad_attended = jnp.einsum(
        "re,de->rd", grad_branch, attention_output_weight, preferred_element_type=jnp.float32
    ).astype(jnp.bfloat16)
    grad_heads = grad_attended.reshape(seq_count, HEADS, head_width)
    grad_soft = jnp.einsum(
        "shc,skhc->shk",
        grad_heads,
        head_split(values, seq_count),
        preferred_element_type=jnp.float32,
    )
    row_inner = jnp.sum(soft_first * grad_soft, axis=-1, keepdims=True)
    grad_scores = (soft_first * (grad_soft - row_inner)).astype(jnp.bfloat16)
    soft_low = soft_first.astype(jnp.bfloat16)
    grad_queries = (
        jnp.einsum(
            "shk,skhc->shc",
            grad_scores,
            head_split(keys_low, seq_count),
            preferred_element_type=jnp.float32,
        )
        * scaling
    )
    grad_q_low = grad_queries.reshape(seq_count, model_width).astype(jnp.bfloat16)
    tokens = token_rows.reshape(seq_count, seq_length, model_width)
    both = jnp.concatenate([grad_scores, soft_low], axis=1)
    mixed = jnp.einsum("sgk,skd->sgd", both, tokens, preferred_element_type=jnp.float32).astype(
        jnp.bfloat16
    )
    scaled_queries = (queries.astype(jnp.float32) * scaling).astype(jnp.bfloat16)
    split_weight = query_key_value_weight.reshape(model_width, 3, HEADS, head_width)
    back_rows = jnp.concatenate(
        [
            jnp.einsum(
                "shc,dhc->shd",
                scaled_queries.reshape(seq_count, HEADS, head_width),
                split_weight[:, 1],
                preferred_element_type=jnp.float32,
            ),
            jnp.einsum(
                "shc,dhc->shd",
                grad_heads,
                split_weight[:, 2],
                preferred_element_type=jnp.float32,
            ),
        ],
        axis=1,
    ).astype(jnp.bfloat16)
    grad_tokens = jnp.einsum("sgk,sgd->skd", both, back_rows, preferred_element_type=jnp.float32)
    first_extra = grad_one + jnp.einsum(
        "se,de->sd",
        grad_q_low,
        query_key_value_weight[:, :model_width],
        preferred_element_type=jnp.float32,
    )
    is_first = (jnp.arange(seq_length) == 0)[None, :, None]
    grad_tokens = grad_tokens + jnp.where(is_first, first_extra[:, None, :], 0.0)
    soft_total = jnp.sum(soft_low.astype(jnp.float32), axis=-1, keepdims=True)
    vector_parts = jnp.stack(
        [
            jnp.sum(grad_q_low.astype(jnp.float32), axis=0),
            jnp.sum(grad_heads.astype(jnp.float32) * soft_total, axis=0).reshape(model_width),
            jnp.sum(grad_branch.astype(jnp.float32), axis=0),
            gain_one,
            shift_one,
            jnp.sum(grad_ffn.astype(jnp.float32), axis=0),
            gain_two,
            shift_two,
        ]
    )
    bias_part = jnp.sum(grad_hidden.astype(jnp.float32), axis=0)
    left = (
        activated_hidden,
        normed_low,
        attended,
        jnp.concatenate(
            [jnp.broadcast_to(tokens[:, :1, :], (seq_count, HEADS, model_width)), mixed], axis=1
        ),
    )
    right = (
        grad_ffn,
        grad_hidden,
        grad_branch,
        jnp.concatenate([grad_q_low, scaled_queries, grad_attended], axis=1),
    )
    return (
        grad_tokens.reshape(token_rows.shape),
        left,
        right,
        vector_parts,
        bias_part,
    )


def left_message(left, wq_size, np_size):
    activated, normed, attended, mixed = left
    rows, groups, model_width = mixed.shape
    part = model_width // wq_size
    columns = 3 * model_width // np_size
    head_width = model_width // HEADS
    group = math.gcd(head_width, columns)
    mixed = jnp.repeat(mixed, head_width // group, axis=1)
    mixed = mixed.reshape(rows, np_size, columns // group, wq_size, part)
    mixed = mixed.transpose(3, 1, 0, 2, 4).reshape(wq_size, np_size, rows, columns // group * part)

    def same(matrix):
        pieces = matrix.reshape(rows, wq_size, -1).transpose(1, 0, 2)
        return jnp.broadcast_to(pieces[:, None], (wq_size, np_size) + pieces.shape[1:])

    return jnp.concatenate([same(activated), same(normed), same(attended), mixed], axis=3)


def right_message(right, np_size):
    rows = right[0].shape[0]
    return jnp.concatenate(
        [member.reshape(rows, np_size, -1).transpose(1, 0, 2) for member in right], axis=2
    )


def weight_grads(left, right, model_width, ff_width, wq_size, np_size):
    rows = left.shape[0]
    part, ff_part = model_width // wq_size, ff_width // wq_size
    columns = 3 * model_width // np_size
    group = math.gcd(model_width // HEADS, columns)
    right_sizes = (model_width // np_size, ff_width // np_size, model_width // np_size)
    cut = [ff_part, ff_part + part, ff_part + 2 * part]
    activated, normed, attended, mixed = jnp.split(left, cut, axis=1)
    cut = [right_sizes[0], right_sizes[0] + right_sizes[1], sum(right_sizes)]
    grad_ffn, grad_hidden, grad_branch, grad_projected = jnp.split(right, cut, axis=1)

    def outer(one, two):
        return jnp.einsum("sd,se->de", one, two, preferred_element_type=jnp.float32)

    w_qkv = jnp.einsum(
        "sgd,sgc->dgc",
        mixed.reshape(rows, columns // group, part),
        grad_projected.reshape(rows, columns // group, group),
        preferred_element_type=jnp.float32,
    ).reshape(part, columns)
    return (
        w_qkv,
        outer(attended, grad_branch),
        outer(normed, grad_hidden),
        outer(activated, grad_ffn),
    )


BLK=256
F32=jnp.float32; BF=jnp.bfloat16
NEG=-1e30; EPS=1e-12
def dot(a,b): return jnp.dot(a,b,preferred_element_type=F32)
def norm(u,g,b):
    c=u-jnp.mean(u,axis=-1,keepdims=True)
    s=jnp.mean(c*c,axis=-1,keepdims=True)
    return c*lax.rsqrt(s+EPS)*g+b
def put_first(ref, e, i, cols, v):
    if e==1:
        ref[pl.ds(8+i,1),cols]=v[0:1]
    else:
        for j in range(4): ref[pl.ds(4*i+j,1),cols]=v[64*j:64*j+1]
def make_bias(bias_ref, slot, lens, slots):
    n=BLK//slots
    key=lax.broadcasted_iota(jnp.int32,(BLK,BLK),0)
    qry=lax.broadcasted_iota(jnp.int32,(BLK,BLK),1)
    ok=key<lens[0]
    if n>1:
        ok=ok&(qry<slots)
        for j in range(1,n):
            ok=ok|((key>=j*slots)&(key<j*slots+lens[j])&(qry>=j*slots)&(qry<(j+1)*slots))
    bias_ref[...]=jnp.where(ok,0.0,NEG)
def attend_block(row, x_ref, wqkv, vec, bias_ref, k_ref, v_ref, att_ref, q0_ref, e, i):
    x=x_ref[pl.ds(row,BLK),:]
    for g in range(3):
        cs=pl.ds(g*256,256)
        q4=dot(x,wqkv[:,g*256:g*256+256])+vec[0:1,g*256:g*256+256]
        q4=q4.astype(BF)
        k4=dot(x,wqkv[:,768+g*256:768+g*256+256]).astype(BF)
        v4=(dot(x,wqkv[:,1536+g*256:1536+g*256+256])+vec[1:2,g*256:g*256+256]).astype(BF)
        k_ref[pl.ds(row,BLK),cs]=k4
        v_ref[pl.ds(row,BLK),cs]=v4
        put_first(q0_ref,e,i,slice(g*256,g*256+256),q4.astype(F32))
        qT=(q4.astype(F32)*0.125).T.astype(BF)
        vT=v4.astype(F32).T.astype(BF)
        lane=lax.broadcasted_iota(jnp.int32,(BLK,256),1)
        outs=[]
        for h in range(4):
            kh=jnp.where((lane>=64*h)&(lane<64*h+64),k4,jnp.zeros_like(k4))
            s=dot(kh,qT)+bias_ref[...]
            m=jnp.max(s,axis=0,keepdims=True)
            p=jnp.exp(s-m)
            l=jnp.sum(p,axis=0,keepdims=True)
            o=dot(vT[64*h:64*h+64,:],p.astype(BF))
            outs.append(o*(1.0/l))
        oT=jnp.concatenate(outs,axis=0)
        att_ref[pl.ds(row,BLK),cs]=oT.T.astype(BF)
def out_block(row, x_ref, att_ref, wo, vec, n_ref, a0_ref, p1_ref, e, i):
    att=att_ref[pl.ds(row,BLK),:]
    put_first(a0_ref,e,i,slice(None),att.astype(F32))
    pre=x_ref[pl.ds(row,BLK),:].astype(F32)+dot(att,wo[...])+vec[2:3,:]
    put_first(p1_ref,e,i,slice(None),pre)
    n_ref[pl.ds(row,BLK),:]=norm(pre,vec[3:4,:],vec[4:5,:])
def gelu(u):
    return 0.5*u*(1.0+jnp.tanh(0.7978845608028654*(u+0.044715*(u*u*u))))
def up_block(row, n_ref, wup, hb, act_ref, h0_ref, e, i, arow):
    nl=n_ref[pl.ds(row,BLK),:].astype(BF)
    for t in range(12):
        cs=slice(t*256,t*256+256)
        h=dot(nl,wup[:,cs])+hb[0:1,cs]
        put_first(h0_ref,e,i,cs,h)
        act_ref[pl.ds(arow,BLK),cs]=gelu(h).astype(BF)
def down_block(row, n_ref, act_ref, wdown, vec, o_ref, p2_ref, hd_ref, e, i, arow):
    f=dot(act_ref[pl.ds(arow,BLK),:],wdown[...])+vec[5:6,:]
    pre=n_ref[pl.ds(row,BLK),:]+f
    put_first(p2_ref,e,i,slice(None),pre)
    enc=norm(pre,vec[6:7,:],vec[7:8,:])
    put_first(hd_ref,e,i,slice(None),enc)
    o_ref[pl.ds(row,BLK),:]=enc.astype(BF)

def dot_nt(a,b): return lax.dot_general(a,b,(((1,),(1,)),((),())),preferred_element_type=F32)
def gelu_slope(u):
    t=jnp.tanh(0.7978845608028654*(u+0.044715*(u*u*u)))
    return 0.5*(1.0+t)+0.5*u*(1.0-t*t)*(0.7978845608028654*(1.0+0.134145*(u*u)))
def norm_grad(u,g,gy):
    c=u-jnp.mean(u,axis=-1,keepdims=True)
    r=lax.rsqrt(jnp.mean(c*c,axis=-1,keepdims=True)+EPS)
    t=gy*g
    gu=r*(t-jnp.mean(t,axis=-1,keepdims=True)-c*(r*r)*jnp.mean(t*c,axis=-1,keepdims=True))
    return gu, jnp.sum(gy*c*r,axis=0,keepdims=True), jnp.sum(gy,axis=0,keepdims=True)
def heads_apart(rows, count):
    n=rows.shape[0]
    wide=jnp.concatenate([jnp.broadcast_to(rows[i:i+1],(16,768)) for i in range(n)],axis=0)
    r=lax.broadcasted_iota(jnp.int32,wide.shape,0)%16
    l=lax.broadcasted_iota(jnp.int32,wide.shape,1)//64
    return jnp.where(r==l,wide,0.0)
def pick_matrix(off, lane0):
    r=lax.broadcasted_iota(jnp.int32,(256,128),0); l=lax.broadcasted_iota(jnp.int32,(256,128),1)
    return jnp.where((r-off==l-lane0)&(l>=lane0)&(l<lane0+48),1.0,0.0).astype(BF)
MESH = pl.DeviceIdType.MESH

class Gather:
    def __init__(self, units, ins, outs, send, recv):
        self.units, self.ins, self.outs, self.send, self.recv = units, ins, outs, send, recv
        w, self.y = lax.axis_index("wq"), lax.axis_index("np")
        self.w = w
        self.z, self.x, self.c = w // 4, (w // 2) % 2, w % 2
        self.pending = {}
    def dev(self, dz=0, fx=False, fy=False, fc=False):
        x = 1 - self.x if fx else self.x
        c = 1 - self.c if fc else self.c
        y = 1 - self.y if fy else self.y
        return ((self.z + dz) * 4 + x * 2 + c, y)
    def barrier(self):
        bar = pltpu.get_barrier_semaphore()
        def sig(**k): pl.semaphore_signal(bar, inc=1, device_id=self.dev(**k), device_id_type=MESH)
        sig(fx=True); sig(fy=True); sig(fc=True)
        @pl.when(self.z > 0)
        def _(): sig(dz=-1)
        @pl.when(self.z < 3)
        def _(): sig(dz=1)
        pl.semaphore_wait(bar, 3 + (self.z + 3) // 4 + (6 - self.z) // 4)
    def view(self, u, z=None, x=None, y=None, c=None):
        a, e, kind, r0, rn = self.units[u]
        o = self.outs[a]
        r, w = self.ins[a].shape[1:]
        zs = slice(None) if z is None else z
        xs = slice(None) if x is None else x
        cs = slice(None) if y is None else pl.ds(pl.multiple_of(y * w, 128), w)
        return o.at[e, zs, xs, pl.ds(pl.multiple_of((self.c if c is None else c) * r + r0, 16), rn), cs]
    def copy(self, u, sem, src, dst, dev):
        return pltpu.make_async_remote_copy(src_ref=src, dst_ref=dst, send_sem=self.send.at[u, sem], recv_sem=self.recv.at[u, sem], device_id=dev, device_id_type=MESH)
    def own_src(self, u):
        a, e, kind, r0, rn = self.units[u]
        return self.ins[a].at[e, pl.ds(r0, rn)]
    def zview(self, u, core, z):
        kind = self.units[u][2]
        if not kind: return self.view(u, z=z, x=self.x, y=self.y)
        if core == 0: return self.view(u, z=z, x=None, y=self.y)
        return self.view(u, z=z, x=self.x, y=None)
    def step(self, u, s):
        for core in (0, 1):
            pl.when(self.c == core)(lambda core=core: self._step(u, s, core))
    def A(self, core): return dict(fx=True) if core == 0 else dict(fy=True)
    def B(self, core): return dict(fy=True) if core == 0 else dict(fx=True)
    def a_src(self, u, core):
        kind = self.units[u][2]
        z = None if not kind else self.z
        return self.view(u, z=z, x=self.x, y=self.y)
    def a_got(self, u, core):
        kind = self.units[u][2]
        z = None if not kind else self.z
        return self.view(u, z=z, x=1 - self.x, y=self.y) if core == 0 else self.view(u, z=z, x=self.x, y=1 - self.y)
    def b_src(self, u, core):
        return self.view(u, x=None, y=self.y) if core == 0 else self.view(u, x=self.x, y=None)
    def b_got(self, u, core):
        return self.view(u, x=None, y=1 - self.y) if core == 0 else self.view(u, x=1 - self.x, y=None)
    def local(self, u, sem, ref):
        self.copy(u, sem, ref, ref, self.dev(fc=True)).start()
    def z_send(self, u, core, hop):
        z = self.z
        @pl.when((z - hop >= 0) & (z + 1 <= 3))
        def _():
            v = self.zview(u, core, z - hop)
            src = self.own_src(u) if (hop == 0 and not self.units[u][2]) else v
            self.copy(u, 2 + hop, src, v, self.dev(dz=1)).start()
        @pl.when((z + hop <= 3) & (z - 1 >= 0))
        def _():
            v = self.zview(u, core, z + hop)
            src = self.own_src(u) if (hop == 0 and not self.units[u][2]) else v
            self.copy(u, 5 + hop, src, v, self.dev(dz=-1)).start()
    def z_wait(self, u, core, hop):
        z = self.z
        @pl.when(z - 1 - hop >= 0)
        def _():
            v = self.zview(u, core, z - 1 - hop)
            self.copy(u, 2 + hop, v, v, self.dev(fc=True)).wait_recv()
            self.local(u, 11 + hop, v)
        @pl.when(z + 1 + hop <= 3)
        def _():
            v = self.zview(u, core, z + 1 + hop)
            self.copy(u, 5 + hop, v, v, self.dev(fc=True)).wait_recv()
            self.local(u, 14 + hop, v)
    def _step(self, u, s, core):
        F = not self.units[u][2]
        own = self.view(u, z=self.z, x=self.x, y=self.y)
        if s == 0:
            src = self.own_src(u)
            self.copy(u, 8, src, own, self.dev(fc=True)).start()
            pltpu.make_async_copy(src, own, self.send.at[u, 17]).start()
            if F:
                self.z_send(u, core, 0)
            else:
                self.copy(u, 0, src, own, self.dev(**self.A(core))).start()
        if s == 1:
            pltpu.make_async_copy(self.own_src(u), own, self.send.at[u, 17]).wait()
            if F:
                self.z_wait(u, core, 0); self.z_send(u, core, 1)
            else:
                g = self.a_got(u, core)
                self.copy(u, 0, g, g, self.dev(fc=True)).wait_recv()
                self.z_send(u, core, 0)
                self.local(u, 9, g)
        if s == 2:
            if F: self.z_wait(u, core, 1); self.z_send(u, core, 2)
            else: self.z_wait(u, core, 0); self.z_send(u, core, 1)
        if s == 3:
            if F:
                self.z_wait(u, core, 2)
                v = self.a_src(u, core)
                self.copy(u, 0, v, v, self.dev(**self.A(core))).start()
            else:
                self.z_wait(u, core, 1); self.z_send(u, core, 2)
        if s == 4:
            if F:
                g = self.a_got(u, core)
                self.copy(u, 0, g, g, self.dev(fc=True)).wait_recv()
            else:
                self.z_wait(u, core, 2)
            v = self.b_src(u, core)
            self.copy(u, 1, v, v, self.dev(**self.B(core))).start()
            if F: self.local(u, 9, g)
        if s == 5:
            g = self.b_got(u, core)
            self.copy(u, 1, g, g, self.dev(fc=True)).wait_recv()
            self.local(u, 10, g)
        if s == 6:
            self.finish_recv(u, core); self.finish_send(u, core)
    def finish_recv(self, u, core):
        other = 1 - core
        c = 1 - self.c
        kind = self.units[u][2]
        def got(sem, v): self.copy(u, sem, v, v, self.dev(fc=True)).wait_recv()
        sv = lambda **k: self.view(u, c=c, **k)
        got(8, sv(z=self.z, x=self.x, y=self.y))
        za = None if not kind else self.z
        got(9, sv(z=za, x=1 - self.x, y=self.y) if other == 0 else sv(z=za, x=self.x, y=1 - self.y))
        got(10, sv(x=None, y=1 - self.y) if other == 0 else sv(x=1 - self.x, y=None))
        def zv(z):
            if not kind: return sv(z=z, x=self.x, y=self.y)
            return sv(z=z, x=None, y=self.y) if other == 0 else sv(z=z, x=self.x, y=None)
        for hop in range(3):
            pl.when(self.z - 1 - hop >= 0)(lambda hop=hop: got(11 + hop, zv(self.z - 1 - hop)))
            pl.when(self.z + 1 + hop <= 3)(lambda hop=hop: got(14 + hop, zv(self.z + 1 + hop)))
    def finish_send(self, u, core):
        def sent(sem, v): self.copy(u, sem, v, v, self.dev(fc=True)).wait_send()
        own = self.view(u, z=self.z, x=self.x, y=self.y)
        sent(8, own)
        sent(0, self.a_src(u, core)); sent(1, self.b_src(u, core))
        sent(9, self.a_got(u, core)); sent(10, self.b_got(u, core))
        z = self.z
        for hop in range(3):
            pl.when((z - hop >= 0) & (z + 1 <= 3))(lambda hop=hop: sent(2 + hop, self.zview(u, core, z - hop)))
            pl.when((z + hop <= 3) & (z - 1 >= 0))(lambda hop=hop: sent(5 + hop, self.zview(u, core, z + hop)))
            pl.when(z - 1 - hop >= 0)(lambda hop=hop: sent(11 + hop, self.zview(u, core, z - 1 - hop)))
            pl.when(z + 1 + hop <= 3)(lambda hop=hop: sent(14 + hop, self.zview(u, core, z + 1 + hop)))

class Place:
    def __init__(self):
        self.w=lax.axis_index("wq"); self.y=lax.axis_index("np")
        self.z,self.x,self.c=self.w//4,(self.w//2)%2,self.w%2
        self.me=self.w*2+self.y
    def dev(self, z=None, fx=False, fy=False, fc=False):
        x=1-self.x if fx else self.x
        c=1-self.c if fc else self.c
        y=1-self.y if fy else self.y
        return ((self.z if z is None else z)*4+x*2+c, y)

class HeadGather:
    def __init__(self,pos,buf,send,recv):
        self.pos,self.buf,self.send,self.recv=pos,buf,send,recv
    def rc(self,sem,ref,dev):
        return pltpu.make_async_remote_copy(src_ref=ref,dst_ref=ref,send_sem=self.send.at[sem],recv_sem=self.recv.at[sem],device_id=dev,device_id_type=MESH)
    def phase(self,s):
        pos,buf=self.pos,self.buf
        z,x,c,y=pos.z,pos.x,pos.c,pos.y
        sib=pos.dev(fc=True)
        def arrived(sem,ref): self.rc(sem,ref,sib).wait_recv()
        own=buf.at[z,x,c,y]
        col=lambda fx,fy,core: buf.at[:,1-x if fx else x,core,1-y if fy else y]
        ways=((3,True,True),(4,True,False),(5,False,True))
        if s==0:
            for k in (1,2,3): self.rc(k-1,own,pos.dev(z=(z+k)%4)).start()
        if s==1:
            for k in (1,2,3): arrived(k-1,buf.at[(z+4-k)%4,x,c,y])
            for sem,fx,fy in ways: self.rc(sem,col(False,False,c),pos.dev(fx=fx,fy=fy)).start()
            self.rc(6,col(False,False,c),sib).start()
        if s==2:
            for sem,fx,fy in ways[1:]+ways[:1]:
                arrived(sem,col(fx,fy,c)); self.rc(sem+4,col(fx,fy,c),sib).start()
        if s==3:
            o=1-c
            arrived(6,col(False,False,o))
            for sem,fx,fy in ways: arrived(sem+4,col(fx,fy,o))
            for k in (1,2,3): self.rc(k-1,own,sib).wait_send()
            for sem in (3,4,5,6): self.rc(sem,col(False,False,c),sib).wait_send()
            for sem,fx,fy in ways: self.rc(sem+4,col(fx,fy,c),sib).wait_send()

CHUNKS=((0,1152,False),(1152,512,False),(1664,256,True),(1920,768,False),(2688,384,True))
class RightGather:
    def __init__(self,pos,src,buf,send,recv):
        self.pos,self.src,self.buf,self.send,self.recv=pos,src,buf,send,recv
    def rc(self,ch,sem,src,dst,dev):
        return pltpu.make_async_remote_copy(src_ref=src,dst_ref=dst,send_sem=self.send.at[ch,sem],recv_sem=self.recv.at[ch,sem],device_id=dev,device_id_type=MESH)
    def view(self,ch,z=None,x=None,c=None,y=None):
        p=self.pos; c0,w,_=CHUNKS[ch]
        f=lambda v: slice(None) if v is None else v
        return self.buf.at[f(z),p.x if x is None else x,p.c if c is None else c,f(y),:,c0:c0+w]
    def half(self,ch,y):
        c0,w,_=CHUNKS[ch]
        return self.src.at[y,:,c0:c0+w]
    def column(self,ch,z,c=None):
        p=self.pos; c0,w,x_first=CHUNKS[ch]
        return self.buf.at[z,slice(None) if x_first else p.x,p.c if c is None else c,:,:,c0:c0+w]
    def across(self,ch,x,c=None):
        p=self.pos
        return self.view(ch,z=p.z if CHUNKS[ch][2] else None,x=x,c=c)
    def step(self,ch,s):
        p=self.pos; z,y=p.z,p.y; x_first=CHUNKS[ch][2]
        sib=p.dev(fc=True)
        def arrived(sem,v): self.rc(ch,sem,v,v,sib).wait_recv()
        def local(sem,v): self.rc(ch,sem,v,v,sib).start()
        def z_send(hop):
            @pl.when((z-hop>=0)&(z+1<=3))
            def _():
                v=self.column(ch,z-hop); self.rc(ch,2+hop,v,v,p.dev(z=z+1)).start()
            @pl.when((z+hop<=3)&(z-1>=0))
            def _():
                v=self.column(ch,z+hop); self.rc(ch,5+hop,v,v,p.dev(z=z-1)).start()
        def z_wait(hop):
            @pl.when(z-1-hop>=0)
            def _():
                v=self.column(ch,z-1-hop); arrived(2+hop,v); local(9+hop,v)
            @pl.when(z+1+hop<=3)
            def _():
                v=self.column(ch,z+1+hop); arrived(5+hop,v); local(12+hop,v)
        def x_send():
            v=self.across(ch,p.x); self.rc(ch,1,v,v,p.dev(fx=True)).start()
        def x_wait():
            g=self.across(ch,1-p.x); arrived(1,g); local(15,g)
        own=self.view(ch,z=z,y=y)
        if s==0:
            self.rc(ch,0,self.half(ch,1-y),own,p.dev(fy=True)).start()
            pltpu.make_async_copy(self.half(ch,y),own,self.send.at[ch,16]).start()
        if s==1:
            pltpu.make_async_copy(self.half(ch,y),own,self.send.at[ch,16]).wait()
            arrived(0,self.view(ch,z=z,y=1-y))
            if x_first: x_send()
            else: z_send(0)
            local(8,self.view(ch,z=z))
        if x_first:
            if s==2: x_wait(); z_send(0)
            if s==3: z_wait(0); z_send(1)
            if s==4: z_wait(1); z_send(2)
            if s==5: z_wait(2)
        else:
            if s==2: z_wait(0); z_send(1)
            if s==3: z_wait(1); z_send(2)
            if s==4: z_wait(2); x_send()
            if s==5: x_wait()
        if s==6:
            o=1-p.c
            arrived(8,self.view(ch,z=z,c=o)); arrived(15,self.across(ch,1-p.x,c=o))
            def sent(sem,v): self.rc(ch,sem,v,v,sib).wait_send()
            sent(0,own); sent(1,self.across(ch,p.x)); sent(8,self.view(ch,z=z)); sent(15,self.across(ch,1-p.x))
            for hop in range(3):
                pl.when(z-1-hop>=0)(lambda hop=hop: arrived(9+hop,self.column(ch,z-1-hop,c=o)))
                pl.when(z+1+hop<=3)(lambda hop=hop: arrived(12+hop,self.column(ch,z+1+hop,c=o)))
                pl.when((z-hop>=0)&(z+1<=3))(lambda hop=hop: sent(2+hop,self.column(ch,z-hop)))
                pl.when((z+hop<=3)&(z-1>=0))(lambda hop=hop: sent(5+hop,self.column(ch,z+hop)))
                pl.when(z-1-hop>=0)(lambda hop=hop: sent(9+hop,self.column(ch,z-1-hop)))
                pl.when(z+1+hop<=3)(lambda hop=hop: sent(12+hop,self.column(ch,z+1+hop)))

class LeftCopies:
    def __init__(self,pos,left,buf,spans,send,recv):
        self.pos,self.left,self.buf,self.spans,self.send,self.recv=pos,left,buf,spans,send,recv
    def each(self,d,go):
        t=(self.pos.me+d)%32
        w,y=t//2,t%2
        for half,(r0,n) in enumerate(self.spans):
            @pl.when(y==half)
            def _():
                go(pltpu.make_async_remote_copy(src_ref=self.left.at[w,pl.ds(r0,n)],dst_ref=self.buf.at[self.pos.me,pl.ds(0,n)],send_sem=self.send.at[d],recv_sem=self.recv.at[d],device_id=(w,y),device_id_type=MESH))
    def start(self,batch):
        def lap(k,kept):
            self.each(4*k+batch,lambda cp: cp.start()); return kept
        lax.fori_loop(0 if batch else 1,8,lap,0)
        if batch: return
        for half,(r0,n) in enumerate(self.spans):
            @pl.when(self.pos.y==half)
            def _(): self.buf[self.pos.me,0:n,:]=self.left[self.pos.w,r0:r0+n,:]
    def finish(self):
        def lap(d,kept):
            self.each(d,lambda cp: cp.wait_send())
            s=(self.pos.me+32-d)%32
            for half,(r0,n) in enumerate(self.spans):
                @pl.when(self.pos.y==half)
                def _():
                    v=self.buf.at[s,pl.ds(0,n)]
                    pltpu.make_async_remote_copy(src_ref=v,dst_ref=v,send_sem=self.send.at[d],recv_sem=self.recv.at[d],device_id=(self.pos.w,self.pos.y),device_id_type=MESH).wait_recv()
            return kept
        lax.fori_loop(1,32,lap,0)

def similarity(pos,buf,marks,loss,gr,gs_s,gt_s):
    g=buf[...].reshape(32,16,768).astype(F32)
    q=g[:,0:8].reshape(256,768).astype(BF); p=g[:,8:16].reshape(256,768).astype(BF)
    m=jnp.sum(marks[...].reshape(8,32,256),axis=0)
    m=m[0:16]+m[16:32]
    m=(m[:,0:128]+m[:,128:256]).astype(F32)
    row=lambda r: jnp.broadcast_to(jnp.concatenate([m[r:r+1],m[r+1:r+2]],axis=1),(256,256))
    qset=row(0).T; gold=row(2).T; pset=row(4)
    lane=lax.broadcasted_iota(jnp.int32,(256,256),1).astype(F32)
    is_gold=gold==lane
    usable=(qset==pset)|is_gold
    sim=dot_nt(q,p)*(768**-0.5)
    masked=jnp.where(usable,sim,NEG)
    high=jnp.max(masked,axis=1,keepdims=True)
    tot=high+jnp.log(jnp.sum(jnp.where(usable,jnp.exp(masked-high),0.0),axis=1,keepdims=True))
    gsc=jnp.sum(jnp.where(is_gold,sim,0.0),axis=1,keepdims=True)
    loss[0,0]=jnp.sum(tot-gsc)*(1.0/256)
    soft=jnp.where(usable,jnp.exp(masked-tot),0.0)
    gsim=soft-jnp.where(is_gold,1.0,0.0)
    gs_s[...]=gsim; gt_s[...]=gsim.T
    me8=pl.ds(pl.multiple_of(pos.me*8,8),8)
    gr[0:8,:]=dot(gs_s[me8,:].astype(BF),p)*(768**-0.5)
    gr[8:16,:]=dot(gt_s[me8,:].astype(BF),q)*(768**-0.5)

EARLY=((0,16),(0,112)); LATE=((0,64),(48,64))
SLOTS=(64,256); NB=(2,6)
def window(s):
    w=min(48*s//128*128,128)
    return w,48*s-w
def two(ref,e,w): return jnp.concatenate([ref[e,w//128],ref[e,w//128+1]],axis=1)
def select_rows(ref,s):
    w,off=window(s)
    cat=lambda e: jnp.concatenate([two(ref,e,w),two(ref,e,w+384)],axis=0).astype(BF)
    m=dot(cat(0),pick_matrix(off,0))+dot(cat(1),pick_matrix(off,64))
    n=ref.shape[2]
    return m[0:n],m[n:2*n]
def select_wide(ref,s):
    w,off=window(s)
    cat=lambda e: jnp.concatenate([ref[e,:,384*m+w:384*m+w+256] for m in range(8)],axis=0).astype(BF)
    m=dot(cat(0),pick_matrix(off,0))+dot(cat(1),pick_matrix(off,64))
    return [m[8*k:8*k+8] for k in range(8)]
def early_messages(ls,left):
    for s in range(8):
        for k,r in enumerate(select_rows(ls,s)): left[s+8*k]=r.astype(BF)
def late_messages(ll,lb,stage,left):
    for j in range(16): stage[j,0:8,:]=jnp.zeros((8,128),F32)
    for s in range(8):
        for m,r in enumerate(select_wide(lb,s)):
            n=8*m+s
            stage[n//4,n%4:n%4+1,:]=r[0:1]
    for s in range(8):
        for k,r in enumerate(select_rows(ll,s)):
            j=s+8*k
            left[j,0:48,:]=r[0:48].astype(BF); left[j,64:112,:]=r[48:96].astype(BF)
            left[j,48:64,:]=jnp.concatenate([r[96:104],stage[j,0:8]],axis=0).astype(BF)

def early_block(e,i,lens,K,X,qa_s,P_s,ls):
    slots=SLOTS[e]; n=256//slots; R=16*n; row=i*256; pr=(96 if e==0 else 0)+i*R
    k=K[row:row+256,:]; x=X[row:row+256,:]
    s=dot_nt(qa_s[e,i*R:i*R+R,:],k)
    key=lax.broadcasted_iota(jnp.int32,(R,256),1)
    if n==1: ok=key<lens[i]
    else:
        grp=lax.broadcasted_iota(jnp.int32,(R,256),0)//16
        ok=(grp<0)
        for j in range(n): ok=ok|((grp==j)&(key>=j*slots)&(key<j*slots+lens[i*n+j]))
    s=jnp.where(ok,s,NEG)
    p=jnp.exp(s-jnp.max(s,axis=1,keepdims=True))
    p=p*(1.0/jnp.sum(p,axis=1,keepdims=True))
    P_s[pr:pr+R,:]=p
    mix=dot(p.astype(BF),x)
    for j in range(n):
        slot=i*n+j
        first=x[j*slots:j*slots+1].astype(F32)
        for c in range(6):
            cc=slice(128*c,128*c+128)
            ls[e,c,pl.ds(16+slot,12,stride=8),:]=mix[16*j:16*j+12,cc]
            ls[e,c,slot:slot+1,:]=first[:,cc]
def late_block(e,i,K,V,X,ga_s,P_s,ll,gq_s,sv_s,tmix):
    slots=SLOTS[e]; n=256//slots; R=16*n; row=i*256; pr=(96 if e==0 else 0)+i*R
    gab=ga_s[e,i*R:i*R+R,:]
    p=P_s[pr:pr+R,:]
    gs=dot_nt(gab,V[row:row+256,:])
    gs=p*(gs-jnp.sum(p*gs,axis=1,keepdims=True))
    gsb=gs.astype(BF); pb=p.astype(BF)
    tmix[i,0:R,:]=gsb; tmix[i,R:2*R,:]=pb
    gq=dot(gsb,K[row:row+256,:])
    r0=lax.broadcasted_iota(jnp.int32,(R,768),0); hl=lax.broadcasted_iota(jnp.int32,(R,768),1)//64
    gq=jnp.where(r0%16==hl,gq,0.0)*0.125
    st=jnp.sum(pb.astype(F32),axis=1,keepdims=True)
    sv_s[e]=sv_s[e]+jnp.sum(st*gab.astype(F32),axis=0,keepdims=True)
    mix=dot(gsb,X[row:row+256,:])
    for j in range(n):
        slot=i*n+j
        gq_s[e,slot:slot+1,:]=jnp.sum(gq[16*j:16*j+16],axis=0,keepdims=True)
        for c in range(6): ll[e,c,pl.ds(slot,12,stride=8),:]=mix[16*j:16*j+12,128*c:128*c+128]

def colsum(m): return jnp.sum(m.astype(F32),axis=0,keepdims=True)

class Products:
    def __init__(self,pos,eb,lb,rbuf,bq,bp,wqkv,wout,win,wback,gvec,gbin,w_up,w_dn,hb):
        self.__dict__.update(locals())
    def right(self,c0,w):
        r=self.rbuf[:,:,:,:,:,c0:c0+w].reshape(32,16,w).astype(F32)
        self.bq[:,c0:c0+w]=r[:,0:8].reshape(256,w).astype(BF)
        self.bp[:,c0:c0+w]=r[:,8:16].reshape(256,w).astype(BF)
    def pair(self,buf,r0):
        t=buf[:,r0:r0+16,:].astype(F32)
        return [t[:,8*i:8*i+8].reshape(256,128) for i in (0,1)]
    def put(self,out,rows,cols,tt,c0,w):
        tt=tt.T.astype(BF)
        out[0,rows,cols]=dot(tt,self.bq[:,c0:c0+w])[0:48]
        out[1,rows,cols]=dot(tt,self.bp[:,c0:c0+w])[64:112]
    def mixed(self,buf,r0,heads,col0,dst0):
        low=lax.broadcasted_iota(jnp.int32,(128,128),1)<64
        for h in range(0,heads,2):
            a,b=[v.T.astype(BF) for v in self.pair(buf,r0+8*h)]
            cs=slice(col0+64*h,col0+64*h+128); ds=slice(dst0+64*h,dst0+64*h+128)
            self.wqkv[0,:,ds]=jnp.where(low,dot(a,self.bq[:,cs]),dot(b,self.bq[:,cs]))[0:48]
            self.wqkv[1,:,ds]=jnp.where(low,dot(a,self.bp[:,cs]),dot(b,self.bp[:,cs]))[64:112]
    def feed_forward(self,e):
        b=(self.bq,self.bp)[e]; w,y=self.pos.w,self.pos.y
        nl=b[:,0:768]
        r=lax.broadcasted_iota(jnp.int32,(768,128),0); l=lax.broadcasted_iota(jnp.int32,(768,128),1)
        mine=dot(nl,jnp.where((r==48*w+l)&(l<48),1.0,0.0).astype(BF)).T[0:48].astype(BF)
        for t in range(4):
            cols=pl.ds(pl.multiple_of(y*1536+384*t,128),384)
            hid=dot(nl,self.w_up[e,:,cols])+self.hb[e,:,cols]
            gh=(dot_nt(b[:,1152:1920],self.w_dn[e,cols,:])*gelu_slope(hid)).astype(BF)
            self.win[e,:,384*t:384*t+384]=dot(mine,gh)
        cols=pl.ds(pl.multiple_of(192*w//128*128,128),256)
        act=gelu(dot(nl,self.w_up[e,:,cols])+self.hb[e,:,cols]).astype(BF).astype(F32).T.astype(BF)
        back=dot(act,b[:,pl.ds(pl.multiple_of(1152+y*384,128),384)])
        self.wback[e]=jnp.where(w%2==1,back[64:256],back[0:192])
    def second(self):
        al=slice(None)
        x0,att=self.pair(self.eb,0)
        self.put(self.wout,al,al,att,1920,384)
        @pl.when(self.pos.y==0)
        def _(): self.put(self.wqkv,al,slice(0,768),x0,2304,768)
        @pl.when(self.pos.y==1)
        def _(): self.mixed(self.eb,16,12,2304,384)
    def third(self):
        def sums(r0,half):
            vs,bs=[jnp.sum(v.reshape(32,8,128),axis=0) for v in self.pair(self.lb,r0)]
            for e in (0,1):
                ls=slice(64*e,64*e+48)
                self.gvec[e]=vs[4*half:4*half+4,ls]
                for k in (0,1): self.gbin[e:e+1,48*k:48*k+48]=bs[2*half+k:2*half+k+1,ls]
        @pl.when(self.pos.y==0)
        def _():
            self.mixed(self.lb,0,6,768,768)
            sums(48,0)
        @pl.when(self.pos.y==1)
        def _():
            self.mixed(self.lb,16,6,768,0)
            sums(0,1)

def tail_kernel(*refs):
    (ql,pln,qx_h,px_h,qk_h,qv_h,pk_h,pv_h,wqkv_h,wo_h,wup_h,wdn_h,q0,a0,p1,h0,p2,heads,marks,vec,hb,
     loss,tq,tp,uq,up_,extra,wqkv,wout,win,wback,gvec,gbin,
     kv_q,kv_p,w_qkv,w_o,w_up,w_dn,hbuf,gr,gs_s,gt_s,qa_s,ga_s,P_s,ls,ll,lb,stage,left_e,left_l,ebuf,lbuf,rs,rb,rbuf,bq,bp,gq_s,sv_s,
     msem,hsend,hrecv,esend,erecv,lsend,lrecv,rsend,rrecv)=refs
    pos=Place()
    bar=pltpu.get_barrier_semaphore()
    def lap(d,kept):
        t=(pos.me+d)%32
        pl.semaphore_signal(bar,inc=1,device_id=(t//2,t%2),device_id_type=MESH)
        return kept
    lax.fori_loop(1,32,lap,0)
    moves={}
    def move(name,src,dst): moves[name]=pltpu.make_async_copy(src,dst,msem.at[len(moves)]); moves[name].start()
    for n,(h,d) in enumerate(((pk_h,kv_p),(px_h,kv_p),(pv_h,kv_p),(qk_h,kv_q),(qx_h,kv_q),(qv_h,kv_q))): move("kxv"[n%3]+"pq"[n//3],h,d.at[n%3])
    for nm,h,d in (("dn",wdn_h,w_dn),("up",wup_h,w_up),("o",wo_h,w_o),("qkv",wqkv_h,w_qkv)):
        for e in (1,0): move(nm+str(e),h.at[e],d.at[e])
    def need(*names):
        for nm in names:
            if nm in moves: moves.pop(nm).wait()
    hbuf[pos.z,pos.x,pos.c,pos.y]=heads[...].astype(BF)
    for ref in (ls,ll,lb,gq_s,sv_s): ref[...]=jnp.zeros_like(ref)
    pl.semaphore_wait(bar,31)
    hg=HeadGather(pos,hbuf,hsend,hrecv)
    hg.phase(0)
    vv=lambda e: vec[e]
    for e in (1,0):
        rows=slice(8*e,8*e+8)
        q0s=q0[rows,:]*0.125
        qa_s[e]=heads_apart(q0s,8).astype(BF)
        nlow=norm(p1[rows,:],vv(e)[3:4],vv(e)[4:5])
        for c in range(6): ls[e,c,8:16,:]=a0[rows,128*c:128*c+128]
        for half in (0,1):
            rs[half,rows,0:768]=nlow; rs[half,rows,768:1152]=q0s[:,384*half:384*half+384]
    rb[:,:,0:1152]=rs[:,:,0:1152].astype(BF)
    rg=RightGather(pos,rb,rbuf,rsend,rrecv)
    rg.step(0,0)
    need("kp","xp")
    for i in range(2): early_block(1,i,pln,kv_p.at[0],kv_p.at[1],qa_s,P_s,ls)
    hg.phase(1)
    rg.step(0,1)
    for i in range(2,6): early_block(1,i,pln,kv_p.at[0],kv_p.at[1],qa_s,P_s,ls)
    hg.phase(2)
    need("kq","xq")
    for i in range(2): early_block(0,i,ql,kv_q.at[0],kv_q.at[1],qa_s,P_s,ls)
    early_messages(ls,left_e)
    hg.phase(3)
    rg.step(0,2)
    ec=LeftCopies(pos,left_e,ebuf,EARLY,esend,erecv)
    for k in range(4): ec.start(k)
    similarity(pos,hbuf,marks,loss,gr,gs_s,gt_s)
    rg.step(0,3)
    g2,sums,gn={}, {}, {}
    need("dn1","dn0")
    for e in (1,0):
        rows=slice(8*e,8*e+8)
        g2[e],gain2,shift2=norm_grad(p2[rows,:],vv(e)[6:7],gr[rows,:])
        gffn=g2[e].astype(BF).astype(F32)
        for half in (0,1): rs[half,rows,1152:1920]=gffn
        sums[e]=(colsum(gffn),gain2,shift2)
    rb[:,:,1152:1920]=rs[:,:,1152:1920].astype(BF)
    rg.step(1,0); rg.step(2,0)
    need("up1","up0")
    for e in (1,0):
        gh=(dot_nt(g2[e].astype(BF),w_dn[e])*gelu_slope(h0[8*e:8*e+8,:])).astype(BF)
        lb[e,0:1,:]=colsum(gh)
        gn[e]=g2[e]+dot_nt(gh,w_up[e])
    rg.step(1,1); rg.step(2,1); rg.step(0,4)
    need("o1","o0","qkv1","qkv0","vp","vq")
    g1,sums1={}, {}
    for e in (1,0):
        rows=slice(8*e,8*e+8)
        g1[e],gain1,shift1=norm_grad(p1[rows,:],vv(e)[3:4],gn[e])
        gb=g1[e].astype(BF)
        sums1[e]=(colsum(gb),gain1,shift1)
        ga=dot_nt(gb,w_o[e]).astype(BF).astype(F32)
        ga_s[e]=heads_apart(ga,8).astype(BF)
        for half in (0,1): rs[half,rows,1920:2304]=gb[:,384*half:384*half+384].astype(F32)
        rs[1,rows,2304:3072]=ga
    rg.step(1,2); rg.step(2,2)
    for i in range(0,3): late_block(1,i,kv_p.at[0],kv_p.at[2],kv_p.at[1],ga_s,P_s,ll,gq_s,sv_s,tp)
    rg.step(1,3); rg.step(2,3); rg.step(0,5)
    for i in range(3,6): late_block(1,i,kv_p.at[0],kv_p.at[2],kv_p.at[1],ga_s,P_s,ll,gq_s,sv_s,tp)
    rg.step(1,4); rg.step(2,4)
    for i in range(2): late_block(0,i,kv_q.at[0],kv_q.at[2],kv_q.at[1],ga_s,P_s,ll,gq_s,sv_s,tq)
    for e in (1,0):
        rows=slice(8*e,8*e+8)
        gql=gq_s[e].astype(BF)
        rs[0,rows,2304:3072]=gql.astype(F32)
        vs=jnp.concatenate([colsum(gql),sv_s[e,0:1],*sums1[e],*sums[e]],axis=0)
        for c in range(6): ll[e,c,96:104,:]=vs[:,128*c:128*c+128]
    rb[:,:,1920:3072]=rs[:,:,1920:3072].astype(BF)
    rg.step(3,0); rg.step(4,0)
    late_messages(ll,lb,stage,left_l)
    rg.step(3,1); rg.step(4,1)
    lc=LeftCopies(pos,left_l,lbuf,LATE,lsend,lrecv)
    lc.start(1); lc.start(3)
    def back_weights(e):
        uk=dot_nt(qa_s[e],w_qkv[e,:,768:1536]).astype(BF); uv=dot_nt(ga_s[e],w_qkv[e,:,1536:2304]).astype(BF)
        out=(uq,up_)[e]; R=16*256//SLOTS[e]
        for i in range(NB[e]):
            out[i,0:R,:]=uk[i*R:i*R+R]; out[i,R:2*R,:]=uv[i*R:i*R+R]
        extra[8*e:8*e+8,:]=g1[e]+dot_nt(gq_s[e].astype(BF),w_qkv[e,:,0:768])
    back_weights(1)
    rg.step(3,2); rg.step(4,2)
    lc.start(2)
    back_weights(0)
    rg.step(1,5); rg.step(2,5)
    rg.step(3,3); rg.step(4,3)
    lc.start(0)
    rg.step(0,6); rg.step(1,6); rg.step(2,6)
    pr=Products(pos,ebuf,lbuf,rbuf,bq,bp,wqkv,wout,win,wback,gvec,gbin,w_up,w_dn,hb)
    pr.right(0,1920)
    rg.step(3,4); rg.step(4,4)
    pr.feed_forward(1)
    rg.step(3,5); rg.step(4,5)
    pr.feed_forward(0)
    rg.step(3,6); rg.step(4,6)
    pr.right(1920,1152)
    ec.finish()
    pr.second()
    lc.finish()
    pr.third()

def tail_call(*a):
    S=jax.ShapeDtypeStruct; VM=pltpu.VMEM; D=pltpu.SemaphoreType.DMA
    V=pl.BlockSpec(memory_space=pltpu.VMEM); SM=pl.BlockSpec(memory_space=pltpu.SMEM); A=pl.BlockSpec(memory_space=pl.ANY)
    outs=[S((1,1),F32),S((2,128,256),BF),S((6,32,256),BF),S((2,128,768),BF),S((6,32,768),BF),S((16,768),F32),
          S((2,48,1152),F32),S((2,48,384),F32),S((2,48,1536),F32),S((2,192,384),F32),S((2,4,48),F32),S((2,96),F32)]
    scratch=[VM((3,512,768),BF),VM((3,1536,768),BF),VM((2,768,2304),BF),VM((2,768,768),BF),VM((2,768,3072),BF),VM((2,3072,768),BF),
      VM((4,2,2,2,16,768),BF),VM((16,768),F32),VM((256,256),F32),VM((256,256),F32),VM((2,128,768),BF),VM((2,128,768),BF),VM((224,256),F32),
      VM((2,6,112,128),F32),VM((2,6,112,128),F32),VM((2,8,3072),F32),VM((16,8,128),F32),VM((16,112,128),BF),VM((16,112,128),BF),
      VM((32,112,128),BF),VM((32,64,128),BF),VM((2,16,3072),F32),VM((2,16,3072),BF),VM((4,2,2,2,16,3072),BF),VM((256,3072),BF),VM((256,3072),BF),VM((2,8,768),F32),VM((2,8,768),F32),
      D((14,)),D((10,)),D((10,)),D((32,)),D((32,)),D((32,)),D((32,)),D((5,17)),D((5,17))]
    return pl.pallas_call(tail_kernel,out_shape=outs,in_specs=[SM,SM]+[A]*10+[V]*9,out_specs=[SM]+[V]*11,scratch_shapes=scratch,
      compiler_params=pltpu.CompilerParams(collective_id=2,has_side_effects=True,vmem_limit_bytes=62*2**20),name="tail")(*a)

def finish_kernel(loss_in,q_in,p_in,wqkv_in,wout_in,win_in,wback_in,gvec_in,gbin_in,tq,tp,uq,up_,extra,
                  loss,q_out,p_out,gq,gp,wqkv,wout,win,wback,gvec,gbin,slots,sem,osem,*held):
    ways=((p_in,p_out),(q_in,q_out),(win_in,win),(wqkv_in,wqkv),(wback_in,wback),(wout_in,wout))
    loads=[pltpu.make_async_copy(a,h,sem.at[0,k]) for k,((a,b),h) in enumerate(zip(ways,held))]
    stores=[pltpu.make_async_copy(h,b,sem.at[1,k]) for k,((a,b),h) in enumerate(zip(ways,held))]
    for cp in loads: cp.start()
    loss[0,0]=loss_in[0,0]
    gvec[...]=gvec_in[...]; gbin[...]=gbin_in[...]
    flying={}
    for b in range(8):
        e,i=(1,b) if b<6 else (0,b-6)
        mix,u,out=((tq,uq,gq),(tp,up_,gp))[e]
        slot=b%4
        if slot in flying: flying[slot].wait()
        slots[slot]=dot(mix[i].astype(F32).T.astype(BF),u[i])
        n=256//SLOTS[e]
        for j in range(n): slots[slot,j*SLOTS[e]:j*SLOTS[e]+1,:]+=extra[8*e+i*n+j:8*e+i*n+j+1,:]
        flying[slot]=pltpu.make_async_copy(slots.at[slot],out.at[pl.ds(i*256,256)],osem.at[slot])
        flying[slot].start()
        if 1<=b<=6:
            loads[b-1].wait(); stores[b-1].start()
    for cp in flying.values(): cp.wait()
    for cp in stores: cp.wait()
def finish_call(loss,q_out,p_out,grads,tq,tp,uq,up_,extra):
    S=jax.ShapeDtypeStruct; VM=pltpu.VMEM; D=pltpu.SemaphoreType.DMA
    V=pl.BlockSpec(memory_space=pltpu.VMEM); SM=pl.BlockSpec(memory_space=pltpu.SMEM); A=pl.BlockSpec(memory_space=pl.ANY)
    ins=(loss,q_out,p_out,*grads,tq,tp,uq,up_,extra)
    shape=lambda a: S(a.shape,a.dtype)
    outs=[shape(loss),shape(q_out),shape(p_out),S(q_out.shape,F32),S(p_out.shape,F32)]+[shape(g) for g in grads]
    return pl.pallas_call(finish_kernel,out_shape=outs,in_specs=[SM]+[A]*6+[V]*7,out_specs=[SM]+[A]*8+[V]*2,
      scratch_shapes=[VM((4,256,768),F32),D((2,6)),D((4,))]+[VM(a.shape,a.dtype) for a in (p_out,q_out,grads[2],grads[0],grads[3],grads[1])],compiler_params=pltpu.CompilerParams(vmem_limit_bytes=63*2**20),name="finish")(*ins)

STEP, LOAD, P1, P2, P3, P4 = range(6)
NEEDS={P1:0,P2:1,P3:2,P4:3}

def spread_small(tiles, vec, hb):
    r=lax.broadcasted_iota(jnp.int32,(128,256),0); l=lax.broadcasted_iota(jnp.int32,(128,256),1)
    r4=lax.broadcasted_iota(jnp.int32,(128,384),0); l4=lax.broadcasted_iota(jnp.int32,(128,384),1)
    vec[...]=jnp.zeros_like(vec); hb[...]=jnp.zeros_like(hb)
    for w in range(16):
        for y in range(2):
            t=tiles[w//4,(w//2)%2,(w%2)*16:(w%2)*16+16,y*128:y*128+128]
            c=min(48*w//128*128,512); off=48*w-c
            v=dot(t,jnp.where((l-off==r)&(r<48),1.0,0.0).astype(BF))
            for e in (0,1): vec[e,4*y:4*y+4,c:c+256]+=v[4*e:4*e+4]
            c=min((192*w+96*y)//128*128,3072-384); off=192*w+96*y-c
            h=dot(t,jnp.where((l4-off==r4)&(r4<96),1.0,0.0).astype(BF))
            for e in (0,1): hb[e,0:1,c:c+384]+=h[8+e:9+e]

def own_tiles(vectors, hidden_bias, q_set, gold, p_set, stage, small, marks):
    stage[...]=jnp.zeros_like(stage)
    for e in (0,1):
        stage[4*e:4*e+4,0:48]=vectors[e].astype(F32)
        stage[8+e:9+e,0:96]=hidden_bias[e:e+1,:].astype(F32)
    small[0]=stage[...].astype(BF)
    me=lax.axis_index("wq")*2+lax.axis_index("np")
    r=lax.broadcasted_iota(jnp.int32,(16,128),0); place=(r%2)*128+lax.broadcasted_iota(jnp.int32,(16,128),1)-me*8
    count=p_set.shape[0]
    tile=jnp.zeros((16,128),jnp.int32)
    for k in range(8):
        here=place==k
        tile=jnp.where(here&(r//2==0),q_set[k],tile)
        tile=jnp.where(here&(r//2==1),gold[k]//count*8+gold[k]%count,tile)
        tile=jnp.where(here&(r//2==2),p_set[k] if k<count else -1,tile)
    marks[0]=tile

def fused_kernel(units, plan, *refs):
    (ql,pln,q_set,gold,p_set,qx_h,px_h,vectors,hidden_bias)=refs[0:9]; ins=list(refs[9:13]); outs=refs[13:19]
    vec,hb,qo_h,po_h,qk_h,qv_h,pk_h,pv_h,q0,a0,p1,h0,p2,hd=refs[19:33]
    wv=refs[33:37]; qx,px,qo,po,qk,qv,pk,pv,stage,small_src,mark_src,small,bias,att,nrm,act,send,recv,lsem,xsem=refs[37:]
    moves={}
    def move(name,src,dst):
        moves[name]=pltpu.make_async_copy(src,dst,xsem.at[len(moves)]); moves[name].start()
    move("x1",px_h,px); move("x0",qx_h,qx)
    own_tiles(vectors,hidden_bias,q_set,gold,p_set,stage,small_src,mark_src)
    ins+=[small_src,mark_src]
    g=Gather(units,ins,outs,send,recv)
    g.barrier()
    for ref in (q0,a0,p1,h0,p2,hd): ref[...]=jnp.zeros_like(ref)
    X=(qx,px); O=(qo,po); K=(qk,pk); V=(qv,pv); LENS=(ql,pln); SLOTS=(64,256); BASE=(0,512); NB=(2,6)
    HBM=((qk_h,qv_h,qo_h),(pk_h,pv_h,po_h))
    loaded=set()
    def load_copies(a,e):
        if a==5: return []
        if a==4: return [pltpu.make_async_copy(outs[4].at[0],small,lsem.at[a,e,0])]
        rows=outs[a].shape[3]
        return [pltpu.make_async_copy(outs[a].at[e,k//2,k%2],wv[a].at[e,pl.ds(k*rows,rows)],lsem.at[a,e,k]) for k in range(8)]
    def need(a,e):
        if (a,e) in loaded: return
        loaded.add((a,e))
        for cp in load_copies(a,e): cp.wait()
        if a==4: spread_small(small,vec,hb)
        if a==0: moves["x%d"%e].wait()
    for item in plan:
        if item[0]==STEP: g.step(item[1],item[2])
        elif item[0]==LOAD:
            for cp in load_copies(*item[1:]): cp.start()
        else:
            kind,e,lo,hi=item
            need(4,0); need(NEEDS[kind],e)
            n=256//SLOTS[e]
            A=att.at[pl.ds(BASE[e],NB[e]*BLK)]; N=nrm.at[pl.ds(BASE[e],NB[e]*BLK)]
            def body(i,kept):
                row=pl.multiple_of(i*BLK,BLK)
                if kind==P1:
                    make_bias(bias,0,[LENS[e][i*n+j] for j in range(n)],SLOTS[e])
                    attend_block(row,X[e],wv[0].at[e],vec.at[e],bias,K[e],V[e],A,q0,e,i)
                if kind==P2: out_block(row,X[e],A,wv[1].at[e],vec.at[e],N,a0,p1,e,i)
                if kind==P3: up_block(row,N,wv[2].at[e],hb.at[e],act,h0,e,i,row)
                if kind==P4: down_block(row,N,act,wv[3].at[e],vec.at[e],O[e],p2,hd,e,i,row)
                return kept
            if hi-lo==1: body(lo,0)
            else: lax.fori_loop(lo,hi,body,0)
            if hi==NB[e]:
                if kind==P1:
                    move("k%d"%e,K[e],HBM[e][0]); move("v%d"%e,V[e],HBM[e][1])
                if kind==P4: move("o%d"%e,O[e],HBM[e][2])
    for name in moves:
        if name[0]!="x": moves[name].wait()

def fused_call(ql,pln,q_set,gold,p_set,qx,px,vectors,hidden_bias,arrays,units,plan):
    S=jax.ShapeDtypeStruct; VM=pltpu.VMEM; D=pltpu.SemaphoreType.DMA
    V=pl.BlockSpec(memory_space=pltpu.VMEM); SM=pl.BlockSpec(memory_space=pltpu.SMEM); A=pl.BlockSpec(memory_space=pl.ANY)
    outs=[S((a.shape[0],4,2,2*a.shape[1],2*a.shape[2]),a.dtype) for a in arrays]+[S((1,4,2,32,256),BF),S((1,4,2,32,256),jnp.int32)]
    outs+=[S((2,8,768),F32),S((2,1,3072),F32),S(qx.shape,BF),S(px.shape,BF),S(qx.shape,BF),S(qx.shape,BF),S(px.shape,BF),S(px.shape,BF),S((16,768),F32),S((16,768),F32),S((16,768),F32),S((16,3072),F32),S((16,768),F32),S((16,768),F32)]
    big=[VM(qx.shape,BF),VM(px.shape,BF)]+[VM(qx.shape,BF),VM(px.shape,BF)]+[VM(qx.shape,BF)]*2+[VM(px.shape,BF)]*2
    return pl.pallas_call(functools.partial(fused_kernel,units,plan),out_shape=outs,in_specs=[SM]*5+[A,A,V,V]+[A]*4,out_specs=[A]*6+[V,V]+[A]*6+[V]*6,
      scratch_shapes=[VM((2,768,2304),BF),VM((2,768,768),BF),VM((2,768,3072),BF),VM((2,3072,768),BF)]+big+[VM((16,128),F32),VM((1,16,128),BF),VM((1,16,128),jnp.int32),VM((4,2,32,256),BF),VM((256,256),F32),VM((2048,768),BF),VM((2048,768),F32),VM((1536,3072),BF),D((len(units),18)),D((len(units),18)),D((6,2,8)),D((8,))],
      compiler_params=pltpu.CompilerParams(collective_id=1,has_side_effects=True,vmem_limit_bytes=63*2**20),name="fused")(ql,pln,q_set,gold,p_set,qx,px,vectors,hidden_bias,*arrays)


GATHER_UNITS = (
    (4, 0, False, 0, 16), (5, 0, False, 0, 16), (0, 1, False, 0, 16), (0, 1, False, 16, 16),
    (0, 1, False, 32, 16), (1, 1, True, 0, 16), (1, 1, True, 16, 16), (1, 1, True, 32, 16),
    (0, 0, False, 0, 48), (2, 1, False, 0, 48), (1, 0, True, 0, 48), (3, 1, True, 0, 64),
    (3, 1, True, 64, 64), (3, 1, True, 128, 64), (2, 0, True, 0, 48), (3, 0, True, 0, 64),
    (3, 0, True, 64, 64), (3, 0, True, 128, 64),
)
GATHER_PLAN = (
    (STEP, 0, 0), (STEP, 1, 0), (STEP, 2, 0), (STEP, 3, 0), (STEP, 4, 0), (STEP, 5, 0),
    (STEP, 6, 0), (STEP, 7, 0), (STEP, 0, 1), (STEP, 1, 1), (STEP, 2, 1), (STEP, 5, 1),
    (STEP, 3, 1), (STEP, 0, 2), (STEP, 6, 1), (STEP, 7, 1), (STEP, 1, 2), (STEP, 4, 1),
    (STEP, 2, 2), (STEP, 5, 2), (STEP, 0, 3), (STEP, 3, 2), (STEP, 6, 2), (STEP, 1, 3),
    (STEP, 7, 2), (STEP, 0, 4), (STEP, 4, 2), (STEP, 2, 3), (STEP, 1, 4), (STEP, 5, 3),
    (STEP, 0, 5), (STEP, 8, 0), (STEP, 3, 3), (STEP, 6, 3), (STEP, 0, 6), (LOAD, 4, 0),
    (STEP, 7, 3), (STEP, 2, 4), (STEP, 4, 3), (STEP, 5, 4), (STEP, 1, 5), (STEP, 9, 0),
    (STEP, 1, 6), (LOAD, 5, 0), (STEP, 3, 4), (STEP, 8, 1), (STEP, 6, 4), (STEP, 7, 4),
    (STEP, 2, 5), (STEP, 10, 0), (STEP, 2, 6), (STEP, 4, 4), (STEP, 9, 1), (STEP, 5, 5),
    (STEP, 11, 0), (STEP, 5, 6), (STEP, 8, 2), (STEP, 3, 5), (STEP, 12, 0), (STEP, 6, 5),
    (STEP, 13, 0), (STEP, 3, 6), (STEP, 9, 2), (STEP, 7, 5), (STEP, 14, 0), (STEP, 6, 6),
    (STEP, 10, 1), (STEP, 7, 6), (LOAD, 1, 1), (STEP, 8, 3), (STEP, 4, 5), (STEP, 15, 0),
    (STEP, 11, 1), (STEP, 12, 1), (STEP, 9, 3), (STEP, 4, 6), (LOAD, 0, 1), (STEP, 13, 1),
    (STEP, 10, 2), (STEP, 14, 1), (STEP, 11, 2), (P1, 1, 0, 1), (STEP, 8, 4), (STEP, 12, 2),
    (STEP, 15, 1), (STEP, 13, 2), (P1, 1, 1, 2), (STEP, 10, 3), (STEP, 9, 4), (P1, 1, 2, 3),
    (STEP, 14, 2), (STEP, 11, 3), (P1, 1, 3, 4), (STEP, 12, 3), (STEP, 8, 5), (STEP, 16, 0),
    (STEP, 15, 2), (P1, 1, 4, 5), (STEP, 8, 6), (LOAD, 0, 0), (STEP, 13, 3), (STEP, 10, 4),
    (P1, 1, 5, 6), (STEP, 14, 3), (P1, 0, 0, 1), (STEP, 9, 5), (STEP, 17, 0), (STEP, 11, 4),
    (STEP, 12, 4), (STEP, 16, 1), (P1, 0, 1, 2), (STEP, 10, 5), (STEP, 9, 6), (LOAD, 2, 1),
    (STEP, 15, 3), (STEP, 17, 1), (STEP, 13, 4), (P2, 1, 0, 1), (STEP, 10, 6), (LOAD, 1, 0),
    (STEP, 11, 5), (P2, 1, 1, 4), (STEP, 11, 6), (P2, 1, 4, 6), (STEP, 12, 5), (STEP, 14, 4),
    (P2, 0, 0, 2), (STEP, 12, 6), (STEP, 16, 2), (P3, 1, 0, 1), (P3, 1, 1, 2), (STEP, 13, 5),
    (STEP, 15, 4), (P3, 1, 2, 3), (STEP, 13, 6), (LOAD, 3, 1), (STEP, 17, 2), (STEP, 16, 3),
    (P3, 1, 3, 4), (P3, 1, 4, 5), (STEP, 17, 3), (P3, 1, 5, 6), (P4, 1, 0, 2), (STEP, 14, 5),
    (STEP, 16, 4), (STEP, 17, 4), (P4, 1, 2, 4), (STEP, 14, 6), (LOAD, 2, 0), (P4, 1, 4, 5),
    (STEP, 15, 5), (P4, 1, 5, 6), (P3, 0, 0, 1), (STEP, 15, 6), (STEP, 16, 5), (P3, 0, 1, 2),
    (STEP, 16, 6), (STEP, 17, 5), (STEP, 17, 6), (LOAD, 3, 0), (P4, 0, 0, 2),
)


def kernel_shards(
    q_embed, p_embed, q_len, p_len, q_set, p_set, gold, wqkv, wout, wup, wdown, vectors, hidden_bias
):
    arrays = (wqkv, wout, wup, wdown)
    done = fused_call(
        q_len, p_len, q_set, gold, p_set, q_embed, p_embed, vectors, hidden_bias, arrays, GATHER_UNITS, GATHER_PLAN
    )
    weights = tuple(
        member.reshape(2, 16 * shard.shape[1], 2 * shard.shape[2])
        for member, shard in zip(done[:4], arrays)
    )
    vec, bias, q_out, p_out, q_keys, q_values, p_keys, p_values, q0, a0, p1, h0, p2, heads = done[6:]
    loss, tq, tp, uq, up, extra, *grads = tail_call(
        q_len, p_len, q_embed, p_embed, q_keys, q_values, p_keys, p_values, *weights,
        q0, a0, p1, h0, p2, heads, done[5], vec, bias,
    )
    loss, *rest = finish_call(loss, q_out, p_out, grads, tq, tp, uq, up, extra)
    return (loss[0, 0], *rest)


def kernels_fit(q_embed, p_embed, q_len, p_len):
    return (
        lax.axis_size("wq") == 16
        and lax.axis_size("np") == 2
        and q_embed.shape == (512, 768)
        and p_embed.shape == (1536, 768)
        and q_len.shape == (8,)
        and p_len.shape == (6,)
    )


def shards(
    q_embed,
    p_embed,
    q_len,
    p_len,
    q_set,
    p_set,
    gold,
    query_key_value_weight,
    attention_output_weight,
    up_weight,
    down_weight,
    vectors,
    hidden_bias,
):
    if kernels_fit(q_embed, p_embed, q_len, p_len):
        return kernel_shards(
            q_embed,
            p_embed,
            q_len,
            p_len,
            q_set,
            p_set,
            gold,
            query_key_value_weight,
            attention_output_weight,
            up_weight,
            down_weight,
            vectors,
            hidden_bias,
        )
    gathered = gather_weights(
        query_key_value_weight,
        attention_output_weight,
        up_weight,
        down_weight,
        vectors,
        hidden_bias,
    )
    wq_size, np_size = lax.axis_size("wq"), lax.axis_size("np")
    both_axes = ("wq", "np")
    q_weights = tuple((member[0] for member in gathered))
    p_weights = tuple((member[1] for member in gathered))
    p_encoded, p_stored = encode_forward(p_embed, p_len, p_weights)
    q_encoded, q_stored = encode_forward(q_embed, q_len, q_weights)
    model_width = q_embed.shape[1]
    ff_width = gathered[2].shape[2]
    q_count = q_len.shape[0]
    p_count = p_len.shape[0]
    own_heads = jnp.concatenate([first_rows(q_encoded, q_count), first_rows(p_encoded, p_count)])
    heads = lax.all_gather(own_heads, both_axes, axis=0)
    marks = lax.all_gather(jnp.concatenate([q_set, gold, p_set]), both_axes, axis=0)
    q_heads = heads[:, :q_count].reshape(-1, model_width)
    p_heads = heads[:, q_count:].reshape(-1, model_width)
    q_sets = marks[:, :q_count].reshape(-1)
    golds = marks[:, q_count : 2 * q_count].reshape(-1)
    p_sets = marks[:, 2 * q_count :].reshape(-1)
    scaling = model_width ** (-0.5)
    similar = (
        jnp.einsum("qd,pd->qp", q_heads, p_heads, preferred_element_type=jnp.float32) * scaling
    )
    is_gold = jnp.arange(p_heads.shape[0], dtype=jnp.int32)[None, :] == golds[:, None]
    usable = (q_sets[:, None] == p_sets[None, :]) | is_gold
    masked = jnp.where(usable, similar, NEGATIVE)
    highest = jnp.max(masked, axis=1)
    total = jnp.sum(jnp.where(usable, jnp.exp(masked - highest[:, None]), 0.0), axis=1)
    log_total = highest + jnp.log(total)
    gold_score = jnp.sum(jnp.where(is_gold, similar, 0.0), axis=1)
    loss = jnp.mean(log_total - gold_score)
    soft_rows = jnp.where(usable, jnp.exp(masked - log_total[:, None]), 0.0)
    grad_similar = (soft_rows - is_gold.astype(jnp.float32)).astype(jnp.bfloat16)
    me = lax.axis_index("wq") * np_size + lax.axis_index("np")
    grad_q_first = (
        jnp.einsum(
            "qp,pd->qd",
            lax.dynamic_slice_in_dim(grad_similar, me * q_count, q_count, 0),
            p_heads,
            preferred_element_type=jnp.float32,
        )
        * scaling
    )
    grad_p_first = (
        jnp.einsum(
            "qp,qd->pd",
            lax.dynamic_slice_in_dim(grad_similar, me * p_count, p_count, 1),
            q_heads,
            preferred_element_type=jnp.float32,
        )
        * scaling
    )
    q_back = encode_backward(q_embed, q_weights, q_stored, grad_q_first)
    p_back = encode_backward(p_embed, p_weights, p_stored, grad_p_first)
    left = jnp.concatenate(
        [left_message(member[1], wq_size, np_size) for member in (q_back, p_back)], axis=2
    )
    left = left.reshape((wq_size * np_size,) + left.shape[2:])
    left = lax.all_to_all(left, both_axes, 0, 0)
    right = jnp.concatenate([right_message(member[2], np_size) for member in (q_back, p_back)], axis=1)
    right = lax.all_gather(lax.all_to_all(right, "np", 0, 0), "wq", axis=0)
    right = right.reshape((wq_size * np_size,) + right.shape[2:])
    sums = jnp.concatenate(
        [
            jnp.stack([q_back[3], p_back[3]])
            .reshape(2, np_size, -1, wq_size, model_width // wq_size)
            .transpose(3, 1, 0, 2, 4)
            .reshape(wq_size * np_size, -1),
            jnp.stack([q_back[4], p_back[4]])
            .reshape(2, wq_size * np_size, -1)
            .transpose(1, 0, 2)
            .reshape(wq_size * np_size, -1),
        ],
        axis=1,
    )
    sums = jnp.sum(lax.all_to_all(sums, both_axes, 0, 0), axis=0)
    grad_vectors = sums[: sums.shape[0] - 2 * ff_width // (wq_size * np_size)].reshape(
        2, -1, model_width // wq_size
    )
    grad_b_in = sums[sums.shape[0] - 2 * ff_width // (wq_size * np_size) :].reshape(2, -1)
    q_weight_grads = weight_grads(
        left[:, :q_count].reshape(-1, left.shape[2]),
        right[:, :q_count].reshape(-1, right.shape[2]),
        model_width,
        ff_width,
        wq_size,
        np_size,
    )
    p_weight_grads = weight_grads(
        left[:, q_count:].reshape(-1, left.shape[2]),
        right[:, q_count:].reshape(-1, right.shape[2]),
        model_width,
        ff_width,
        wq_size,
        np_size,
    )
    shared = tuple(jnp.stack(pair) for pair in zip(q_weight_grads, p_weight_grads))
    return (
        loss,
        q_encoded,
        p_encoded,
        q_back[0],
        p_back[0],
        shared[0],
        shared[1],
        shared[2],
        shared[3],
        grad_vectors,
        grad_b_in,
    )


def solution(mesh):
    return jax.shard_map(
        shards,
        mesh=mesh,
        in_specs=(
            P(("wq", "np"), None),
            P(("wq", "np"), None),
            P(("wq", "np")),
            P(("wq", "np")),
            P(("wq", "np")),
            P(("wq", "np")),
            P(("wq", "np")),
            P(None, "wq", "np"),
            P(None, "wq", "np"),
            P(None, "wq", "np"),
            P(None, "wq", "np"),
            P(None, "np", "wq"),
            P(None, ("wq", "np")),
        ),
        out_specs=(
            P(),
            P(("wq", "np"), None),
            P(("wq", "np"), None),
            P(("wq", "np"), None),
            P(("wq", "np"), None),
            P(None, "wq", "np"),
            P(None, "wq", "np"),
            P(None, "wq", "np"),
            P(None, "wq", "np"),
            P(None, "np", "wq"),
            P(None, ("wq", "np")),
        ),
        check_vma=False,
    )
```
